32 devices in a mesh: dp: 4 (over z), seq: 8 (over y, x, core).
Axes of the slice: x: 2, y: 2, z: 4, core: 2. Of those that a mesh axis runs over, the one named last changes fastest.
Arguments:
- hidden_in: bfloat16 [4, 1024, 2048], P('dp', 'seq'), may hold values from -6 to 6
- segment_ids: int32 [4, 1024], P('dp', 'seq'), may hold values from 0 to 7, as said below
- position_ids: int32 [4, 1024], P('dp', 'seq'), may hold values from 0 to 1023, as said below
- w_qkv: bfloat16 [2048, 6144], P(('dp', 'seq')), may hold values from -0.125 to 0.125
- w_out: bfloat16 [2048, 2048], P(('dp', 'seq')), may hold values from -0.125 to 0.125
- w_up: bfloat16 [2048, 8192], P(None, ('dp', 'seq')), may hold values from -0.125 to 0.125
- w_down: bfloat16 [8192, 2048], P(('dp', 'seq')), may hold values from -0.0625 to 0.0625
- gain_attn: bfloat16 [2048], P(('dp', 'seq')), may hold values from 0.25 to 1.75
- gain_attn_sub: bfloat16 [2048], P(('dp', 'seq')), may hold values from 0.25 to 1.75
- gain_ffn: bfloat16 [2048], P(('dp', 'seq')), may hold values from 0.25 to 1.75
- gain_ffn_sub: bfloat16 [8192], P(('dp', 'seq')), may hold values from 0.25 to 1.75
- ema_qkv: float32 [2048, 6144], P(('dp', 'seq')), may hold values from -0.125 to 0.125
- ema_out: float32 [2048, 2048], P(('dp', 'seq')), may hold values from -0.125 to 0.125
- ema_up: float32 [2048, 8192], P(None, ('dp', 'seq')), may hold values from -0.125 to 0.125
- ema_down: float32 [8192, 2048], P(('dp', 'seq')), may hold values from -0.0625 to 0.0625
- ema_gain_attn: float32 [2048], P(('dp', 'seq')), may hold values from 0.3 to 1.7
- ema_gain_attn_sub: float32 [2048], P(('dp', 'seq')), may hold values from 0.3 to 1.7
- ema_gain_ffn: float32 [2048], P(('dp', 'seq')), may hold values from 0.3 to 1.7
- ema_gain_ffn_sub: float32 [8192], P(('dp', 'seq')), may hold values from 0.3 to 1.7
- out_grad: bfloat16 [4, 1024, 2048], P('dp', 'seq'), may hold values from -6 to 6
Outputs:
- output: bfloat16 [4, 1024, 2048], P('dp', 'seq')
- input_grad: bfloat16 [4, 1024, 2048], P('dp', 'seq')
- grad_w_qkv: float32 [2048, 6144], P(('dp', 'seq'))
- grad_w_out: float32 [2048, 2048], P(('dp', 'seq'))
- grad_w_up: float32 [2048, 8192], P(None, ('dp', 'seq'))
- grad_w_down: float32 [8192, 2048], P(('dp', 'seq'))
- grad_gain_attn: float32 [2048], P(('dp', 'seq'))
- grad_gain_attn_sub: float32 [2048], P(('dp', 'seq'))
- grad_gain_ffn: float32 [2048], P(('dp', 'seq'))
- grad_gain_ffn_sub: float32 [8192], P(('dp', 'seq'))
- new_ema_qkv: float32 [2048, 6144], P(('dp', 'seq'))
- new_ema_out: float32 [2048, 2048], P(('dp', 'seq'))
- new_ema_up: float32 [2048, 8192], P(None, ('dp', 'seq'))
- new_ema_down: float32 [8192, 2048], P(('dp', 'seq'))
- new_ema_gain_attn: float32 [2048], P(('dp', 'seq'))
- new_ema_gain_attn_sub: float32 [2048], P(('dp', 'seq'))
- new_ema_gain_ffn: float32 [2048], P(('dp', 'seq'))
- new_ema_gain_ffn_sub: float32 [8192], P(('dp', 'seq'))
The draws below stay inside these ranges and needn't reach their ends.
Inputs may be any that keep to these rules, and one draw needn't show every extreme that they name: Along each row segment_ids start at 0 and rise by 0 or 1 from one token to the next, so that every document is a run of consecutive tokens. The first row is one document; every other row holds 8 documents. position_ids is each token's offset from the first token of its document (0 at the row's first token and wherever segment_ids rises).
All inputs are finite; a program needn't handle non-finite values.
Results may differ from the reference program's by a relative error of at most 0.02.
Values may be sent and summed in bfloat16 or wider, within the bound.
A program may use at most 256 MiB of HBM per device.

```python
import math
import jax
import jax.numpy as jnp
from jax import lax

D = 2048
HEADS = 32
HD = 64
FF = 8192
ROWS = 4
LENGTH = 1024


def doc_layout(key):
    row_keys = jax.random.split(jax.random.fold_in(key, 11), ROWS)
    picks = jax.vmap(lambda row_key: jax.random.permutation(row_key, LENGTH - 1)[:7])(row_keys) + 1
    column = jnp.broadcast_to(jnp.arange(LENGTH, dtype=jnp.int32)[None, :], (ROWS, LENGTH))
    picked = jnp.any(column[:, :, None] == picks[:, None, :], axis=2)
    row_index = jnp.arange(ROWS, dtype=jnp.int32)[:, None]
    starts = picked & (row_index > 0) | (column == 0)
    segment = jnp.cumsum(starts.astype(jnp.int32), axis=1) - 1
    first_at = lax.cummax(jnp.where(starts, column, 0), axis=1)
    return (segment.astype(jnp.int32), (column - first_at).astype(jnp.int32))


def draw_segment_ids(key, part):
    return doc_layout(key)[0]


def draw_position_ids(key, part):
    return doc_layout(key)[1]


def steps_of(rng, extent, cuts, low, top_value):
    gain, own = 1.0, jax.random.fold_in(rng, 6)
    for axis_at, parts in cuts:
        draws = jnp.exp(jax.random.uniform(jax.random.fold_in(own, axis_at), (parts,), jnp.float32, low / len(cuts), top_value / len(cuts)))
        gain = gain * jnp.repeat(draws, extent[axis_at] // parts).reshape([-1 if axis == axis_at else 1 for axis in range(len(extent))])
    return gain


def noise(stream_key, dims, deviation, limit, cuts=(), kind=jnp.bfloat16):
    loudness = steps_of(stream_key, dims, cuts, -0.22, 0.18) if cuts else 1.0
    values = jax.random.normal(stream_key, dims, jnp.float32) * deviation * loudness
    return jnp.minimum(jnp.maximum(values, -limit), limit).astype(kind)


def setup_inputs(seed: int = 0) -> dict:
    streams_of = jax.random.split(jax.random.key(seed), 21)
    return {
        "hidden_in": noise(streams_of[0], (ROWS, LENGTH, D), 1.0, 6.0, ((0, 4), (1, 8))),
        "segment_ids": draw_segment_ids(jax.random.fold_in(streams_of[20], 71), 0),
        "position_ids": draw_position_ids(jax.random.fold_in(streams_of[20], 71), 0),
        "w_qkv": noise(streams_of[3], (D, 3 * D), D ** -0.5, 0.125, ((0, 32),)),
        "w_out": noise(streams_of[4], (D, D), D ** -0.5, 0.125, ((0, 32),)),
        "w_up": noise(streams_of[5], (D, FF), D ** -0.5, 0.125, ((1, 32),)),
        "w_down": noise(streams_of[6], (FF, D), FF ** -0.5, 0.0625, ((0, 32),)),
        "gain_attn": jnp.clip(1.0 + 0.15 * jax.random.normal(streams_of[7], (D,), jnp.float32), 0.25, 1.75).astype(jnp.bfloat16),
        "gain_attn_sub": jnp.clip(1.0 + 0.15 * jax.random.normal(streams_of[8], (D,), jnp.float32), 0.25, 1.75).astype(jnp.bfloat16),
        "gain_ffn": jnp.clip(1.0 + 0.15 * jax.random.normal(streams_of[9], (D,), jnp.float32), 0.25, 1.75).astype(jnp.bfloat16),
        "gain_ffn_sub": jnp.clip(1.0 + 0.15 * jax.random.normal(streams_of[10], (FF,), jnp.float32), 0.25, 1.75).astype(jnp.bfloat16),
        "ema_qkv": noise(streams_of[11], (D, 3 * D), D ** -0.5, 0.125, ((0, 32),), jnp.float32),
        "ema_out": noise(streams_of[12], (D, D), D ** -0.5, 0.125, ((0, 32),), jnp.float32),
        "ema_up": noise(streams_of[13], (D, FF), D ** -0.5, 0.125, ((1, 32),), jnp.float32),
        "ema_down": noise(streams_of[14], (FF, D), FF ** -0.5, 0.0625, ((0, 32),), jnp.float32),
        "ema_gain_attn": jnp.clip(0.3 + 1.40000004 * jax.random.uniform(streams_of[15], (D,), jnp.float32) ** steps_of(streams_of[15], (D,), ((0, 32),), -0.2, 0.2), 0.3, 1.7),
        "ema_gain_attn_sub": jnp.clip(0.3 + 1.40000004 * jax.random.uniform(streams_of[16], (D,), jnp.float32) ** steps_of(streams_of[16], (D,), ((0, 32),), -0.2, 0.2), 0.3, 1.7),
        "ema_gain_ffn": jnp.clip(0.3 + 1.40000004 * jax.random.uniform(streams_of[17], (D,), jnp.float32) ** steps_of(streams_of[17], (D,), ((0, 32),), -0.2, 0.2), 0.3, 1.7),
        "ema_gain_ffn_sub": jnp.clip(0.3 + 1.40000004 * jax.random.uniform(streams_of[18], (FF,), jnp.float32) ** steps_of(streams_of[18], (FF,), ((0, 32),), -0.2, 0.2), 0.3, 1.7),
        "out_grad": noise(streams_of[19], (ROWS, LENGTH, D), 1.0, 6.0, ((0, 4), (1, 8))),
    }


@jax.custom_vjp
def low(v):
    return lax.optimization_barrier(v.astype(jnp.bfloat16)).astype(jnp.float32)

@jax.custom_vjp
def low_back(v):
    return v

def low_keep(v):
    return (low(v), None)

def low_pass(kept, grad):
    return (grad,)

def back_keep(v):
    return (v, None)

def back_low(kept, grad):
    return (low(grad),)
low.defvjp(low_keep, low_pass)
low_back.defvjp(back_keep, back_low)
NEG_FILL = -1000000000.0
NORM_EPS = 1e-05
EMA_DECAY = 0.7

def highest(left_op, right_op):
    return jnp.dot(left_op, right_op, precision=lax.Precision.HIGHEST, preferred_element_type=jnp.float32)

def normalize(values):
    centered = values - lax.optimization_barrier(jnp.mean(values, axis=-1, keepdims=True))
    return centered * lax.rsqrt(lax.optimization_barrier(jnp.mean(centered * centered, axis=-1, keepdims=True)) + NORM_EPS)

def exact_gelu(values):
    return jax.nn.gelu(values, approximate=False)

def swap_pairs(values):
    dims_of = values.shape
    return values.reshape(dims_of[:-1] + (dims_of[-1] // 2, 2))[..., ::-1].reshape(dims_of)

def rotate(values, cosine, sine_table, factor):
    return (values * cosine + swap_pairs(values) * sine_table) * factor

def xpos_tables(positions):
    half_count = HD // 2
    index_half = jnp.arange(half_count).astype(jnp.float32)
    inverse = jnp.exp(-(2.0 * index_half / HD) * math.log(10000.0))
    decay_base = (2.0 * index_half + 0.4 * HD) / (1.4 * HD)
    where_at = positions.astype(jnp.float32)[:, None]
    angles = where_at * inverse[None, :]
    factor = jnp.exp(where_at / 512.0 * jnp.log(decay_base)[None, :])
    sign_row = jnp.where(jnp.arange(HD) % 2 == 0, -1.0, 1.0).astype(jnp.float32)
    cosine = jnp.tile(jnp.repeat(jnp.cos(angles), 2, axis=1), (1, HEADS))
    sine_table = jnp.tile(jnp.repeat(jnp.sin(angles), 2, axis=1) * sign_row[None, :], (1, HEADS))
    factor_table = jnp.tile(jnp.repeat(factor, 2, axis=1), (1, HEADS))
    return (cosine, sine_table, factor_table)

def layer_row(row_in, seg_row, pos_row, params):
    w_qkv, w_out, w_up, w_down, gain_attn, gain_attn_sub, gain_ffn, gain_ffn_sub = params
    cosine, sine_table, factor = xpos_tables(pos_row)
    attn_in = low(normalize(row_in) * gain_attn)
    qkv = low_back(highest(attn_in, w_qkv))
    scale = HD ** (-0.5)
    queries = low_back(low(rotate(qkv[:, :D], cosine, sine_table, factor) * scale))
    keys = low_back(low(rotate(qkv[:, D:2 * D], cosine, sine_table, 1.0 / factor)))
    values = low_back(low(qkv[:, 2 * D:]))
    positions = jnp.arange(LENGTH)
    allowed = (positions[None, :] <= positions[:, None]) & (seg_row[None, :] == seg_row[:, None])

    def one_head(inputs):
        head_query, head_key, head_value = inputs
        scores = low_back(highest(head_query, head_key.T))
        scores = jnp.where(allowed, scores, NEG_FILL)
        shifted = jnp.exp(scores - lax.optimization_barrier(jnp.max(scores, axis=-1, keepdims=True)))
        probs = low(shifted / lax.optimization_barrier(jnp.sum(shifted, axis=-1, keepdims=True)))
        return highest(probs, head_value)

    def split_heads(whole):
        return whole.reshape(LENGTH, HEADS, HD).transpose(1, 0, 2)
    attended = lax.map(jax.checkpoint(one_head), (split_heads(queries), split_heads(keys), split_heads(values)))
    attended = low_back(low(attended.transpose(1, 0, 2).reshape(LENGTH, D)))
    attn_sub = low(normalize(attended) * gain_attn_sub)
    hmid = row_in + low_back(highest(attn_sub, w_out))
    ffn_in = low(normalize(hmid) * gain_ffn)
    up_val = low_back(highest(ffn_in, w_up))
    ffn_sub = low(normalize(exact_gelu(up_val)) * gain_ffn_sub)
    return hmid + highest(ffn_sub, w_down)

def reference(hidden_in, segment_ids, position_ids, w_qkv, w_out, w_up, w_down, gain_attn, gain_attn_sub, gain_ffn, gain_ffn_sub, ema_qkv, ema_out, ema_up, ema_down, ema_gain_attn, ema_gain_attn_sub, ema_gain_ffn, ema_gain_ffn_sub, out_grad):
    weights = (w_qkv, w_out, w_up, w_down, gain_attn, gain_attn_sub, gain_ffn, gain_ffn_sub)
    params = tuple((weight.astype(jnp.float32) for weight in weights))

    def row_step(totals, inputs):
        row_in, seg_row, pos_row, cot_row = inputs
        result, pull = jax.vjp(lambda first_in, param_in: layer_row(first_in, seg_row, pos_row, param_in), row_in.astype(jnp.float32), params)
        grad_in, grad_params = pull(cot_row.astype(jnp.float32))
        totals = jax.tree.map(lambda total, extra: total + extra, totals, grad_params)
        return (totals, (result.astype(jnp.bfloat16), grad_in.astype(jnp.bfloat16)))
    zeros = tuple((jnp.zeros(param.shape, jnp.float32) for param in params))
    grads, (output, input_grad) = lax.scan(row_step, zeros, (hidden_in, segment_ids, position_ids, out_grad))
    emas = (ema_qkv, ema_out, ema_up, ema_down, ema_gain_attn, ema_gain_attn_sub, ema_gain_ffn, ema_gain_ffn_sub)
    fresh = tuple((EMA_DECAY * average + (1.0 - EMA_DECAY) * param for average, param in zip(emas, params)))
    return (output, input_grad, grads[0], grads[1], grads[2], grads[3], grads[4], grads[5], grads[6], grads[7], fresh[0], fresh[1], fresh[2], fresh[3], fresh[4], fresh[5], fresh[6], fresh[7])
```

```python
import math

import jax
import jax.numpy as jnp
from jax import lax
from jax.sharding import Mesh
from jax.sharding import PartitionSpec as P

HEADS = 32
HD = 64

NEG_FILL = -1000000000.0
NORM_EPS = 1e-05
EMA_DECAY = 0.7
LOW = jnp.bfloat16
F32 = jnp.float32
SEQ = ("chip", "core")
TP = ("dp", "core")
ALL = ("dp", "chip", "core")


def moments(values):
    mean = jnp.mean(values, axis=-1, keepdims=True)
    centered = values - mean
    scaler = lax.rsqrt(jnp.mean(centered * centered, axis=-1, keepdims=True) + NORM_EPS)
    return (centered * scaler, scaler)


def norm_back(scaled_grad, normed, scaler):
    first_mean = jnp.mean(scaled_grad, axis=-1, keepdims=True)
    second_mean = jnp.mean(scaled_grad * normed, axis=-1, keepdims=True)
    return scaler * (scaled_grad - first_mean - normed * second_mean)


def exact_gelu(values):
    return jax.nn.gelu(values, approximate=False)


def swap_pairs(values):
    dims_of = values.shape
    return values.reshape(dims_of[:-1] + (dims_of[-1] // 2, 2))[..., ::-1].reshape(dims_of)


def rotate(values, cosine, sine_table, factor):
    return (values * cosine + swap_pairs(values) * sine_table) * factor


def unrotate(grads, cosine, sine_table, factor):
    scaled = grads * factor
    return scaled * cosine + swap_pairs(scaled * sine_table)


def xpos_tables(positions, heads):
    half_count = HD // 2
    index_half = jnp.arange(half_count).astype(F32)
    inverse = jnp.exp(-(2.0 * index_half / HD) * math.log(10000.0))
    decay_base = (2.0 * index_half + 0.4 * HD) / (1.4 * HD)
    where_at = positions.astype(F32)[:, None]
    angles = where_at * inverse[None, :]
    factor = jnp.exp(where_at / 512.0 * jnp.log(decay_base)[None, :])
    sign_row = jnp.where(jnp.arange(HD) % 2 == 0, -1.0, 1.0).astype(F32)
    cosine = jnp.tile(jnp.repeat(jnp.cos(angles), 2, axis=1), (1, heads))
    sine_table = jnp.tile(jnp.repeat(jnp.sin(angles), 2, axis=1) * sign_row[None, :], (1, heads))
    factor_table = jnp.tile(jnp.repeat(factor, 2, axis=1), (1, heads))
    return (cosine, sine_table, factor_table)


def dot(left_op, right_op):
    return jnp.dot(left_op, right_op, preferred_element_type=F32)


def rows_product(operand, weight_rows):
    return lax.dot_general(
        operand, weight_rows, (((1,), (1,)), ((), ())), preferred_element_type=F32
    )


def token_product(left_op, right_op):
    return lax.dot_general(left_op, right_op, (((0,), (0,)), ((), ())), preferred_element_type=F32)


def block_allowed(seg_block, offset, seg_row, block_rows):
    query_pos = offset + jnp.arange(block_rows)
    key_pos = jnp.arange(seg_row.shape[0])
    return ((key_pos[None, :] <= query_pos[:, None]) & (seg_row[None, :] == seg_block[:, None]))[
        None
    ]


def attend_row(query_row, key_row, value_row, seg_row, block_rows):
    length = query_row.shape[0]
    block_count = length // block_rows
    query_blocks = query_row.reshape((block_count, block_rows) + query_row.shape[1:])
    seg_blocks = seg_row.reshape(block_count, block_rows)
    offsets = jnp.arange(block_count) * block_rows

    def one_block(inputs):
        query_block, seg_block, offset = inputs
        allowed = block_allowed(seg_block, offset, seg_row, block_rows)
        scores = jnp.einsum(
            "qhd,khd->hqk", query_block, key_row, preferred_element_type=jnp.float32
        )
        scores = jnp.where(allowed, scores, NEG_FILL)
        top_score = jnp.max(scores, axis=-1, keepdims=True)
        shifted = jnp.exp(scores - top_score)
        total = jnp.sum(shifted, axis=-1, keepdims=True)
        probs = (shifted / total).astype(jnp.bfloat16)
        attended = jnp.einsum("hqk,khd->qhd", probs, value_row, preferred_element_type=jnp.float32)
        return (attended, top_score + jnp.log(total))

    attended, log_total = lax.map(one_block, (query_blocks, seg_blocks, offsets))
    return (attended.reshape(query_row.shape), log_total)


def attend_back_row(query_row, key_row, value_row, seg_row, grad_row, log_total, block_rows):
    length = query_row.shape[0]
    block_count = length // block_rows
    query_blocks = query_row.reshape((block_count, block_rows) + query_row.shape[1:])
    grad_blocks = grad_row.reshape((block_count, block_rows) + grad_row.shape[1:])
    seg_blocks = seg_row.reshape(block_count, block_rows)
    offsets = jnp.arange(block_count) * block_rows

    def one_block(totals, inputs):
        key_total, value_total = totals
        query_block, grad_block, seg_block, offset, block_total = inputs
        allowed = block_allowed(seg_block, offset, seg_row, block_rows)
        scores = jnp.einsum(
            "qhd,khd->hqk", query_block, key_row, preferred_element_type=jnp.float32
        )
        scores = jnp.where(allowed, scores, NEG_FILL)
        probs = jnp.exp(scores - block_total)
        grad_probs = jnp.einsum(
            "qhd,khd->hqk", grad_block, value_row, preferred_element_type=jnp.float32
        )
        delta = jnp.sum(probs * grad_probs, axis=-1, keepdims=True)
        grad_scores = jnp.where(allowed, probs * (grad_probs - delta), 0.0).astype(jnp.bfloat16)
        grad_query = jnp.einsum(
            "hqk,khd->qhd", grad_scores, key_row, preferred_element_type=jnp.float32
        )
        key_total = key_total + jnp.einsum(
            "hqk,qhd->khd", grad_scores, query_block, preferred_element_type=jnp.float32
        )
        value_total = value_total + jnp.einsum(
            "hqk,qhd->khd",
            probs.astype(jnp.bfloat16),
            grad_block,
            preferred_element_type=jnp.float32,
        )
        return ((key_total, value_total), grad_query)

    zeros = jnp.zeros(key_row.shape, jnp.float32)
    (key_grad, value_grad), query_grad = lax.scan(
        one_block, (zeros, zeros), (query_blocks, grad_blocks, seg_blocks, offsets, log_total)
    )
    return (query_grad.reshape(query_row.shape), key_grad, value_grad)


def body(
    hidden_in,
    segment_ids,
    position_ids,
    w_qkv,
    w_out,
    w_up,
    w_down,
    gain_attn,
    gain_attn_sub,
    gain_ffn,
    gain_ffn_sub,
    ema_qkv,
    ema_out,
    ema_up,
    ema_down,
    ema_gain_attn,
    ema_gain_attn_sub,
    ema_gain_ffn,
    ema_gain_ffn_sub,
    out_grad,
):
    _, tokens, width = hidden_in.shape
    planes, chips = lax.axis_size("dp"), lax.axis_size("chip")
    seqs = 2 * chips
    length = tokens * seqs
    heads = HEADS // seqs
    span = heads * HD
    part = w_qkv.shape[0]
    strided = part % HD == 0
    group_tokens = planes * 2 * tokens
    width_ff = w_down.shape[0] * planes * seqs
    block_rows = min(512, length)
    scale = HD ** (-0.5)
    seq_index = lax.axis_index(SEQ)

    def gain_rows(weight, gain):
        return (weight.astype(F32) * gain.astype(F32)[:, None]).astype(LOW)

    qkv_scaled = gain_rows(w_qkv, gain_attn)
    out_scaled = gain_rows(w_out, gain_attn_sub)
    down_scaled = gain_rows(w_down, gain_ffn_sub)
    if strided:
        qkv_send = qkv_scaled.reshape(part, 3, planes, seqs, HD).transpose(3, 0, 1, 2, 4)
    else:
        qkv_send = qkv_scaled.reshape(part, 3, seqs, span).transpose(2, 0, 1, 3)
    qkv_send = qkv_send.reshape(seqs, part, 3 * span)
    qkv_plane = lax.all_to_all(qkv_send, SEQ, split_axis=0, concat_axis=0, tiled=True)
    qkv_mine = lax.all_gather(
        qkv_plane.reshape(seqs * part, 3 * span), "dp", axis=0, tiled=True
    )
    if strided:
        out_mine = lax.all_gather(out_scaled, "dp", axis=0, tiled=True)
    else:
        out_all = lax.all_gather(out_scaled, ALL, axis=0, tiled=True)
        out_mine = lax.dynamic_slice_in_dim(out_all, seq_index * span, span, axis=0)
    gain_three = lax.all_gather(gain_ffn, ALL, axis=0, tiled=True).astype(F32)

    x_in = hidden_in[0].astype(F32)
    normed_one, scaler_one = moments(x_in)
    normed_low = normed_one.astype(LOW)
    row_in = lax.all_gather(normed_low, SEQ, axis=0, tiled=True)
    row_positions = lax.all_gather(position_ids[0], SEQ, axis=0, tiled=True)
    row_segments = lax.all_gather(segment_ids[0], SEQ, axis=0, tiled=True)
    cosine, sine_table, factor = xpos_tables(row_positions, heads)
    qkv_raw = dot(row_in, qkv_mine)
    queries = (rotate(qkv_raw[:, :span], cosine, sine_table, factor) * scale).astype(LOW)
    keys = rotate(qkv_raw[:, span : 2 * span], cosine, sine_table, 1.0 / factor).astype(LOW)
    values = qkv_raw[:, 2 * span :].astype(LOW)

    def by_head(whole):
        return whole.reshape(length, heads, HD)

    attended, log_total = attend_row(
        by_head(queries), by_head(keys), by_head(values), row_segments, block_rows
    )
    attended = attended.reshape(length, span).astype(LOW)
    attended_wide = attended.astype(F32)
    out_part = dot(attended, out_mine)
    column_part = jnp.sum(out_mine.astype(F32), axis=0)
    out_sum = lax.psum_scatter(
        out_part.astype(LOW), SEQ, scatter_dimension=0, tiled=True
    ).astype(F32)
    column_sum = lax.psum(column_part, SEQ)
    sums = lax.psum_scatter(
        jnp.stack([jnp.sum(attended_wide, axis=1), jnp.sum(attended_wide**2, axis=1)], axis=1),
        SEQ,
        scatter_dimension=0,
        tiled=True,
    )
    mean_two = sums[:, :1] / width
    scaler_two = lax.rsqrt(sums[:, 1:] / width - mean_two * mean_two + NORM_EPS)
    projected = scaler_two * (out_sum - mean_two * column_sum[None, :])
    hmid = x_in + projected
    normed_three, scaler_three = moments(hmid)
    ffn_in = (normed_three * gain_three).astype(LOW)

    grad_low = out_grad[0]
    grad_top = grad_low.astype(F32)
    up_mine = lax.all_gather(w_up, "chip", axis=1, tiled=True)
    down_mine = lax.all_gather(down_scaled, "chip", axis=0, tiled=True)
    grad_flat = lax.all_gather(grad_low, TP, axis=0, tiled=True)
    ffn_flat = lax.all_gather(ffn_in, TP, axis=0, tiled=True)
    weighted = rows_product(grad_flat, down_mine)
    up_slice = dot(ffn_flat, up_mine)
    activated, gelu_pull = jax.vjp(exact_gelu, up_slice)
    stats = lax.psum(
        jnp.stack(
            [
                jnp.sum(activated, axis=1),
                jnp.sum(activated * activated, axis=1),
                jnp.sum(weighted * activated, axis=1),
                jnp.sum(weighted, axis=1),
            ]
        ),
        TP,
    )[:, :, None]
    act_mean = stats[0] / width_ff
    scaler_four = lax.rsqrt(stats[1] / width_ff - act_mean * act_mean + NORM_EPS)
    normed_four = (activated - act_mean) * scaler_four
    normed_four_low = normed_four.astype(LOW)
    first_mean = stats[3] / width_ff
    second_mean = scaler_four * (stats[2] - act_mean * stats[3]) / width_ff
    d_act = scaler_four * (weighted - first_mean - normed_four * second_mean)
    (d_up,) = gelu_pull(d_act)
    d_up_low = d_up.astype(LOW)
    d_ffn_in = lax.psum_scatter(
        rows_product(d_up_low, up_mine).astype(LOW), TP, scatter_dimension=0, tiled=True
    ).astype(F32)
    ffn_out = lax.psum_scatter(
        dot(normed_four_low, down_mine).astype(LOW), TP, scatter_dimension=0, tiled=True
    ).astype(F32)
    grad_up = token_product(ffn_flat, d_up_low)
    grad_down = token_product(normed_four_low, grad_flat)
    sum_up = lax.psum_scatter(
        grad_up.astype(LOW), "chip", scatter_dimension=1, tiled=True
    ).astype(F32)
    sum_down = lax.psum_scatter(
        grad_down.astype(LOW), "chip", scatter_dimension=0, tiled=True
    ).astype(F32)
    output = (hmid + ffn_out).astype(LOW)[None]

    grad_gain_three = lax.psum_scatter(
        jnp.sum(d_ffn_in * normed_three, axis=0), ALL, scatter_dimension=0, tiled=True
    )
    d_hmid = grad_top + norm_back(d_ffn_in * gain_three, normed_three, scaler_three)
    d_hmid_low = d_hmid.astype(LOW)
    d_hmid_wide = d_hmid_low.astype(F32)
    first_two = jnp.sum(d_hmid_wide * column_sum[None, :], axis=1, keepdims=True) / width
    second_two = jnp.sum(d_hmid_wide * projected, axis=1, keepdims=True) / width
    row_grad = lax.all_gather(d_hmid_low, SEQ, axis=0, tiled=True)
    row_stats = lax.all_gather(
        jnp.concatenate([mean_two, scaler_two, first_two, second_two], axis=1),
        SEQ,
        axis=0,
        tiled=True,
    )
    mean_row, scaler_row, first_row, second_row = (row_stats[:, i : i + 1] for i in range(4))
    normed_two = (attended_wide - mean_row) * scaler_row
    d_sub = rows_product(row_grad, out_mine)
    d_attended = (scaler_row * (d_sub - first_row - normed_two * second_row)).astype(LOW)
    grad_out = token_product(normed_two.astype(LOW), row_grad)
    query_grad, key_grad, value_grad = attend_back_row(
        by_head(queries),
        by_head(keys),
        by_head(values),
        row_segments,
        by_head(d_attended),
        log_total,
        block_rows,
    )

    def flat(whole):
        return whole.reshape(length, span).astype(LOW).astype(F32)

    d_query_raw = unrotate(flat(query_grad), cosine, sine_table, factor) * scale
    d_key_raw = unrotate(flat(key_grad), cosine, sine_table, 1.0 / factor)
    d_qkv = jnp.concatenate([d_query_raw, d_key_raw, flat(value_grad)], axis=1).astype(LOW)
    grad_qkv = token_product(row_in, d_qkv)
    d_in = lax.psum_scatter(
        rows_product(d_qkv, qkv_mine).astype(LOW), SEQ, scatter_dimension=0, tiled=True
    ).astype(F32)
    input_grad = (d_hmid + norm_back(d_in, normed_one, scaler_one)).astype(LOW)[None]

    plane_qkv = lax.psum_scatter(grad_qkv.astype(LOW), "dp", scatter_dimension=0, tiled=True)
    part_qkv = lax.all_to_all(
        plane_qkv.reshape(seqs, part, 3 * span), SEQ, split_axis=0, concat_axis=0, tiled=True
    )
    if strided:
        sum_qkv = part_qkv.reshape(seqs, part, 3, planes, HD).transpose(1, 2, 3, 0, 4)
        sum_out = lax.psum_scatter(grad_out.astype(LOW), "dp", scatter_dimension=0, tiled=True)
    else:
        sum_qkv = part_qkv.reshape(seqs, part, 3, span).transpose(1, 2, 0, 3)
        spread = lax.dynamic_update_slice_in_dim(
            jnp.zeros((width, width), LOW), grad_out.astype(LOW), seq_index * span, axis=0
        )
        sum_out = lax.psum_scatter(spread, ALL, scatter_dimension=0, tiled=True)
    sum_qkv = sum_qkv.reshape(part, 3 * width).astype(F32)
    sum_out = sum_out.astype(F32)

    def finish(total, weight, gain):
        wide = weight.astype(F32)
        return (total * gain.astype(F32)[:, None], jnp.sum(total * wide, axis=1))

    sum_qkv, grad_gain_one = finish(sum_qkv, w_qkv, gain_attn)
    sum_out, grad_gain_two = finish(sum_out, w_out, gain_attn_sub)
    sum_down, grad_gain_four = finish(sum_down, w_down, gain_ffn_sub)

    def averaged(average, weight):
        return EMA_DECAY * average + (1.0 - EMA_DECAY) * weight.astype(F32)

    return (
        output,
        input_grad,
        sum_qkv,
        sum_out,
        sum_up,
        sum_down,
        grad_gain_one,
        grad_gain_two,
        grad_gain_three,
        grad_gain_four,
        averaged(ema_qkv, w_qkv),
        averaged(ema_out, w_out),
        averaged(ema_up, w_up),
        averaged(ema_down, w_down),
        averaged(ema_gain_attn, gain_attn),
        averaged(ema_gain_attn_sub, gain_attn_sub),
        averaged(ema_gain_ffn, gain_ffn),
        averaged(ema_gain_ffn_sub, gain_ffn_sub),
    )


def solution(mesh):
    split = Mesh(
        mesh.devices.reshape(mesh.shape["dp"], mesh.shape["seq"] // 2, 2), ("dp", "chip", "core")
    )
    tokens = P("dp", SEQ, None)
    ids = P("dp", SEQ)
    rows = P(ALL, None)
    columns = P(None, ALL)
    vector = P(ALL)
    weights = (rows, rows, columns, rows)
    gains = (vector,) * 4
    return jax.shard_map(
        body,
        mesh=split,
        in_specs=(tokens, ids, ids, *weights, *gains, *weights, *gains, tokens),
        out_specs=(tokens, tokens, *weights, *gains, *weights, *gains),
        check_vma=False,
    )
```

```python
import functools
import math

import jax
import jax.numpy as jnp
from jax import lax
from jax.experimental import pallas as pl
from jax.experimental.pallas import tpu as pltpu
from jax.sharding import Mesh
from jax.sharding import PartitionSpec as P

HEADS = 32
HD = 64

NEG_FILL = -1000000000.0
NORM_EPS = 1e-05
EMA_DECAY = 0.7
LOW = jnp.bfloat16
F32 = jnp.float32
SEQ = ("chip", "core")
TP = ("dp", "core")
ALL = ("dp", "chip", "core")


def moments(values):
    mean = jnp.mean(values, axis=-1, keepdims=True)
    centered = values - mean
    scaler = lax.rsqrt(jnp.mean(centered * centered, axis=-1, keepdims=True) + NORM_EPS)
    return (centered * scaler, scaler)


def norm_back(scaled_grad, normed, scaler):
    first_mean = jnp.mean(scaled_grad, axis=-1, keepdims=True)
    second_mean = jnp.mean(scaled_grad * normed, axis=-1, keepdims=True)
    return scaler * (scaled_grad - first_mean - normed * second_mean)


def exact_gelu(values):
    return jax.nn.gelu(values, approximate=False)


def token_tables(positions):
    half_count = HD // 2
    index_half = jnp.arange(half_count).astype(F32)
    inverse = jnp.exp(-(2.0 * index_half / HD) * math.log(10000.0))
    decay_base = (2.0 * index_half + 0.4 * HD) / (1.4 * HD)
    where_at = positions.astype(F32)[:, None]
    angles = where_at * inverse[None, :]
    factor = jnp.exp(where_at / 512.0 * jnp.log(decay_base)[None, :])
    sign_row = jnp.where(jnp.arange(HD) % 2 == 0, -1.0, 1.0).astype(F32)
    cosine = jnp.repeat(jnp.cos(angles), 2, axis=1)
    sine = jnp.repeat(jnp.sin(angles), 2, axis=1) * sign_row[None, :]
    factor = jnp.repeat(factor, 2, axis=1)
    grow = factor * HD ** (-0.5)
    where_block = jnp.broadcast_to(where_at, (positions.shape[0], HD))
    return jnp.concatenate(
        [cosine * grow, sine * grow, HD**0.5 / (factor * factor), where_block], axis=1
    )


def dot(left_op, right_op):
    return jnp.dot(left_op, right_op, preferred_element_type=F32)


def rows_product(operand, weight_rows):
    return lax.dot_general(
        operand, weight_rows, (((1,), (1,)), ((), ())), preferred_element_type=F32
    )


def token_product(left_op, right_op):
    return lax.dot_general(left_op, right_op, (((0,), (0,)), ((), ())), preferred_element_type=F32)


MESH = pl.DeviceIdType.MESH
HBM = pl.BlockSpec(memory_space=pl.ANY)
VMEM = pl.BlockSpec(memory_space=pltpu.VMEM)
VMEM_BYTES = 56 * 1024 * 1024


def shape(dims, kind):
    return jax.ShapeDtypeStruct(dims, kind)


def pairs_of(*counts):
    return [pltpu.SemaphoreType.DMA((count,)) for count in counts for _ in range(2)]


def call(kernel, name, outs, args, in_specs, out_specs, scratch, collective=None):
    return pl.pallas_call(
        kernel,
        name=name,
        out_shape=outs,
        in_specs=in_specs,
        out_specs=out_specs,
        scratch_shapes=scratch,
        compiler_params=pltpu.CompilerParams(
            collective_id=collective,
            has_side_effects=collective is not None,
            vmem_limit_bytes=VMEM_BYTES,
        ),
    )(*args)


def place():
    return (lax.axis_index("dp"), lax.axis_index("chip"), lax.axis_index("core"))


def remote(source, target, sems, index, device):
    return pltpu.make_async_remote_copy(
        src_ref=source,
        dst_ref=target,
        send_sem=sems[0].at[index],
        recv_sem=sems[1].at[index],
        device_id=device,
        device_id_type=MESH,
    )


def greet(barrier, devices):
    for device in devices:
        pl.semaphore_signal(barrier, inc=1, device_id=device, device_id_type=MESH)


def greet_line(barrier, planes, here):
    z, c, core = here

    @pl.when(z < planes - 1)
    def _():
        greet(barrier, [(z + 1, c, core)])

    @pl.when(z > 0)
    def _():
        greet(barrier, [(z - 1, c, core)])


def line_peers(planes, here):
    z = here[0]
    return (2 * planes - 2 - z) // planes + (z + planes - 1) // planes


def chip_peers(chips, here):
    z, c, core = here
    return [(z, lax.rem(c + k, chips), core) for k in range(1, chips)]


def plane_peers(chips, here):
    z, c, core = here
    seqs = 2 * chips
    me = 2 * c + core
    ids = [lax.rem(me + k, seqs) for k in range(1, seqs)]
    return [(z, index // 2, lax.rem(index, 2)) for index in ids]


def column_block(whole, units, index):
    if len(whole.shape) == 3:
        return whole.at[index]
    return whole.at[:, pl.ds(pl.multiple_of(index * units, 128), units)]


class ChipSwap:
    def __init__(self, chips, here, source, slots, sems):
        z, c, core = here
        self.sends = [
            remote(source(device[1]), slots.at[c], sems, k, device)
            for k, device in enumerate(chip_peers(chips, here), 1)
        ]
        self.waits = [
            remote(source(c), slots.at[lax.rem(c + chips - k, chips)], sems, k, here)
            for k in range(1, chips)
        ]
        self.keep = (source(c), slots.at[c])

    def start(self, local):
        for copy in self.sends:
            copy.start()
        self.held = pltpu.make_async_copy(*self.keep, local)
        self.held.start()

    def finish(self):
        self.held.wait()
        for send, wait in zip(self.sends, self.waits):
            send.wait_send()
            wait.wait_recv()


class PlaneGather:
    def __init__(self, chips, here, block, out, far, near):
        self.chips, self.here, self.block, self.out = chips, here, block, out
        self.far, self.near = far, near
        z, c, core = here
        self.me = 2 * c + core
        self.partner = (z, c, 1 - core)

    def source(self, k, core):
        return 2 * lax.rem(self.here[1] + self.chips - k, self.chips) + core

    def sends(self):
        mine = self.out.at[self.me]
        copies = [
            remote(self.block, mine, self.far, k, device)
            for k, device in enumerate(chip_peers(self.chips, self.here), 1)
        ]
        return [*copies, remote(self.block, mine, self.near, 0, self.partner)]

    def start(self):
        for copy in self.sends():
            copy.start()

    def passed(self, k):
        index = self.source(k, self.here[2])
        return remote(self.out.at[index], self.out.at[index], self.near, k, self.partner)

    def forward(self):
        for k in range(1, self.chips):
            index = self.source(k, self.here[2])
            remote(self.block, self.out.at[index], self.far, k, self.partner).wait_recv()
            self.passed(k).start()

    def finish(self):
        for copy in self.sends():
            copy.wait_send()
        for k in range(1, self.chips):
            self.passed(k).wait_send()
        for k in range(self.chips):
            index = self.source(k, 1 - self.here[2])
            remote(self.block, self.out.at[index], self.near, k, self.partner).wait_recv()


class LineGather:
    def __init__(self, planes, here, block, up, down):
        self.planes, self.here, self.block = planes, here, block
        self.up, self.down = up, down

    def upward(self, d):
        z, c, core = self.here
        block = self.block(z - d)
        return remote(block, block, self.up, d, (z + 1, c, core))

    def downward(self, d):
        z, c, core = self.here
        block = self.block(z + d)
        return remote(block, block, self.down, d, (z - 1, c, core))

    def each(self, d, act_up, act_down):
        z, planes = self.here[0], self.planes
        pl.when((z < planes - 1) & (z - d >= 0))(lambda: act_up(self.upward(d)))
        pl.when((z > 0) & (z + d < planes))(lambda: act_down(self.downward(d)))

    def start(self):
        self.each(0, lambda copy: copy.start(), lambda copy: copy.start())

    def step(self, d, arrived=None):
        z, c, core = self.here
        planes = self.planes

        def below():
            block = self.block(z - d)
            remote(block, block, self.up, d - 1, (z, c, core)).wait_recv()
            if d < planes - 1:
                pl.when(z < planes - 1)(lambda: self.upward(d).start())
            if arrived is not None:
                arrived(z - d)

        def above():
            block = self.block(z + d)
            remote(block, block, self.down, d - 1, (z, c, core)).wait_recv()
            if d < planes - 1:
                pl.when(z > 0)(lambda: self.downward(d).start())
            if arrived is not None:
                arrived(z + d)

        pl.when(z - d >= 0)(below)
        pl.when(z + d < planes)(above)

    def finish(self):
        for d in range(self.planes - 1):
            self.each(d, lambda copy: copy.wait_send(), lambda copy: copy.wait_send())


def attention_gather_kernel(
    planes, chips, x_ref, meta_ref, qkv_ref, out_ref, gain_ref, up_ref,
    row_ref, metas_ref, qkvs_ref, outs_ref, gains_ref, ups_ref,
    *sems,
):
    here = place()
    z, c, core = here
    seqs = 2 * chips
    count = planes * seqs
    me = 2 * c + core
    flat = z * seqs + me
    groups = [sems[2 * i : 2 * i + 2] for i in range(11)]
    swap_sems, x_far, x_near, meta_far, meta_near, up, down, up_two, down_two = groups[:9]
    gain_sems, up_sems = groups[9:]
    local = sems[22]
    barrier = pltpu.get_barrier_semaphore()

    def device_of(k):
        other = lax.rem(flat + k, count)
        return (other // seqs, lax.rem(other, seqs) // 2, lax.rem(other, 2))

    def signal(k, carry):
        greet(barrier, [device_of(k)])
        return carry

    lax.fori_loop(1, count, signal, 0)
    pl.semaphore_wait(barrier, count - 1)

    mine = pltpu.make_async_copy(qkv_ref.at[me], qkvs_ref.at[z, me], local.at[0])
    keeps = [
        pltpu.make_async_copy(x_ref, row_ref.at[me], local.at[1]),
        pltpu.make_async_copy(meta_ref, metas_ref.at[me], local.at[2]),
        pltpu.make_async_copy(gain_ref, gains_ref.at[flat], local.at[3]),
    ]
    own_out = pltpu.make_async_copy(out_ref, outs_ref.at[z], local.at[4])
    units = up_ref.shape[1]
    keeps.append(pltpu.make_async_copy(up_ref, column_block(ups_ref, units, c), local.at[5]))
    ups = [
        remote(up_ref, column_block(ups_ref, units, c), up_sems, k, device)
        for k, device in enumerate(chip_peers(chips, here), 1)
    ]
    swaps = [
        remote(qkv_ref.at[2 * device[1] + device[2]], qkvs_ref.at[z, me], swap_sems, k, device)
        for k, device in enumerate(plane_peers(chips, here), 1)
    ]
    mine.start()
    own_out.start()
    for copy in swaps:
        copy.start()
    rows = PlaneGather(chips, here, x_ref, row_ref, x_far, x_near)
    metas = PlaneGather(chips, here, meta_ref, metas_ref, meta_far, meta_near)
    rows.start()
    metas.start()
    for copy in keeps:
        copy.start()

    def gain_copy(k):
        return remote(gain_ref, gains_ref.at[flat], gain_sems, k, device_of(k))

    def gain_start(k, carry):
        gain_copy(k).start()
        return carry

    lax.fori_loop(1, count, gain_start, 0)

    mine.wait()
    own_out.wait()
    for k in range(1, seqs):
        index = lax.rem(me + seqs - k, seqs)
        remote(qkv_ref.at[0], qkvs_ref.at[z, index], swap_sems, k, here).wait_recv()
    line = LineGather(planes, here, lambda t: qkvs_ref.at[t], up, down)
    line_two = LineGather(planes, here, lambda t: outs_ref.at[t], up_two, down_two)
    line.start()
    line_two.start()
    rows.forward()
    metas.forward()
    for copy in ups:
        copy.start()
    for d in range(1, planes):
        line.step(d)
        line_two.step(d)
    line.finish()
    line_two.finish()
    rows.finish()
    metas.finish()
    for copy in swaps:
        copy.wait_send()
    for copy in keeps:
        copy.wait()
    for k in range(1, chips):
        ups[k - 1].wait_send()
        other = lax.rem(c + chips - k, chips)
        remote(up_ref, column_block(ups_ref, units, other), up_sems, k, here).wait_recv()

    def gain_wait(k, carry):
        gain_copy(k).wait_send()
        other = lax.rem(flat + count - k, count)
        remote(gain_ref, gains_ref.at[other], gain_sems, k, here).wait_recv()
        return carry

    lax.fori_loop(1, count, gain_wait, 0)


def attention_gather(planes, chips, x_block, meta, qkv_blocks, out_rows, gain_tile, up_block):
    seqs = 2 * chips
    part, wide = qkv_blocks.shape[1:]
    width, units = up_block.shape
    return call(
        functools.partial(attention_gather_kernel, planes, chips),
        "attention_gather",
        [
            shape((seqs, *x_block.shape), LOW),
            shape((seqs, *meta.shape), F32),
            shape((planes, seqs, part, wide), LOW),
            shape((planes, *out_rows.shape), LOW),
            shape((planes * seqs, *gain_tile.shape), F32),
            shape(
                (width, chips * units) if units % 128 == 0 else (chips, width, units), LOW
            ),
        ],
        (x_block, meta, qkv_blocks, out_rows, gain_tile, up_block),
        [HBM] * 6,
        [HBM] * 6,
        [
            *pairs_of(seqs, *[chips] * 4, *[planes] * 4, planes * seqs, chips),
            pltpu.SemaphoreType.DMA((6,)),
        ],
        1,
    )


def plane_gather_kernel(
    planes, chips, x_ref, stat_ref, tile_ref, row_ref, stats_ref, tiles_ref, *sems
):
    here = place()
    z, c, core = here
    seqs = 2 * chips
    count = planes * seqs
    me = 2 * c + core
    flat = z * seqs + me
    x_far, x_near, s_far, s_near, tile_sems = [sems[2 * i : 2 * i + 2] for i in range(5)]
    local = sems[10]
    barrier = pltpu.get_barrier_semaphore()

    def device_of(k):
        other = lax.rem(flat + k, count)
        return (other // seqs, lax.rem(other, seqs) // 2, lax.rem(other, 2))

    def signal(k, carry):
        greet(barrier, [device_of(k)])
        return carry

    lax.fori_loop(1, count, signal, 0)
    pl.semaphore_wait(barrier, count - 1)
    rows = PlaneGather(chips, here, x_ref, row_ref, x_far, x_near)
    stats = PlaneGather(chips, here, stat_ref, stats_ref, s_far, s_near)
    rows.start()
    stats.start()
    keeps = [
        pltpu.make_async_copy(x_ref, row_ref.at[me], local.at[0]),
        pltpu.make_async_copy(stat_ref, stats_ref.at[me], local.at[1]),
        pltpu.make_async_copy(tile_ref.at[flat], tiles_ref.at[flat], local.at[2]),
    ]
    for copy in keeps:
        copy.start()

    def tile_copy(k):
        other = lax.rem(flat + k, count)
        return remote(tile_ref.at[other], tiles_ref.at[flat], tile_sems, k, device_of(k))

    def tile_start(k, carry):
        tile_copy(k).start()
        return carry

    lax.fori_loop(1, count, tile_start, 0)
    rows.forward()
    stats.forward()
    rows.finish()
    stats.finish()
    for copy in keeps:
        copy.wait()

    def tile_wait(k, carry):
        tile_copy(k).wait_send()
        other = lax.rem(flat + count - k, count)
        remote(tile_ref.at[0], tiles_ref.at[other], tile_sems, k, here).wait_recv()
        return carry

    lax.fori_loop(1, count, tile_wait, 0)


def plane_gather(planes, chips, x_block, stats, tiles):
    seqs = 2 * chips
    return call(
        functools.partial(plane_gather_kernel, planes, chips),
        "plane_gather",
        [
            shape((seqs, *x_block.shape), x_block.dtype),
            shape((seqs, *stats.shape), stats.dtype),
            shape(tiles.shape, tiles.dtype),
        ],
        (x_block, stats, tiles),
        [HBM] * 3,
        [HBM] * 3,
        [
            *pairs_of(chips, chips, chips, chips, planes * seqs),
            pltpu.SemaphoreType.DMA((3,)),
        ],
        2,
    )


COLUMNS = 512


def product(left, right, columns, turned):
    if turned:
        return lax.dot_general(
            left, right[columns, :], (((1,), (1,)), ((), ())), preferred_element_type=F32
        )
    return jnp.dot(left, right[:, columns], preferred_element_type=F32)


class PlaneScatter:
    def __init__(self, chips, here, left, right, turned, near_out, near_in, far_out, far_in, near, far):
        self.chips, self.here = chips, here
        self.left, self.right, self.turned = left, right, turned
        self.near_out, self.near_in, self.far_out, self.far_in = near_out, near_in, far_out, far_in
        self.near, self.far = near, far
        self.width = near_out.shape[-1]

    def target(self, k):
        return lax.rem(self.here[1] + k, self.chips)

    def near_copy(self, k):
        z, c, core = self.here
        return remote(self.near_out.at[k], self.near_in.at[k], self.near, k, (z, c, 1 - core))

    def far_copy(self, k):
        z, _, core = self.here
        return remote(self.far_out.at[k], self.far_in.at[k], self.far, k, (z, self.target(k), core))

    def tiles(self):
        return [pl.ds(at, COLUMNS) for at in range(0, self.width, COLUMNS)]

    def start(self):
        core = self.here[2]
        order = [*range(1, self.chips), 0]
        for k in order:
            left = self.left[2 * self.target(k) + 1 - core]
            for columns in self.tiles():
                part = product(left, self.right, columns, self.turned)
                self.near_out[k, :, columns] = part.astype(LOW)
            self.near_copy(k).start()
        for k in order:
            left = self.left[2 * self.target(k) + core]
            self.near_copy(k).wait_recv()
            for columns in self.tiles():
                part = product(left, self.right, columns, self.turned)
                self.far_out[k, :, columns] = (
                    part + self.near_in[k, :, columns].astype(F32)
                ).astype(LOW)
            if k:
                self.far_copy(k).start()

    def finish(self, out_ref):
        for k in range(1, self.chips):
            self.far_copy(k).wait_recv()
        for columns in self.tiles():
            total = self.far_out[0, :, columns].astype(F32)
            for k in range(1, self.chips):
                total = total + self.far_in[k, :, columns].astype(F32)
            out_ref[:, columns] = total
        for k in range(self.chips):
            self.near_copy(k).wait_send()
        for k in range(1, self.chips):
            self.far_copy(k).wait_send()


def out_scatter_kernel(
    chips, left_ref, right_ref, tile_ref, out_ref, tiles_ref,
    near_out, near_in, far_out, far_in, *sems,
):
    here = place()
    z, c, core = here
    seqs = 2 * chips
    me = 2 * c + core
    near, far, tile_sems = [sems[2 * i : 2 * i + 2] for i in range(3)]
    barrier = pltpu.get_barrier_semaphore()
    peers = plane_peers(chips, here)
    greet(barrier, peers)
    pl.semaphore_wait(barrier, len(peers))
    swaps = [
        remote(tile_ref.at[2 * device[1] + device[2]], tiles_ref.at[me], tile_sems, k, device)
        for k, device in enumerate(peers, 1)
    ]
    for copy in swaps:
        copy.start()
    keep = pltpu.make_async_copy(tile_ref.at[me], tiles_ref.at[me], sems[6].at[0])
    keep.start()
    work = PlaneScatter(
        chips, here, left_ref, right_ref, False, near_out, near_in, far_out, far_in, near, far
    )
    work.start()
    work.finish(out_ref)
    keep.wait()
    for k in range(1, seqs):
        swaps[k - 1].wait_send()
        index = lax.rem(me + seqs - k, seqs)
        remote(tile_ref.at[0], tiles_ref.at[index], tile_sems, k, here).wait_recv()


def out_scatter(chips, left, right, tiles):
    _, tokens, _ = left.shape
    width = right.shape[1]
    return call(
        functools.partial(out_scatter_kernel, chips),
        "out_scatter",
        [shape((tokens, width), F32), shape(tiles.shape, F32)],
        (left, right, tiles),
        [VMEM, VMEM, VMEM],
        [VMEM, VMEM],
        [
            *[pltpu.VMEM((chips, tokens, width), LOW)] * 4,
            *pairs_of(chips, chips, 2 * chips),
            pltpu.SemaphoreType.DMA((1,)),
        ],
        3,
    )


class LineScatter:
    def __init__(self, planes, here, rows, own, above, below, up, down):
        self.planes, self.here, self.rows, self.own = planes, here, rows, own
        self.above, self.below, self.up, self.down = above, below, up, down

    def upward(self, t):
        z, c, core = self.here
        return remote(self.below.at[t], self.below.at[t], self.up, t, (z + 1, c, core))

    def downward(self, t):
        z, c, core = self.here
        return remote(self.above.at[t], self.above.at[t], self.down, t, (z - 1, c, core))

    def add(self, slot, t, fresh):
        for rows in self.rows:
            total = self.own(t, rows)
            if not fresh:
                total = total + slot[t, rows].astype(F32)
            slot[t, rows] = total.astype(LOW)

    def step(self, i):
        z, planes = self.here[0], self.planes
        top, low = planes - 1 - i, i

        def rise():
            @pl.when(z > 0)
            def _():
                self.upward(top).wait_recv()
                self.add(self.below, top, False)

            @pl.when(z == 0)
            def _():
                self.add(self.below, top, True)

            self.upward(top).start()

        def fall():
            @pl.when(z < planes - 1)
            def _():
                self.downward(low).wait_recv()
                self.add(self.above, low, False)

            @pl.when(z == planes - 1)
            def _():
                self.add(self.above, low, True)

            self.downward(low).start()

        pl.when(z < top)(rise)
        pl.when(z > low)(fall)

    def finish(self, store):
        z, planes = self.here[0], self.planes

        @pl.when(z > 0)
        def _():
            self.upward(z).wait_recv()

        @pl.when(z < planes - 1)
        def _():
            self.downward(z).wait_recv()

        def both():
            for rows in self.rows:
                total = self.own(z, rows) + self.below[z, rows].astype(F32)
                store(rows, total + self.above[z, rows].astype(F32))

        def lowest():
            for rows in self.rows:
                store(rows, self.own(z, rows) + self.above[z, rows].astype(F32))

        def highest():
            for rows in self.rows:
                store(rows, self.own(z, rows) + self.below[z, rows].astype(F32))

        pl.when((z > 0) & (z < planes - 1))(both)
        pl.when(z == 0)(lowest)
        pl.when(z == planes - 1)(highest)
        for i in range(planes - 1):
            pl.when(z < planes - 1 - i)(lambda i=i: self.upward(planes - 1 - i).wait_send())
            pl.when(z > i)(lambda i=i: self.downward(i).wait_send())


def row_tiles(count, size):
    return [pl.ds(at, size) for at in range(0, count, size)]


def in_scatter_kernel(
    planes, chips, left_ref, right_ref, grad_ref, out_ref, parts_ref,
    near_out, near_in, far_out, far_in, above, below, mine, *sems,
):
    here = place()
    z, c, core = here
    seqs = 2 * chips
    me = 2 * c + core
    near, far, up, down, swap_sems = [sems[2 * i : 2 * i + 2] for i in range(5)]
    barrier = pltpu.get_barrier_semaphore()
    peers = plane_peers(chips, here)
    greet(barrier, peers)
    greet_line(barrier, planes, here)
    pl.semaphore_wait(barrier, len(peers) + line_peers(planes, here))
    part = mine.shape[1]
    line = LineScatter(
        planes,
        here,
        row_tiles(seqs, 1),
        lambda t, rows: grad_ref[t, rows].astype(F32),
        above,
        below,
        up,
        down,
    )
    line.step(0)
    work = PlaneScatter(
        chips, here, left_ref, right_ref, True, near_out, near_in, far_out, far_in, near, far
    )
    work.start()
    for i in range(1, planes - 1):
        line.step(i)

    def store(rows, total):
        mine[rows] = total.astype(LOW)

    line.finish(store)
    swaps = [
        remote(mine.at[2 * device[1] + device[2]], parts_ref.at[me], swap_sems, k, device)
        for k, device in enumerate(peers, 1)
    ]
    for copy in swaps:
        copy.start()
    parts_ref[me] = mine[me]
    work.finish(out_ref)
    for k in range(1, seqs):
        swaps[k - 1].wait_send()
        index = lax.rem(me + seqs - k, seqs)
        remote(mine.at[0], parts_ref.at[index], swap_sems, k, here).wait_recv()


def in_scatter(planes, chips, left, right, grads):
    _, tokens, _ = left.shape
    width = right.shape[0]
    seqs = 2 * chips
    part, wide = grads.shape[2:]
    return call(
        functools.partial(in_scatter_kernel, planes, chips),
        "in_scatter",
        [shape((tokens, width), F32), shape((seqs, part, wide), LOW)],
        (left, right, grads),
        [VMEM] * 3,
        [VMEM] * 2,
        [
            *[pltpu.VMEM((chips, tokens, width), LOW)] * 4,
            *[pltpu.VMEM((planes, seqs, part, wide), LOW)] * 2,
            pltpu.VMEM((seqs, part, wide), LOW),
            *pairs_of(chips, chips, planes, planes, seqs),
        ],
        4,
    )


def line_gather_kernel(planes, x_ref, out_ref, *sems):
    here = place()
    z, c, core = here
    up, down, near = [sems[2 * i : 2 * i + 2] for i in range(3)]
    partner = (z, c, 1 - core)
    barrier = pltpu.get_barrier_semaphore()
    greet(barrier, [partner])
    greet_line(barrier, planes, here)
    pl.semaphore_wait(barrier, 1 + line_peers(planes, here))
    keep = pltpu.make_async_copy(x_ref, out_ref.at[z, core], sems[6].at[0])
    keep.start()
    keep.wait()

    def passed(t):
        return remote(out_ref.at[t, core], out_ref.at[t, core], near, t, partner)

    line = LineGather(planes, here, lambda t: out_ref.at[t, core], up, down)
    line.start()
    passed(z).start()
    for d in range(1, planes):
        line.step(d, lambda t: passed(t).start())
    line.finish()
    for t in range(planes):
        passed(t).wait_send()
        remote(x_ref, out_ref.at[t, 1 - core], near, t, partner).wait_recv()


def line_gather(planes, x_block):
    return call(
        functools.partial(line_gather_kernel, planes),
        "line_gather",
        shape((planes, 2, *x_block.shape), x_block.dtype),
        (x_block,),
        [HBM],
        HBM,
        [*pairs_of(planes, planes, planes), pltpu.SemaphoreType.DMA((1,))],
        5,
    )


def sums_kernel(planes, x_ref, out_ref, slots, *sems):
    here = place()
    z, c, core = here
    count = 2 * planes
    me = 2 * z + core
    barrier = pltpu.get_barrier_semaphore()
    ids = [lax.rem(me + k, count) for k in range(1, count)]
    peers = [(index // 2, c, lax.rem(index, 2)) for index in ids]
    greet(barrier, peers)
    pl.semaphore_wait(barrier, len(peers))
    copies = [remote(x_ref, slots.at[k], sems, k, device) for k, device in enumerate(peers, 1)]
    for copy in copies:
        copy.start()
    for copy in copies:
        copy.wait_send()
        copy.wait_recv()
    total = x_ref[...]
    for k in range(1, count):
        total = total + slots[k]
    out_ref[...] = total


def group_sums(planes, stats):
    return call(
        functools.partial(sums_kernel, planes),
        "group_sums",
        shape(stats.shape, F32),
        (stats,),
        [VMEM],
        VMEM,
        [pltpu.VMEM((2 * planes, *stats.shape), F32), *pairs_of(2 * planes)],
        6,
    )


class PairScatter:
    def __init__(self, planes, here, left, right, turned, near_out, near_in, own, line, near):
        self.planes, self.here = planes, here
        self.left, self.right, self.turned = left, right, turned
        self.near_out, self.near_in, self.own, self.near = near_out, near_in, own, near
        tokens, width = near_out.shape[1:]
        self.tiles = [pl.ds(at, COLUMNS) for at in range(0, width, COLUMNS)]
        self.line = LineScatter(
            planes,
            here,
            row_tiles(tokens, 32),
            lambda t, rows: own[t, rows].astype(F32),
            *line,
        )

    def near_copy(self, t):
        z, c, core = self.here
        return remote(self.near_out.at[t], self.near_in.at[t], self.near, t, (z, c, 1 - core))

    def start(self):
        core = self.here[2]
        order = []
        for i in range((self.planes + 1) // 2):
            order += [self.planes - 1 - i, i] if self.planes - 1 - i != i else [i]
        for t in order:
            left = self.left[t, 1 - core]
            for columns in self.tiles:
                part = product(left, self.right, columns, self.turned)
                self.near_out[t, :, columns] = part.astype(LOW)
            self.near_copy(t).start()
        for t in order:
            left = self.left[t, core]
            self.near_copy(t).wait_recv()
            for columns in self.tiles:
                part = product(left, self.right, columns, self.turned)
                self.own[t, :, columns] = (
                    part + self.near_in[t, :, columns].astype(F32)
                ).astype(LOW)
        self.line.step(0)

    def finish(self, out_ref):
        def store(rows, total):
            out_ref[rows] = total

        self.line.finish(store)
        for t in range(self.planes):
            self.near_copy(t).wait_send()

    @staticmethod
    def scratch(planes, tokens, width):
        return [pltpu.VMEM((planes, tokens, width), LOW)] * 5


def line_scatter_kernel(
    planes, chips, left_ref, right_ref, grad_ref, out_ref, slots_ref,
    near_out, near_in, own, above, below, *sems,
):
    here = place()
    z, c, core = here
    near, up, down, swap_sems = [sems[2 * i : 2 * i + 2] for i in range(4)]
    barrier = pltpu.get_barrier_semaphore()
    peers = [(z, c, 1 - core), *chip_peers(chips, here)]
    greet(barrier, peers)
    greet_line(barrier, planes, here)
    pl.semaphore_wait(barrier, len(peers) + line_peers(planes, here))
    swap = ChipSwap(chips, here, lambda index: grad_ref.at[index], slots_ref, swap_sems)
    swap.start(sems[8].at[0])
    work = PairScatter(
        planes, here, left_ref, right_ref, True, near_out, near_in, own,
        (above, below, up, down), near,
    )
    work.start()
    for i in range(1, planes - 1):
        work.line.step(i)
    work.finish(out_ref)
    swap.finish()


def line_scatter(planes, chips, left, right, grads):
    tokens, width = left.shape[2], right.shape[0]
    return call(
        functools.partial(line_scatter_kernel, planes, chips),
        "line_scatter",
        [shape((tokens, width), F32), shape(grads.shape, LOW)],
        (left, right, grads),
        [VMEM, VMEM, HBM],
        [VMEM, HBM],
        [
            *PairScatter.scratch(planes, tokens, width),
            *pairs_of(planes, planes, planes, chips),
            pltpu.SemaphoreType.DMA((1,)),
        ],
        7,
    )


def swap_lanes(values):
    lane = lax.broadcasted_iota(jnp.int32, values.shape, 1)
    return jnp.where(
        lax.rem(lane, 2) == 0,
        pltpu.roll(values, values.shape[1] - 1, 1),
        pltpu.roll(values, 1, 1),
    )


def twice(table):
    return jnp.concatenate([table, table], axis=1)


def turns(meta_ref, rows):
    cosine, sine, shrink = [twice(meta_ref[rows, pl.ds(i * HD, HD)]) for i in range(3)]
    return (cosine, sine, cosine * shrink, sine * shrink)


def allowed_block(meta_ref, rows, size, columns):
    query = rows + lax.broadcasted_iota(jnp.int32, (size, columns), 0)
    key = lax.broadcasted_iota(jnp.int32, (size, columns), 1)
    offset = meta_ref[pl.ds(rows, size), pl.ds(3 * HD, 1)].astype(jnp.int32)
    return (key <= query) & (key >= query - offset)


BLOCK = 256


def attention_kernel(heads, raw_ref, meta_ref, q_ref, k_ref, v_ref, out_ref, log_ref, wide):
    length = raw_ref.shape[0]
    span = heads * HD
    for rows in row_tiles(length, BLOCK):
        tables = turns(meta_ref, rows)
        for pair in range(heads // 2):
            lanes = pl.ds(2 * HD * pair, 2 * HD)
            query = raw_ref[rows, lanes]
            query = (query * tables[0] + swap_lanes(query) * tables[1]).astype(LOW)
            key = raw_ref[rows, pl.ds(span + 2 * HD * pair, 2 * HD)]
            key = (key * tables[2] + swap_lanes(key) * tables[3]).astype(LOW)
            value = raw_ref[rows, pl.ds(2 * span + 2 * HD * pair, 2 * HD)].astype(LOW)
            for half in range(2):
                at = slice(half * HD, (half + 1) * HD)
                q_ref[2 * pair + half, rows] = query[:, at]
                k_ref[2 * pair + half, rows] = key[:, at]
                v_ref[2 * pair + half, rows] = value[:, at]
    log_ref[...] = jnp.zeros(log_ref.shape, F32)

    def one_head(head, carry):
        for start in range(0, length, BLOCK):
            columns = start + BLOCK
            rows = pl.ds(start, BLOCK)
            scores = lax.dot_general(
                q_ref[head, rows],
                k_ref[head, pl.ds(0, columns)],
                (((1,), (1,)), ((), ())),
                preferred_element_type=F32,
            )
            allowed = allowed_block(meta_ref, start, BLOCK, columns)
            scores = jnp.where(allowed, scores, NEG_FILL)
            top = jnp.max(scores, axis=1, keepdims=True)
            shifted = jnp.exp(scores - top)
            total = jnp.sum(shifted, axis=1, keepdims=True)
            probs = (shifted * (1.0 / total)).astype(LOW)
            wide[head, rows] = jnp.dot(
                probs, v_ref[head, pl.ds(0, columns)], preferred_element_type=F32
            )
            lane = lax.broadcasted_iota(jnp.int32, (BLOCK, 128), 1)
            log_ref[rows] = jnp.where(lane == head, top + jnp.log(total), log_ref[rows])
        return carry

    lax.fori_loop(0, heads, one_head, 0)
    for rows in row_tiles(length, BLOCK):
        out_ref[rows] = jnp.concatenate(
            [wide[head, rows] for head in range(heads)], axis=1
        ).astype(LOW)


def attention(heads, raw, meta):
    length = raw.shape[0]
    return call(
        functools.partial(attention_kernel, heads),
        "attention",
        [
            *[shape((heads, length, HD), LOW)] * 3,
            shape((length, heads * HD), LOW),
            shape((length, 128), F32),
        ],
        (raw, meta),
        [VMEM] * 2,
        [VMEM] * 5,
        [pltpu.VMEM((heads, length, HD), F32)],
    )


def attention_back_kernel(
    planes, chips, heads,
    q_ref, k_ref, v_ref, att_ref, sub_ref, stat_ref, log_ref, meta_ref, left_ref, right_ref, up_ref,
    out_ref, normed_ref, ffn_ref, slots_ref,
    grad, dq, dk, dv, near_out, near_in, own, above, below, *sems,
):
    here = place()
    z, c, core = here
    near, up, down, swap_sems = [sems[2 * i : 2 * i + 2] for i in range(4)]
    barrier = pltpu.get_barrier_semaphore()
    peers = [(z, c, 1 - core), *chip_peers(chips, here)]
    greet(barrier, peers)
    greet_line(barrier, planes, here)
    pl.semaphore_wait(barrier, len(peers) + line_peers(planes, here))
    units = slots_ref.shape[2]
    swap = ChipSwap(
        chips, here, lambda index: column_block(up_ref, units, index), slots_ref, swap_sems
    )
    swap.start(sems[8].at[0])
    work = PairScatter(
        planes, here, left_ref, right_ref, False, near_out, near_in, own,
        (above, below, up, down), near,
    )
    work.start()
    length = att_ref.shape[0]
    span = heads * HD
    for rows in row_tiles(length, BLOCK):
        mean, scaler, first, second = (stat_ref[rows, pl.ds(i, 1)] for i in range(4))
        normed = (att_ref[rows].astype(F32) - mean) * scaler
        normed_ref[rows] = normed.astype(LOW)
        d_att = (scaler * (sub_ref[rows] - first - normed * second)).astype(LOW)
        for head in range(heads):
            grad[head, rows] = d_att[:, head * HD : (head + 1) * HD]
    dk[...] = jnp.zeros(dk.shape, F32)
    dv[...] = jnp.zeros(dv.shape, F32)

    def one_head(head, carry):
        for start in range(0, length, BLOCK):
            columns = start + BLOCK
            rows = pl.ds(start, BLOCK)
            keys = pl.ds(0, columns)
            query, key = q_ref[head, rows], k_ref[head, keys]
            out_grad = grad[head, rows]
            scores = lax.dot_general(
                query, key, (((1,), (1,)), ((), ())), preferred_element_type=F32
            )
            allowed = allowed_block(meta_ref, start, BLOCK, columns)
            lane = lax.broadcasted_iota(jnp.int32, (BLOCK, 128), 1)
            log_total = jnp.sum(
                jnp.where(lane == head, log_ref[rows], 0.0), axis=1, keepdims=True
            )
            probs = jnp.where(allowed, jnp.exp(scores - log_total), 0.0)
            d_probs = lax.dot_general(
                out_grad, v_ref[head, keys], (((1,), (1,)), ((), ())), preferred_element_type=F32
            )
            delta = jnp.sum(probs * d_probs, axis=1, keepdims=True)
            d_scores = (probs * (d_probs - delta)).astype(LOW)
            dq[head, rows] = jnp.dot(d_scores, key, preferred_element_type=F32)
            dk[head, keys] += token_product(d_scores, query)
            dv[head, keys] += token_product(probs.astype(LOW), out_grad)
        return carry

    first = 0
    for i in range(1, planes - 1):
        last = -(-heads * i // (planes - 1))
        lax.fori_loop(first, last, one_head, 0)
        first = last
        work.line.step(i)
    lax.fori_loop(first, heads, one_head, 0)
    for rows in row_tiles(length, BLOCK):
        tables = turns(meta_ref, rows)
        for pair in range(heads // 2):
            both = [
                jnp.concatenate(
                    [whole[2 * pair, rows], whole[2 * pair + 1, rows]], axis=1
                ).astype(LOW)
                for whole in (dq, dk, dv)
            ]
            query, key = both[0].astype(F32), both[1].astype(F32)
            query = query * tables[0] + swap_lanes(query * tables[1])
            key = key * tables[2] + swap_lanes(key * tables[3])
            out_ref[rows, pl.ds(2 * HD * pair, 2 * HD)] = query.astype(LOW)
            out_ref[rows, pl.ds(span + 2 * HD * pair, 2 * HD)] = key.astype(LOW)
            out_ref[rows, pl.ds(2 * span + 2 * HD * pair, 2 * HD)] = both[2]
    work.finish(ffn_ref)
    swap.finish()


def attention_back(planes, chips, heads, units, attention_args, left, right, up_grads):
    length, span = attention_args[3].shape
    tokens, width = left.shape[2], right.shape[1]
    return call(
        functools.partial(attention_back_kernel, planes, chips, heads),
        "attention_back",
        [
            shape((length, 3 * span), LOW),
            shape((length, span), LOW),
            shape((tokens, width), F32),
            shape((chips, width, units), LOW),
        ],
        (*attention_args, left, right, up_grads),
        [*[VMEM] * 10, HBM],
        [*[VMEM] * 3, HBM],
        [
            pltpu.VMEM((heads, length, HD), LOW),
            *[pltpu.VMEM((heads, length, HD), F32)] * 3,
            *PairScatter.scratch(planes, tokens, width),
            *pairs_of(planes, planes, planes, chips),
            pltpu.SemaphoreType.DMA((1,)),
        ],
        8,
    )


def body(
    hidden_in,
    segment_ids,
    position_ids,
    w_qkv,
    w_out,
    w_up,
    w_down,
    gain_attn,
    gain_attn_sub,
    gain_ffn,
    gain_ffn_sub,
    ema_qkv,
    ema_out,
    ema_up,
    ema_down,
    ema_gain_attn,
    ema_gain_attn_sub,
    ema_gain_ffn,
    ema_gain_ffn_sub,
    out_grad,
):
    _, tokens, width = hidden_in.shape
    planes, chips = lax.axis_size("dp"), lax.axis_size("chip")
    seqs = 2 * chips
    length = tokens * seqs
    heads = HEADS // seqs
    span = heads * HD
    part = w_qkv.shape[0]
    strided = part % HD == 0
    group_tokens = planes * 2 * tokens
    width_ff = w_down.shape[0] * planes * seqs
    seq_index = lax.axis_index(SEQ)

    def gain_rows(weight, gain):
        return (weight.astype(F32) * gain.astype(F32)[:, None]).astype(LOW)

    qkv_scaled = gain_rows(w_qkv, gain_attn)
    out_scaled = gain_rows(w_out, gain_attn_sub)
    down_scaled = gain_rows(w_down, gain_ffn_sub)
    if strided:
        qkv_send = qkv_scaled.reshape(part, 3, planes, seqs, HD).transpose(3, 0, 1, 2, 4)
    else:
        qkv_send = qkv_scaled.reshape(part, 3, seqs, span).transpose(2, 0, 1, 3)
    qkv_send = qkv_send.reshape(seqs, part, 3 * span)
    x_in = hidden_in[0].astype(F32)
    normed_one, scaler_one = moments(x_in)
    normed_low = normed_one.astype(LOW)
    gain_tile = jnp.zeros((8, 128), F32).at[0, :part].set(gain_ffn.astype(F32))

    row_in, meta, qkv_mine, out_mine, gain_tiles, up_mine = attention_gather(
        planes,
        chips,
        normed_low,
        token_tables(position_ids[0]),
        qkv_send,
        out_scaled,
        gain_tile,
        w_up,
    )
    if up_mine.ndim == 3:
        up_mine = up_mine.transpose(1, 0, 2).reshape(width, -1)
    row_in = row_in.reshape(length, width)
    meta = meta.reshape(length, -1)
    qkv_mine = qkv_mine.reshape(width, 3 * span)
    if strided:
        out_mine = out_mine.reshape(span, width)
    else:
        out_all = lax.all_gather(out_scaled, ALL, axis=0, tiled=True)
        out_mine = lax.dynamic_slice_in_dim(out_all, seq_index * span, span, axis=0)
    grad_low, gain_tiles = lax.optimization_barrier((out_grad[0], gain_tiles))
    grad_flat = lax.all_gather(grad_low, TP, axis=0, tiled=True)
    queries, keys, values, attended, log_total = attention(heads, dot(row_in, qkv_mine), meta)
    down_scaled, attended = lax.optimization_barrier((down_scaled, attended))
    down_mine = lax.all_gather(down_scaled, "chip", axis=0, tiled=True)
    attended_wide = attended.astype(F32)
    column_part = jnp.sum(out_mine.astype(F32), axis=0)
    token_sums = jnp.stack(
        [jnp.sum(attended_wide, axis=1), jnp.sum(attended_wide * attended_wide, axis=1)]
    ).reshape(2, seqs, tokens)
    tiles = jnp.concatenate(
        [
            jnp.swapaxes(token_sums, 0, 1),
            jnp.zeros((seqs, 6, tokens), F32),
            jnp.broadcast_to(column_part.reshape(1, -1, tokens), (seqs, width // tokens, tokens)),
        ],
        axis=1,
    )
    out_sum, tiles = out_scatter(chips, attended.reshape(seqs, tokens, span), out_mine, tiles)
    tiles = jnp.sum(tiles, axis=0)
    column_sum = tiles[8:].reshape(width)
    sums = tiles[:2].T
    gain_three = gain_tiles[:, 0, :part].reshape(width)
    mean_two = sums[:, :1] / width
    scaler_two = lax.rsqrt(sums[:, 1:] / width - mean_two * mean_two + NORM_EPS)
    projected = scaler_two * (out_sum - mean_two * column_sum[None, :])
    hmid = x_in + projected
    normed_three, scaler_three = moments(hmid)
    ffn_in = (normed_three * gain_three).astype(LOW)

    grad_top = grad_low.astype(F32)
    ffn_flat = line_gather(planes, ffn_in).reshape(group_tokens, width)
    weighted = rows_product(grad_flat, down_mine)
    up_slice = dot(ffn_flat, up_mine)
    activated, gelu_pull = jax.vjp(exact_gelu, up_slice)
    stats = group_sums(
        planes,
        jnp.stack(
            [
                jnp.sum(activated, axis=1),
                jnp.sum(activated * activated, axis=1),
                jnp.sum(weighted * activated, axis=1),
                jnp.sum(weighted, axis=1),
            ]
        ),
    )[:, :, None]
    act_mean = stats[0] / width_ff
    scaler_four = lax.rsqrt(stats[1] / width_ff - act_mean * act_mean + NORM_EPS)
    normed_four = (activated - act_mean) * scaler_four
    normed_four_low = normed_four.astype(LOW)
    first_mean = stats[3] / width_ff
    second_mean = scaler_four * (stats[2] - act_mean * stats[3]) / width_ff
    d_act = scaler_four * (weighted - first_mean - normed_four * second_mean)
    (d_up,) = gelu_pull(d_act)
    d_up_low = d_up.astype(LOW)
    grad_up = token_product(ffn_flat, d_up_low).astype(LOW)
    grad_down = token_product(normed_four_low, grad_flat).astype(LOW)
    units = w_up.shape[1]
    if units % 128:
        grad_up = grad_up.reshape(width, chips, units).transpose(1, 0, 2)
    d_up_low, grad_up = lax.optimization_barrier((d_up_low, grad_up))
    d_ffn_in, down_slots = line_scatter(
        planes,
        chips,
        d_up_low.reshape(planes, 2, tokens, -1),
        up_mine,
        grad_down.reshape(chips, -1, width),
    )

    gain_part = jnp.sum(d_ffn_in * normed_three, axis=0).reshape(planes * seqs, 1, part)
    gain_part = jnp.pad(gain_part, ((0, 0), (0, 7), (0, 128 - part)))
    d_hmid = grad_top + norm_back(d_ffn_in * gain_three, normed_three, scaler_three)
    d_hmid_low = d_hmid.astype(LOW)
    d_hmid_wide = d_hmid_low.astype(F32)
    first_two = jnp.sum(d_hmid_wide * column_sum[None, :], axis=1, keepdims=True) / width
    second_two = jnp.sum(d_hmid_wide * projected, axis=1, keepdims=True) / width
    token_stats = jnp.concatenate([mean_two, scaler_two, first_two, second_two], axis=1)
    row_grad, row_stats, gain_part = plane_gather(
        planes, chips, d_hmid_low, jnp.pad(token_stats, ((0, 0), (0, 124))), gain_part
    )
    row_grad = row_grad.reshape(length, width)
    row_stats = row_stats.reshape(length, 128)
    grad_gain_three = jnp.sum(gain_part, axis=0)[0, :part]
    d_sub = rows_product(row_grad, out_mine)
    d_qkv, normed_two, ffn_out, up_slots = attention_back(
        planes,
        chips,
        heads,
        units,
        (queries, keys, values, attended, d_sub, row_stats, log_total, meta),
        normed_four_low.reshape(planes, 2, tokens, -1),
        down_mine,
        grad_up,
    )
    output = (hmid + ffn_out).astype(LOW)[None]
    sum_up = jnp.sum(up_slots.astype(F32), axis=0)
    sum_down = jnp.sum(down_slots.astype(F32), axis=0)
    grad_out = token_product(normed_two, row_grad)
    grad_qkv = token_product(row_in, d_qkv).astype(LOW)
    d_in, part_qkv = in_scatter(
        planes,
        chips,
        d_qkv.reshape(seqs, tokens, 3 * span),
        qkv_mine,
        grad_qkv.reshape(planes, seqs, part, 3 * span),
    )
    input_grad = (d_hmid + norm_back(d_in, normed_one, scaler_one)).astype(LOW)[None]

    if strided:
        sum_qkv = part_qkv.reshape(seqs, part, 3, planes, HD).transpose(1, 2, 3, 0, 4)
        sum_out = lax.psum_scatter(grad_out.astype(LOW), "dp", scatter_dimension=0, tiled=True)
    else:
        sum_qkv = part_qkv.reshape(seqs, part, 3, span).transpose(1, 2, 0, 3)
        spread = lax.dynamic_update_slice_in_dim(
            jnp.zeros((width, width), LOW), grad_out.astype(LOW), seq_index * span, axis=0
        )
        sum_out = lax.psum_scatter(spread, ALL, scatter_dimension=0, tiled=True)
    sum_qkv = sum_qkv.reshape(part, 3 * width).astype(F32)
    sum_out = sum_out.astype(F32)

    def finish(total, weight, gain):
        wide = weight.astype(F32)
        return (total * gain.astype(F32)[:, None], jnp.sum(total * wide, axis=1))

    sum_qkv, grad_gain_one = finish(sum_qkv, w_qkv, gain_attn)
    sum_out, grad_gain_two = finish(sum_out, w_out, gain_attn_sub)
    sum_down, grad_gain_four = finish(sum_down, w_down, gain_ffn_sub)

    def averaged(average, weight):
        return EMA_DECAY * average + (1.0 - EMA_DECAY) * weight.astype(F32)

    return (
        output,
        input_grad,
        sum_qkv,
        sum_out,
        sum_up,
        sum_down,
        grad_gain_one,
        grad_gain_two,
        grad_gain_three,
        grad_gain_four,
        averaged(ema_qkv, w_qkv),
        averaged(ema_out, w_out),
        averaged(ema_up, w_up),
        averaged(ema_down, w_down),
        averaged(ema_gain_attn, gain_attn),
        averaged(ema_gain_attn_sub, gain_attn_sub),
        averaged(ema_gain_ffn, gain_ffn),
        averaged(ema_gain_ffn_sub, gain_ffn_sub),
    )


def solution(mesh):
    split = Mesh(
        mesh.devices.reshape(mesh.shape["dp"], mesh.shape["seq"] // 2, 2), ("dp", "chip", "core")
    )
    tokens = P("dp", SEQ, None)
    ids = P("dp", SEQ)
    rows = P(ALL, None)
    columns = P(None, ALL)
    vector = P(ALL)
    weights = (rows, rows, columns, rows)
    gains = (vector,) * 4
    return jax.shard_map(
        body,
        mesh=split,
        in_specs=(tokens, ids, ids, *weights, *gains, *weights, *gains, tokens),
        out_specs=(tokens, tokens, *weights, *gains, *weights, *gains),
        check_vma=False,
    )
```

```python
import functools
import math

import jax
import jax.numpy as jnp
from jax import lax
from jax.experimental import pallas as pl
from jax.experimental.pallas import tpu as pltpu
from jax.sharding import Mesh
from jax.sharding import PartitionSpec as P

HEADS = 32
HD = 64

NEG_FILL = -1000000000.0
NORM_EPS = 1e-05
EMA_DECAY = 0.7
LOW = jnp.bfloat16
F32 = jnp.float32
SEQ = ("chip", "core")
TP = ("dp", "core")
ALL = ("dp", "chip", "core")


def moments(values):
    mean = jnp.mean(values, axis=-1, keepdims=True)
    centered = values - mean
    scaler = lax.rsqrt(jnp.mean(centered * centered, axis=-1, keepdims=True) + NORM_EPS)
    return (centered * scaler, scaler)


def norm_back(scaled_grad, normed, scaler):
    first_mean = jnp.mean(scaled_grad, axis=-1, keepdims=True)
    second_mean = jnp.mean(scaled_grad * normed, axis=-1, keepdims=True)
    return scaler * (scaled_grad - first_mean - normed * second_mean)


def exact_gelu(values):
    return jax.nn.gelu(values, approximate=False)


def token_tables(positions):
    half_count = HD // 2
    index_half = jnp.arange(half_count).astype(F32)
    inverse = jnp.exp(-(2.0 * index_half / HD) * math.log(10000.0))
    decay_base = (2.0 * index_half + 0.4 * HD) / (1.4 * HD)
    where_at = positions.astype(F32)[:, None]
    angles = where_at * inverse[None, :]
    factor = jnp.exp(where_at / 512.0 * jnp.log(decay_base)[None, :])
    sign_row = jnp.where(jnp.arange(HD) % 2 == 0, -1.0, 1.0).astype(F32)
    cosine = jnp.repeat(jnp.cos(angles), 2, axis=1)
    sine = jnp.repeat(jnp.sin(angles), 2, axis=1) * sign_row[None, :]
    factor = jnp.repeat(factor, 2, axis=1)
    grow = factor * HD ** (-0.5)
    where_block = jnp.broadcast_to(where_at, (positions.shape[0], HD))
    return jnp.concatenate(
        [cosine * grow, sine * grow, HD**0.5 / (factor * factor), where_block], axis=1
    )


def dot(left_op, right_op):
    return jnp.dot(left_op, right_op, preferred_element_type=F32)


def rows_product(operand, weight_rows):
    return lax.dot_general(
        operand, weight_rows, (((1,), (1,)), ((), ())), preferred_element_type=F32
    )


def token_product(left_op, right_op):
    return lax.dot_general(left_op, right_op, (((0,), (0,)), ((), ())), preferred_element_type=F32)


MESH = pl.DeviceIdType.MESH
HBM = pl.BlockSpec(memory_space=pl.ANY)
VMEM = pl.BlockSpec(memory_space=pltpu.VMEM)
VMEM_BYTES = 56 * 1024 * 1024


def shape(dims, kind):
    return jax.ShapeDtypeStruct(dims, kind)


def pairs_of(*counts):
    return [pltpu.SemaphoreType.DMA((count,)) for count in counts for _ in range(2)]


def call(kernel, name, outs, args, in_specs, out_specs, scratch, collective=None):
    return pl.pallas_call(
        kernel,
        name=name,
        out_shape=outs,
        in_specs=in_specs,
        out_specs=out_specs,
        scratch_shapes=scratch,
        compiler_params=pltpu.CompilerParams(
            collective_id=collective,
            has_side_effects=collective is not None,
            vmem_limit_bytes=VMEM_BYTES,
        ),
    )(*args)


def place():
    return (lax.axis_index("dp"), lax.axis_index("chip"), lax.axis_index("core"))


def remote(source, target, sems, index, device):
    return pltpu.make_async_remote_copy(
        src_ref=source,
        dst_ref=target,
        send_sem=sems[0].at[index],
        recv_sem=sems[1].at[index],
        device_id=device,
        device_id_type=MESH,
    )


def greet(barrier, devices):
    for device in devices:
        pl.semaphore_signal(barrier, inc=1, device_id=device, device_id_type=MESH)


def greet_line(barrier, planes, here):
    z, c, core = here

    @pl.when(z < planes - 1)
    def _():
        greet(barrier, [(z + 1, c, core)])

    @pl.when(z > 0)
    def _():
        greet(barrier, [(z - 1, c, core)])


def line_peers(planes, here):
    z = here[0]
    return (2 * planes - 2 - z) // planes + (z + planes - 1) // planes


def chip_peers(chips, here):
    z, c, core = here
    return [(z, lax.rem(c + k, chips), core) for k in range(1, chips)]


def plane_peers(chips, here):
    z, c, core = here
    seqs = 2 * chips
    me = 2 * c + core
    ids = [lax.rem(me + k, seqs) for k in range(1, seqs)]
    return [(z, index // 2, lax.rem(index, 2)) for index in ids]


def column_block(whole, units, index):
    if len(whole.shape) == 3:
        return whole.at[index]
    return whole.at[:, pl.ds(pl.multiple_of(index * units, 128), units)]


class ChipSwap:
    def __init__(self, chips, here, source, slots, sems):
        z, c, core = here
        self.sends = [
            remote(source(device[1]), slots.at[c], sems, k, device)
            for k, device in enumerate(chip_peers(chips, here), 1)
        ]
        self.waits = [
            remote(source(c), slots.at[lax.rem(c + chips - k, chips)], sems, k, here)
            for k in range(1, chips)
        ]
        self.keep = (source(c), slots.at[c])

    def start(self, local):
        for copy in self.sends:
            copy.start()
        self.held = pltpu.make_async_copy(*self.keep, local)
        self.held.start()

    def finish(self):
        self.held.wait()
        for send, wait in zip(self.sends, self.waits):
            send.wait_send()
            wait.wait_recv()


class PlaneGather:
    def __init__(self, chips, here, block, out, far, near):
        self.chips, self.here, self.block, self.out = chips, here, block, out
        self.far, self.near = far, near
        z, c, core = here
        self.me = 2 * c + core
        self.partner = (z, c, 1 - core)

    def source(self, k, core):
        return 2 * lax.rem(self.here[1] + self.chips - k, self.chips) + core

    def sends(self):
        mine = self.out.at[self.me]
        copies = [
            remote(self.block, mine, self.far, k, device)
            for k, device in enumerate(chip_peers(self.chips, self.here), 1)
        ]
        return [*copies, remote(self.block, mine, self.near, 0, self.partner)]

    def start(self):
        for copy in self.sends():
            copy.start()

    def passed(self, k):
        index = self.source(k, self.here[2])
        return remote(self.out.at[index], self.out.at[index], self.near, k, self.partner)

    def forward(self):
        for k in range(1, self.chips):
            index = self.source(k, self.here[2])
            remote(self.block, self.out.at[index], self.far, k, self.partner).wait_recv()
            self.passed(k).start()

    def finish(self):
        for copy in self.sends():
            copy.wait_send()
        for k in range(1, self.chips):
            self.passed(k).wait_send()
        for k in range(self.chips):
            index = self.source(k, 1 - self.here[2])
            remote(self.block, self.out.at[index], self.near, k, self.partner).wait_recv()


class LineGather:
    def __init__(self, planes, here, parts, up, down):
        self.planes, self.here, self.parts = planes, here, parts
        self.up, self.down = up, down
        self.count = len(parts(here[0]))

    def upward(self, d, p):
        z, c, core = self.here
        block = self.parts(z - d)[p]
        return remote(block, block, self.up, d * self.count + p, (z + 1, c, core))

    def downward(self, d, p):
        z, c, core = self.here
        block = self.parts(z + d)[p]
        return remote(block, block, self.down, d * self.count + p, (z - 1, c, core))

    def each(self, d, p, act):
        z, planes = self.here[0], self.planes
        pl.when((z < planes - 1) & (z - d >= 0))(lambda: act(self.upward(d, p)))
        pl.when((z > 0) & (z + d < planes))(lambda: act(self.downward(d, p)))

    def start(self):
        for p in range(self.count):
            self.each(0, p, lambda copy: copy.start())

    def step(self, d, arrived=None):
        z, planes = self.here[0], self.planes

        def below(p):
            block = self.parts(z - d)[p]
            remote(block, block, self.up, (d - 1) * self.count + p, self.here).wait_recv()
            if d < planes - 1:
                pl.when(z < planes - 1)(lambda: self.upward(d, p).start())
            if arrived is not None:
                arrived(z - d, p)

        def above(p):
            block = self.parts(z + d)[p]
            remote(block, block, self.down, (d - 1) * self.count + p, self.here).wait_recv()
            if d < planes - 1:
                pl.when(z > 0)(lambda: self.downward(d, p).start())
            if arrived is not None:
                arrived(z + d, p)

        for p in range(self.count):
            pl.when(z - d >= 0)(lambda p=p: below(p))
            pl.when(z + d < planes)(lambda p=p: above(p))

    def finish(self):
        for d in range(self.planes - 1):
            for p in range(self.count):
                self.each(d, p, lambda copy: copy.wait_send())


class GroupGather:
    PARTS = 2

    def __init__(self, planes, here, block, out, up, down, near):
        self.planes, self.here, self.block, self.out, self.near = planes, here, block, out, near
        self.partner = (here[0], here[1], 1 - here[2])
        size = block.shape[0] // self.PARTS
        self.slices = [pl.ds(p * size, size) for p in range(self.PARTS)]
        core = here[2]
        self.line = LineGather(planes, here, lambda t: self.parts(t, core), up, down)

    def parts(self, t, core):
        return [self.out.at[t, core, rows] for rows in self.slices]

    def passed(self, t, p):
        block = self.parts(t, self.here[2])[p]
        return remote(block, block, self.near, t * self.PARTS + p, self.partner)

    def start(self, local):
        z, _, core = self.here
        keep = pltpu.make_async_copy(self.block, self.out.at[z, core], local)
        keep.start()
        keep.wait()
        self.line.start()
        for p in range(self.PARTS):
            self.passed(z, p).start()

    def step(self, d):
        self.line.step(d, lambda t, p: self.passed(t, p).start())

    def finish(self):
        self.line.finish()
        for t in range(self.planes):
            for p in range(self.PARTS):
                self.passed(t, p).wait_send()
                block = self.parts(t, 1 - self.here[2])[p]
                remote(block, block, self.near, t * self.PARTS + p, self.partner).wait_recv()

    @classmethod
    def sems(cls, planes):
        return pairs_of(*[planes * cls.PARTS] * 3)


def attention_gather_kernel(
    planes, chips, x_ref, meta_ref, qkv_ref, out_ref, gain_ref, up_ref,
    row_ref, metas_ref, qkvs_ref, outs_ref, gains_ref, ups_ref,
    *sems,
):
    here = place()
    z, c, core = here
    seqs = 2 * chips
    count = planes * seqs
    me = 2 * c + core
    flat = z * seqs + me
    groups = [sems[2 * i : 2 * i + 2] for i in range(11)]
    swap_sems, x_far, x_near, meta_far, meta_near, up, down, up_two, down_two = groups[:9]
    gain_sems, up_sems = groups[9:]
    local = sems[22]
    barrier = pltpu.get_barrier_semaphore()

    def device_of(k):
        other = lax.rem(flat + k, count)
        return (other // seqs, lax.rem(other, seqs) // 2, lax.rem(other, 2))

    def signal(k, carry):
        greet(barrier, [device_of(k)])
        return carry

    lax.fori_loop(1, count, signal, 0)
    pl.semaphore_wait(barrier, count - 1)

    mine = pltpu.make_async_copy(qkv_ref.at[me], qkvs_ref.at[z, me], local.at[0])
    keeps = [
        pltpu.make_async_copy(x_ref, row_ref.at[me], local.at[1]),
        pltpu.make_async_copy(meta_ref, metas_ref.at[me], local.at[2]),
        pltpu.make_async_copy(gain_ref, gains_ref.at[flat], local.at[3]),
    ]
    own_out = pltpu.make_async_copy(out_ref, outs_ref.at[z], local.at[4])
    units = up_ref.shape[1]
    keeps.append(pltpu.make_async_copy(up_ref, column_block(ups_ref, units, c), local.at[5]))
    ups = [
        remote(up_ref, column_block(ups_ref, units, c), up_sems, k, device)
        for k, device in enumerate(chip_peers(chips, here), 1)
    ]
    swaps = [
        remote(qkv_ref.at[2 * device[1] + device[2]], qkvs_ref.at[z, me], swap_sems, k, device)
        for k, device in enumerate(plane_peers(chips, here), 1)
    ]
    mine.start()
    own_out.start()
    for copy in swaps:
        copy.start()
    rows = PlaneGather(chips, here, x_ref, row_ref, x_far, x_near)
    metas = PlaneGather(chips, here, meta_ref, metas_ref, meta_far, meta_near)
    rows.start()
    metas.start()
    for copy in keeps:
        copy.start()

    def gain_copy(k):
        return remote(gain_ref, gains_ref.at[flat], gain_sems, k, device_of(k))

    def gain_start(k, carry):
        gain_copy(k).start()
        return carry

    lax.fori_loop(1, count, gain_start, 0)

    mine.wait()
    own_out.wait()
    for k in range(1, seqs):
        index = lax.rem(me + seqs - k, seqs)
        remote(qkv_ref.at[0], qkvs_ref.at[z, index], swap_sems, k, here).wait_recv()
    half = seqs // 2
    line = LineGather(
        planes, here, lambda t: [qkvs_ref.at[t, pl.ds(i * half, half)] for i in range(2)], up, down
    )
    line_two = LineGather(planes, here, lambda t: [outs_ref.at[t]], up_two, down_two)
    line.start()
    line_two.start()
    rows.forward()
    metas.forward()
    for copy in ups:
        copy.start()
    for d in range(1, planes):
        line.step(d)
        line_two.step(d)
    line.finish()
    line_two.finish()
    rows.finish()
    metas.finish()
    for copy in swaps:
        copy.wait_send()
    for copy in keeps:
        copy.wait()
    for k in range(1, chips):
        ups[k - 1].wait_send()
        other = lax.rem(c + chips - k, chips)
        remote(up_ref, column_block(ups_ref, units, other), up_sems, k, here).wait_recv()

    def gain_wait(k, carry):
        gain_copy(k).wait_send()
        other = lax.rem(flat + count - k, count)
        remote(gain_ref, gains_ref.at[other], gain_sems, k, here).wait_recv()
        return carry

    lax.fori_loop(1, count, gain_wait, 0)


def attention_gather(planes, chips, x_block, meta, qkv_blocks, out_rows, gain_tile, up_block):
    seqs = 2 * chips
    part, wide = qkv_blocks.shape[1:]
    width, units = up_block.shape
    return call(
        functools.partial(attention_gather_kernel, planes, chips),
        "attention_gather",
        [
            shape((seqs, *x_block.shape), LOW),
            shape((seqs, *meta.shape), F32),
            shape((planes, seqs, part, wide), LOW),
            shape((planes, *out_rows.shape), LOW),
            shape((planes * seqs, *gain_tile.shape), F32),
            shape(
                (width, chips * units) if units % 128 == 0 else (chips, width, units), LOW
            ),
        ],
        (x_block, meta, qkv_blocks, out_rows, gain_tile, up_block),
        [HBM] * 6,
        [HBM] * 6,
        [
            *pairs_of(
                seqs, *[chips] * 4, *[2 * planes] * 2, *[planes] * 2, planes * seqs, chips
            ),
            pltpu.SemaphoreType.DMA((6,)),
        ],
        1,
    )


COLUMNS = 512


def product(left, right, columns, turned):
    if turned:
        return lax.dot_general(
            left, right[columns, :], (((1,), (1,)), ((), ())), preferred_element_type=F32
        )
    return jnp.dot(left, right[:, columns], preferred_element_type=F32)


class PlaneScatter:
    def __init__(self, chips, here, left, right, turned, buffers, near, far):
        self.chips, self.here = chips, here
        self.left, self.right, self.turned = left, right, turned
        self.near_out, self.near_in, self.far_out, self.far_in = buffers
        self.near, self.far = near, far
        self.tokens, width = self.near_out.shape[1:]
        self.tiles = [pl.ds(at, COLUMNS) for at in range(0, width, COLUMNS)]
        self.order = [*range(1, chips), 0]

    def target(self, k):
        return lax.rem(self.here[1] + k, self.chips)

    def near_copy(self, i):
        z, c, core = self.here
        at = (slice(None), slice(None), self.tiles[i])
        return remote(self.near_out.at[at], self.near_in.at[at], self.near, i, (z, c, 1 - core))

    def far_copy(self, k, i):
        z, _, core = self.here
        at = (k, slice(None), self.tiles[i])
        index = k * len(self.tiles) + i
        return remote(
            self.far_out.at[at], self.far_in.at[at], self.far, index, (z, self.target(k), core)
        )

    def rows(self, position):
        return slice(position * self.tokens, (position + 1) * self.tokens)

    def start(self):
        core = self.here[2]
        blocks = [self.left[2 * self.target(k) + 1 - core] for k in self.order]
        left = jnp.concatenate(blocks, axis=0)
        for i, columns in enumerate(self.tiles):
            part = product(left, self.right, columns, self.turned).astype(LOW)
            for position, k in enumerate(self.order):
                self.near_out[k, :, columns] = part[self.rows(position)]
            self.near_copy(i).start()
        blocks = [self.left[2 * self.target(k) + core] for k in self.order]
        left = jnp.concatenate(blocks, axis=0)
        for i, columns in enumerate(self.tiles):
            part = product(left, self.right, columns, self.turned)
            self.near_copy(i).wait_recv()
            for position, k in enumerate(self.order):
                self.far_out[k, :, columns] = (
                    part[self.rows(position)] + self.near_in[k, :, columns].astype(F32)
                ).astype(LOW)
                if k:
                    self.far_copy(k, i).start()

    def finish(self, out_ref):
        for i, columns in enumerate(self.tiles):
            total = self.far_out[0, :, columns].astype(F32)
            for k in range(1, self.chips):
                self.far_copy(k, i).wait_recv()
                total = total + self.far_in[k, :, columns].astype(F32)
            out_ref[:, columns] = total
        for i in range(len(self.tiles)):
            self.near_copy(i).wait_send()
            for k in range(1, self.chips):
                self.far_copy(k, i).wait_send()

    @staticmethod
    def scratch(chips, tokens, width):
        return [pltpu.VMEM((chips, tokens, width), LOW)] * 4

    @staticmethod
    def sems(chips, width):
        return pairs_of(width // COLUMNS, chips * (width // COLUMNS))


def out_scatter_kernel(
    planes, chips, left_ref, right_ref, tile_ref, grad_ref, out_ref, tiles_ref, grads_ref,
    near_out, near_in, far_out, far_in, *sems,
):
    here = place()
    z, c, core = here
    seqs = 2 * chips
    me = 2 * c + core
    near, far, tile_sems, up, down, pair = [sems[2 * i : 2 * i + 2] for i in range(6)]
    local = sems[12]
    barrier = pltpu.get_barrier_semaphore()
    peers = plane_peers(chips, here)
    greet(barrier, peers)
    greet_line(barrier, planes, here)
    pl.semaphore_wait(barrier, len(peers) + line_peers(planes, here))
    group = GroupGather(planes, here, grad_ref, grads_ref, up, down, pair)
    group.start(local.at[0])
    swaps = [
        remote(tile_ref.at[2 * device[1] + device[2]], tiles_ref.at[me], tile_sems, k, device)
        for k, device in enumerate(peers, 1)
    ]
    for copy in swaps:
        copy.start()
    keep = pltpu.make_async_copy(tile_ref.at[me], tiles_ref.at[me], local.at[1])
    keep.start()
    work = PlaneScatter(
        chips, here, left_ref, right_ref, False, (near_out, near_in, far_out, far_in), near, far
    )
    work.start()
    for d in range(1, planes):
        group.step(d)
    work.finish(out_ref)
    group.finish()
    keep.wait()
    for k in range(1, seqs):
        swaps[k - 1].wait_send()
        index = lax.rem(me + seqs - k, seqs)
        remote(tile_ref.at[0], tiles_ref.at[index], tile_sems, k, here).wait_recv()


def out_scatter(planes, chips, left, right, tiles, grad):
    _, tokens, _ = left.shape
    width = right.shape[1]
    return call(
        functools.partial(out_scatter_kernel, planes, chips),
        "out_scatter",
        [
            shape((tokens, width), F32),
            shape(tiles.shape, F32),
            shape((planes, 2, *grad.shape), LOW),
        ],
        (left, right, tiles, grad),
        [VMEM, VMEM, VMEM, HBM],
        [VMEM, VMEM, HBM],
        [
            *PlaneScatter.scratch(chips, tokens, width),
            *PlaneScatter.sems(chips, width),
            *pairs_of(2 * chips),
            *GroupGather.sems(planes),
            pltpu.SemaphoreType.DMA((2,)),
        ],
        3,
    )


class LineScatter:
    def __init__(self, planes, here, parts, own, above, below, up, down):
        self.planes, self.here, self.parts, self.own = planes, here, parts, own
        self.above, self.below, self.up, self.down = above, below, up, down

    def upward(self, t, p):
        z, c, core = self.here
        block = self.below.at[(t, *self.parts[p][0])]
        return remote(block, block, self.up, t * len(self.parts) + p, (z + 1, c, core))

    def downward(self, t, p):
        z, c, core = self.here
        block = self.above.at[(t, *self.parts[p][0])]
        return remote(block, block, self.down, t * len(self.parts) + p, (z - 1, c, core))

    def add(self, slot, t, p, fresh):
        for tile in self.parts[p][1]:
            total = self.own(t, tile)
            if not fresh:
                total = total + slot[(t, *tile)].astype(F32)
            slot[(t, *tile)] = total.astype(LOW)

    def step(self, i):
        z, planes = self.here[0], self.planes
        top, low = planes - 1 - i, i

        def rise(p):
            @pl.when(z > 0)
            def _():
                self.upward(top, p).wait_recv()
                self.add(self.below, top, p, False)

            @pl.when(z == 0)
            def _():
                self.add(self.below, top, p, True)

            self.upward(top, p).start()

        def fall(p):
            @pl.when(z < planes - 1)
            def _():
                self.downward(low, p).wait_recv()
                self.add(self.above, low, p, False)

            @pl.when(z == planes - 1)
            def _():
                self.add(self.above, low, p, True)

            self.downward(low, p).start()

        for p in range(len(self.parts)):
            pl.when(z < top)(lambda p=p: rise(p))
            pl.when(z > low)(lambda p=p: fall(p))

    def finish(self, store):
        z, planes = self.here[0], self.planes

        def total(tile, *slots):
            value = self.own(z, tile)
            for slot in slots:
                value = value + slot[(z, *tile)].astype(F32)
            store(tile, value)

        for p, (_, tiles) in enumerate(self.parts):

            @pl.when(z > 0)
            def _(p=p):
                self.upward(z, p).wait_recv()

            @pl.when(z < planes - 1)
            def _(p=p):
                self.downward(z, p).wait_recv()

            @pl.when((z > 0) & (z < planes - 1))
            def _(tiles=tiles):
                for tile in tiles:
                    total(tile, self.below, self.above)

            @pl.when(z == 0)
            def _(tiles=tiles):
                for tile in tiles:
                    total(tile, self.above)

            @pl.when(z == planes - 1)
            def _(tiles=tiles):
                for tile in tiles:
                    total(tile, self.below)

        for i in range(planes - 1):
            for p in range(len(self.parts)):
                pl.when(z < planes - 1 - i)(
                    lambda i=i, p=p: self.upward(planes - 1 - i, p).wait_send()
                )
                pl.when(z > i)(lambda i=i, p=p: self.downward(i, p).wait_send())


def row_tiles(count, size):
    return [pl.ds(at, size) for at in range(0, count, size)]


def in_scatter_kernel(
    planes, chips, heads, strided, left_ref, right_ref, grad_ref, up_ref, weight_ref, gain_ref,
    out_ref, total_ref, gains_ref, slots_ref,
    near_out, near_in, far_out, far_in, above, below, mine, parts, *sems,
):
    here = place()
    z, c, core = here
    seqs = 2 * chips
    me = 2 * c + core
    near, far, up, down, swap_sems, chip_sems = [sems[2 * i : 2 * i + 2] for i in range(6)]
    barrier = pltpu.get_barrier_semaphore()
    peers = plane_peers(chips, here)
    greet(barrier, peers)
    greet_line(barrier, planes, here)
    pl.semaphore_wait(barrier, len(peers) + line_peers(planes, here))
    half = seqs // 2
    line = LineScatter(
        planes,
        here,
        [((pl.ds(p * half, half),), [(pl.ds(p * half + i, 1),) for i in range(half)]) for p in range(2)],
        lambda t, tile: grad_ref[(t, *tile)].astype(F32),
        above,
        below,
        up,
        down,
    )
    line.step(0)
    work = PlaneScatter(
        chips, here, left_ref, right_ref, True, (near_out, near_in, far_out, far_in), near, far
    )
    work.start()
    units = slots_ref.shape[2]
    ups = ChipSwap(
        chips, here, lambda index: column_block(up_ref, units, index), slots_ref, chip_sems
    )
    ups.start(sems[12].at[0])
    for i in range(1, planes - 1):
        line.step(i)

    def store(tile, total):
        mine[tile] = total.astype(LOW)

    line.finish(store)
    swaps = [
        remote(mine.at[2 * device[1] + device[2]], parts.at[me], swap_sems, k, device)
        for k, device in enumerate(peers, 1)
    ]
    for copy in swaps:
        copy.start()
    parts[me] = mine[me]
    work.finish(out_ref)
    for k in range(1, seqs):
        swaps[k - 1].wait_send()
        index = lax.rem(me + seqs - k, seqs)
        remote(mine.at[0], parts.at[index], swap_sems, k, here).wait_recv()
    span = heads * HD
    width = seqs * span
    gain = gain_ref[:, pl.ds(0, 1)]
    summed = jnp.zeros(gain.shape, F32)
    for i in range(3):
        step, pieces = (seqs * HD, planes) if strided else (width, 1)
        size = step // seqs
        for piece in range(pieces):
            at = i * span + piece * size
            columns = pl.ds(i * width + piece * step, step)
            total = jnp.concatenate(
                [parts[s, :, pl.ds(at, size)].astype(F32) for s in range(seqs)], axis=1
            )
            weight = weight_ref[:, columns].astype(F32)
            summed = summed + jnp.sum(total * weight, axis=1, keepdims=True)
            total_ref[:, columns] = total * gain
    gains_ref[...] = jnp.broadcast_to(summed, gains_ref.shape)
    ups.finish()


def in_scatter(planes, chips, heads, strided, left, right, grads, up_grads, weight, gain, units):
    _, tokens, _ = left.shape
    width = right.shape[0]
    seqs = 2 * chips
    part, wide = grads.shape[2:]
    return call(
        functools.partial(in_scatter_kernel, planes, chips, heads, strided),
        "in_scatter",
        [
            shape((tokens, width), F32),
            shape(weight.shape, F32),
            shape((part, 128), F32),
            shape((chips, width, units), LOW),
        ],
        (left, right, grads, up_grads, weight, gain),
        [VMEM, VMEM, VMEM, HBM, VMEM, VMEM],
        [VMEM, VMEM, VMEM, HBM],
        [
            *PlaneScatter.scratch(chips, tokens, width),
            *[pltpu.VMEM((planes, seqs, part, wide), LOW)] * 2,
            *[pltpu.VMEM((seqs, part, wide), LOW)] * 2,
            *PlaneScatter.sems(chips, width),
            *pairs_of(2 * planes, 2 * planes, seqs, chips),
            pltpu.SemaphoreType.DMA((1,)),
        ],
        4,
    )


def line_gather_kernel(planes, x_ref, out_ref, *sems):
    here = place()
    z, c, core = here
    up, down, near = [sems[2 * i : 2 * i + 2] for i in range(3)]
    barrier = pltpu.get_barrier_semaphore()
    greet(barrier, [(z, c, 1 - core)])
    greet_line(barrier, planes, here)
    pl.semaphore_wait(barrier, 1 + line_peers(planes, here))
    group = GroupGather(planes, here, x_ref, out_ref, up, down, near)
    group.start(sems[6].at[0])
    for d in range(1, planes):
        group.step(d)
    group.finish()


def line_gather(planes, x_block):
    return call(
        functools.partial(line_gather_kernel, planes),
        "line_gather",
        shape((planes, 2, *x_block.shape), x_block.dtype),
        (x_block,),
        [HBM],
        HBM,
        [*GroupGather.sems(planes), pltpu.SemaphoreType.DMA((1,))],
        5,
    )


def sums_kernel(planes, x_ref, out_ref, slots, *sems):
    here = place()
    z, c, core = here
    count = 2 * planes
    me = 2 * z + core
    barrier = pltpu.get_barrier_semaphore()
    ids = [lax.rem(me + k, count) for k in range(1, count)]
    peers = [(index // 2, c, lax.rem(index, 2)) for index in ids]
    greet(barrier, peers)
    pl.semaphore_wait(barrier, len(peers))
    copies = [remote(x_ref, slots.at[k], sems, k, device) for k, device in enumerate(peers, 1)]
    for copy in copies:
        copy.start()
    for copy in copies:
        copy.wait_send()
        copy.wait_recv()
    total = x_ref[...]
    for k in range(1, count):
        total = total + slots[k]
    out_ref[...] = total


def group_sums(planes, stats):
    return call(
        functools.partial(sums_kernel, planes),
        "group_sums",
        shape(stats.shape, F32),
        (stats,),
        [VMEM],
        VMEM,
        [pltpu.VMEM((2 * planes, *stats.shape), F32), *pairs_of(2 * planes)],
        6,
    )


class PairScatter:
    PARTS = 2

    def __init__(self, planes, here, left, right, turned, buffers, near, up, down):
        self.planes, self.here = planes, here
        self.left, self.right, self.turned = left, right, turned
        self.near_out, self.near_in, self.own, above, below = buffers
        self.near = near
        self.tokens, width = self.near_out.shape[1:]
        self.tiles = [pl.ds(at, COLUMNS) for at in range(0, width, COLUMNS)]
        size = width // self.PARTS
        every = slice(None)
        parts = [
            ((every, pl.ds(at, size)), [(rows, pl.ds(at, size)) for rows in row_tiles(self.tokens, 32)])
            for at in range(0, width, size)
        ]
        self.line = LineScatter(
            planes,
            here,
            parts,
            lambda t, tile: self.own[(t, *tile)].astype(F32),
            above,
            below,
            up,
            down,
        )

    def near_copy(self, i):
        z, c, core = self.here
        at = (slice(None), slice(None), self.tiles[i])
        return remote(self.near_out.at[at], self.near_in.at[at], self.near, i, (z, c, 1 - core))

    def start(self):
        core, tokens = self.here[2], self.tokens
        left = jnp.concatenate([self.left[t, 1 - core] for t in range(self.planes)], axis=0)
        for i, columns in enumerate(self.tiles):
            part = product(left, self.right, columns, self.turned).astype(LOW)
            for t in range(self.planes):
                self.near_out[t, :, columns] = part[t * tokens : (t + 1) * tokens]
            self.near_copy(i).start()
        left = jnp.concatenate([self.left[t, core] for t in range(self.planes)], axis=0)
        for i, columns in enumerate(self.tiles):
            part = product(left, self.right, columns, self.turned)
            self.near_copy(i).wait_recv()
            for t in range(self.planes):
                self.own[t, :, columns] = (
                    part[t * tokens : (t + 1) * tokens] + self.near_in[t, :, columns].astype(F32)
                ).astype(LOW)
        self.line.step(0)

    def finish(self, out_ref):
        def store(tile, total):
            out_ref[tile] = total

        self.line.finish(store)
        for i in range(len(self.tiles)):
            self.near_copy(i).wait_send()

    @staticmethod
    def scratch(planes, tokens, width):
        return [pltpu.VMEM((planes, tokens, width), LOW)] * 5

    @classmethod
    def sems(cls, planes, width):
        return pairs_of(width // COLUMNS, cls.PARTS * planes, cls.PARTS * planes)


def line_scatter_kernel(
    planes, chips, left_ref, right_ref, grad_ref, out_ref, slots_ref,
    near_out, near_in, own, above, below, *sems,
):
    here = place()
    z, c, core = here
    near, up, down, swap_sems = [sems[2 * i : 2 * i + 2] for i in range(4)]
    barrier = pltpu.get_barrier_semaphore()
    peers = [(z, c, 1 - core), *chip_peers(chips, here)]
    greet(barrier, peers)
    greet_line(barrier, planes, here)
    pl.semaphore_wait(barrier, len(peers) + line_peers(planes, here))
    swap = ChipSwap(chips, here, lambda index: grad_ref.at[index], slots_ref, swap_sems)
    swap.start(sems[8].at[0])
    work = PairScatter(
        planes, here, left_ref, right_ref, True, (near_out, near_in, own, above, below),
        near, up, down,
    )
    work.start()
    for i in range(1, planes - 1):
        work.line.step(i)
    work.finish(out_ref)
    swap.finish()


def line_scatter(planes, chips, left, right, grads):
    tokens, width = left.shape[2], right.shape[0]
    return call(
        functools.partial(line_scatter_kernel, planes, chips),
        "line_scatter",
        [shape((tokens, width), F32), shape(grads.shape, LOW)],
        (left, right, grads),
        [VMEM, VMEM, HBM],
        [VMEM, HBM],
        [
            *PairScatter.scratch(planes, tokens, width),
            *PairScatter.sems(planes, width),
            *pairs_of(chips),
            pltpu.SemaphoreType.DMA((1,)),
        ],
        7,
    )


def plane_gather_kernel(
    planes, chips, x_ref, stat_ref, tile_ref, left_ref, right_ref,
    row_ref, stats_ref, tiles_ref, ffn_ref,
    near_out, near_in, own, above, below, *sems,
):
    here = place()
    z, c, core = here
    seqs = 2 * chips
    count = planes * seqs
    me = 2 * c + core
    flat = z * seqs + me
    x_far, x_near, s_far, s_near, tile_sems, near, up, down = [
        sems[2 * i : 2 * i + 2] for i in range(8)
    ]
    local = sems[16]
    barrier = pltpu.get_barrier_semaphore()

    def device_of(k):
        other = lax.rem(flat + k, count)
        return (other // seqs, lax.rem(other, seqs) // 2, lax.rem(other, 2))

    def signal(k, carry):
        greet(barrier, [device_of(k)])
        return carry

    lax.fori_loop(1, count, signal, 0)
    pl.semaphore_wait(barrier, count - 1)
    rows = PlaneGather(chips, here, x_ref, row_ref, x_far, x_near)
    stats = PlaneGather(chips, here, stat_ref, stats_ref, s_far, s_near)
    rows.start()
    stats.start()
    keeps = [
        pltpu.make_async_copy(x_ref, row_ref.at[me], local.at[0]),
        pltpu.make_async_copy(stat_ref, stats_ref.at[me], local.at[1]),
        pltpu.make_async_copy(tile_ref.at[flat], tiles_ref.at[flat], local.at[2]),
    ]
    for copy in keeps:
        copy.start()

    def tile_copy(k):
        other = lax.rem(flat + k, count)
        return remote(tile_ref.at[other], tiles_ref.at[flat], tile_sems, k, device_of(k))

    def tile_start(k, carry):
        tile_copy(k).start()
        return carry

    lax.fori_loop(1, count, tile_start, 0)
    work = PairScatter(
        planes, here, left_ref, right_ref, False, (near_out, near_in, own, above, below),
        near, up, down,
    )
    work.start()
    for i in range(1, planes - 1):
        if i == planes - 2:
            rows.forward()
            stats.forward()
        work.line.step(i)
    rows.finish()
    stats.finish()
    work.finish(ffn_ref)
    for copy in keeps:
        copy.wait()

    def tile_wait(k, carry):
        tile_copy(k).wait_send()
        other = lax.rem(flat + count - k, count)
        remote(tile_ref.at[0], tiles_ref.at[other], tile_sems, k, here).wait_recv()
        return carry

    lax.fori_loop(1, count, tile_wait, 0)


def plane_gather(planes, chips, x_block, stats, tiles, left, right):
    seqs = 2 * chips
    tokens, width = x_block.shape
    return call(
        functools.partial(plane_gather_kernel, planes, chips),
        "plane_gather",
        [
            shape((seqs, *x_block.shape), x_block.dtype),
            shape((seqs, *stats.shape), stats.dtype),
            shape(tiles.shape, tiles.dtype),
            shape((tokens, width), F32),
        ],
        (x_block, stats, tiles, left, right),
        [HBM, HBM, HBM, VMEM, VMEM],
        [HBM, HBM, HBM, VMEM],
        [
            *PairScatter.scratch(planes, tokens, width),
            *pairs_of(chips, chips, chips, chips, planes * seqs),
            *PairScatter.sems(planes, width),
            pltpu.SemaphoreType.DMA((3,)),
        ],
        2,
    )


def swap_lanes(values):
    lane = lax.broadcasted_iota(jnp.int32, values.shape, 1)
    return jnp.where(
        lax.rem(lane, 2) == 0,
        pltpu.roll(values, values.shape[1] - 1, 1),
        pltpu.roll(values, 1, 1),
    )


def twice(table):
    return jnp.concatenate([table, table], axis=1)


def turns(meta_ref, rows):
    cosine, sine, shrink = [twice(meta_ref[rows, pl.ds(i * HD, HD)]) for i in range(3)]
    return (cosine, sine, cosine * shrink, sine * shrink)


def allowed_block(meta_ref, rows, size, columns):
    query = rows + lax.broadcasted_iota(jnp.int32, (size, columns), 0)
    key = lax.broadcasted_iota(jnp.int32, (size, columns), 1)
    offset = meta_ref[pl.ds(rows, size), pl.ds(3 * HD, 1)].astype(jnp.int32)
    return (key <= query) & (key >= query - offset)


BLOCK = 256


def attention_kernel(heads, raw_ref, meta_ref, q_ref, k_ref, v_ref, out_ref, log_ref, wide):
    length = raw_ref.shape[0]
    span = heads * HD
    for rows in row_tiles(length, BLOCK):
        tables = turns(meta_ref, rows)
        for pair in range(heads // 2):
            lanes = pl.ds(2 * HD * pair, 2 * HD)
            query = raw_ref[rows, lanes]
            query = (query * tables[0] + swap_lanes(query) * tables[1]).astype(LOW)
            key = raw_ref[rows, pl.ds(span + 2 * HD * pair, 2 * HD)]
            key = (key * tables[2] + swap_lanes(key) * tables[3]).astype(LOW)
            value = raw_ref[rows, pl.ds(2 * span + 2 * HD * pair, 2 * HD)].astype(LOW)
            for half in range(2):
                at = slice(half * HD, (half + 1) * HD)
                q_ref[2 * pair + half, rows] = query[:, at]
                k_ref[2 * pair + half, rows] = key[:, at]
                v_ref[2 * pair + half, rows] = value[:, at]
    log_ref[...] = jnp.zeros(log_ref.shape, F32)

    def one_head(head, carry):
        for start in range(0, length, BLOCK):
            columns = start + BLOCK
            rows = pl.ds(start, BLOCK)
            scores = lax.dot_general(
                q_ref[head, rows],
                k_ref[head, pl.ds(0, columns)],
                (((1,), (1,)), ((), ())),
                preferred_element_type=F32,
            )
            allowed = allowed_block(meta_ref, start, BLOCK, columns)
            scores = jnp.where(allowed, scores, NEG_FILL)
            top = jnp.max(scores, axis=1, keepdims=True)
            shifted = jnp.exp(scores - top)
            total = jnp.sum(shifted, axis=1, keepdims=True)
            probs = (shifted * (1.0 / total)).astype(LOW)
            wide[head, rows] = jnp.dot(
                probs, v_ref[head, pl.ds(0, columns)], preferred_element_type=F32
            )
            lane = lax.broadcasted_iota(jnp.int32, (BLOCK, 128), 1)
            log_ref[rows] = jnp.where(lane == head, top + jnp.log(total), log_ref[rows])
        return carry

    lax.fori_loop(0, heads, one_head, 0)
    for rows in row_tiles(length, BLOCK):
        out_ref[rows] = jnp.concatenate(
            [wide[head, rows] for head in range(heads)], axis=1
        ).astype(LOW)


def attention(heads, raw, meta):
    length = raw.shape[0]
    return call(
        functools.partial(attention_kernel, heads),
        "attention",
        [
            *[shape((heads, length, HD), LOW)] * 3,
            shape((length, heads * HD), LOW),
            shape((length, 128), F32),
        ],
        (raw, meta),
        [VMEM] * 2,
        [VMEM] * 5,
        [pltpu.VMEM((heads, length, HD), F32)],
    )


def attention_back_kernel(
    planes, heads, strided,
    q_ref, k_ref, v_ref, att_ref, row_ref, right_ref, stat_ref, log_ref, meta_ref,
    out_ref, total_ref,
    grad, dq, dk, dv, normed_all, own, above, below, *sems,
):
    here = place()
    up, down = sems[:2], sems[2:]
    barrier = pltpu.get_barrier_semaphore()
    greet_line(barrier, planes, here)
    pl.semaphore_wait(barrier, line_peers(planes, here))
    length, span = att_ref.shape
    part, width = own.shape[1:]
    for rows in row_tiles(length, BLOCK):
        mean, scaler, first, second = (stat_ref[rows, pl.ds(i, 1)] for i in range(4))
        d_sub = product(row_ref[rows], right_ref, slice(None), True)
        normed = (att_ref[rows].astype(F32) - mean) * scaler
        normed_all[rows] = normed.astype(LOW)
        d_att = (scaler * (d_sub - first - normed * second)).astype(LOW)
        for head in range(heads):
            grad[head, rows] = d_att[:, head * HD : (head + 1) * HD]
    for at in range(0, width, COLUMNS):
        columns = pl.ds(at, COLUMNS)
        term = token_product(normed_all[...], row_ref[:, columns]).astype(LOW)
        for t in range(planes):
            own[t, :, columns] = term[t * part : (t + 1) * part]
    line = LineScatter(
        planes,
        here,
        [((slice(None),), [(rows,) for rows in row_tiles(part, 16)])],
        lambda t, tile: own[(t, *tile)].astype(F32),
        above,
        below,
        up,
        down,
    )
    if strided:
        line.step(0)
    dk[...] = jnp.zeros(dk.shape, F32)
    dv[...] = jnp.zeros(dv.shape, F32)

    def one_head(head, carry):
        for start in range(0, length, BLOCK):
            columns = start + BLOCK
            rows = pl.ds(start, BLOCK)
            keys = pl.ds(0, columns)
            query, key = q_ref[head, rows], k_ref[head, keys]
            out_grad = grad[head, rows]
            scores = lax.dot_general(
                query, key, (((1,), (1,)), ((), ())), preferred_element_type=F32
            )
            allowed = allowed_block(meta_ref, start, BLOCK, columns)
            lane = lax.broadcasted_iota(jnp.int32, (BLOCK, 128), 1)
            log_total = jnp.sum(
                jnp.where(lane == head, log_ref[rows], 0.0), axis=1, keepdims=True
            )
            probs = jnp.where(allowed, jnp.exp(scores - log_total), 0.0)
            d_probs = lax.dot_general(
                out_grad, v_ref[head, keys], (((1,), (1,)), ((), ())), preferred_element_type=F32
            )
            delta = jnp.sum(probs * d_probs, axis=1, keepdims=True)
            d_scores = (probs * (d_probs - delta)).astype(LOW)
            dq[head, rows] = jnp.dot(d_scores, key, preferred_element_type=F32)
            dk[head, keys] += token_product(d_scores, query)
            dv[head, keys] += token_product(probs.astype(LOW), out_grad)
        return carry

    first = 0
    for i in range(1, planes - 1):
        last = -(-heads * i // (planes - 1))
        lax.fori_loop(first, last, one_head, 0)
        first = last
        if strided:
            line.step(i)
    lax.fori_loop(first, heads, one_head, 0)
    for rows in row_tiles(length, BLOCK):
        tables = turns(meta_ref, rows)
        for pair in range(heads // 2):
            both = [
                jnp.concatenate(
                    [whole[2 * pair, rows], whole[2 * pair + 1, rows]], axis=1
                ).astype(LOW)
                for whole in (dq, dk, dv)
            ]
            query, key = both[0].astype(F32), both[1].astype(F32)
            query = query * tables[0] + swap_lanes(query * tables[1])
            key = key * tables[2] + swap_lanes(key * tables[3])
            out_ref[rows, pl.ds(2 * HD * pair, 2 * HD)] = query.astype(LOW)
            out_ref[rows, pl.ds(span + 2 * HD * pair, 2 * HD)] = key.astype(LOW)
            out_ref[rows, pl.ds(2 * span + 2 * HD * pair, 2 * HD)] = both[2]
    if strided:

        def store(tile, total):
            total_ref[tile] = total

        line.finish(store)
    else:
        for t in range(planes):
            total_ref[pl.ds(t * part, part)] = own[t].astype(F32)


def attention_back(planes, heads, strided, part, args):
    length, span = args[3].shape
    width = args[4].shape[1]
    return call(
        functools.partial(attention_back_kernel, planes, heads, strided),
        "attention_back",
        [shape((length, 3 * span), LOW), shape((part if strided else span, width), F32)],
        args,
        [VMEM] * 9,
        [VMEM] * 2,
        [
            pltpu.VMEM((heads, length, HD), LOW),
            *[pltpu.VMEM((heads, length, HD), F32)] * 3,
            pltpu.VMEM((length, span), LOW),
            *[pltpu.VMEM((planes, part, width), LOW)] * 3,
            *pairs_of(planes, planes),
        ],
        8,
    )


def body(
    hidden_in,
    segment_ids,
    position_ids,
    w_qkv,
    w_out,
    w_up,
    w_down,
    gain_attn,
    gain_attn_sub,
    gain_ffn,
    gain_ffn_sub,
    ema_qkv,
    ema_out,
    ema_up,
    ema_down,
    ema_gain_attn,
    ema_gain_attn_sub,
    ema_gain_ffn,
    ema_gain_ffn_sub,
    out_grad,
):
    _, tokens, width = hidden_in.shape
    planes, chips = lax.axis_size("dp"), lax.axis_size("chip")
    seqs = 2 * chips
    length = tokens * seqs
    heads = HEADS // seqs
    span = heads * HD
    part = w_qkv.shape[0]
    strided = part % HD == 0
    group_tokens = planes * 2 * tokens
    width_ff = w_down.shape[0] * planes * seqs
    seq_index = lax.axis_index(SEQ)

    def gain_rows(weight, gain):
        return (weight.astype(F32) * gain.astype(F32)[:, None]).astype(LOW)

    qkv_scaled = gain_rows(w_qkv, gain_attn)
    out_scaled = gain_rows(w_out, gain_attn_sub)
    down_scaled = gain_rows(w_down, gain_ffn_sub)
    if strided:
        qkv_send = qkv_scaled.reshape(part, 3, planes, seqs, HD).transpose(3, 0, 1, 2, 4)
    else:
        qkv_send = qkv_scaled.reshape(part, 3, seqs, span).transpose(2, 0, 1, 3)
    qkv_send = qkv_send.reshape(seqs, part, 3 * span)
    x_in = hidden_in[0].astype(F32)
    normed_one, scaler_one = moments(x_in)
    normed_low = normed_one.astype(LOW)
    gain_tile = jnp.zeros((8, 128), F32).at[0, :part].set(gain_ffn.astype(F32))

    row_in, meta, qkv_mine, out_mine, gain_tiles, up_mine = attention_gather(
        planes,
        chips,
        normed_low,
        token_tables(position_ids[0]),
        qkv_send,
        out_scaled,
        gain_tile,
        w_up,
    )
    if up_mine.ndim == 3:
        up_mine = up_mine.transpose(1, 0, 2).reshape(width, -1)
    row_in = row_in.reshape(length, width)
    meta = meta.reshape(length, -1)
    qkv_mine = qkv_mine.reshape(width, 3 * span)
    if strided:
        out_mine = out_mine.reshape(span, width)
    else:
        out_all = lax.all_gather(out_scaled, ALL, axis=0, tiled=True)
        out_mine = lax.dynamic_slice_in_dim(out_all, seq_index * span, span, axis=0)
    queries, keys, values, attended, log_total = attention(heads, dot(row_in, qkv_mine), meta)
    down_scaled, attended = lax.optimization_barrier((down_scaled, attended))
    down_mine = lax.all_gather(down_scaled, "chip", axis=0, tiled=True)
    attended_wide = attended.astype(F32)
    column_part = jnp.sum(out_mine.astype(F32), axis=0)
    token_sums = jnp.stack(
        [jnp.sum(attended_wide, axis=1), jnp.sum(attended_wide * attended_wide, axis=1)]
    ).reshape(2, seqs, tokens)
    tiles = jnp.concatenate(
        [
            jnp.swapaxes(token_sums, 0, 1),
            jnp.zeros((seqs, 6, tokens), F32),
            jnp.broadcast_to(column_part.reshape(1, -1, tokens), (seqs, width // tokens, tokens)),
        ],
        axis=1,
    )
    grad_low = out_grad[0]
    out_sum, tiles, grad_flat = out_scatter(
        planes, chips, attended.reshape(seqs, tokens, span), out_mine, tiles, grad_low
    )
    grad_flat = grad_flat.reshape(group_tokens, width)
    tiles = jnp.sum(tiles, axis=0)
    column_sum = tiles[8:].reshape(width)
    sums = tiles[:2].T
    gain_three = gain_tiles[:, 0, :part].reshape(width)
    mean_two = sums[:, :1] / width
    scaler_two = lax.rsqrt(sums[:, 1:] / width - mean_two * mean_two + NORM_EPS)
    projected = scaler_two * (out_sum - mean_two * column_sum[None, :])
    hmid = x_in + projected
    normed_three, scaler_three = moments(hmid)
    ffn_in = (normed_three * gain_three).astype(LOW)

    grad_top = grad_low.astype(F32)
    ffn_flat = line_gather(planes, ffn_in).reshape(group_tokens, width)
    weighted = rows_product(grad_flat, down_mine)
    up_slice = dot(ffn_flat, up_mine)
    activated, gelu_pull = jax.vjp(exact_gelu, up_slice)
    stats = group_sums(
        planes,
        jnp.stack(
            [
                jnp.sum(activated, axis=1),
                jnp.sum(activated * activated, axis=1),
                jnp.sum(weighted * activated, axis=1),
                jnp.sum(weighted, axis=1),
            ]
        ),
    )[:, :, None]
    act_mean = stats[0] / width_ff
    scaler_four = lax.rsqrt(stats[1] / width_ff - act_mean * act_mean + NORM_EPS)
    normed_four = (activated - act_mean) * scaler_four
    normed_four_low = normed_four.astype(LOW)
    first_mean = stats[3] / width_ff
    second_mean = scaler_four * (stats[2] - act_mean * stats[3]) / width_ff
    d_act = scaler_four * (weighted - first_mean - normed_four * second_mean)
    (d_up,) = gelu_pull(d_act)
    d_up_low = d_up.astype(LOW)
    grad_up = token_product(ffn_flat, d_up_low).astype(LOW)
    grad_down = token_product(normed_four_low, grad_flat).astype(LOW)
    units = w_up.shape[1]
    if units % 128:
        grad_up = grad_up.reshape(width, chips, units).transpose(1, 0, 2)
    d_up_low, grad_up = lax.optimization_barrier((d_up_low, grad_up))
    d_ffn_in, down_slots = line_scatter(
        planes,
        chips,
        d_up_low.reshape(planes, 2, tokens, -1),
        up_mine,
        grad_down.reshape(chips, -1, width),
    )

    gain_part = jnp.sum(d_ffn_in * normed_three, axis=0).reshape(planes * seqs, 1, part)
    gain_part = jnp.pad(gain_part, ((0, 0), (0, 7), (0, 128 - part)))
    d_hmid = grad_top + norm_back(d_ffn_in * gain_three, normed_three, scaler_three)
    d_hmid_low = d_hmid.astype(LOW)
    d_hmid_wide = d_hmid_low.astype(F32)
    first_two = jnp.sum(d_hmid_wide * column_sum[None, :], axis=1, keepdims=True) / width
    second_two = jnp.sum(d_hmid_wide * projected, axis=1, keepdims=True) / width
    token_stats = jnp.concatenate([mean_two, scaler_two, first_two, second_two], axis=1)
    row_grad, row_stats, gain_part, ffn_out = plane_gather(
        planes,
        chips,
        d_hmid_low,
        jnp.pad(token_stats, ((0, 0), (0, 124))),
        gain_part,
        normed_four_low.reshape(planes, 2, tokens, -1),
        down_mine,
    )
    output = (hmid + ffn_out).astype(LOW)[None]
    row_grad = row_grad.reshape(length, width)
    row_stats = row_stats.reshape(length, 128)
    grad_gain_three = jnp.sum(gain_part, axis=0)[0, :part]
    d_qkv, sum_out = attention_back(
        planes,
        heads,
        strided,
        part,
        (queries, keys, values, attended, row_grad, out_mine, row_stats, log_total, meta),
    )
    grad_qkv = token_product(row_in, d_qkv).astype(LOW)
    d_in, sum_qkv, grad_gain_one, up_slots = in_scatter(
        planes,
        chips,
        heads,
        strided,
        d_qkv.reshape(seqs, tokens, 3 * span),
        qkv_mine,
        grad_qkv.reshape(planes, seqs, part, 3 * span),
        grad_up,
        w_qkv,
        jnp.broadcast_to(gain_attn.astype(F32)[:, None], (part, 128)),
        units,
    )
    grad_gain_one = grad_gain_one[:, 0]
    sum_up = jnp.sum(up_slots.astype(F32), axis=0)
    sum_down = jnp.sum(down_slots.astype(F32), axis=0)
    input_grad = (d_hmid + norm_back(d_in, normed_one, scaler_one)).astype(LOW)[None]

    if not strided:
        spread = lax.dynamic_update_slice_in_dim(
            jnp.zeros((width, width), LOW), sum_out.astype(LOW), seq_index * span, axis=0
        )
        sum_out = lax.psum_scatter(spread, ALL, scatter_dimension=0, tiled=True).astype(F32)

    def finish(total, weight, gain):
        wide = weight.astype(F32)
        return (total * gain.astype(F32)[:, None], jnp.sum(total * wide, axis=1))

    sum_out, grad_gain_two = finish(sum_out, w_out, gain_attn_sub)
    sum_down, grad_gain_four = finish(sum_down, w_down, gain_ffn_sub)

    def averaged(average, weight):
        return EMA_DECAY * average + (1.0 - EMA_DECAY) * weight.astype(F32)

    return (
        output,
        input_grad,
        sum_qkv,
        sum_out,
        sum_up,
        sum_down,
        grad_gain_one,
        grad_gain_two,
        grad_gain_three,
        grad_gain_four,
        averaged(ema_qkv, w_qkv),
        averaged(ema_out, w_out),
        averaged(ema_up, w_up),
        averaged(ema_down, w_down),
        averaged(ema_gain_attn, gain_attn),
        averaged(ema_gain_attn_sub, gain_attn_sub),
        averaged(ema_gain_ffn, gain_ffn),
        averaged(ema_gain_ffn_sub, gain_ffn_sub),
    )


def solution(mesh):
    split = Mesh(
        mesh.devices.reshape(mesh.shape["dp"], mesh.shape["seq"] // 2, 2), ("dp", "chip", "core")
    )
    tokens = P("dp", SEQ, None)
    ids = P("dp", SEQ)
    rows = P(ALL, None)
    columns = P(None, ALL)
    vector = P(ALL)
    weights = (rows, rows, columns, rows)
    gains = (vector,) * 4
    return jax.shard_map(
        body,
        mesh=split,
        in_specs=(tokens, ids, ids, *weights, *gains, *weights, *gains, tokens),
        out_specs=(tokens, tokens, *weights, *gains, *weights, *gains),
        check_vma=False,
    )
```

```python
import functools
import math

import jax
import jax.numpy as jnp
from jax import lax
from jax.experimental import pallas as pl
from jax.experimental.pallas import tpu as pltpu
from jax.sharding import Mesh
from jax.sharding import PartitionSpec as P

HEADS = 32
HD = 64

NEG_FILL = -1000000000.0
NORM_EPS = 1e-05
EMA_DECAY = 0.7
LOW = jnp.bfloat16
F32 = jnp.float32
SEQ = ("chip", "core")
TP = ("dp", "core")
ALL = ("dp", "chip", "core")


def moments(values):
    mean = jnp.mean(values, axis=-1, keepdims=True)
    centered = values - mean
    scaler = lax.rsqrt(jnp.mean(centered * centered, axis=-1, keepdims=True) + NORM_EPS)
    return (centered * scaler, scaler)


def norm_back(scaled_grad, normed, scaler):
    first_mean = jnp.mean(scaled_grad, axis=-1, keepdims=True)
    second_mean = jnp.mean(scaled_grad * normed, axis=-1, keepdims=True)
    return scaler * (scaled_grad - first_mean - normed * second_mean)


def token_tables(positions):
    half_count = HD // 2
    index_half = jnp.arange(half_count).astype(F32)
    inverse = jnp.exp(-(2.0 * index_half / HD) * math.log(10000.0))
    decay_base = (2.0 * index_half + 0.4 * HD) / (1.4 * HD)
    where_at = positions.astype(F32)[:, None]
    angles = where_at * inverse[None, :]
    factor = jnp.exp(where_at / 512.0 * jnp.log(decay_base)[None, :])
    sign_row = jnp.where(jnp.arange(HD) % 2 == 0, -1.0, 1.0).astype(F32)
    cosine = jnp.repeat(jnp.cos(angles), 2, axis=1)
    sine = jnp.repeat(jnp.sin(angles), 2, axis=1) * sign_row[None, :]
    factor = jnp.repeat(factor, 2, axis=1)
    grow = factor * HD ** (-0.5)
    where_block = jnp.broadcast_to(where_at, (positions.shape[0], HD))
    return jnp.concatenate(
        [cosine * grow, sine * grow, HD**0.5 / (factor * factor), where_block], axis=1
    )


def dot(left_op, right_op):
    return jnp.dot(left_op, right_op, preferred_element_type=F32)


def rows_product(operand, weight_rows):
    return lax.dot_general(
        operand, weight_rows, (((1,), (1,)), ((), ())), preferred_element_type=F32
    )


def token_product(left_op, right_op):
    return lax.dot_general(left_op, right_op, (((0,), (0,)), ((), ())), preferred_element_type=F32)


MESH = pl.DeviceIdType.MESH
HBM = pl.BlockSpec(memory_space=pl.ANY)
VMEM = pl.BlockSpec(memory_space=pltpu.VMEM)
VMEM_BYTES = 60 * 1024 * 1024


def shape(dims, kind):
    return jax.ShapeDtypeStruct(dims, kind)


def pairs_of(*counts):
    return [pltpu.SemaphoreType.DMA((count,)) for count in counts for _ in range(2)]


def call(kernel, name, outs, args, in_specs, out_specs, scratch, collective=None):
    return pl.pallas_call(
        kernel,
        name=name,
        out_shape=outs,
        in_specs=in_specs,
        out_specs=out_specs,
        scratch_shapes=scratch,
        compiler_params=pltpu.CompilerParams(
            collective_id=collective,
            has_side_effects=collective is not None,
            vmem_limit_bytes=VMEM_BYTES,
        ),
    )(*args)


def place():
    return (lax.axis_index("dp"), lax.axis_index("chip"), lax.axis_index("core"))


def remote(source, target, sems, index, device):
    return pltpu.make_async_remote_copy(
        src_ref=source,
        dst_ref=target,
        send_sem=sems[0].at[index],
        recv_sem=sems[1].at[index],
        device_id=device,
        device_id_type=MESH,
    )


def greet(barrier, devices):
    for device in devices:
        pl.semaphore_signal(barrier, inc=1, device_id=device, device_id_type=MESH)


def greet_line(barrier, planes, here):
    z, c, core = here

    @pl.when(z < planes - 1)
    def _():
        greet(barrier, [(z + 1, c, core)])

    @pl.when(z > 0)
    def _():
        greet(barrier, [(z - 1, c, core)])


def line_peers(planes, here):
    z = here[0]
    return (2 * planes - 2 - z) // planes + (z + planes - 1) // planes


def chip_peers(chips, here):
    z, c, core = here
    return [(z, lax.rem(c + k, chips), core) for k in range(1, chips)]


def plane_peers(chips, here):
    z, c, core = here
    seqs = 2 * chips
    me = 2 * c + core
    ids = [lax.rem(me + k, seqs) for k in range(1, seqs)]
    return [(z, index // 2, lax.rem(index, 2)) for index in ids]


def column_block(whole, units, index):
    if len(whole.shape) == 3:
        return whole.at[index]
    return whole.at[:, pl.ds(pl.multiple_of(index * units, 128), units)]


def half_block(whole, slots, index, half):
    rows, units = slots.shape[1:]
    at = pl.ds(half * rows, rows)
    if len(whole.shape) == 3:
        return whole.at[index, at]
    return whole.at[at, pl.ds(pl.multiple_of(index * units, 128), units)]


class ChipSwap:
    def __init__(self, chips, here, source, slots, sems):
        z, c, core = here
        self.sends = [
            remote(source(device[1]), slots.at[c], sems, k, device)
            for k, device in enumerate(chip_peers(chips, here), 1)
        ]
        self.waits = [
            remote(source(c), slots.at[lax.rem(c + chips - k, chips)], sems, k, here)
            for k in range(1, chips)
        ]
        self.keep = (source(c), slots.at[c])

    def start(self, local):
        for copy in self.sends:
            copy.start()
        self.held = pltpu.make_async_copy(*self.keep, local)
        self.held.start()

    def finish(self):
        self.held.wait()
        for send, wait in zip(self.sends, self.waits):
            send.wait_send()
            wait.wait_recv()


class PlaneGather:
    def __init__(self, chips, here, block, out, far, near):
        self.chips, self.here, self.block, self.out = chips, here, block, out
        self.far, self.near = far, near
        z, c, core = here
        self.me = 2 * c + core
        self.partner = (z, c, 1 - core)

    def source(self, k, core):
        return 2 * lax.rem(self.here[1] + self.chips - k, self.chips) + core

    def sends(self):
        mine = self.out.at[self.me]
        copies = [
            remote(self.block, mine, self.far, k, device)
            for k, device in enumerate(chip_peers(self.chips, self.here), 1)
        ]
        return [*copies, remote(self.block, mine, self.near, 0, self.partner)]

    def start(self):
        for copy in self.sends():
            copy.start()

    def passed(self, k):
        index = self.source(k, self.here[2])
        return remote(self.out.at[index], self.out.at[index], self.near, k, self.partner)

    def forward(self):
        for k in range(1, self.chips):
            index = self.source(k, self.here[2])
            remote(self.block, self.out.at[index], self.far, k, self.partner).wait_recv()
            self.passed(k).start()

    def finish(self):
        for copy in self.sends():
            copy.wait_send()
        for k in range(1, self.chips):
            self.passed(k).wait_send()
        for k in range(self.chips):
            index = self.source(k, 1 - self.here[2])
            remote(self.block, self.out.at[index], self.near, k, self.partner).wait_recv()


class LineGather:
    def __init__(self, planes, here, parts, up, down):
        self.planes, self.here, self.parts = planes, here, parts
        self.up, self.down = up, down
        self.count = len(parts(here[0]))

    def upward(self, d, p):
        z, c, core = self.here
        block = self.parts(z - d)[p]
        return remote(block, block, self.up, d * self.count + p, (z + 1, c, core))

    def downward(self, d, p):
        z, c, core = self.here
        block = self.parts(z + d)[p]
        return remote(block, block, self.down, d * self.count + p, (z - 1, c, core))

    def each(self, d, p, act):
        z, planes = self.here[0], self.planes
        pl.when((z < planes - 1) & (z - d >= 0))(lambda: act(self.upward(d, p)))
        pl.when((z > 0) & (z + d < planes))(lambda: act(self.downward(d, p)))

    def start(self):
        for p in range(self.count):
            self.each(0, p, lambda copy: copy.start())

    def step(self, d, arrived=None):
        z, planes = self.here[0], self.planes

        def below(p):
            block = self.parts(z - d)[p]
            remote(block, block, self.up, (d - 1) * self.count + p, self.here).wait_recv()
            if d < planes - 1:
                pl.when(z < planes - 1)(lambda: self.upward(d, p).start())
            if arrived is not None:
                arrived(z - d, p)

        def above(p):
            block = self.parts(z + d)[p]
            remote(block, block, self.down, (d - 1) * self.count + p, self.here).wait_recv()
            if d < planes - 1:
                pl.when(z > 0)(lambda: self.downward(d, p).start())
            if arrived is not None:
                arrived(z + d, p)

        for p in range(self.count):
            pl.when(z - d >= 0)(lambda p=p: below(p))
            pl.when(z + d < planes)(lambda p=p: above(p))

    def finish(self):
        for d in range(self.planes - 1):
            for p in range(self.count):
                self.each(d, p, lambda copy: copy.wait_send())


class GroupGather:
    PARTS = 2

    def __init__(self, planes, here, block, out, up, down, near):
        self.planes, self.here, self.block, self.out, self.near = planes, here, block, out, near
        self.partner = (here[0], here[1], 1 - here[2])
        size = block.shape[0] // self.PARTS
        self.slices = [pl.ds(p * size, size) for p in range(self.PARTS)]
        core = here[2]
        self.line = LineGather(planes, here, lambda t: self.parts(t, core), up, down)

    def parts(self, t, core):
        return [self.out.at[t, core, rows] for rows in self.slices]

    def passed(self, t, p):
        block = self.parts(t, self.here[2])[p]
        return remote(block, block, self.near, t * self.PARTS + p, self.partner)

    def start(self, local):
        z, _, core = self.here
        keep = pltpu.make_async_copy(self.block, self.out.at[z, core], local)
        keep.start()
        keep.wait()
        self.line.start()
        for p in range(self.PARTS):
            self.passed(z, p).start()

    def step(self, d):
        self.line.step(d, lambda t, p: self.passed(t, p).start())

    def other(self, t):
        for p in range(self.PARTS):
            block = self.parts(t, 1 - self.here[2])[p]
            remote(block, block, self.near, t * self.PARTS + p, self.partner).wait_recv()

    def finish(self):
        self.line.finish()
        for t in range(self.planes):
            for p in range(self.PARTS):
                self.passed(t, p).wait_send()

    @classmethod
    def sems(cls, planes):
        return pairs_of(*[planes * cls.PARTS] * 3)


def attention_gather_kernel(
    planes, chips, x_ref, meta_ref, qkv_ref, out_ref, gain_ref, up_ref,
    row_ref, metas_ref, qkvs_ref, outs_ref, gains_ref, ups_ref,
    *sems,
):
    here = place()
    z, c, core = here
    seqs = 2 * chips
    count = planes * seqs
    me = 2 * c + core
    flat = z * seqs + me
    groups = [sems[2 * i : 2 * i + 2] for i in range(11)]
    swap_sems, x_far, x_near, meta_far, meta_near, up, down, up_two, down_two = groups[:9]
    gain_sems, up_sems = groups[9:]
    local = sems[22]
    barrier = pltpu.get_barrier_semaphore()

    def device_of(k):
        other = lax.rem(flat + k, count)
        return (other // seqs, lax.rem(other, seqs) // 2, lax.rem(other, 2))

    def signal(k, carry):
        greet(barrier, [device_of(k)])
        return carry

    lax.fori_loop(1, count, signal, 0)
    pl.semaphore_wait(barrier, count - 1)

    mine = pltpu.make_async_copy(qkv_ref.at[me], qkvs_ref.at[z, me], local.at[0])
    keeps = [
        pltpu.make_async_copy(x_ref, row_ref.at[me], local.at[1]),
        pltpu.make_async_copy(meta_ref, metas_ref.at[me], local.at[2]),
        pltpu.make_async_copy(gain_ref, gains_ref.at[flat], local.at[3]),
    ]
    own_out = pltpu.make_async_copy(out_ref, outs_ref.at[z], local.at[4])
    units = up_ref.shape[1]
    keeps.append(pltpu.make_async_copy(up_ref, column_block(ups_ref, units, c), local.at[5]))
    ups = [
        remote(up_ref, column_block(ups_ref, units, c), up_sems, k, device)
        for k, device in enumerate(chip_peers(chips, here), 1)
    ]
    swaps = [
        remote(qkv_ref.at[2 * device[1] + device[2]], qkvs_ref.at[z, me], swap_sems, k, device)
        for k, device in enumerate(plane_peers(chips, here), 1)
    ]
    mine.start()
    own_out.start()
    for copy in swaps:
        copy.start()
    rows = PlaneGather(chips, here, x_ref, row_ref, x_far, x_near)
    metas = PlaneGather(chips, here, meta_ref, metas_ref, meta_far, meta_near)
    rows.start()
    metas.start()
    for copy in keeps:
        copy.start()

    def gain_copy(k):
        return remote(gain_ref, gains_ref.at[flat], gain_sems, k, device_of(k))

    def gain_start(k, carry):
        gain_copy(k).start()
        return carry

    lax.fori_loop(1, count, gain_start, 0)

    mine.wait()
    own_out.wait()
    for k in range(1, seqs):
        index = lax.rem(me + seqs - k, seqs)
        remote(qkv_ref.at[0], qkvs_ref.at[z, index], swap_sems, k, here).wait_recv()
    half = seqs // 2
    line = LineGather(
        planes, here, lambda t: [qkvs_ref.at[t, pl.ds(i * half, half)] for i in range(2)], up, down
    )
    line_two = LineGather(planes, here, lambda t: [outs_ref.at[t]], up_two, down_two)
    line.start()
    line_two.start()
    rows.forward()
    metas.forward()
    for copy in ups:
        copy.start()
    for d in range(1, planes):
        line.step(d)
        line_two.step(d)
    line.finish()
    line_two.finish()
    rows.finish()
    metas.finish()
    for copy in swaps:
        copy.wait_send()
    for copy in keeps:
        copy.wait()
    for k in range(1, chips):
        ups[k - 1].wait_send()
        other = lax.rem(c + chips - k, chips)
        remote(up_ref, column_block(ups_ref, units, other), up_sems, k, here).wait_recv()

    def gain_wait(k, carry):
        gain_copy(k).wait_send()
        other = lax.rem(flat + count - k, count)
        remote(gain_ref, gains_ref.at[other], gain_sems, k, here).wait_recv()
        return carry

    lax.fori_loop(1, count, gain_wait, 0)


def attention_gather(planes, chips, x_block, meta, qkv_blocks, out_rows, gain_tile, up_block):
    seqs = 2 * chips
    part, wide = qkv_blocks.shape[1:]
    width, units = up_block.shape
    return call(
        functools.partial(attention_gather_kernel, planes, chips),
        "attention_gather",
        [
            shape((seqs, *x_block.shape), LOW),
            shape((seqs, *meta.shape), F32),
            shape((planes, seqs, part, wide), LOW),
            shape((planes, *out_rows.shape), LOW),
            shape((planes * seqs, *gain_tile.shape), F32),
            shape(
                (width, chips * units) if units % 128 == 0 else (chips, width, units), LOW
            ),
        ],
        (x_block, meta, qkv_blocks, out_rows, gain_tile, up_block),
        [HBM] * 6,
        [HBM] * 6,
        [
            *pairs_of(
                seqs, *[chips] * 4, *[2 * planes] * 2, *[planes] * 2, planes * seqs, chips
            ),
            pltpu.SemaphoreType.DMA((6,)),
        ],
        1,
    )


COLUMNS = 512


def product(left, right, columns, turned):
    if turned:
        return lax.dot_general(
            left, right[columns, :], (((1,), (1,)), ((), ())), preferred_element_type=F32
        )
    return jnp.dot(left, right[:, columns], preferred_element_type=F32)


class PlaneScatter:
    def __init__(self, chips, here, left, right, turned, buffers, near, far):
        self.chips, self.here = chips, here
        self.left, self.right, self.turned = left, right, turned
        self.near_out, self.near_in, self.far_out, self.far_in = buffers
        self.near, self.far = near, far
        self.tokens, width = self.near_out.shape[1:]
        self.tiles = [pl.ds(at, COLUMNS) for at in range(0, width, COLUMNS)]
        self.order = [*range(1, chips), 0]

    def target(self, k):
        return lax.rem(self.here[1] + k, self.chips)

    def near_copy(self, i):
        z, c, core = self.here
        at = (slice(None), slice(None), self.tiles[i])
        return remote(self.near_out.at[at], self.near_in.at[at], self.near, i, (z, c, 1 - core))

    def far_copy(self, k, i):
        z, _, core = self.here
        at = (k, slice(None), self.tiles[i])
        index = k * len(self.tiles) + i
        return remote(
            self.far_out.at[at], self.far_in.at[at], self.far, index, (z, self.target(k), core)
        )

    def rows(self, position):
        return slice(position * self.tokens, (position + 1) * self.tokens)

    def start(self):
        core = self.here[2]
        blocks = [self.left[2 * self.target(k) + 1 - core] for k in self.order]
        left = jnp.concatenate(blocks, axis=0)
        for i, columns in enumerate(self.tiles):
            part = product(left, self.right, columns, self.turned).astype(LOW)
            for position, k in enumerate(self.order):
                self.near_out[k, :, columns] = part[self.rows(position)]
            self.near_copy(i).start()
        blocks = [self.left[2 * self.target(k) + core] for k in self.order]
        left = jnp.concatenate(blocks, axis=0)
        for i, columns in enumerate(self.tiles):
            part = product(left, self.right, columns, self.turned)
            self.near_copy(i).wait_recv()
            for position, k in enumerate(self.order):
                self.far_out[k, :, columns] = (
                    part[self.rows(position)] + self.near_in[k, :, columns].astype(F32)
                ).astype(LOW)
                if k:
                    self.far_copy(k, i).start()

    def finish(self, out_ref):
        for i, columns in enumerate(self.tiles):
            total = self.far_out[0, :, columns].astype(F32)
            for k in range(1, self.chips):
                self.far_copy(k, i).wait_recv()
                total = total + self.far_in[k, :, columns].astype(F32)
            out_ref[:, columns] = total
        for i in range(len(self.tiles)):
            self.near_copy(i).wait_send()
            for k in range(1, self.chips):
                self.far_copy(k, i).wait_send()

    @staticmethod
    def scratch(chips, tokens, width):
        return [pltpu.VMEM((chips, tokens, width), LOW)] * 4

    @staticmethod
    def sems(chips, width):
        return pairs_of(width // COLUMNS, chips * (width // COLUMNS))


def out_scatter_kernel(
    planes, chips, left_ref, right_ref, tile_ref, grad_ref, out_ref, tiles_ref, grads_ref,
    near_out, near_in, far_out, far_in, *sems,
):
    here = place()
    z, c, core = here
    seqs = 2 * chips
    me = 2 * c + core
    near, far, tile_sems, up, down, pair = [sems[2 * i : 2 * i + 2] for i in range(6)]
    local = sems[12]
    barrier = pltpu.get_barrier_semaphore()
    peers = plane_peers(chips, here)
    greet(barrier, peers)
    greet_line(barrier, planes, here)
    pl.semaphore_wait(barrier, len(peers) + line_peers(planes, here))
    group = GroupGather(planes, here, grad_ref, grads_ref, up, down, pair)
    group.start(local.at[0])
    swaps = [
        remote(tile_ref.at[2 * device[1] + device[2]], tiles_ref.at[me], tile_sems, k, device)
        for k, device in enumerate(peers, 1)
    ]
    for copy in swaps:
        copy.start()
    keep = pltpu.make_async_copy(tile_ref.at[me], tiles_ref.at[me], local.at[1])
    keep.start()
    work = PlaneScatter(
        chips, here, left_ref, right_ref, False, (near_out, near_in, far_out, far_in), near, far
    )
    work.start()
    for d in range(1, planes):
        group.step(d)
    work.finish(out_ref)
    group.finish()
    for t in range(planes):
        group.other(t)
    keep.wait()
    for k in range(1, seqs):
        swaps[k - 1].wait_send()
        index = lax.rem(me + seqs - k, seqs)
        remote(tile_ref.at[0], tiles_ref.at[index], tile_sems, k, here).wait_recv()


def out_scatter(planes, chips, left, right, tiles, grad):
    _, tokens, _ = left.shape
    width = right.shape[1]
    return call(
        functools.partial(out_scatter_kernel, planes, chips),
        "out_scatter",
        [
            shape((tokens, width), F32),
            shape(tiles.shape, F32),
            shape((planes, 2, *grad.shape), LOW),
        ],
        (left, right, tiles, grad),
        [VMEM, VMEM, VMEM, HBM],
        [VMEM, VMEM, HBM],
        [
            *PlaneScatter.scratch(chips, tokens, width),
            *PlaneScatter.sems(chips, width),
            *pairs_of(2 * chips),
            *GroupGather.sems(planes),
            pltpu.SemaphoreType.DMA((2,)),
        ],
        3,
    )


class LineScatter:
    def __init__(self, planes, here, count, part, tiles, own, slots, up, down):
        self.planes, self.here, self.count = planes, here, count
        self.part, self.tiles, self.own, self.slots = part, tiles, own, slots
        self.up, self.down = up, down
        self.steps = (planes - 1) * count

    def upward(self, t, p):
        z, c, core = self.here
        block = self.slots.at[(t, *self.part(p))]
        return remote(block, block, self.up, t * self.count + p, (z + 1, c, core))

    def downward(self, t, p, last):
        z, c, core = self.here
        block = self.slots.at[(t, *self.part(p))]
        target = self.slots.at[(self.planes, *self.part(p))] if last else block
        return remote(block, target, self.down, t * self.count + p, (z - 1, c, core))

    def add(self, t, p, fresh):
        for tile in self.tiles(p):
            total = self.own(t, tile)
            if not fresh:
                total = total + self.slots[(t, *tile)].astype(F32)
            self.slots[(t, *tile)] = total.astype(LOW)

    def step(self, i):
        z, planes, count = self.here[0], self.planes, self.count
        rise, fall = i - z, i - (planes - 1 - z)

        @pl.when((rise >= 0) & (rise < (planes - 1 - z) * count))
        def _():
            t, p = planes - 1 - rise // count, lax.rem(rise, count)

            @pl.when(z > 0)
            def _():
                self.upward(t, p).wait_recv()
                self.add(t, p, False)

            @pl.when(z == 0)
            def _():
                self.add(t, p, True)

            self.upward(t, p).start()

        @pl.when((fall >= 0) & (fall < z * count))
        def _():
            t, p = fall // count, lax.rem(fall, count)

            @pl.when(z < planes - 1)
            def _():
                self.downward(t, p, False).wait_recv()
                self.add(t, p, False)

            @pl.when(z == planes - 1)
            def _():
                self.add(t, p, True)

            pl.when(t == z - 1)(lambda: self.downward(t, p, True).start())
            pl.when(t < z - 1)(lambda: self.downward(t, p, False).start())

    def finish(self, store):
        z, planes = self.here[0], self.planes

        def total(tile, *slots):
            value = self.own(z, tile)
            for slot in slots:
                value = value + self.slots[(slot, *tile)].astype(F32)
            store(tile, value)

        for p in range(self.count):
            tiles = self.tiles(p)

            @pl.when(z > 0)
            def _(p=p):
                self.upward(z, p).wait_recv()

            @pl.when(z < planes - 1)
            def _(p=p):
                self.downward(z, p, True).wait_recv()

            @pl.when((z > 0) & (z < planes - 1))
            def _(tiles=tiles):
                for tile in tiles:
                    total(tile, z, planes)

            @pl.when(z == 0)
            def _(tiles=tiles):
                for tile in tiles:
                    total(tile, planes)

            @pl.when(z == planes - 1)
            def _(tiles=tiles):
                for tile in tiles:
                    total(tile, z)

        for t in range(planes):
            for p in range(self.count):
                pl.when(z < t)(lambda t=t, p=p: self.upward(t, p).wait_send())
                pl.when(z > t)(lambda t=t, p=p: self.downward(t, p, False).wait_send())


def row_tiles(count, size):
    return [pl.ds(at, size) for at in range(0, count, size)]


def in_scatter_kernel(
    planes, chips, heads, strided, left_ref, right_ref, grad_ref, up_ref, weight_ref, gain_ref,
    out_ref, total_ref, gains_ref, slots_ref,
    near_out, near_in, far_out, far_in, sums, mine, parts, *sems,
):
    here = place()
    z, c, core = here
    seqs = 2 * chips
    me = 2 * c + core
    near, far, up, down, swap_sems, chip_sems = [sems[2 * i : 2 * i + 2] for i in range(6)]
    barrier = pltpu.get_barrier_semaphore()
    peers = plane_peers(chips, here)
    greet(barrier, peers)
    greet_line(barrier, planes, here)
    pl.semaphore_wait(barrier, len(peers) + line_peers(planes, here))
    half = seqs // 2
    line = LineScatter(
        planes,
        here,
        2,
        lambda p: (pl.ds(p * half, half),),
        lambda p: [(pl.ds(p * half + i, 1),) for i in range(half)],
        lambda t, tile: grad_ref[(t, *tile)].astype(F32),
        sums,
        up,
        down,
    )
    line.step(0)
    work = PlaneScatter(
        chips, here, left_ref, right_ref, True, (near_out, near_in, far_out, far_in), near, far
    )
    work.start()
    ups = ChipSwap(
        chips, here, lambda index: half_block(up_ref, slots_ref, index, 1), slots_ref, chip_sems
    )
    ups.start(sems[12].at[0])
    for i in range(1, line.steps):
        line.step(i)

    def store(tile, total):
        mine[tile] = total.astype(LOW)

    line.finish(store)
    swaps = [
        remote(mine.at[2 * device[1] + device[2]], parts.at[me], swap_sems, k, device)
        for k, device in enumerate(peers, 1)
    ]
    for copy in swaps:
        copy.start()
    parts[me] = mine[me]
    work.finish(out_ref)
    for k in range(1, seqs):
        swaps[k - 1].wait_send()
        index = lax.rem(me + seqs - k, seqs)
        remote(mine.at[0], parts.at[index], swap_sems, k, here).wait_recv()
    span = heads * HD
    width = seqs * span
    gain = gain_ref[:, pl.ds(0, 1)]
    summed = jnp.zeros(gain.shape, F32)
    for i in range(3):
        step, pieces = (seqs * HD, planes) if strided else (width, 1)
        size = step // seqs
        for piece in range(pieces):
            at = i * span + piece * size
            columns = pl.ds(i * width + piece * step, step)
            total = jnp.concatenate(
                [parts[s, :, pl.ds(at, size)].astype(F32) for s in range(seqs)], axis=1
            )
            weight = weight_ref[:, columns].astype(F32)
            summed = summed + jnp.sum(total * weight, axis=1, keepdims=True)
            total_ref[:, columns] = total * gain
    gains_ref[...] = jnp.broadcast_to(summed, gains_ref.shape)
    ups.finish()


def in_scatter(planes, chips, heads, strided, left, right, grads, up_grads, weight, gain, units):
    _, tokens, _ = left.shape
    width = right.shape[0]
    seqs = 2 * chips
    part, wide = grads.shape[2:]
    return call(
        functools.partial(in_scatter_kernel, planes, chips, heads, strided),
        "in_scatter",
        [
            shape((tokens, width), F32),
            shape(weight.shape, F32),
            shape((part, 128), F32),
            shape((chips, width // 2, units), LOW),
        ],
        (left, right, grads, up_grads, weight, gain),
        [VMEM, VMEM, VMEM, HBM, VMEM, VMEM],
        [VMEM, VMEM, VMEM, HBM],
        [
            *PlaneScatter.scratch(chips, tokens, width),
            pltpu.VMEM((planes + 1, seqs, part, wide), LOW),
            *[pltpu.VMEM((seqs, part, wide), LOW)] * 2,
            *PlaneScatter.sems(chips, width),
            *pairs_of(2 * planes, 2 * planes, seqs, chips),
            pltpu.SemaphoreType.DMA((1,)),
        ],
        4,
    )


class PairScatter:
    PARTS = 2

    def __init__(self, planes, here, left, right, turned, buffers, near, up, down):
        self.planes, self.here = planes, here
        self.left, self.right, self.turned = left, right, turned
        self.near_out, self.own, slots = buffers
        self.near = near
        self.tokens, width = self.near_out.shape[1:]
        self.tiles = [pl.ds(at, COLUMNS) for at in range(0, width, COLUMNS)]
        size = width // self.PARTS

        def part(p):
            at = p * size if isinstance(p, int) else pl.multiple_of(p * size, 128)
            return (slice(None), pl.ds(at, size))

        self.line = LineScatter(
            planes,
            here,
            self.PARTS,
            part,
            lambda p: [(rows, part(p)[1]) for rows in row_tiles(self.tokens, 32)],
            lambda t, tile: self.own[(t, *tile)].astype(F32),
            slots,
            up,
            down,
        )

    def near_copy(self, i):
        z, c, core = self.here
        at = (slice(None), slice(None), self.tiles[i])
        return remote(self.near_out.at[at], self.own.at[at], self.near, i, (z, c, 1 - core))

    def start(self):
        core, tokens = self.here[2], self.tokens
        left = jnp.concatenate([self.left[t, 1 - core] for t in range(self.planes)], axis=0)
        for i, columns in enumerate(self.tiles):
            part = product(left, self.right, columns, self.turned).astype(LOW)
            for t in range(self.planes):
                self.near_out[t, :, columns] = part[t * tokens : (t + 1) * tokens]
            self.near_copy(i).start()
        left = jnp.concatenate([self.left[t, core] for t in range(self.planes)], axis=0)
        for i, columns in enumerate(self.tiles):
            part = product(left, self.right, columns, self.turned)
            self.near_copy(i).wait_recv()
            for t in range(self.planes):
                self.own[t, :, columns] = (
                    part[t * tokens : (t + 1) * tokens] + self.own[t, :, columns].astype(F32)
                ).astype(LOW)
        self.line.step(0)

    def finish(self, out_ref):
        def store(tile, total):
            out_ref[tile] = total

        self.line.finish(store)
        for i in range(len(self.tiles)):
            self.near_copy(i).wait_send()

    @staticmethod
    def scratch(planes, tokens, width):
        return [
            *[pltpu.VMEM((planes, tokens, width), LOW)] * 2,
            pltpu.VMEM((planes + 1, tokens, width), LOW),
        ]

    @classmethod
    def sems(cls, planes, width):
        return pairs_of(width // COLUMNS, cls.PARTS * planes, cls.PARTS * planes)


def feed_forward_kernel(
    planes, chips, width_ff, x_ref, up_ref, grads_ref, down_ref,
    out_ref, normed_ref, downs_ref, gup_ref, slots_ref,
    rows, ups, grads, downs, back, act, slope, stat, stat_out, stat_in,
    normed, d_up, near_out, own, sums, gup, gdown, *sems,
):
    here = place()
    z, c, core = here
    count = 2 * planes
    me = 2 * z + core
    up, down, near, chip_sems, stat_sems, pair, rise, fall, swap_sems = [
        sems[2 * i : 2 * i + 2] for i in range(9)
    ]
    local = sems[18]
    tokens, width = x_ref.shape
    units = ups.shape[1]
    load_up = pltpu.make_async_copy(up_ref, ups, local.at[0])
    load_grads = pltpu.make_async_copy(grads_ref, grads, local.at[1])
    load_up.start()
    load_grads.start()
    barrier = pltpu.get_barrier_semaphore()
    ids = [lax.rem(me + k, count) for k in range(1, count)]
    group_peers = [(index // 2, c, lax.rem(index, 2)) for index in ids]
    peers = [*group_peers, *chip_peers(chips, here)]
    greet(barrier, peers)
    pl.semaphore_wait(barrier, len(peers))

    group = GroupGather(planes, here, x_ref, rows, up, down, near)
    group.start(local.at[2])
    keep = pltpu.make_async_copy(down_ref, downs.at[c], local.at[3])
    keep.start()
    sends = [
        remote(down_ref, downs.at[c], chip_sems, k, device)
        for k, device in enumerate(chip_peers(chips, here), 1)
    ]
    for copy in sends:
        copy.start()
    load_up.wait()

    step = 16
    lane = lax.broadcasted_iota(jnp.int32, (step, 128), 1)

    def forward(t):
        group.other(t)
        block = rows[t].reshape(2 * tokens, width)
        for at in range(0, units, COLUMNS):
            columns = pl.ds(at, COLUMNS)
            act[t, :, columns] = jnp.dot(block, ups[:, columns], preferred_element_type=F32)

        def some(i, carry):
            at = pl.ds(pl.multiple_of(i * step, step), step)
            value = act[t, at]
            phi = 0.5 * (1.0 + lax.erf(value * math.sqrt(0.5)))
            result = value * phi
            act[t, at] = result
            slope[t, at] = phi + value * (
                jnp.exp(value * value * -0.5) * (1.0 / math.sqrt(2.0 * math.pi))
            )
            total = jnp.sum(result, axis=1, keepdims=True)
            square = jnp.sum(result * result, axis=1, keepdims=True)
            stat[t, at] = jnp.where(lane == 0, total, jnp.where(lane == 1, square, 0.0))
            return carry

        lax.fori_loop(0, 2 * tokens // step, some, 0)

    forward(z)
    for d in range(1, planes):
        group.step(d)
        if d > 1:
            pl.when(z - d + 1 >= 0)(lambda d=d: forward(z - d + 1))
            pl.when(z + d - 1 < planes)(lambda d=d: forward(z + d - 1))
    pl.when(z - planes + 1 >= 0)(lambda: forward(z - planes + 1))
    pl.when(z + planes - 1 < planes)(lambda: forward(z + planes - 1))
    group.finish()
    keep.wait()
    load_grads.wait()
    for k in range(1, chips):
        sends[k - 1].wait_send()
        other = lax.rem(c + chips - k, chips)
        remote(down_ref, downs.at[other], chip_sems, k, here).wait_recv()
    out_downs = pltpu.make_async_copy(downs, downs_ref, local.at[4])
    out_downs.start()

    def backward(t, carry):
        block = grads[t].reshape(2 * tokens, width)
        size = units // chips
        for chip in range(chips):
            columns = pl.ds(chip * size, size)
            back[t, :, columns] = rows_product(block, downs[chip])

        def some(i, inner):
            at = pl.ds(pl.multiple_of(i * step, step), step)
            value = back[t, at]
            cross = jnp.sum(value * act[t, at], axis=1, keepdims=True)
            total = jnp.sum(value, axis=1, keepdims=True)
            stat[t, at] = jnp.where(lane == 2, cross, jnp.where(lane == 3, total, stat[t, at]))
            return inner

        lax.fori_loop(0, 2 * tokens // step, some, 0)
        for half in range(2):
            turned = stat[t, pl.ds(half * tokens, tokens)].T
            stat_out[2 * t + half] = turned[:8]
        return carry

    lax.fori_loop(0, planes, backward, 0)
    copies = [
        remote(stat_out, stat_in.at[k], stat_sems, k, device)
        for k, device in enumerate(group_peers, 1)
    ]
    for copy in copies:
        copy.start()
    for copy in copies:
        copy.wait_send()
        copy.wait_recv()

    def finish(t, carry):
        for half in range(2):
            total = stat_out[2 * t + half]
            for k in range(1, count):
                total = total + stat_in[k, 2 * t + half]
            padded = jnp.concatenate([total, jnp.zeros((128 - 8, tokens), F32)], axis=0)
            stat[t, pl.ds(half * tokens, tokens)] = padded.T

        def some(i, inner):
            at = pl.ds(pl.multiple_of(i * step, step), step)
            figures = stat[t, at] * (1.0 / width_ff)
            mean, square, cross, first = (figures[:, j : j + 1] for j in range(4))
            scaler = lax.rsqrt(square - mean * mean + NORM_EPS)
            second = scaler * (cross - mean * first)
            unit = (act[t, at] - mean) * scaler
            normed[t, at] = unit.astype(LOW)
            d_act = scaler * (back[t, at] - first - unit * second)
            d_up[t, at] = (d_act * slope[t, at]).astype(LOW)
            return inner

        lax.fori_loop(0, 2 * tokens // step, some, 0)
        return carry

    lax.fori_loop(0, planes, finish, 0)
    out_normed = pltpu.make_async_copy(normed, normed_ref, local.at[5])
    out_normed.start()
    work = PairScatter(
        planes, here, Halves(d_up, tokens), ups, True, (near_out, own, sums), pair, rise, fall
    )
    work.start()

    flat_normed, flat_d_up = (
        whole[...].reshape(planes * 2 * tokens, units) for whole in (normed, d_up)
    )
    size = units // chips
    swap = ChipSwap(chips, here, lambda index: gdown.at[index], slots_ref, swap_sems)
    turns_left = list(range(1, work.line.steps))

    def turn():
        if turns_left:
            work.line.step(turns_left.pop(0))

    together = max(1, 256 // size)
    for chip in range(0, chips, together):
        left = flat_normed[:, chip * size : (chip + together) * size]
        for at in range(0, width, COLUMNS):
            columns = pl.ds(at, COLUMNS)
            right = grads[:, :, :, columns].reshape(planes * 2 * tokens, COLUMNS)
            term = token_product(left, right).astype(LOW)
            for i in range(together):
                gdown[chip + i, :, columns] = term[i * size : (i + 1) * size]
        turn()
    swap.start(local.at[6])
    chunk = gup.shape[1]
    out_gups = [
        pltpu.make_async_copy(
            gup.at[i % 2], gup_ref.at[pl.ds(i * chunk, chunk)], local.at[7 + i % 2]
        )
        for i in range(width // chunk)
    ]
    for i in range(width // chunk):
        turn()
        left = rows[:, :, :, pl.ds(i * chunk, chunk)].reshape(planes * 2 * tokens, chunk)
        term = token_product(left, flat_d_up).astype(LOW)
        if i > 1:
            out_gups[i - 2].wait()
        gup[i % 2] = term
        out_gups[i].start()
    while turns_left:
        turn()
    work.finish(out_ref)
    swap.finish()
    out_downs.wait()
    out_normed.wait()
    for copy in out_gups[-2:]:
        copy.wait()


class Halves:
    def __init__(self, whole, tokens):
        self.whole, self.tokens = whole, tokens

    def __getitem__(self, at):
        t, core = at
        rows = pl.ds(pl.multiple_of(core * self.tokens, self.tokens), self.tokens)
        return self.whole[t, rows]


def feed_forward(planes, chips, width_ff, x_block, up_mine, grads, down_block):
    tokens, width = x_block.shape
    units = up_mine.shape[1]
    size = down_block.shape[0]
    wide = (planes, 2 * tokens, units)
    return call(
        functools.partial(feed_forward_kernel, planes, chips, width_ff),
        "feed_forward",
        [
            shape((tokens, width), F32),
            shape(wide, LOW),
            shape((chips, size, width), LOW),
            shape((width, units), LOW),
            shape((chips, size, width), LOW),
        ],
        (x_block, up_mine, grads, down_block),
        [HBM] * 4,
        [VMEM, HBM, HBM, HBM, HBM],
        [
            pltpu.VMEM((planes, 2, tokens, width), LOW),
            pltpu.VMEM((width, units), LOW),
            pltpu.VMEM((planes, 2, tokens, width), LOW),
            pltpu.VMEM((chips, size, width), LOW),
            *[pltpu.VMEM(wide, F32)] * 3,
            pltpu.VMEM((planes, 2 * tokens, 128), F32),
            pltpu.VMEM((2 * planes, 8, 128), F32),
            pltpu.VMEM((2 * planes, 2 * planes, 8, 128), F32),
            *[pltpu.VMEM(wide, LOW)] * 2,
            *PairScatter.scratch(planes, tokens, width),
            pltpu.VMEM((2, 256, units), LOW),
            pltpu.VMEM((chips, size, width), LOW),
            *GroupGather.sems(planes),
            *pairs_of(chips, 2 * planes),
            *PairScatter.sems(planes, width),
            *pairs_of(chips),
            pltpu.SemaphoreType.DMA((9,)),
        ],
        7,
    )


def plane_gather_kernel(
    planes, chips, x_ref, stat_ref, tile_ref, left_ref, right_ref,
    row_ref, stats_ref, tiles_ref, ffn_ref,
    near_out, own, sums, *sems,
):
    here = place()
    z, c, core = here
    seqs = 2 * chips
    count = planes * seqs
    me = 2 * c + core
    flat = z * seqs + me
    x_far, x_near, s_far, s_near, tile_sems, near, up, down = [
        sems[2 * i : 2 * i + 2] for i in range(8)
    ]
    local = sems[16]
    barrier = pltpu.get_barrier_semaphore()

    def device_of(k):
        other = lax.rem(flat + k, count)
        return (other // seqs, lax.rem(other, seqs) // 2, lax.rem(other, 2))

    def signal(k, carry):
        greet(barrier, [device_of(k)])
        return carry

    lax.fori_loop(1, count, signal, 0)
    pl.semaphore_wait(barrier, count - 1)
    rows = PlaneGather(chips, here, x_ref, row_ref, x_far, x_near)
    stats = PlaneGather(chips, here, stat_ref, stats_ref, s_far, s_near)
    rows.start()
    stats.start()
    keeps = [
        pltpu.make_async_copy(x_ref, row_ref.at[me], local.at[0]),
        pltpu.make_async_copy(stat_ref, stats_ref.at[me], local.at[1]),
        pltpu.make_async_copy(tile_ref.at[flat], tiles_ref.at[flat], local.at[2]),
    ]
    for copy in keeps:
        copy.start()

    def tile_copy(k):
        other = lax.rem(flat + k, count)
        return remote(tile_ref.at[other], tiles_ref.at[flat], tile_sems, k, device_of(k))

    def tile_start(k, carry):
        tile_copy(k).start()
        return carry

    lax.fori_loop(1, count, tile_start, 0)
    work = PairScatter(
        planes, here, Halves(left_ref, x_ref.shape[0]), right_ref, False, (near_out, own, sums),
        near, up, down,
    )
    work.start()
    for i in range(1, work.line.steps):
        if i == work.line.steps // 2:
            rows.forward()
            stats.forward()
        work.line.step(i)
    rows.finish()
    stats.finish()
    work.finish(ffn_ref)
    for copy in keeps:
        copy.wait()

    def tile_wait(k, carry):
        tile_copy(k).wait_send()
        other = lax.rem(flat + count - k, count)
        remote(tile_ref.at[0], tiles_ref.at[other], tile_sems, k, here).wait_recv()
        return carry

    lax.fori_loop(1, count, tile_wait, 0)


def plane_gather(planes, chips, x_block, stats, tiles, left, right):
    seqs = 2 * chips
    tokens, width = x_block.shape
    return call(
        functools.partial(plane_gather_kernel, planes, chips),
        "plane_gather",
        [
            shape((seqs, *x_block.shape), x_block.dtype),
            shape((seqs, *stats.shape), stats.dtype),
            shape(tiles.shape, tiles.dtype),
            shape((tokens, width), F32),
        ],
        (x_block, stats, tiles, left, right),
        [HBM, HBM, HBM, VMEM, VMEM],
        [HBM, HBM, HBM, VMEM],
        [
            *PairScatter.scratch(planes, tokens, width),
            *pairs_of(chips, chips, chips, chips, planes * seqs),
            *PairScatter.sems(planes, width),
            pltpu.SemaphoreType.DMA((3,)),
        ],
        2,
    )


def swap_lanes(values):
    lane = lax.broadcasted_iota(jnp.int32, values.shape, 1)
    return jnp.where(
        lax.rem(lane, 2) == 0,
        pltpu.roll(values, values.shape[1] - 1, 1),
        pltpu.roll(values, 1, 1),
    )


def twice(table):
    return jnp.concatenate([table, table], axis=1)


def turns(meta_ref, rows):
    cosine, sine, shrink = [twice(meta_ref[rows, pl.ds(i * HD, HD)]) for i in range(3)]
    return (cosine, sine, cosine * shrink, sine * shrink)


def allowed_block(meta_ref, rows, size, columns):
    query = rows + lax.broadcasted_iota(jnp.int32, (size, columns), 0)
    key = lax.broadcasted_iota(jnp.int32, (size, columns), 1)
    offset = meta_ref[pl.ds(rows, size), pl.ds(3 * HD, 1)].astype(jnp.int32)
    return (key <= query) & (key >= query - offset)


BLOCK = 256


def attention_kernel(heads, raw_ref, meta_ref, q_ref, k_ref, v_ref, out_ref, log_ref, wide):
    length = raw_ref.shape[0]
    span = heads * HD
    for rows in row_tiles(length, BLOCK):
        tables = turns(meta_ref, rows)
        for pair in range(heads // 2):
            lanes = pl.ds(2 * HD * pair, 2 * HD)
            query = raw_ref[rows, lanes]
            query = (query * tables[0] + swap_lanes(query) * tables[1]).astype(LOW)
            key = raw_ref[rows, pl.ds(span + 2 * HD * pair, 2 * HD)]
            key = (key * tables[2] + swap_lanes(key) * tables[3]).astype(LOW)
            value = raw_ref[rows, pl.ds(2 * span + 2 * HD * pair, 2 * HD)].astype(LOW)
            for half in range(2):
                at = slice(half * HD, (half + 1) * HD)
                q_ref[2 * pair + half, rows] = query[:, at]
                k_ref[2 * pair + half, rows] = key[:, at]
                v_ref[2 * pair + half, rows] = value[:, at]
    log_ref[...] = jnp.zeros(log_ref.shape, F32)

    def one_head(head, carry):
        for start in range(0, length, BLOCK):
            columns = start + BLOCK
            rows = pl.ds(start, BLOCK)
            scores = lax.dot_general(
                q_ref[head, rows],
                k_ref[head, pl.ds(0, columns)],
                (((1,), (1,)), ((), ())),
                preferred_element_type=F32,
            )
            allowed = allowed_block(meta_ref, start, BLOCK, columns)
            scores = jnp.where(allowed, scores, NEG_FILL)
            top = jnp.max(scores, axis=1, keepdims=True)
            shifted = jnp.exp(scores - top)
            total = jnp.sum(shifted, axis=1, keepdims=True)
            probs = (shifted * (1.0 / total)).astype(LOW)
            wide[head, rows] = jnp.dot(
                probs, v_ref[head, pl.ds(0, columns)], preferred_element_type=F32
            )
            lane = lax.broadcasted_iota(jnp.int32, (BLOCK, 128), 1)
            log_ref[rows] = jnp.where(lane == head, top + jnp.log(total), log_ref[rows])
        return carry

    lax.fori_loop(0, heads, one_head, 0)
    for rows in row_tiles(length, BLOCK):
        out_ref[rows] = jnp.concatenate(
            [wide[head, rows] for head in range(heads)], axis=1
        ).astype(LOW)


def attention(heads, raw, meta):
    length = raw.shape[0]
    return call(
        functools.partial(attention_kernel, heads),
        "attention",
        [
            *[shape((heads, length, HD), LOW)] * 3,
            shape((length, heads * HD), LOW),
            shape((length, 128), F32),
        ],
        (raw, meta),
        [VMEM] * 2,
        [VMEM] * 5,
        [pltpu.VMEM((heads, length, HD), F32)],
    )


def attention_back_kernel(
    planes, chips, heads, strided,
    q_ref, k_ref, v_ref, att_ref, row_ref, right_ref, stat_ref, log_ref, meta_ref, up_ref,
    out_ref, total_ref, slots_ref,
    grad, dq, dk, dv, normed_all, own, sums, *sems,
):
    here = place()
    up, down, swap_sems = [sems[2 * i : 2 * i + 2] for i in range(3)]
    barrier = pltpu.get_barrier_semaphore()
    greet(barrier, chip_peers(chips, here))
    greet_line(barrier, planes, here)
    pl.semaphore_wait(barrier, chips - 1 + line_peers(planes, here))
    swap = ChipSwap(
        chips, here, lambda index: half_block(up_ref, slots_ref, index, 0), slots_ref, swap_sems
    )
    swap.start(sems[6].at[0])
    length, span = att_ref.shape
    part, width = own.shape[1:]
    for rows in row_tiles(length, BLOCK):
        mean, scaler, first, second = (stat_ref[rows, pl.ds(i, 1)] for i in range(4))
        d_sub = product(row_ref[rows], right_ref, slice(None), True)
        normed = (att_ref[rows].astype(F32) - mean) * scaler
        normed_all[rows] = normed.astype(LOW)
        d_att = (scaler * (d_sub - first - normed * second)).astype(LOW)
        for head in range(heads):
            grad[head, rows] = d_att[:, head * HD : (head + 1) * HD]
    for at in range(0, width, COLUMNS):
        columns = pl.ds(at, COLUMNS)
        term = token_product(normed_all[...], row_ref[:, columns]).astype(LOW)
        for t in range(planes):
            own[t, :, columns] = term[t * part : (t + 1) * part]
    line = LineScatter(
        planes,
        here,
        1,
        lambda p: (slice(None),),
        lambda p: [(rows,) for rows in row_tiles(part, 16)],
        lambda t, tile: own[(t, *tile)].astype(F32),
        sums,
        up,
        down,
    )
    if strided:
        line.step(0)
    dk[...] = jnp.zeros(dk.shape, F32)
    dv[...] = jnp.zeros(dv.shape, F32)

    def one_head(head, carry):
        for start in range(0, length, BLOCK):
            columns = start + BLOCK
            rows = pl.ds(start, BLOCK)
            keys = pl.ds(0, columns)
            query, key = q_ref[head, rows], k_ref[head, keys]
            out_grad = grad[head, rows]
            scores = lax.dot_general(
                query, key, (((1,), (1,)), ((), ())), preferred_element_type=F32
            )
            allowed = allowed_block(meta_ref, start, BLOCK, columns)
            lane = lax.broadcasted_iota(jnp.int32, (BLOCK, 128), 1)
            log_total = jnp.sum(
                jnp.where(lane == head, log_ref[rows], 0.0), axis=1, keepdims=True
            )
            probs = jnp.where(allowed, jnp.exp(scores - log_total), 0.0)
            d_probs = lax.dot_general(
                out_grad, v_ref[head, keys], (((1,), (1,)), ((), ())), preferred_element_type=F32
            )
            delta = jnp.sum(probs * d_probs, axis=1, keepdims=True)
            d_scores = (probs * (d_probs - delta)).astype(LOW)
            dq[head, rows] = jnp.dot(d_scores, key, preferred_element_type=F32)
            dk[head, keys] += token_product(d_scores, query)
            dv[head, keys] += token_product(probs.astype(LOW), out_grad)
        return carry

    first = 0
    for i in range(1, planes - 1):
        last = -(-heads * i // (planes - 1))
        lax.fori_loop(first, last, one_head, 0)
        first = last
        if strided:
            line.step(i)
    lax.fori_loop(first, heads, one_head, 0)
    for rows in row_tiles(length, BLOCK):
        tables = turns(meta_ref, rows)
        for pair in range(heads // 2):
            both = [
                jnp.concatenate(
                    [whole[2 * pair, rows], whole[2 * pair + 1, rows]], axis=1
                ).astype(LOW)
                for whole in (dq, dk, dv)
            ]
            query, key = both[0].astype(F32), both[1].astype(F32)
            query = query * tables[0] + swap_lanes(query * tables[1])
            key = key * tables[2] + swap_lanes(key * tables[3])
            out_ref[rows, pl.ds(2 * HD * pair, 2 * HD)] = query.astype(LOW)
            out_ref[rows, pl.ds(span + 2 * HD * pair, 2 * HD)] = key.astype(LOW)
            out_ref[rows, pl.ds(2 * span + 2 * HD * pair, 2 * HD)] = both[2]
    if strided:

        def store(tile, total):
            total_ref[tile] = total

        line.finish(store)
    else:
        for t in range(planes):
            total_ref[pl.ds(t * part, part)] = own[t].astype(F32)
    swap.finish()


def attention_back(planes, chips, heads, strided, part, units, args):
    length, span = args[3].shape
    width = args[4].shape[1]
    return call(
        functools.partial(attention_back_kernel, planes, chips, heads, strided),
        "attention_back",
        [
            shape((length, 3 * span), LOW),
            shape((part if strided else span, width), F32),
            shape((chips, width // 2, units), LOW),
        ],
        args,
        [*[VMEM] * 9, HBM],
        [*[VMEM] * 2, HBM],
        [
            pltpu.VMEM((heads, length, HD), LOW),
            *[pltpu.VMEM((heads, length, HD), F32)] * 3,
            pltpu.VMEM((length, span), LOW),
            pltpu.VMEM((planes, part, width), LOW),
            pltpu.VMEM((planes + 1, part, width), LOW),
            *pairs_of(planes, planes, chips),
            pltpu.SemaphoreType.DMA((1,)),
        ],
        8,
    )


def body(
    hidden_in,
    segment_ids,
    position_ids,
    w_qkv,
    w_out,
    w_up,
    w_down,
    gain_attn,
    gain_attn_sub,
    gain_ffn,
    gain_ffn_sub,
    ema_qkv,
    ema_out,
    ema_up,
    ema_down,
    ema_gain_attn,
    ema_gain_attn_sub,
    ema_gain_ffn,
    ema_gain_ffn_sub,
    out_grad,
):
    _, tokens, width = hidden_in.shape
    planes, chips = lax.axis_size("dp"), lax.axis_size("chip")
    seqs = 2 * chips
    length = tokens * seqs
    heads = HEADS // seqs
    span = heads * HD
    part = w_qkv.shape[0]
    strided = part % HD == 0
    width_ff = w_down.shape[0] * planes * seqs
    seq_index = lax.axis_index(SEQ)

    def gain_rows(weight, gain):
        return (weight.astype(F32) * gain.astype(F32)[:, None]).astype(LOW)

    qkv_scaled = gain_rows(w_qkv, gain_attn)
    out_scaled = gain_rows(w_out, gain_attn_sub)
    down_scaled = gain_rows(w_down, gain_ffn_sub)
    if strided:
        qkv_send = qkv_scaled.reshape(part, 3, planes, seqs, HD).transpose(3, 0, 1, 2, 4)
    else:
        qkv_send = qkv_scaled.reshape(part, 3, seqs, span).transpose(2, 0, 1, 3)
    qkv_send = qkv_send.reshape(seqs, part, 3 * span)
    x_in = hidden_in[0].astype(F32)
    normed_one, scaler_one = moments(x_in)
    normed_low = normed_one.astype(LOW)
    gain_tile = jnp.zeros((8, 128), F32).at[0, :part].set(gain_ffn.astype(F32))

    row_in, meta, qkv_mine, out_mine, gain_tiles, up_mine = attention_gather(
        planes,
        chips,
        normed_low,
        token_tables(position_ids[0]),
        qkv_send,
        out_scaled,
        gain_tile,
        w_up,
    )
    if up_mine.ndim == 3:
        up_mine = up_mine.transpose(1, 0, 2).reshape(width, -1)
    row_in = row_in.reshape(length, width)
    meta = meta.reshape(length, -1)
    qkv_mine = qkv_mine.reshape(width, 3 * span)
    if strided:
        out_mine = out_mine.reshape(span, width)
    else:
        out_all = lax.all_gather(out_scaled, ALL, axis=0, tiled=True)
        out_mine = lax.dynamic_slice_in_dim(out_all, seq_index * span, span, axis=0)
    queries, keys, values, attended, log_total = attention(heads, dot(row_in, qkv_mine), meta)
    attended_wide = attended.astype(F32)
    column_part = jnp.sum(out_mine.astype(F32), axis=0)
    token_sums = jnp.stack(
        [jnp.sum(attended_wide, axis=1), jnp.sum(attended_wide * attended_wide, axis=1)]
    ).reshape(2, seqs, tokens)
    tiles = jnp.concatenate(
        [
            jnp.swapaxes(token_sums, 0, 1),
            jnp.zeros((seqs, 6, tokens), F32),
            jnp.broadcast_to(column_part.reshape(1, -1, tokens), (seqs, width // tokens, tokens)),
        ],
        axis=1,
    )
    grad_low = out_grad[0]
    out_sum, tiles, grad_flat = out_scatter(
        planes, chips, attended.reshape(seqs, tokens, span), out_mine, tiles, grad_low
    )
    tiles = jnp.sum(tiles, axis=0)
    column_sum = tiles[8:].reshape(width)
    sums = tiles[:2].T
    gain_three = gain_tiles[:, 0, :part].reshape(width)
    mean_two = sums[:, :1] / width
    scaler_two = lax.rsqrt(sums[:, 1:] / width - mean_two * mean_two + NORM_EPS)
    projected = scaler_two * (out_sum - mean_two * column_sum[None, :])
    hmid = x_in + projected
    normed_three, scaler_three = moments(hmid)
    ffn_in = (normed_three * gain_three).astype(LOW)

    grad_top = grad_low.astype(F32)
    units = w_up.shape[1]
    d_ffn_in, normed_four, down_mine, grad_up, down_slots = feed_forward(
        planes, chips, width_ff, ffn_in, up_mine, grad_flat, down_scaled
    )
    down_mine = down_mine.reshape(-1, width)
    if units % 128:
        grad_up = grad_up.reshape(width, chips, units).transpose(1, 0, 2)

    gain_part = jnp.sum(d_ffn_in * normed_three, axis=0).reshape(planes * seqs, 1, part)
    gain_part = jnp.pad(gain_part, ((0, 0), (0, 7), (0, 128 - part)))
    d_hmid = grad_top + norm_back(d_ffn_in * gain_three, normed_three, scaler_three)
    d_hmid_low = d_hmid.astype(LOW)
    d_hmid_wide = d_hmid_low.astype(F32)
    first_two = jnp.sum(d_hmid_wide * column_sum[None, :], axis=1, keepdims=True) / width
    second_two = jnp.sum(d_hmid_wide * projected, axis=1, keepdims=True) / width
    token_stats = jnp.concatenate([mean_two, scaler_two, first_two, second_two], axis=1)
    row_grad, row_stats, gain_part, ffn_out = plane_gather(
        planes,
        chips,
        d_hmid_low,
        jnp.pad(token_stats, ((0, 0), (0, 124))),
        gain_part,
        normed_four,
        down_mine,
    )
    output = (hmid + ffn_out).astype(LOW)[None]
    row_grad = row_grad.reshape(length, width)
    row_stats = row_stats.reshape(length, 128)
    grad_gain_three = jnp.sum(gain_part, axis=0)[0, :part]
    d_qkv, sum_out, upper_slots = attention_back(
        planes,
        chips,
        heads,
        strided,
        part,
        units,
        (queries, keys, values, attended, row_grad, out_mine, row_stats, log_total, meta, grad_up),
    )
    grad_qkv = token_product(row_in, d_qkv).astype(LOW)
    d_in, sum_qkv, grad_gain_one, lower_slots = in_scatter(
        planes,
        chips,
        heads,
        strided,
        d_qkv.reshape(seqs, tokens, 3 * span),
        qkv_mine,
        grad_qkv.reshape(planes, seqs, part, 3 * span),
        grad_up,
        w_qkv,
        jnp.broadcast_to(gain_attn.astype(F32)[:, None], (part, 128)),
        units,
    )
    grad_gain_one = grad_gain_one[:, 0]
    sum_up = jnp.concatenate(
        [jnp.sum(slots.astype(F32), axis=0) for slots in (upper_slots, lower_slots)], axis=0
    )
    sum_down = jnp.sum(down_slots.astype(F32), axis=0)
    input_grad = (d_hmid + norm_back(d_in, normed_one, scaler_one)).astype(LOW)[None]

    if not strided:
        spread = lax.dynamic_update_slice_in_dim(
            jnp.zeros((width, width), LOW), sum_out.astype(LOW), seq_index * span, axis=0
        )
        sum_out = lax.psum_scatter(spread, ALL, scatter_dimension=0, tiled=True).astype(F32)

    def finish(total, weight, gain):
        wide = weight.astype(F32)
        return (total * gain.astype(F32)[:, None], jnp.sum(total * wide, axis=1))

    sum_out, grad_gain_two = finish(sum_out, w_out, gain_attn_sub)
    sum_down, grad_gain_four = finish(sum_down, w_down, gain_ffn_sub)

    def averaged(average, weight):
        return EMA_DECAY * average + (1.0 - EMA_DECAY) * weight.astype(F32)

    return (
        output,
        input_grad,
        sum_qkv,
        sum_out,
        sum_up,
        sum_down,
        grad_gain_one,
        grad_gain_two,
        grad_gain_three,
        grad_gain_four,
        averaged(ema_qkv, w_qkv),
        averaged(ema_out, w_out),
        averaged(ema_up, w_up),
        averaged(ema_down, w_down),
        averaged(ema_gain_attn, gain_attn),
        averaged(ema_gain_attn_sub, gain_attn_sub),
        averaged(ema_gain_ffn, gain_ffn),
        averaged(ema_gain_ffn_sub, gain_ffn_sub),
    )


def solution(mesh):
    split = Mesh(
        mesh.devices.reshape(mesh.shape["dp"], mesh.shape["seq"] // 2, 2), ("dp", "chip", "core")
    )
    tokens = P("dp", SEQ, None)
    ids = P("dp", SEQ)
    rows = P(ALL, None)
    columns = P(None, ALL)
    vector = P(ALL)
    weights = (rows, rows, columns, rows)
    gains = (vector,) * 4
    return jax.shard_map(
        body,
        mesh=split,
        in_specs=(tokens, ids, ids, *weights, *gains, *weights, *gains, tokens),
        out_specs=(tokens, tokens, *weights, *gains, *weights, *gains),
        check_vma=False,
    )
```

```python
import functools
import math

import jax
import jax.numpy as jnp
from jax import lax
from jax.experimental import pallas as pl
from jax.experimental.pallas import tpu as pltpu
from jax.sharding import Mesh
from jax.sharding import PartitionSpec as P

HEADS = 32
HD = 64

NEG_FILL = -1000000000.0
NORM_EPS = 1e-05
EMA_DECAY = 0.7
LOW = jnp.bfloat16
F32 = jnp.float32
SEQ = ("chip", "core")
TP = ("dp", "core")
ALL = ("dp", "chip", "core")


def moments(values):
    mean = jnp.mean(values, axis=-1, keepdims=True)
    centered = values - mean
    scaler = lax.rsqrt(jnp.mean(centered * centered, axis=-1, keepdims=True) + NORM_EPS)
    return (centered * scaler, scaler)


def norm_back(scaled_grad, normed, scaler):
    first_mean = jnp.mean(scaled_grad, axis=-1, keepdims=True)
    second_mean = jnp.mean(scaled_grad * normed, axis=-1, keepdims=True)
    return scaler * (scaled_grad - first_mean - normed * second_mean)


def token_tables(positions):
    half_count = HD // 2
    index_half = jnp.arange(half_count).astype(F32)
    inverse = jnp.exp(-(2.0 * index_half / HD) * math.log(10000.0))
    decay_base = (2.0 * index_half + 0.4 * HD) / (1.4 * HD)
    where_at = positions.astype(F32)[:, None]
    angles = where_at * inverse[None, :]
    factor = jnp.exp(where_at / 512.0 * jnp.log(decay_base)[None, :])
    sign_row = jnp.where(jnp.arange(HD) % 2 == 0, -1.0, 1.0).astype(F32)
    cosine = jnp.repeat(jnp.cos(angles), 2, axis=1)
    sine = jnp.repeat(jnp.sin(angles), 2, axis=1) * sign_row[None, :]
    factor = jnp.repeat(factor, 2, axis=1)
    grow = factor * HD ** (-0.5)
    where_block = jnp.broadcast_to(where_at, (positions.shape[0], HD))
    return jnp.concatenate(
        [cosine * grow, sine * grow, HD**0.5 / (factor * factor), where_block], axis=1
    )


def dot(left_op, right_op):
    return jnp.dot(left_op, right_op, preferred_element_type=F32)


def rows_product(operand, weight_rows):
    return lax.dot_general(
        operand, weight_rows, (((1,), (1,)), ((), ())), preferred_element_type=F32
    )


def token_product(left_op, right_op):
    return lax.dot_general(left_op, right_op, (((0,), (0,)), ((), ())), preferred_element_type=F32)


MESH = pl.DeviceIdType.MESH
HBM = pl.BlockSpec(memory_space=pl.ANY)
VMEM = pl.BlockSpec(memory_space=pltpu.VMEM)
VMEM_BYTES = 60 * 1024 * 1024


def shape(dims, kind):
    return jax.ShapeDtypeStruct(dims, kind)


def pairs_of(*counts):
    return [pltpu.SemaphoreType.DMA((count,)) for count in counts for _ in range(2)]


def call(kernel, name, outs, args, in_specs, out_specs, scratch, collective=None):
    return pl.pallas_call(
        kernel,
        name=name,
        out_shape=outs,
        in_specs=in_specs,
        out_specs=out_specs,
        scratch_shapes=scratch,
        compiler_params=pltpu.CompilerParams(
            collective_id=collective,
            has_side_effects=collective is not None,
            vmem_limit_bytes=VMEM_BYTES,
        ),
    )(*args)


def place():
    return (lax.axis_index("dp"), lax.axis_index("chip"), lax.axis_index("core"))


def remote(source, target, sems, index, device):
    return pltpu.make_async_remote_copy(
        src_ref=source,
        dst_ref=target,
        send_sem=sems[0].at[index],
        recv_sem=sems[1].at[index],
        device_id=device,
        device_id_type=MESH,
    )


def greet(barrier, devices):
    for device in devices:
        pl.semaphore_signal(barrier, inc=1, device_id=device, device_id_type=MESH)


def greet_line(barrier, planes, here):
    z, c, core = here

    @pl.when(z < planes - 1)
    def _():
        greet(barrier, [(z + 1, c, core)])

    @pl.when(z > 0)
    def _():
        greet(barrier, [(z - 1, c, core)])


def line_peers(planes, here):
    z = here[0]
    return (2 * planes - 2 - z) // planes + (z + planes - 1) // planes


def chip_peers(chips, here):
    z, c, core = here
    return [(z, lax.rem(c + k, chips), core) for k in range(1, chips)]


def plane_peers(chips, here):
    z, c, core = here
    seqs = 2 * chips
    me = 2 * c + core
    ids = [lax.rem(me + k, seqs) for k in range(1, seqs)]
    return [(z, index // 2, lax.rem(index, 2)) for index in ids]


def column_block(whole, units, index):
    if len(whole.shape) == 3:
        return whole.at[index]
    return whole.at[:, pl.ds(pl.multiple_of(index * units, 128), units)]


def half_block(whole, slots, index, half):
    rows, units = slots.shape[1:]
    at = pl.ds(half * rows, rows)
    if len(whole.shape) == 3:
        return whole.at[index, at]
    return whole.at[at, pl.ds(pl.multiple_of(index * units, 128), units)]


class ChipSwap:
    def __init__(self, chips, here, source, slots, sems):
        z, c, core = here
        self.sends = [
            remote(source(device[1]), slots.at[c], sems, k, device)
            for k, device in enumerate(chip_peers(chips, here), 1)
        ]
        self.waits = [
            remote(source(c), slots.at[lax.rem(c + chips - k, chips)], sems, k, here)
            for k in range(1, chips)
        ]
        self.keep = (source(c), slots.at[c])

    def start(self, local):
        for copy in self.sends:
            copy.start()
        self.held = pltpu.make_async_copy(*self.keep, local)
        self.held.start()

    def finish(self):
        self.held.wait()
        for send, wait in zip(self.sends, self.waits):
            send.wait_send()
            wait.wait_recv()


class PlaneGather:
    def __init__(self, chips, here, block, out, far, near):
        self.chips, self.here, self.block, self.out = chips, here, block, out
        self.far, self.near = far, near
        z, c, core = here
        self.me = 2 * c + core
        self.partner = (z, c, 1 - core)

    def source(self, k, core):
        return 2 * lax.rem(self.here[1] + self.chips - k, self.chips) + core

    def sends(self):
        mine = self.out.at[self.me]
        copies = [
            remote(self.block, mine, self.far, k, device)
            for k, device in enumerate(chip_peers(self.chips, self.here), 1)
        ]
        return [*copies, remote(self.block, mine, self.near, 0, self.partner)]

    def start(self):
        for copy in self.sends():
            copy.start()

    def passed(self, k):
        index = self.source(k, self.here[2])
        return remote(self.out.at[index], self.out.at[index], self.near, k, self.partner)

    def forward(self):
        for k in range(1, self.chips):
            index = self.source(k, self.here[2])
            remote(self.block, self.out.at[index], self.far, k, self.partner).wait_recv()
            self.passed(k).start()

    def finish(self):
        for copy in self.sends():
            copy.wait_send()
        for k in range(1, self.chips):
            self.passed(k).wait_send()
        for k in range(self.chips):
            index = self.source(k, 1 - self.here[2])
            remote(self.block, self.out.at[index], self.near, k, self.partner).wait_recv()


class LineGather:
    def __init__(self, planes, here, parts, up, down):
        self.planes, self.here, self.parts = planes, here, parts
        self.up, self.down = up, down
        self.count = len(parts(here[0]))

    def upward(self, d, p):
        z, c, core = self.here
        block = self.parts(z - d)[p]
        return remote(block, block, self.up, d * self.count + p, (z + 1, c, core))

    def downward(self, d, p):
        z, c, core = self.here
        block = self.parts(z + d)[p]
        return remote(block, block, self.down, d * self.count + p, (z - 1, c, core))

    def each(self, d, p, act):
        z, planes = self.here[0], self.planes
        pl.when((z < planes - 1) & (z - d >= 0))(lambda: act(self.upward(d, p)))
        pl.when((z > 0) & (z + d < planes))(lambda: act(self.downward(d, p)))

    def start(self):
        for p in range(self.count):
            self.each(0, p, lambda copy: copy.start())

    def step(self, d, arrived=None):
        z, planes = self.here[0], self.planes

        def below(p):
            block = self.parts(z - d)[p]
            remote(block, block, self.up, (d - 1) * self.count + p, self.here).wait_recv()
            if d < planes - 1:
                pl.when(z < planes - 1)(lambda: self.upward(d, p).start())
            if arrived is not None:
                arrived(z - d, p)

        def above(p):
            block = self.parts(z + d)[p]
            remote(block, block, self.down, (d - 1) * self.count + p, self.here).wait_recv()
            if d < planes - 1:
                pl.when(z > 0)(lambda: self.downward(d, p).start())
            if arrived is not None:
                arrived(z + d, p)

        for p in range(self.count):
            pl.when(z - d >= 0)(lambda p=p: below(p))
            pl.when(z + d < planes)(lambda p=p: above(p))

    def finish(self):
        for d in range(self.planes - 1):
            for p in range(self.count):
                self.each(d, p, lambda copy: copy.wait_send())


class GroupGather:
    PARTS = 2

    def __init__(self, planes, here, block, out, up, down, near):
        self.planes, self.here, self.block, self.out, self.near = planes, here, block, out, near
        self.partner = (here[0], here[1], 1 - here[2])
        size = block.shape[0] // self.PARTS
        self.slices = [pl.ds(p * size, size) for p in range(self.PARTS)]
        core = here[2]
        self.line = LineGather(planes, here, lambda t: self.parts(t, core), up, down)

    def parts(self, t, core):
        return [self.out.at[t, core, rows] for rows in self.slices]

    def passed(self, t, p):
        block = self.parts(t, self.here[2])[p]
        return remote(block, block, self.near, t * self.PARTS + p, self.partner)

    def start(self, local):
        z, _, core = self.here
        keep = pltpu.make_async_copy(self.block, self.out.at[z, core], local)
        keep.start()
        keep.wait()
        self.line.start()
        for p in range(self.PARTS):
            self.passed(z, p).start()

    def step(self, d):
        self.line.step(d, lambda t, p: self.passed(t, p).start())

    def other(self, t):
        for p in range(self.PARTS):
            block = self.parts(t, 1 - self.here[2])[p]
            remote(block, block, self.near, t * self.PARTS + p, self.partner).wait_recv()

    def finish(self):
        self.line.finish()
        for t in range(self.planes):
            for p in range(self.PARTS):
                self.passed(t, p).wait_send()

    @classmethod
    def sems(cls, planes):
        return pairs_of(*[planes * cls.PARTS] * 3)


COLUMNS = 512


def product(left, right, columns, turned):
    if turned:
        return lax.dot_general(
            left, right[columns, :], (((1,), (1,)), ((), ())), preferred_element_type=F32
        )
    return jnp.dot(left, right[:, columns], preferred_element_type=F32)


class PlaneScatter:
    def __init__(self, chips, here, left, right, turned, buffers, near, far):
        self.chips, self.here = chips, here
        self.left, self.right, self.turned = left, right, turned
        self.near_out, self.near_in, self.far_out, self.far_in = buffers
        self.near, self.far = near, far
        self.tokens, width = self.near_out.shape[1:]
        self.tiles = [pl.ds(at, COLUMNS) for at in range(0, width, COLUMNS)]
        self.order = [*range(1, chips), 0]

    def target(self, k):
        return lax.rem(self.here[1] + k, self.chips)

    def near_copy(self, i):
        z, c, core = self.here
        at = (slice(None), slice(None), self.tiles[i])
        return remote(self.near_out.at[at], self.near_in.at[at], self.near, i, (z, c, 1 - core))

    def far_copy(self, k, i):
        z, _, core = self.here
        at = (k, slice(None), self.tiles[i])
        index = k * len(self.tiles) + i
        return remote(
            self.far_out.at[at], self.far_in.at[at], self.far, index, (z, self.target(k), core)
        )

    def rows(self, position):
        return slice(position * self.tokens, (position + 1) * self.tokens)

    def start(self):
        core = self.here[2]
        blocks = [self.left[2 * self.target(k) + 1 - core] for k in self.order]
        left = jnp.concatenate(blocks, axis=0)
        for i, columns in enumerate(self.tiles):
            part = product(left, self.right, columns, self.turned).astype(LOW)
            for position, k in enumerate(self.order):
                self.near_out[k, :, columns] = part[self.rows(position)]
            self.near_copy(i).start()
        blocks = [self.left[2 * self.target(k) + core] for k in self.order]
        left = jnp.concatenate(blocks, axis=0)
        for i, columns in enumerate(self.tiles):
            part = product(left, self.right, columns, self.turned)
            self.near_copy(i).wait_recv()
            for position, k in enumerate(self.order):
                self.far_out[k, :, columns] = (
                    part[self.rows(position)] + self.near_in[k, :, columns].astype(F32)
                ).astype(LOW)
                if k:
                    self.far_copy(k, i).start()

    def finish(self, out_ref):
        for i, columns in enumerate(self.tiles):
            total = self.far_out[0, :, columns].astype(F32)
            for k in range(1, self.chips):
                self.far_copy(k, i).wait_recv()
                total = total + self.far_in[k, :, columns].astype(F32)
            out_ref[:, columns] = total
        for i in range(len(self.tiles)):
            self.near_copy(i).wait_send()
            for k in range(1, self.chips):
                self.far_copy(k, i).wait_send()

    @staticmethod
    def scratch(chips, tokens, width):
        return [pltpu.VMEM((chips, tokens, width), LOW)] * 4

    @staticmethod
    def sems(chips, width):
        return pairs_of(width // COLUMNS, chips * (width // COLUMNS))


class LineScatter:
    def __init__(self, planes, here, count, part, tiles, own, slots, up, down):
        self.planes, self.here, self.count = planes, here, count
        self.part, self.tiles, self.own, self.slots = part, tiles, own, slots
        self.up, self.down = up, down
        self.steps = (planes - 1) * count

    def upward(self, t, p):
        z, c, core = self.here
        block = self.slots.at[(t, *self.part(p))]
        return remote(block, block, self.up, t * self.count + p, (z + 1, c, core))

    def downward(self, t, p, last):
        z, c, core = self.here
        block = self.slots.at[(t, *self.part(p))]
        target = self.slots.at[(self.planes, *self.part(p))] if last else block
        return remote(block, target, self.down, t * self.count + p, (z - 1, c, core))

    def add(self, t, p, fresh):
        for tile in self.tiles(p):
            total = self.own(t, tile)
            if not fresh:
                total = total + self.slots[(t, *tile)].astype(F32)
            self.slots[(t, *tile)] = total.astype(LOW)

    def step(self, i):
        z, planes, count = self.here[0], self.planes, self.count
        rise, fall = i - z, i - (planes - 1 - z)

        @pl.when((rise >= 0) & (rise < (planes - 1 - z) * count))
        def _():
            t, p = planes - 1 - rise // count, lax.rem(rise, count)

            @pl.when(z > 0)
            def _():
                self.upward(t, p).wait_recv()
                self.add(t, p, False)

            @pl.when(z == 0)
            def _():
                self.add(t, p, True)

            self.upward(t, p).start()

        @pl.when((fall >= 0) & (fall < z * count))
        def _():
            t, p = fall // count, lax.rem(fall, count)

            @pl.when(z < planes - 1)
            def _():
                self.downward(t, p, False).wait_recv()
                self.add(t, p, False)

            @pl.when(z == planes - 1)
            def _():
                self.add(t, p, True)

            pl.when(t == z - 1)(lambda: self.downward(t, p, True).start())
            pl.when(t < z - 1)(lambda: self.downward(t, p, False).start())

    def finish(self, store):
        z, planes = self.here[0], self.planes

        def total(tile, *slots):
            value = self.own(z, tile)
            for slot in slots:
                value = value + self.slots[(slot, *tile)].astype(F32)
            store(tile, value)

        for p in range(self.count):
            tiles = self.tiles(p)

            @pl.when(z > 0)
            def _(p=p):
                self.upward(z, p).wait_recv()

            @pl.when(z < planes - 1)
            def _(p=p):
                self.downward(z, p, True).wait_recv()

            @pl.when((z > 0) & (z < planes - 1))
            def _(tiles=tiles):
                for tile in tiles:
                    total(tile, z, planes)

            @pl.when(z == 0)
            def _(tiles=tiles):
                for tile in tiles:
                    total(tile, planes)

            @pl.when(z == planes - 1)
            def _(tiles=tiles):
                for tile in tiles:
                    total(tile, z)

        for t in range(planes):
            for p in range(self.count):
                pl.when(z < t)(lambda t=t, p=p: self.upward(t, p).wait_send())
                pl.when(z > t)(lambda t=t, p=p: self.downward(t, p, False).wait_send())


def row_tiles(count, size):
    return [pl.ds(at, size) for at in range(0, count, size)]


def in_scatter_kernel(
    planes, chips, heads, strided, left_ref, right_ref, grad_ref, up_ref, weight_ref, gain_ref,
    out_ref, total_ref, gains_ref, slots_ref,
    near_out, near_in, far_out, far_in, sums, mine, parts, *sems,
):
    here = place()
    z, c, core = here
    seqs = 2 * chips
    me = 2 * c + core
    near, far, up, down, swap_sems, chip_sems = [sems[2 * i : 2 * i + 2] for i in range(6)]
    barrier = pltpu.get_barrier_semaphore()
    peers = plane_peers(chips, here)
    greet(barrier, peers)
    greet_line(barrier, planes, here)
    pl.semaphore_wait(barrier, len(peers) + line_peers(planes, here))
    half = seqs // 2
    line = LineScatter(
        planes,
        here,
        2,
        lambda p: (pl.ds(p * half, half),),
        lambda p: [(pl.ds(p * half + i, 1),) for i in range(half)],
        lambda t, tile: grad_ref[(t, *tile)].astype(F32),
        sums,
        up,
        down,
    )
    line.step(0)
    work = PlaneScatter(
        chips, here, left_ref, right_ref, True, (near_out, near_in, far_out, far_in), near, far
    )
    work.start()
    ups = ChipSwap(
        chips, here, lambda index: half_block(up_ref, slots_ref, index, 1), slots_ref, chip_sems
    )
    ups.start(sems[12].at[0])
    for i in range(1, line.steps):
        line.step(i)

    def store(tile, total):
        mine[tile] = total.astype(LOW)

    line.finish(store)
    swaps = [
        remote(mine.at[2 * device[1] + device[2]], parts.at[me], swap_sems, k, device)
        for k, device in enumerate(peers, 1)
    ]
    for copy in swaps:
        copy.start()
    parts[me] = mine[me]
    work.finish(out_ref)
    for k in range(1, seqs):
        swaps[k - 1].wait_send()
        index = lax.rem(me + seqs - k, seqs)
        remote(mine.at[0], parts.at[index], swap_sems, k, here).wait_recv()
    span = heads * HD
    width = seqs * span
    gain = gain_ref[:, pl.ds(0, 1)]
    summed = jnp.zeros(gain.shape, F32)
    for i in range(3):
        step, pieces = (seqs * HD, planes) if strided else (width, 1)
        size = step // seqs
        for piece in range(pieces):
            at = i * span + piece * size
            columns = pl.ds(i * width + piece * step, step)
            total = jnp.concatenate(
                [parts[s, :, pl.ds(at, size)].astype(F32) for s in range(seqs)], axis=1
            )
            weight = weight_ref[:, columns].astype(F32)
            summed = summed + jnp.sum(total * weight, axis=1, keepdims=True)
            total_ref[:, columns] = total * gain
    gains_ref[...] = jnp.broadcast_to(summed, gains_ref.shape)
    ups.finish()


def in_scatter(planes, chips, heads, strided, left, right, grads, up_grads, weight, gain, units):
    _, tokens, _ = left.shape
    width = right.shape[0]
    seqs = 2 * chips
    part, wide = grads.shape[2:]
    return call(
        functools.partial(in_scatter_kernel, planes, chips, heads, strided),
        "in_scatter",
        [
            shape((tokens, width), F32),
            shape(weight.shape, F32),
            shape((part, 128), F32),
            shape((chips, width // 2, units), LOW),
        ],
        (left, right, grads, up_grads, weight, gain),
        [VMEM, VMEM, VMEM, HBM, VMEM, VMEM],
        [VMEM, VMEM, VMEM, HBM],
        [
            *PlaneScatter.scratch(chips, tokens, width),
            pltpu.VMEM((planes + 1, seqs, part, wide), LOW),
            *[pltpu.VMEM((seqs, part, wide), LOW)] * 2,
            *PlaneScatter.sems(chips, width),
            *pairs_of(2 * planes, 2 * planes, seqs, chips),
            pltpu.SemaphoreType.DMA((1,)),
        ],
        4,
    )


class PairScatter:
    PARTS = 2

    def __init__(self, planes, here, left, right, turned, buffers, near, up, down):
        self.planes, self.here = planes, here
        self.left, self.right, self.turned = left, right, turned
        self.near_out, self.own, slots = buffers
        self.near = near
        self.tokens, width = self.near_out.shape[1:]
        self.tiles = [pl.ds(at, COLUMNS) for at in range(0, width, COLUMNS)]
        size = width // self.PARTS

        def part(p):
            at = p * size if isinstance(p, int) else pl.multiple_of(p * size, 128)
            return (slice(None), pl.ds(at, size))

        self.line = LineScatter(
            planes,
            here,
            self.PARTS,
            part,
            lambda p: [(rows, part(p)[1]) for rows in row_tiles(self.tokens, 32)],
            lambda t, tile: self.own[(t, *tile)].astype(F32),
            slots,
            up,
            down,
        )

    def near_copy(self, i):
        z, c, core = self.here
        at = (slice(None), slice(None), self.tiles[i])
        return remote(self.near_out.at[at], self.own.at[at], self.near, i, (z, c, 1 - core))

    def start(self):
        core, tokens = self.here[2], self.tokens
        left = jnp.concatenate([self.left[t, 1 - core] for t in range(self.planes)], axis=0)
        for i, columns in enumerate(self.tiles):
            part = product(left, self.right, columns, self.turned).astype(LOW)
            for t in range(self.planes):
                self.near_out[t, :, columns] = part[t * tokens : (t + 1) * tokens]
            self.near_copy(i).start()
        left = jnp.concatenate([self.left[t, core] for t in range(self.planes)], axis=0)
        for i, columns in enumerate(self.tiles):
            part = product(left, self.right, columns, self.turned)
            self.near_copy(i).wait_recv()
            for t in range(self.planes):
                self.own[t, :, columns] = (
                    part[t * tokens : (t + 1) * tokens] + self.own[t, :, columns].astype(F32)
                ).astype(LOW)
        self.line.step(0)

    def finish(self, out_ref):
        def store(tile, total):
            out_ref[tile] = total

        self.line.finish(store)
        for i in range(len(self.tiles)):
            self.near_copy(i).wait_send()

    @staticmethod
    def scratch(planes, tokens, width):
        return [
            *[pltpu.VMEM((planes, tokens, width), LOW)] * 2,
            pltpu.VMEM((planes + 1, tokens, width), LOW),
        ]

    @classmethod
    def sems(cls, planes, width):
        return pairs_of(width // COLUMNS, cls.PARTS * planes, cls.PARTS * planes)


def feed_forward_kernel(
    planes, chips, width_ff, x_ref, up_ref, grads_ref, down_ref,
    out_ref, normed_ref, downs_ref, gup_ref, slots_ref,
    rows, ups, grads, downs, back, act, slope, stat, stat_out, stat_in,
    normed, d_up, near_out, own, sums, gup, gdown, *sems,
):
    here = place()
    z, c, core = here
    count = 2 * planes
    me = 2 * z + core
    up, down, near, chip_sems, stat_sems, pair, rise, fall, swap_sems = [
        sems[2 * i : 2 * i + 2] for i in range(9)
    ]
    local = sems[18]
    tokens, width = x_ref.shape
    units = ups.shape[1]
    load_up = pltpu.make_async_copy(up_ref, ups, local.at[0])
    load_grads = pltpu.make_async_copy(grads_ref, grads, local.at[1])
    load_up.start()
    load_grads.start()
    barrier = pltpu.get_barrier_semaphore()
    ids = [lax.rem(me + k, count) for k in range(1, count)]
    group_peers = [(index // 2, c, lax.rem(index, 2)) for index in ids]
    peers = [*group_peers, *chip_peers(chips, here)]
    greet(barrier, peers)
    pl.semaphore_wait(barrier, len(peers))

    group = GroupGather(planes, here, x_ref, rows, up, down, near)
    group.start(local.at[2])
    keep = pltpu.make_async_copy(down_ref, downs.at[c], local.at[3])
    keep.start()
    sends = [
        remote(down_ref, downs.at[c], chip_sems, k, device)
        for k, device in enumerate(chip_peers(chips, here), 1)
    ]
    for copy in sends:
        copy.start()
    load_up.wait()

    step = 16
    lane = lax.broadcasted_iota(jnp.int32, (step, 128), 1)

    def forward(t):
        group.other(t)
        block = rows[t].reshape(2 * tokens, width)
        for at in range(0, units, COLUMNS):
            columns = pl.ds(at, COLUMNS)
            act[t, :, columns] = jnp.dot(block, ups[:, columns], preferred_element_type=F32)

        def some(i, carry):
            at = pl.ds(pl.multiple_of(i * step, step), step)
            value = act[t, at]
            phi = 0.5 * (1.0 + lax.erf(value * math.sqrt(0.5)))
            result = value * phi
            act[t, at] = result
            slope[t, at] = phi + value * (
                jnp.exp(value * value * -0.5) * (1.0 / math.sqrt(2.0 * math.pi))
            )
            total = jnp.sum(result, axis=1, keepdims=True)
            square = jnp.sum(result * result, axis=1, keepdims=True)
            stat[t, at] = jnp.where(lane == 0, total, jnp.where(lane == 1, square, 0.0))
            return carry

        lax.fori_loop(0, 2 * tokens // step, some, 0)

    forward(z)
    for d in range(1, planes):
        group.step(d)
        if d > 1:
            pl.when(z - d + 1 >= 0)(lambda d=d: forward(z - d + 1))
            pl.when(z + d - 1 < planes)(lambda d=d: forward(z + d - 1))
    pl.when(z - planes + 1 >= 0)(lambda: forward(z - planes + 1))
    pl.when(z + planes - 1 < planes)(lambda: forward(z + planes - 1))
    group.finish()
    keep.wait()
    load_grads.wait()
    for k in range(1, chips):
        sends[k - 1].wait_send()
        other = lax.rem(c + chips - k, chips)
        remote(down_ref, downs.at[other], chip_sems, k, here).wait_recv()
    out_downs = pltpu.make_async_copy(downs, downs_ref, local.at[4])
    out_downs.start()

    def backward(t, carry):
        block = grads[t].reshape(2 * tokens, width)
        size = units // chips
        for chip in range(chips):
            columns = pl.ds(chip * size, size)
            back[t, :, columns] = rows_product(block, downs[chip])

        def some(i, inner):
            at = pl.ds(pl.multiple_of(i * step, step), step)
            value = back[t, at]
            cross = jnp.sum(value * act[t, at], axis=1, keepdims=True)
            total = jnp.sum(value, axis=1, keepdims=True)
            stat[t, at] = jnp.where(lane == 2, cross, jnp.where(lane == 3, total, stat[t, at]))
            return inner

        lax.fori_loop(0, 2 * tokens // step, some, 0)
        for half in range(2):
            turned = stat[t, pl.ds(half * tokens, tokens)].T
            stat_out[2 * t + half] = turned[:8]
        return carry

    lax.fori_loop(0, planes, backward, 0)
    copies = [
        remote(stat_out, stat_in.at[k], stat_sems, k, device)
        for k, device in enumerate(group_peers, 1)
    ]
    for copy in copies:
        copy.start()
    for copy in copies:
        copy.wait_send()
        copy.wait_recv()

    def finish(t, carry):
        for half in range(2):
            total = stat_out[2 * t + half]
            for k in range(1, count):
                total = total + stat_in[k, 2 * t + half]
            padded = jnp.concatenate([total, jnp.zeros((128 - 8, tokens), F32)], axis=0)
            stat[t, pl.ds(half * tokens, tokens)] = padded.T

        def some(i, inner):
            at = pl.ds(pl.multiple_of(i * step, step), step)
            figures = stat[t, at] * (1.0 / width_ff)
            mean, square, cross, first = (figures[:, j : j + 1] for j in range(4))
            scaler = lax.rsqrt(square - mean * mean + NORM_EPS)
            second = scaler * (cross - mean * first)
            unit = (act[t, at] - mean) * scaler
            normed[t, at] = unit.astype(LOW)
            d_act = scaler * (back[t, at] - first - unit * second)
            d_up[t, at] = (d_act * slope[t, at]).astype(LOW)
            return inner

        lax.fori_loop(0, 2 * tokens // step, some, 0)
        return carry

    lax.fori_loop(0, planes, finish, 0)
    out_normed = pltpu.make_async_copy(normed, normed_ref, local.at[5])
    out_normed.start()
    work = PairScatter(
        planes, here, Halves(d_up, tokens), ups, True, (near_out, own, sums), pair, rise, fall
    )
    work.start()

    flat_normed, flat_d_up = (
        whole[...].reshape(planes * 2 * tokens, units) for whole in (normed, d_up)
    )
    size = units // chips
    swap = ChipSwap(chips, here, lambda index: gdown.at[index], slots_ref, swap_sems)
    turns_left = list(range(1, work.line.steps))

    def turn():
        if turns_left:
            work.line.step(turns_left.pop(0))

    together = max(1, 256 // size)
    for chip in range(0, chips, together):
        left = flat_normed[:, chip * size : (chip + together) * size]
        for at in range(0, width, COLUMNS):
            columns = pl.ds(at, COLUMNS)
            right = grads[:, :, :, columns].reshape(planes * 2 * tokens, COLUMNS)
            term = token_product(left, right).astype(LOW)
            for i in range(together):
                gdown[chip + i, :, columns] = term[i * size : (i + 1) * size]
        if chip // together % 2:
            turn()
    swap.start(local.at[6])
    chunk = gup.shape[1]
    out_gups = [
        pltpu.make_async_copy(
            gup.at[i % 2], gup_ref.at[pl.ds(i * chunk, chunk)], local.at[7 + i % 2]
        )
        for i in range(width // chunk)
    ]
    for i in range(width // chunk):
        if i % 2 == 0:
            turn()
        left = rows[:, :, :, pl.ds(i * chunk, chunk)].reshape(planes * 2 * tokens, chunk)
        term = token_product(left, flat_d_up).astype(LOW)
        if i > 1:
            out_gups[i - 2].wait()
        gup[i % 2] = term
        out_gups[i].start()
    while turns_left:
        turn()
    work.finish(out_ref)
    swap.finish()
    out_downs.wait()
    out_normed.wait()
    for copy in out_gups[-2:]:
        copy.wait()


class Halves:
    def __init__(self, whole, tokens):
        self.whole, self.tokens = whole, tokens

    def __getitem__(self, at):
        t, core = at
        rows = pl.ds(pl.multiple_of(core * self.tokens, self.tokens), self.tokens)
        return self.whole[t, rows]


def feed_forward(planes, chips, width_ff, x_block, up_mine, grads, down_block):
    tokens, width = x_block.shape
    units = up_mine.shape[1]
    size = down_block.shape[0]
    wide = (planes, 2 * tokens, units)
    return call(
        functools.partial(feed_forward_kernel, planes, chips, width_ff),
        "feed_forward",
        [
            shape((tokens, width), F32),
            shape(wide, LOW),
            shape((chips, size, width), LOW),
            shape((width, units), LOW),
            shape((chips, size, width), LOW),
        ],
        (x_block, up_mine, grads, down_block),
        [HBM] * 4,
        [VMEM, HBM, HBM, HBM, HBM],
        [
            pltpu.VMEM((planes, 2, tokens, width), LOW),
            pltpu.VMEM((width, units), LOW),
            pltpu.VMEM((planes, 2, tokens, width), LOW),
            pltpu.VMEM((chips, size, width), LOW),
            *[pltpu.VMEM(wide, F32)] * 3,
            pltpu.VMEM((planes, 2 * tokens, 128), F32),
            pltpu.VMEM((2 * planes, 8, 128), F32),
            pltpu.VMEM((2 * planes, 2 * planes, 8, 128), F32),
            *[pltpu.VMEM(wide, LOW)] * 2,
            *PairScatter.scratch(planes, tokens, width),
            pltpu.VMEM((2, 256, units), LOW),
            pltpu.VMEM((chips, size, width), LOW),
            *GroupGather.sems(planes),
            *pairs_of(chips, 2 * planes),
            *PairScatter.sems(planes, width),
            *pairs_of(chips),
            pltpu.SemaphoreType.DMA((9,)),
        ],
        7,
    )


def plane_gather_kernel(
    planes, chips, x_ref, stat_ref, tile_ref, left_ref, right_ref,
    row_ref, stats_ref, tiles_ref, ffn_ref,
    near_out, own, sums, *sems,
):
    here = place()
    z, c, core = here
    seqs = 2 * chips
    count = planes * seqs
    me = 2 * c + core
    flat = z * seqs + me
    x_far, x_near, s_far, s_near, tile_sems, near, up, down = [
        sems[2 * i : 2 * i + 2] for i in range(8)
    ]
    local = sems[16]
    barrier = pltpu.get_barrier_semaphore()

    def device_of(k):
        other = lax.rem(flat + k, count)
        return (other // seqs, lax.rem(other, seqs) // 2, lax.rem(other, 2))

    def signal(k, carry):
        greet(barrier, [device_of(k)])
        return carry

    lax.fori_loop(1, count, signal, 0)
    pl.semaphore_wait(barrier, count - 1)
    rows = PlaneGather(chips, here, x_ref, row_ref, x_far, x_near)
    stats = PlaneGather(chips, here, stat_ref, stats_ref, s_far, s_near)
    rows.start()
    stats.start()
    keeps = [
        pltpu.make_async_copy(x_ref, row_ref.at[me], local.at[0]),
        pltpu.make_async_copy(stat_ref, stats_ref.at[me], local.at[1]),
        pltpu.make_async_copy(tile_ref.at[flat], tiles_ref.at[flat], local.at[2]),
    ]
    for copy in keeps:
        copy.start()

    def tile_copy(k):
        other = lax.rem(flat + k, count)
        return remote(tile_ref.at[other], tiles_ref.at[flat], tile_sems, k, device_of(k))

    def tile_start(k, carry):
        tile_copy(k).start()
        return carry

    lax.fori_loop(1, count, tile_start, 0)
    work = PairScatter(
        planes, here, Halves(left_ref, x_ref.shape[0]), right_ref, False, (near_out, own, sums),
        near, up, down,
    )
    work.start()
    for i in range(1, work.line.steps):
        if i == work.line.steps // 2:
            rows.forward()
            stats.forward()
        work.line.step(i)
    rows.finish()
    stats.finish()
    work.finish(ffn_ref)
    for copy in keeps:
        copy.wait()

    def tile_wait(k, carry):
        tile_copy(k).wait_send()
        other = lax.rem(flat + count - k, count)
        remote(tile_ref.at[0], tiles_ref.at[other], tile_sems, k, here).wait_recv()
        return carry

    lax.fori_loop(1, count, tile_wait, 0)


def plane_gather(planes, chips, x_block, stats, tiles, left, right):
    seqs = 2 * chips
    tokens, width = x_block.shape
    return call(
        functools.partial(plane_gather_kernel, planes, chips),
        "plane_gather",
        [
            shape((seqs, *x_block.shape), x_block.dtype),
            shape((seqs, *stats.shape), stats.dtype),
            shape(tiles.shape, tiles.dtype),
            shape((tokens, width), F32),
        ],
        (x_block, stats, tiles, left, right),
        [HBM, HBM, HBM, VMEM, VMEM],
        [HBM, HBM, HBM, VMEM],
        [
            *PairScatter.scratch(planes, tokens, width),
            *pairs_of(chips, chips, chips, chips, planes * seqs),
            *PairScatter.sems(planes, width),
            pltpu.SemaphoreType.DMA((3,)),
        ],
        2,
    )


def swap_lanes(values):
    lane = lax.broadcasted_iota(jnp.int32, values.shape, 1)
    return jnp.where(
        lax.rem(lane, 2) == 0,
        pltpu.roll(values, values.shape[1] - 1, 1),
        pltpu.roll(values, 1, 1),
    )


def twice(table):
    return jnp.concatenate([table, table], axis=1)


def turns(meta_ref, rows):
    cosine, sine, shrink = [twice(meta_ref[rows, pl.ds(i * HD, HD)]) for i in range(3)]
    return (cosine, sine, cosine * shrink, sine * shrink)


def allowed_block(meta_ref, rows, size, columns):
    query = rows + lax.broadcasted_iota(jnp.int32, (size, columns), 0)
    key = lax.broadcasted_iota(jnp.int32, (size, columns), 1)
    offset = meta_ref[pl.ds(rows, size), pl.ds(3 * HD, 1)].astype(jnp.int32)
    return (key <= query) & (key >= query - offset)


BLOCK = 256


def attention_forward_kernel(
    planes, chips, heads, strided,
    x_ref, meta_ref, qkv_ref, out_ref, gain_ref, up_ref, grad_ref,
    q_ref, k_ref, v_ref, att_ref, log_ref, sum_ref,
    rows_ref, metas_ref, qkvs_ref, outs_ref, gains_ref, ups_ref, grads_ref, tiles_ref,
    rows, metas, qkvs, outs, raw, wide, tile, near_out, near_in, far_out, far_in,
    *sems,
):
    here = place()
    z, c, core = here
    seqs = 2 * chips
    count = planes * seqs
    me = 2 * c + core
    flat = z * seqs + me
    groups = [sems[2 * i : 2 * i + 2] for i in range(17)]
    swap_sems, x_far, x_near, meta_far, meta_near, up, down, up_two, down_two = groups[:9]
    gain_sems, up_sems, near, far, tile_sems, grad_up, grad_down, pair = groups[9:]
    local = sems[34]
    tokens, width = x_ref.shape
    part, three = qkv_ref.shape[1:]
    length = seqs * tokens
    span = heads * HD
    barrier = pltpu.get_barrier_semaphore()

    def device_of(k):
        other = lax.rem(flat + k, count)
        return (other // seqs, lax.rem(other, seqs) // 2, lax.rem(other, 2))

    def signal(k, carry):
        greet(barrier, [device_of(k)])
        return carry

    lax.fori_loop(1, count, signal, 0)
    pl.semaphore_wait(barrier, count - 1)

    mine = pltpu.make_async_copy(qkv_ref.at[me], qkvs.at[z, me], local.at[0])
    own_out = pltpu.make_async_copy(out_ref, outs.at[z] if strided else outs, local.at[1])
    units = up_ref.shape[1]
    keeps = [
        pltpu.make_async_copy(x_ref, rows.at[me], local.at[2]),
        pltpu.make_async_copy(meta_ref, metas.at[me], local.at[3]),
        pltpu.make_async_copy(gain_ref, gains_ref.at[flat], local.at[4]),
        pltpu.make_async_copy(up_ref, column_block(ups_ref, units, c), local.at[5]),
    ]
    peers = plane_peers(chips, here)
    swaps = [
        remote(qkv_ref.at[2 * device[1] + device[2]], qkvs.at[z, me], swap_sems, k, device)
        for k, device in enumerate(peers, 1)
    ]
    mine.start()
    own_out.start()
    for copy in swaps:
        copy.start()
    gather = PlaneGather(chips, here, x_ref, rows, x_far, x_near)
    meta_gather = PlaneGather(chips, here, meta_ref, metas, meta_far, meta_near)
    gather.start()
    meta_gather.start()
    for copy in keeps:
        copy.start()

    def gain_copy(k):
        return remote(gain_ref, gains_ref.at[flat], gain_sems, k, device_of(k))

    def gain_start(k, carry):
        gain_copy(k).start()
        return carry

    lax.fori_loop(1, count, gain_start, 0)
    mine.wait()
    own_out.wait()
    for k in range(1, seqs):
        index = lax.rem(me + seqs - k, seqs)
        remote(qkv_ref.at[0], qkvs.at[z, index], swap_sems, k, here).wait_recv()
    half = seqs // 2
    line = LineGather(
        planes, here, lambda t: [qkvs.at[t, pl.ds(i * half, half)] for i in range(2)], up, down
    )
    line_two = LineGather(planes, here, lambda t: [outs.at[t]], up_two, down_two)
    line.start()
    gather.forward()
    meta_gather.forward()
    ups = [
        remote(up_ref, column_block(ups_ref, units, c), up_sems, k, device)
        for k, device in enumerate(chip_peers(chips, here), 1)
    ]
    for copy in ups:
        copy.start()
    gather.finish()
    meta_gather.finish()
    for copy in keeps:
        copy.wait()

    block = seqs * part

    def add(t, fresh=False):
        columns = pl.ds(pl.multiple_of(t * block, 128), block)
        left = rows[:, :, columns].reshape(length, block)
        for i in range(3):
            at = pl.ds(i * span, span)
            term = jnp.dot(left, qkvs[t, :, :, at].reshape(block, span), preferred_element_type=F32)
            raw[:, at] = term if fresh else raw[:, at] + term

    add(z, True)
    for d in range(1, planes):
        line.step(d)
        if d == planes - 1:
            if strided:
                line_two.start()
            group = GroupGather(planes, here, grad_ref, grads_ref, grad_up, grad_down, pair)
            group.start(local.at[6])
        pl.when(z - d >= 0)(lambda d=d: add(z - d))
        pl.when(z + d < planes)(lambda d=d: add(z + d))
    outputs = [
        pltpu.make_async_copy(rows, rows_ref, local.at[7]),
        pltpu.make_async_copy(metas, metas_ref, local.at[8]),
        pltpu.make_async_copy(qkvs, qkvs_ref, local.at[9]),
    ]
    for copy in outputs:
        copy.start()

    table = RowBlocks(metas)
    for at in range(0, length, BLOCK):
        at = pl.ds(at, BLOCK)
        tables = turns(table, at)
        for two in range(heads // 2):
            query = raw[at, pl.ds(2 * HD * two, 2 * HD)]
            query = (query * tables[0] + swap_lanes(query) * tables[1]).astype(LOW)
            key = raw[at, pl.ds(span + 2 * HD * two, 2 * HD)]
            key = (key * tables[2] + swap_lanes(key) * tables[3]).astype(LOW)
            value = raw[at, pl.ds(2 * span + 2 * HD * two, 2 * HD)].astype(LOW)
            for side in range(2):
                lanes = slice(side * HD, (side + 1) * HD)
                q_ref[2 * two + side, at] = query[:, lanes]
                k_ref[2 * two + side, at] = key[:, lanes]
                v_ref[2 * two + side, at] = value[:, lanes]
    log_ref[...] = jnp.zeros(log_ref.shape, F32)

    def one_head(head, carry):
        for start in range(0, length, BLOCK):
            columns = start + BLOCK
            at = pl.ds(start, BLOCK)
            scores = lax.dot_general(
                q_ref[head, at],
                k_ref[head, pl.ds(0, columns)],
                (((1,), (1,)), ((), ())),
                preferred_element_type=F32,
            )
            allowed = allowed_block(table, start, BLOCK, columns)
            scores = jnp.where(allowed, scores, NEG_FILL)
            top = jnp.max(scores, axis=1, keepdims=True)
            shifted = jnp.exp(scores - top)
            total = jnp.sum(shifted, axis=1, keepdims=True)
            probs = (shifted * (1.0 / total)).astype(LOW)
            wide[head, at] = jnp.dot(
                probs, v_ref[head, pl.ds(0, columns)], preferred_element_type=F32
            )
            lane = lax.broadcasted_iota(jnp.int32, (BLOCK, 128), 1)
            log_ref[at] = jnp.where(lane == head, top + jnp.log(total), log_ref[at])
        return carry

    first = 0
    for d in range(1, planes):
        last = -(-heads * d // planes)
        lax.fori_loop(first, last, one_head, 0)
        first = last
        if strided:
            line_two.step(d)
        if d == 1:
            group.step(d)
    lax.fori_loop(first, heads, one_head, 0)
    lane = lax.broadcasted_iota(jnp.int32, (tokens, 128), 1)
    column = jnp.sum(outs[...].astype(F32).reshape(span, width), axis=0, keepdims=True)
    for s in range(seqs):
        at = pl.ds(s * tokens, tokens)
        low = jnp.concatenate([wide[head, at] for head in range(heads)], axis=1).astype(LOW)
        att_ref[s] = low
        value = low.astype(F32)
        total = jnp.sum(value, axis=1, keepdims=True)
        square = jnp.sum(value * value, axis=1, keepdims=True)
        both = jnp.where(lane == 0, total, jnp.where(lane == 1, square, 0.0))
        tile[s, pl.ds(0, 8)] = both.T[:8]
        for i in range(width // 128):
            tile[s, pl.ds(8 + i, 1)] = column[:, i * 128 : (i + 1) * 128]
    out_tiles = [
        remote(tile.at[2 * device[1] + device[2]], tiles_ref.at[me], tile_sems, k, device)
        for k, device in enumerate(peers, 1)
    ]
    for copy in out_tiles:
        copy.start()
    keep = pltpu.make_async_copy(tile.at[me], tiles_ref.at[me], local.at[10])
    keep.start()
    out_outs = pltpu.make_async_copy(outs, outs_ref, local.at[11])
    out_outs.start()
    work = PlaneScatter(
        chips, here, att_ref, Flat(outs, span), False, (near_out, near_in, far_out, far_in), near, far
    )
    work.start()
    for d in range(2, planes):
        group.step(d)
    work.finish(sum_ref)
    group.finish()
    for t in range(planes):
        group.other(t)
    line.finish()
    if strided:
        line_two.finish()
    for copy in [*swaps, *ups]:
        copy.wait_send()
    for k in range(1, chips):
        other = lax.rem(c + chips - k, chips)
        remote(up_ref, column_block(ups_ref, units, other), up_sems, k, here).wait_recv()
    for copy in [keep, out_outs, *outputs]:
        copy.wait()
    for k in range(1, seqs):
        out_tiles[k - 1].wait_send()
        index = lax.rem(me + seqs - k, seqs)
        remote(tile.at[0], tiles_ref.at[index], tile_sems, k, here).wait_recv()

    def gain_wait(k, carry):
        gain_copy(k).wait_send()
        other = lax.rem(flat + count - k, count)
        remote(gain_ref, gains_ref.at[other], gain_sems, k, here).wait_recv()
        return carry

    lax.fori_loop(1, count, gain_wait, 0)


class Flat:
    def __init__(self, blocks, count):
        self.blocks, self.count = blocks, count

    def __getitem__(self, at):
        if len(self.blocks.shape) == 2:
            return self.blocks[at]
        _, columns = at
        return self.blocks[:, :, columns].reshape(self.count, columns.size)


class RowBlocks:
    def __init__(self, blocks):
        self.blocks = blocks

    def __getitem__(self, at):
        rows, columns = at
        size = self.blocks.shape[1]
        first, count = rows.start // size, rows.size // size
        return self.blocks[pl.ds(first, count), :, columns].reshape(rows.size, columns.size)


def attention_forward(
    planes, chips, heads, strided, x_block, meta, qkv_blocks, out_rows, gain_tile, up_block, grad
):
    seqs = 2 * chips
    tokens, width = x_block.shape
    part, wide = qkv_blocks.shape[1:]
    units = up_block.shape[1]
    length = seqs * tokens
    span = heads * HD
    outs = (planes, *out_rows.shape) if strided else out_rows.shape
    tile = (seqs, 8 + width // 128, 128)
    return call(
        functools.partial(attention_forward_kernel, planes, chips, heads, strided),
        "attention_forward",
        [
            *[shape((heads, length, HD), LOW)] * 3,
            shape((seqs, tokens, span), LOW),
            shape((length, 128), F32),
            shape((tokens, width), F32),
            shape((seqs, tokens, width), LOW),
            shape((seqs, *meta.shape), F32),
            shape((planes, seqs, part, wide), LOW),
            shape(outs, LOW),
            shape((planes * seqs, *gain_tile.shape), F32),
            shape((width, chips * units) if units % 128 == 0 else (chips, width, units), LOW),
            shape((planes, 2, *grad.shape), LOW),
            shape(tile, F32),
        ],
        (x_block, meta, qkv_blocks, out_rows, gain_tile, up_block, grad),
        [HBM] * 7,
        [*[VMEM] * 6, *[HBM] * 8],
        [
            pltpu.VMEM((seqs, tokens, width), LOW),
            pltpu.VMEM((seqs, *meta.shape), F32),
            pltpu.VMEM((planes, seqs, part, wide), LOW),
            pltpu.VMEM(outs, LOW),
            pltpu.VMEM((length, 3 * span), F32),
            pltpu.VMEM((heads, length, HD), F32),
            pltpu.VMEM(tile, F32),
            *PlaneScatter.scratch(chips, tokens, width),
            *pairs_of(
                seqs, *[chips] * 4, *[2 * planes] * 2, *[planes] * 2, planes * seqs, chips
            ),
            *PlaneScatter.sems(chips, width),
            *pairs_of(seqs),
            *GroupGather.sems(planes),
            pltpu.SemaphoreType.DMA((12,)),
        ],
        1,
    )


def attention_back_kernel(
    planes, chips, heads, strided,
    q_ref, k_ref, v_ref, att_ref, row_ref, right_ref, stat_ref, log_ref, meta_ref, up_ref,
    out_ref, total_ref, slots_ref,
    grad, dq, dk, dv, normed_all, own, sums, *sems,
):
    here = place()
    up, down, swap_sems = [sems[2 * i : 2 * i + 2] for i in range(3)]
    barrier = pltpu.get_barrier_semaphore()
    greet(barrier, chip_peers(chips, here))
    greet_line(barrier, planes, here)
    pl.semaphore_wait(barrier, chips - 1 + line_peers(planes, here))
    swap = ChipSwap(
        chips, here, lambda index: half_block(up_ref, slots_ref, index, 0), slots_ref, swap_sems
    )
    swap.start(sems[6].at[0])
    length, span = att_ref.shape
    part, width = own.shape[1:]
    for rows in row_tiles(length, BLOCK):
        mean, scaler, first, second = (stat_ref[rows, pl.ds(i, 1)] for i in range(4))
        d_sub = product(row_ref[rows], right_ref, slice(None), True)
        normed = (att_ref[rows].astype(F32) - mean) * scaler
        normed_all[rows] = normed.astype(LOW)
        d_att = (scaler * (d_sub - first - normed * second)).astype(LOW)
        for head in range(heads):
            grad[head, rows] = d_att[:, head * HD : (head + 1) * HD]
    for at in range(0, width, COLUMNS):
        columns = pl.ds(at, COLUMNS)
        term = token_product(normed_all[...], row_ref[:, columns]).astype(LOW)
        for t in range(planes):
            own[t, :, columns] = term[t * part : (t + 1) * part]
    line = LineScatter(
        planes,
        here,
        1,
        lambda p: (slice(None),),
        lambda p: [(rows,) for rows in row_tiles(part, 16)],
        lambda t, tile: own[(t, *tile)].astype(F32),
        sums,
        up,
        down,
    )
    if strided:
        line.step(0)
    dk[...] = jnp.zeros(dk.shape, F32)
    dv[...] = jnp.zeros(dv.shape, F32)

    def one_head(head, carry):
        for start in range(0, length, BLOCK):
            columns = start + BLOCK
            rows = pl.ds(start, BLOCK)
            keys = pl.ds(0, columns)
            query, key = q_ref[head, rows], k_ref[head, keys]
            out_grad = grad[head, rows]
            scores = lax.dot_general(
                query, key, (((1,), (1,)), ((), ())), preferred_element_type=F32
            )
            allowed = allowed_block(meta_ref, start, BLOCK, columns)
            lane = lax.broadcasted_iota(jnp.int32, (BLOCK, 128), 1)
            log_total = jnp.sum(
                jnp.where(lane == head, log_ref[rows], 0.0), axis=1, keepdims=True
            )
            probs = jnp.where(allowed, jnp.exp(scores - log_total), 0.0)
            d_probs = lax.dot_general(
                out_grad, v_ref[head, keys], (((1,), (1,)), ((), ())), preferred_element_type=F32
            )
            delta = jnp.sum(probs * d_probs, axis=1, keepdims=True)
            d_scores = (probs * (d_probs - delta)).astype(LOW)
            dq[head, rows] = jnp.dot(d_scores, key, preferred_element_type=F32)
            dk[head, keys] += token_product(d_scores, query)
            dv[head, keys] += token_product(probs.astype(LOW), out_grad)
        return carry

    first = 0
    for i in range(1, planes - 1):
        last = -(-heads * i // (planes - 1))
        lax.fori_loop(first, last, one_head, 0)
        first = last
        if strided:
            line.step(i)
    lax.fori_loop(first, heads, one_head, 0)
    for rows in row_tiles(length, BLOCK):
        tables = turns(meta_ref, rows)
        for pair in range(heads // 2):
            both = [
                jnp.concatenate(
                    [whole[2 * pair, rows], whole[2 * pair + 1, rows]], axis=1
                ).astype(LOW)
                for whole in (dq, dk, dv)
            ]
            query, key = both[0].astype(F32), both[1].astype(F32)
            query = query * tables[0] + swap_lanes(query * tables[1])
            key = key * tables[2] + swap_lanes(key * tables[3])
            out_ref[rows, pl.ds(2 * HD * pair, 2 * HD)] = query.astype(LOW)
            out_ref[rows, pl.ds(span + 2 * HD * pair, 2 * HD)] = key.astype(LOW)
            out_ref[rows, pl.ds(2 * span + 2 * HD * pair, 2 * HD)] = both[2]
    if strided:

        def store(tile, total):
            total_ref[tile] = total

        line.finish(store)
    else:
        for t in range(planes):
            total_ref[pl.ds(t * part, part)] = own[t].astype(F32)
    swap.finish()


def attention_back(planes, chips, heads, strided, part, units, args):
    length, span = args[3].shape
    width = args[4].shape[1]
    return call(
        functools.partial(attention_back_kernel, planes, chips, heads, strided),
        "attention_back",
        [
            shape((length, 3 * span), LOW),
            shape((part if strided else span, width), F32),
            shape((chips, width // 2, units), LOW),
        ],
        args,
        [*[VMEM] * 9, HBM],
        [*[VMEM] * 2, HBM],
        [
            pltpu.VMEM((heads, length, HD), LOW),
            *[pltpu.VMEM((heads, length, HD), F32)] * 3,
            pltpu.VMEM((length, span), LOW),
            pltpu.VMEM((planes, part, width), LOW),
            pltpu.VMEM((planes + 1, part, width), LOW),
            *pairs_of(planes, planes, chips),
            pltpu.SemaphoreType.DMA((1,)),
        ],
        8,
    )


def body(
    hidden_in,
    segment_ids,
    position_ids,
    w_qkv,
    w_out,
    w_up,
    w_down,
    gain_attn,
    gain_attn_sub,
    gain_ffn,
    gain_ffn_sub,
    ema_qkv,
    ema_out,
    ema_up,
    ema_down,
    ema_gain_attn,
    ema_gain_attn_sub,
    ema_gain_ffn,
    ema_gain_ffn_sub,
    out_grad,
):
    _, tokens, width = hidden_in.shape
    planes, chips = lax.axis_size("dp"), lax.axis_size("chip")
    seqs = 2 * chips
    length = tokens * seqs
    heads = HEADS // seqs
    span = heads * HD
    part = w_qkv.shape[0]
    strided = part % HD == 0
    width_ff = w_down.shape[0] * planes * seqs
    seq_index = lax.axis_index(SEQ)

    def gain_rows(weight, gain):
        return (weight.astype(F32) * gain.astype(F32)[:, None]).astype(LOW)

    qkv_scaled = gain_rows(w_qkv, gain_attn)
    out_scaled = gain_rows(w_out, gain_attn_sub)
    down_scaled = gain_rows(w_down, gain_ffn_sub)
    if strided:
        qkv_send = qkv_scaled.reshape(part, 3, planes, seqs, HD).transpose(3, 0, 1, 2, 4)
    else:
        qkv_send = qkv_scaled.reshape(part, 3, seqs, span).transpose(2, 0, 1, 3)
    qkv_send = qkv_send.reshape(seqs, part, 3 * span)
    x_in = hidden_in[0].astype(F32)
    normed_one, scaler_one = moments(x_in)
    normed_low = normed_one.astype(LOW)
    gain_tile = jnp.zeros((8, 128), F32).at[0, :part].set(gain_ffn.astype(F32))

    if not strided:
        out_all = lax.all_gather(out_scaled, ALL, axis=0, tiled=True)
        out_scaled = lax.dynamic_slice_in_dim(out_all, seq_index * span, span, axis=0)

    grad_low = out_grad[0]
    (
        queries, keys, values, attended, log_total, out_sum,
        row_in, meta, qkv_mine, out_mine, gain_tiles, up_mine, grad_flat, tiles,
    ) = attention_forward(
        planes,
        chips,
        heads,
        strided,
        normed_low,
        token_tables(position_ids[0]),
        qkv_send,
        out_scaled,
        gain_tile,
        w_up,
        grad_low,
    )
    if up_mine.ndim == 3:
        up_mine = up_mine.transpose(1, 0, 2).reshape(width, -1)
    row_in = row_in.reshape(length, width)
    meta = meta.reshape(length, -1)
    qkv_mine = qkv_mine.reshape(width, 3 * span)
    out_mine = out_mine.reshape(span, width)
    attended = attended.reshape(length, span)
    tiles = jnp.sum(tiles, axis=0)
    column_sum = tiles[8:].reshape(width)
    sums = tiles[:2].T
    gain_three = gain_tiles[:, 0, :part].reshape(width)
    mean_two = sums[:, :1] / width
    scaler_two = lax.rsqrt(sums[:, 1:] / width - mean_two * mean_two + NORM_EPS)
    projected = scaler_two * (out_sum - mean_two * column_sum[None, :])
    hmid = x_in + projected
    normed_three, scaler_three = moments(hmid)
    ffn_in = (normed_three * gain_three).astype(LOW)

    grad_top = grad_low.astype(F32)
    units = w_up.shape[1]
    d_ffn_in, normed_four, down_mine, grad_up, down_slots = feed_forward(
        planes, chips, width_ff, ffn_in, up_mine, grad_flat, down_scaled
    )
    down_mine = down_mine.reshape(-1, width)
    if units % 128:
        grad_up = grad_up.reshape(width, chips, units).transpose(1, 0, 2)

    gain_part = jnp.sum(d_ffn_in * normed_three, axis=0).reshape(planes * seqs, 1, part)
    gain_part = jnp.pad(gain_part, ((0, 0), (0, 7), (0, 128 - part)))
    d_hmid = grad_top + norm_back(d_ffn_in * gain_three, normed_three, scaler_three)
    d_hmid_low = d_hmid.astype(LOW)
    d_hmid_wide = d_hmid_low.astype(F32)
    first_two = jnp.sum(d_hmid_wide * column_sum[None, :], axis=1, keepdims=True) / width
    second_two = jnp.sum(d_hmid_wide * projected, axis=1, keepdims=True) / width
    token_stats = jnp.concatenate([mean_two, scaler_two, first_two, second_two], axis=1)
    row_grad, row_stats, gain_part, ffn_out = plane_gather(
        planes,
        chips,
        d_hmid_low,
        jnp.pad(token_stats, ((0, 0), (0, 124))),
        gain_part,
        normed_four,
        down_mine,
    )
    output = (hmid + ffn_out).astype(LOW)[None]
    row_grad = row_grad.reshape(length, width)
    row_stats = row_stats.reshape(length, 128)
    grad_gain_three = jnp.sum(gain_part, axis=0)[0, :part]
    d_qkv, sum_out, upper_slots = attention_back(
        planes,
        chips,
        heads,
        strided,
        part,
        units,
        (queries, keys, values, attended, row_grad, out_mine, row_stats, log_total, meta, grad_up),
    )
    grad_qkv = token_product(row_in, d_qkv).astype(LOW)
    d_in, sum_qkv, grad_gain_one, lower_slots = in_scatter(
        planes,
        chips,
        heads,
        strided,
        d_qkv.reshape(seqs, tokens, 3 * span),
        qkv_mine,
        grad_qkv.reshape(planes, seqs, part, 3 * span),
        grad_up,
        w_qkv,
        jnp.broadcast_to(gain_attn.astype(F32)[:, None], (part, 128)),
        units,
    )
    grad_gain_one = grad_gain_one[:, 0]
    sum_up = jnp.concatenate(
        [jnp.sum(slots.astype(F32), axis=0) for slots in (upper_slots, lower_slots)], axis=0
    )
    sum_down = jnp.sum(down_slots.astype(F32), axis=0)
    input_grad = (d_hmid + norm_back(d_in, normed_one, scaler_one)).astype(LOW)[None]

    if not strided:
        spread = lax.dynamic_update_slice_in_dim(
            jnp.zeros((width, width), LOW), sum_out.astype(LOW), seq_index * span, axis=0
        )
        sum_out = lax.psum_scatter(spread, ALL, scatter_dimension=0, tiled=True).astype(F32)

    def finish(total, weight, gain):
        wide = weight.astype(F32)
        return (total * gain.astype(F32)[:, None], jnp.sum(total * wide, axis=1))

    sum_out, grad_gain_two = finish(sum_out, w_out, gain_attn_sub)
    sum_down, grad_gain_four = finish(sum_down, w_down, gain_ffn_sub)

    def averaged(average, weight):
        return EMA_DECAY * average + (1.0 - EMA_DECAY) * weight.astype(F32)

    return (
        output,
        input_grad,
        sum_qkv,
        sum_out,
        sum_up,
        sum_down,
        grad_gain_one,
        grad_gain_two,
        grad_gain_three,
        grad_gain_four,
        averaged(ema_qkv, w_qkv),
        averaged(ema_out, w_out),
        averaged(ema_up, w_up),
        averaged(ema_down, w_down),
        averaged(ema_gain_attn, gain_attn),
        averaged(ema_gain_attn_sub, gain_attn_sub),
        averaged(ema_gain_ffn, gain_ffn),
        averaged(ema_gain_ffn_sub, gain_ffn_sub),
    )


def solution(mesh):
    split = Mesh(
        mesh.devices.reshape(mesh.shape["dp"], mesh.shape["seq"] // 2, 2), ("dp", "chip", "core")
    )
    tokens = P("dp", SEQ, None)
    ids = P("dp", SEQ)
    rows = P(ALL, None)
    columns = P(None, ALL)
    vector = P(ALL)
    weights = (rows, rows, columns, rows)
    gains = (vector,) * 4
    return jax.shard_map(
        body,
        mesh=split,
        in_specs=(tokens, ids, ids, *weights, *gains, *weights, *gains, tokens),
        out_specs=(tokens, tokens, *weights, *gains, *weights, *gains),
        check_vma=False,
    )
```

```python
import functools
import math

import jax
import jax.numpy as jnp
from jax import lax
from jax.experimental import pallas as pl
from jax.experimental.pallas import tpu as pltpu
from jax.sharding import Mesh
from jax.sharding import PartitionSpec as P

HEADS = 32
HD = 64

NEG_FILL = -1000000000.0
NORM_EPS = 1e-05
EMA_DECAY = 0.7
LOW = jnp.bfloat16
F32 = jnp.float32
SEQ = ("chip", "core")
TP = ("dp", "core")
ALL = ("dp", "chip", "core")


def moments(values):
    mean = jnp.mean(values, axis=-1, keepdims=True)
    centered = values - mean
    scaler = lax.rsqrt(jnp.mean(centered * centered, axis=-1, keepdims=True) + NORM_EPS)
    return (centered * scaler, scaler)


def norm_back(scaled_grad, normed, scaler):
    first_mean = jnp.mean(scaled_grad, axis=-1, keepdims=True)
    second_mean = jnp.mean(scaled_grad * normed, axis=-1, keepdims=True)
    return scaler * (scaled_grad - first_mean - normed * second_mean)


def token_tables(positions):
    half_count = HD // 2
    index_half = jnp.arange(half_count).astype(F32)
    inverse = jnp.exp(-(2.0 * index_half / HD) * math.log(10000.0))
    decay_base = (2.0 * index_half + 0.4 * HD) / (1.4 * HD)
    where_at = positions.astype(F32)[:, None]
    angles = where_at * inverse[None, :]
    factor = jnp.exp(where_at / 512.0 * jnp.log(decay_base)[None, :])
    sign_row = jnp.where(jnp.arange(HD) % 2 == 0, -1.0, 1.0).astype(F32)
    cosine = jnp.repeat(jnp.cos(angles), 2, axis=1)
    sine = jnp.repeat(jnp.sin(angles), 2, axis=1) * sign_row[None, :]
    factor = jnp.repeat(factor, 2, axis=1)
    grow = factor * HD ** (-0.5)
    where_block = jnp.broadcast_to(where_at, (positions.shape[0], HD))
    return jnp.concatenate(
        [cosine * grow, sine * grow, HD**0.5 / (factor * factor), where_block], axis=1
    )


def dot(left_op, right_op):
    return jnp.dot(left_op, right_op, preferred_element_type=F32)


def rows_product(operand, weight_rows):
    return lax.dot_general(
        operand, weight_rows, (((1,), (1,)), ((), ())), preferred_element_type=F32
    )


def token_product(left_op, right_op):
    return lax.dot_general(left_op, right_op, (((0,), (0,)), ((), ())), preferred_element_type=F32)


MESH = pl.DeviceIdType.MESH
HBM = pl.BlockSpec(memory_space=pl.ANY)
VMEM = pl.BlockSpec(memory_space=pltpu.VMEM)
VMEM_BYTES = 60 * 1024 * 1024


def shape(dims, kind):
    return jax.ShapeDtypeStruct(dims, kind)


def pairs_of(*counts):
    return [pltpu.SemaphoreType.DMA((count,)) for count in counts for _ in range(2)]


def call(kernel, name, outs, args, in_specs, out_specs, scratch, collective=None):
    return pl.pallas_call(
        kernel,
        name=name,
        out_shape=outs,
        in_specs=in_specs,
        out_specs=out_specs,
        scratch_shapes=scratch,
        compiler_params=pltpu.CompilerParams(
            collective_id=collective,
            has_side_effects=collective is not None,
            vmem_limit_bytes=VMEM_BYTES,
        ),
    )(*args)


def place():
    return (lax.axis_index("dp"), lax.axis_index("chip"), lax.axis_index("core"))


def remote(source, target, sems, index, device):
    return pltpu.make_async_remote_copy(
        src_ref=source,
        dst_ref=target,
        send_sem=sems[0].at[index],
        recv_sem=sems[1].at[index],
        device_id=device,
        device_id_type=MESH,
    )


def greet(barrier, devices):
    for device in devices:
        pl.semaphore_signal(barrier, inc=1, device_id=device, device_id_type=MESH)


def greet_line(barrier, planes, here):
    z, c, core = here

    @pl.when(z < planes - 1)
    def _():
        greet(barrier, [(z + 1, c, core)])

    @pl.when(z > 0)
    def _():
        greet(barrier, [(z - 1, c, core)])


def line_peers(planes, here):
    z = here[0]
    return (2 * planes - 2 - z) // planes + (z + planes - 1) // planes


def chip_peers(chips, here):
    z, c, core = here
    return [(z, lax.rem(c + k, chips), core) for k in range(1, chips)]


def plane_peers(chips, here):
    z, c, core = here
    seqs = 2 * chips
    me = 2 * c + core
    ids = [lax.rem(me + k, seqs) for k in range(1, seqs)]
    return [(z, index // 2, lax.rem(index, 2)) for index in ids]


def column_block(whole, units, index):
    if len(whole.shape) == 3:
        return whole.at[index]
    return whole.at[:, pl.ds(pl.multiple_of(index * units, 128), units)]


def half_block(whole, slots, index, half):
    rows, units = slots.shape[1:]
    at = pl.ds(half * rows, rows)
    if len(whole.shape) == 3:
        return whole.at[index, at]
    return whole.at[at, pl.ds(pl.multiple_of(index * units, 128), units)]


class ChipSwap:
    def __init__(self, chips, here, source, slots, sems):
        z, c, core = here
        self.sends = [
            remote(source(device[1]), slots.at[c], sems, k, device)
            for k, device in enumerate(chip_peers(chips, here), 1)
        ]
        self.waits = [
            remote(source(c), slots.at[lax.rem(c + chips - k, chips)], sems, k, here)
            for k in range(1, chips)
        ]
        self.keep = (source(c), slots.at[c])

    def start(self, local):
        for copy in self.sends:
            copy.start()
        self.held = pltpu.make_async_copy(*self.keep, local)
        self.held.start()

    def finish(self):
        self.held.wait()
        for send, wait in zip(self.sends, self.waits):
            send.wait_send()
            wait.wait_recv()


class PlaneGather:
    def __init__(self, chips, here, block, out, far, near):
        self.chips, self.here, self.block, self.out = chips, here, block, out
        self.far, self.near = far, near
        z, c, core = here
        self.me = 2 * c + core
        self.partner = (z, c, 1 - core)

    def source(self, k, core):
        return 2 * lax.rem(self.here[1] + self.chips - k, self.chips) + core

    def sends(self):
        mine = self.out.at[self.me]
        copies = [
            remote(self.block, mine, self.far, k, device)
            for k, device in enumerate(chip_peers(self.chips, self.here), 1)
        ]
        return [*copies, remote(self.block, mine, self.near, 0, self.partner)]

    def start(self):
        for copy in self.sends():
            copy.start()

    def passed(self, k):
        index = self.source(k, self.here[2])
        return remote(self.out.at[index], self.out.at[index], self.near, k, self.partner)

    def forward(self):
        for k in range(1, self.chips):
            index = self.source(k, self.here[2])
            remote(self.block, self.out.at[index], self.far, k, self.partner).wait_recv()
            self.passed(k).start()

    def finish(self):
        for copy in self.sends():
            copy.wait_send()
        for k in range(1, self.chips):
            self.passed(k).wait_send()
        for k in range(self.chips):
            index = self.source(k, 1 - self.here[2])
            remote(self.block, self.out.at[index], self.near, k, self.partner).wait_recv()


class LineGather:
    def __init__(self, planes, here, parts, up, down):
        self.planes, self.here, self.parts = planes, here, parts
        self.up, self.down = up, down
        self.count = len(parts(here[0]))

    def upward(self, d, p):
        z, c, core = self.here
        block = self.parts(z - d)[p]
        return remote(block, block, self.up, d * self.count + p, (z + 1, c, core))

    def downward(self, d, p):
        z, c, core = self.here
        block = self.parts(z + d)[p]
        return remote(block, block, self.down, d * self.count + p, (z - 1, c, core))

    def each(self, d, p, act):
        z, planes = self.here[0], self.planes
        pl.when((z < planes - 1) & (z - d >= 0))(lambda: act(self.upward(d, p)))
        pl.when((z > 0) & (z + d < planes))(lambda: act(self.downward(d, p)))

    def start(self):
        for p in range(self.count):
            self.each(0, p, lambda copy: copy.start())

    def step(self, d, arrived=None):
        z, planes = self.here[0], self.planes

        def below(p):
            block = self.parts(z - d)[p]
            remote(block, block, self.up, (d - 1) * self.count + p, self.here).wait_recv()
            if d < planes - 1:
                pl.when(z < planes - 1)(lambda: self.upward(d, p).start())
            if arrived is not None:
                arrived(z - d, p)

        def above(p):
            block = self.parts(z + d)[p]
            remote(block, block, self.down, (d - 1) * self.count + p, self.here).wait_recv()
            if d < planes - 1:
                pl.when(z > 0)(lambda: self.downward(d, p).start())
            if arrived is not None:
                arrived(z + d, p)

        for p in range(self.count):
            pl.when(z - d >= 0)(lambda p=p: below(p))
            pl.when(z + d < planes)(lambda p=p: above(p))

    def finish(self):
        for d in range(self.planes - 1):
            for p in range(self.count):
                self.each(d, p, lambda copy: copy.wait_send())


class GroupGather:
    PARTS = 2

    def __init__(self, planes, here, block, out, up, down, near):
        self.planes, self.here, self.block, self.out, self.near = planes, here, block, out, near
        self.partner = (here[0], here[1], 1 - here[2])
        size = block.shape[0] // self.PARTS
        self.slices = [pl.ds(p * size, size) for p in range(self.PARTS)]
        core = here[2]
        self.line = LineGather(planes, here, lambda t: self.parts(t, core), up, down)

    def parts(self, t, core):
        return [self.out.at[t, core, rows] for rows in self.slices]

    def passed(self, t, p):
        block = self.parts(t, self.here[2])[p]
        return remote(block, block, self.near, t * self.PARTS + p, self.partner)

    def start(self, local):
        z, _, core = self.here
        keep = pltpu.make_async_copy(self.block, self.out.at[z, core], local)
        keep.start()
        keep.wait()
        self.line.start()
        for p in range(self.PARTS):
            self.passed(z, p).start()

    def step(self, d):
        self.line.step(d, lambda t, p: self.passed(t, p).start())

    def other(self, t):
        for p in range(self.PARTS):
            block = self.parts(t, 1 - self.here[2])[p]
            remote(block, block, self.near, t * self.PARTS + p, self.partner).wait_recv()

    def finish(self):
        self.line.finish()
        for t in range(self.planes):
            for p in range(self.PARTS):
                self.passed(t, p).wait_send()

    @classmethod
    def sems(cls, planes):
        return pairs_of(*[planes * cls.PARTS] * 3)


COLUMNS = 512


def product(left, right, columns, turned):
    if turned:
        return lax.dot_general(
            left, right[columns, :], (((1,), (1,)), ((), ())), preferred_element_type=F32
        )
    return jnp.dot(left, right[:, columns], preferred_element_type=F32)


class PlaneScatter:
    def __init__(self, chips, here, left, right, turned, buffers, near, far):
        self.chips, self.here = chips, here
        self.left, self.right, self.turned = left, right, turned
        self.near_out, self.near_in, self.far_out, self.far_in = buffers
        self.near, self.far = near, far
        self.tokens, width = self.near_out.shape[1:]
        self.tiles = [pl.ds(at, COLUMNS) for at in range(0, width, COLUMNS)]
        self.order = [*range(1, chips), 0]

    def target(self, k):
        return lax.rem(self.here[1] + k, self.chips)

    def near_copy(self, i):
        z, c, core = self.here
        at = (slice(None), slice(None), self.tiles[i])
        return remote(self.near_out.at[at], self.near_in.at[at], self.near, i, (z, c, 1 - core))

    def far_copy(self, k, i):
        z, _, core = self.here
        at = (k, slice(None), self.tiles[i])
        index = k * len(self.tiles) + i
        return remote(
            self.far_out.at[at], self.far_in.at[at], self.far, index, (z, self.target(k), core)
        )

    def rows(self, position):
        return slice(position * self.tokens, (position + 1) * self.tokens)

    def start(self):
        core = self.here[2]
        blocks = [self.left[2 * self.target(k) + 1 - core] for k in self.order]
        left = jnp.concatenate(blocks, axis=0)
        for i, columns in enumerate(self.tiles):
            part = product(left, self.right, columns, self.turned).astype(LOW)
            for position, k in enumerate(self.order):
                self.near_out[k, :, columns] = part[self.rows(position)]
            self.near_copy(i).start()
        blocks = [self.left[2 * self.target(k) + core] for k in self.order]
        left = jnp.concatenate(blocks, axis=0)
        for i, columns in enumerate(self.tiles):
            part = product(left, self.right, columns, self.turned)
            self.near_copy(i).wait_recv()
            for position, k in enumerate(self.order):
                self.far_out[k, :, columns] = (
                    part[self.rows(position)] + self.near_in[k, :, columns].astype(F32)
                ).astype(LOW)
                if k:
                    self.far_copy(k, i).start()

    def finish(self, out_ref):
        for i, columns in enumerate(self.tiles):
            total = self.far_out[0, :, columns].astype(F32)
            for k in range(1, self.chips):
                self.far_copy(k, i).wait_recv()
                total = total + self.far_in[k, :, columns].astype(F32)
            out_ref[:, columns] = total
        for i in range(len(self.tiles)):
            self.near_copy(i).wait_send()
            for k in range(1, self.chips):
                self.far_copy(k, i).wait_send()

    @staticmethod
    def scratch(chips, tokens, width):
        return [pltpu.VMEM((chips, tokens, width), LOW)] * 4

    @staticmethod
    def sems(chips, width):
        return pairs_of(width // COLUMNS, chips * (width // COLUMNS))


class LineScatter:
    def __init__(self, planes, here, count, part, tiles, own, slots, up, down):
        self.planes, self.here, self.count = planes, here, count
        self.part, self.tiles, self.own, self.slots = part, tiles, own, slots
        self.up, self.down = up, down
        self.steps = (planes - 1) * count

    def upward(self, t, p):
        z, c, core = self.here
        block = self.slots.at[(t, *self.part(p))]
        return remote(block, block, self.up, t * self.count + p, (z + 1, c, core))

    def downward(self, t, p, last):
        z, c, core = self.here
        block = self.slots.at[(t, *self.part(p))]
        target = self.slots.at[(self.planes, *self.part(p))] if last else block
        return remote(block, target, self.down, t * self.count + p, (z - 1, c, core))

    def add(self, t, p, fresh):
        for tile in self.tiles(p):
            total = self.own(t, tile)
            if not fresh:
                total = total + self.slots[(t, *tile)].astype(F32)
            self.slots[(t, *tile)] = total.astype(LOW)

    def step(self, i):
        z, planes, count = self.here[0], self.planes, self.count
        rise, fall = i - z, i - (planes - 1 - z)

        @pl.when((rise >= 0) & (rise < (planes - 1 - z) * count))
        def _():
            t, p = planes - 1 - rise // count, lax.rem(rise, count)

            @pl.when(z > 0)
            def _():
                self.upward(t, p).wait_recv()
                self.add(t, p, False)

            @pl.when(z == 0)
            def _():
                self.add(t, p, True)

            self.upward(t, p).start()

        @pl.when((fall >= 0) & (fall < z * count))
        def _():
            t, p = fall // count, lax.rem(fall, count)

            @pl.when(z < planes - 1)
            def _():
                self.downward(t, p, False).wait_recv()
                self.add(t, p, False)

            @pl.when(z == planes - 1)
            def _():
                self.add(t, p, True)

            pl.when(t == z - 1)(lambda: self.downward(t, p, True).start())
            pl.when(t < z - 1)(lambda: self.downward(t, p, False).start())

    def finish(self, store):
        z, planes = self.here[0], self.planes

        def total(tile, *slots):
            value = self.own(z, tile)
            for slot in slots:
                value = value + self.slots[(slot, *tile)].astype(F32)
            store(tile, value)

        for p in range(self.count):
            tiles = self.tiles(p)

            @pl.when(z > 0)
            def _(p=p):
                self.upward(z, p).wait_recv()

            @pl.when(z < planes - 1)
            def _(p=p):
                self.downward(z, p, True).wait_recv()

            @pl.when((z > 0) & (z < planes - 1))
            def _(tiles=tiles):
                for tile in tiles:
                    total(tile, z, planes)

            @pl.when(z == 0)
            def _(tiles=tiles):
                for tile in tiles:
                    total(tile, planes)

            @pl.when(z == planes - 1)
            def _(tiles=tiles):
                for tile in tiles:
                    total(tile, z)

        for t in range(planes):
            for p in range(self.count):
                pl.when(z < t)(lambda t=t, p=p: self.upward(t, p).wait_send())
                pl.when(z > t)(lambda t=t, p=p: self.downward(t, p, False).wait_send())


def row_tiles(count, size):
    return [pl.ds(at, size) for at in range(0, count, size)]


def in_scatter_kernel(
    planes, chips, heads, strided, left_ref, right_ref, grad_ref, up_ref, weight_ref, gain_ref,
    out_ref, total_ref, gains_ref, slots_ref,
    near_out, near_in, far_out, far_in, sums, mine, parts, *sems,
):
    here = place()
    z, c, core = here
    seqs = 2 * chips
    me = 2 * c + core
    near, far, up, down, swap_sems, chip_sems = [sems[2 * i : 2 * i + 2] for i in range(6)]
    barrier = pltpu.get_barrier_semaphore()
    peers = plane_peers(chips, here)
    greet(barrier, peers)
    greet_line(barrier, planes, here)
    pl.semaphore_wait(barrier, len(peers) + line_peers(planes, here))
    half = seqs // 2
    line = LineScatter(
        planes,
        here,
        2,
        lambda p: (pl.ds(p * half, half),),
        lambda p: [(pl.ds(p * half + i, 1),) for i in range(half)],
        lambda t, tile: grad_ref[(t, *tile)].astype(F32),
        sums,
        up,
        down,
    )
    line.step(0)
    work = PlaneScatter(
        chips, here, left_ref, right_ref, True, (near_out, near_in, far_out, far_in), near, far
    )
    work.start()
    ups = ChipSwap(
        chips, here, lambda index: half_block(up_ref, slots_ref, index, 1), slots_ref, chip_sems
    )
    ups.start(sems[12].at[0])
    for i in range(1, line.steps):
        line.step(i)

    def store(tile, total):
        mine[tile] = total.astype(LOW)

    line.finish(store)
    swaps = [
        remote(mine.at[2 * device[1] + device[2]], parts.at[me], swap_sems, k, device)
        for k, device in enumerate(peers, 1)
    ]
    for copy in swaps:
        copy.start()
    parts[me] = mine[me]
    work.finish(out_ref)
    for k in range(1, seqs):
        swaps[k - 1].wait_send()
        index = lax.rem(me + seqs - k, seqs)
        remote(mine.at[0], parts.at[index], swap_sems, k, here).wait_recv()
    span = heads * HD
    width = seqs * span
    gain = gain_ref[:, pl.ds(0, 1)]
    summed = jnp.zeros(gain.shape, F32)
    for i in range(3):
        step, pieces = (seqs * HD, planes) if strided else (width, 1)
        size = step // seqs
        for piece in range(pieces):
            at = i * span + piece * size
            columns = pl.ds(i * width + piece * step, step)
            total = jnp.concatenate(
                [parts[s, :, pl.ds(at, size)].astype(F32) for s in range(seqs)], axis=1
            )
            weight = weight_ref[:, columns].astype(F32)
            summed = summed + jnp.sum(total * weight, axis=1, keepdims=True)
            total_ref[:, columns] = total * gain
    gains_ref[...] = jnp.broadcast_to(summed, gains_ref.shape)
    ups.finish()


def in_scatter(planes, chips, heads, strided, left, right, grads, up_grads, weight, gain, units):
    _, tokens, _ = left.shape
    width = right.shape[0]
    seqs = 2 * chips
    part, wide = grads.shape[2:]
    return call(
        functools.partial(in_scatter_kernel, planes, chips, heads, strided),
        "in_scatter",
        [
            shape((tokens, width), F32),
            shape(weight.shape, F32),
            shape((part, 128), F32),
            shape((chips, width // 2, units), LOW),
        ],
        (left, right, grads, up_grads, weight, gain),
        [VMEM, VMEM, VMEM, HBM, VMEM, VMEM],
        [VMEM, VMEM, VMEM, HBM],
        [
            *PlaneScatter.scratch(chips, tokens, width),
            pltpu.VMEM((planes + 1, seqs, part, wide), LOW),
            *[pltpu.VMEM((seqs, part, wide), LOW)] * 2,
            *PlaneScatter.sems(chips, width),
            *pairs_of(2 * planes, 2 * planes, seqs, chips),
            pltpu.SemaphoreType.DMA((1,)),
        ],
        4,
    )


class PairScatter:
    PARTS = 2

    def __init__(self, planes, here, left, right, turned, buffers, near, up, down):
        self.planes, self.here = planes, here
        self.left, self.right, self.turned = left, right, turned
        self.near_out, self.own, slots = buffers
        self.near = near
        self.tokens, width = self.near_out.shape[1:]
        self.tiles = [pl.ds(at, COLUMNS) for at in range(0, width, COLUMNS)]
        size = width // self.PARTS

        def part(p):
            at = p * size if isinstance(p, int) else pl.multiple_of(p * size, 128)
            return (slice(None), pl.ds(at, size))

        self.line = LineScatter(
            planes,
            here,
            self.PARTS,
            part,
            lambda p: [(rows, part(p)[1]) for rows in row_tiles(self.tokens, 32)],
            lambda t, tile: self.own[(t, *tile)].astype(F32),
            slots,
            up,
            down,
        )

    def near_copy(self, i):
        z, c, core = self.here
        at = (slice(None), slice(None), self.tiles[i])
        return remote(self.near_out.at[at], self.own.at[at], self.near, i, (z, c, 1 - core))

    def start(self):
        core, tokens = self.here[2], self.tokens
        left = jnp.concatenate([self.left[t, 1 - core] for t in range(self.planes)], axis=0)
        for i, columns in enumerate(self.tiles):
            part = product(left, self.right, columns, self.turned).astype(LOW)
            for t in range(self.planes):
                self.near_out[t, :, columns] = part[t * tokens : (t + 1) * tokens]
            self.near_copy(i).start()
        left = jnp.concatenate([self.left[t, core] for t in range(self.planes)], axis=0)
        for i, columns in enumerate(self.tiles):
            part = product(left, self.right, columns, self.turned)
            self.near_copy(i).wait_recv()
            for t in range(self.planes):
                self.own[t, :, columns] = (
                    part[t * tokens : (t + 1) * tokens] + self.own[t, :, columns].astype(F32)
                ).astype(LOW)
        self.line.step(0)

    def finish(self, out_ref):
        def store(tile, total):
            out_ref[tile] = total

        self.line.finish(store)
        for i in range(len(self.tiles)):
            self.near_copy(i).wait_send()

    @staticmethod
    def scratch(planes, tokens, width):
        return [
            *[pltpu.VMEM((planes, tokens, width), LOW)] * 2,
            pltpu.VMEM((planes + 1, tokens, width), LOW),
        ]

    @classmethod
    def sems(cls, planes, width):
        return pairs_of(width // COLUMNS, cls.PARTS * planes, cls.PARTS * planes)


def feed_forward_kernel(
    planes, chips, width_ff, x_ref, up_ref, grads_ref, down_ref,
    out_ref, normed_ref, downs_ref, gup_ref, slots_ref,
    rows, ups, grads, downs, back, act, slope, stat, stat_out, stat_in,
    normed, d_up, near_out, own, sums, gup, gdown, *sems,
):
    here = place()
    z, c, core = here
    count = 2 * planes
    me = 2 * z + core
    up, down, near, chip_sems, stat_sems, pair, rise, fall, swap_sems = [
        sems[2 * i : 2 * i + 2] for i in range(9)
    ]
    local = sems[18]
    tokens, width = x_ref.shape
    units = ups.shape[1]
    load_up = pltpu.make_async_copy(up_ref, ups, local.at[0])
    load_grads = pltpu.make_async_copy(grads_ref, grads, local.at[1])
    load_up.start()
    load_grads.start()
    barrier = pltpu.get_barrier_semaphore()
    ids = [lax.rem(me + k, count) for k in range(1, count)]
    group_peers = [(index // 2, c, lax.rem(index, 2)) for index in ids]
    peers = [*group_peers, *chip_peers(chips, here)]
    greet(barrier, peers)
    pl.semaphore_wait(barrier, len(peers))

    group = GroupGather(planes, here, x_ref, rows, up, down, near)
    group.start(local.at[2])
    keep = pltpu.make_async_copy(down_ref, downs.at[c], local.at[3])
    keep.start()
    sends = [
        remote(down_ref, downs.at[c], chip_sems, k, device)
        for k, device in enumerate(chip_peers(chips, here), 1)
    ]
    for copy in sends:
        copy.start()
    load_up.wait()

    step = tokens
    lane = lax.broadcasted_iota(jnp.int32, (step, 128), 1)

    def forward(t):
        group.other(t)
        block = rows[t].reshape(2 * tokens, width)
        for at in range(0, units, COLUMNS):
            columns = pl.ds(at, COLUMNS)
            act[t, :, columns] = jnp.dot(block, ups[:, columns], preferred_element_type=F32)

        def some(i, carry):
            at = pl.ds(pl.multiple_of(i * step, step), step)
            value = act[t, at]
            phi = 0.5 * (1.0 + lax.erf(value * math.sqrt(0.5)))
            result = value * phi
            act[t, at] = result
            slope[t, at] = phi + value * (
                jnp.exp(value * value * -0.5) * (1.0 / math.sqrt(2.0 * math.pi))
            )
            total = jnp.sum(result, axis=1, keepdims=True)
            square = jnp.sum(result * result, axis=1, keepdims=True)
            stat[t, at] = jnp.where(lane == 0, total, jnp.where(lane == 1, square, 0.0))
            return carry

        lax.fori_loop(0, 2 * tokens // step, some, 0)

    forward(z)
    for d in range(1, planes):
        group.step(d)
        if d > 1:
            pl.when(z - d + 1 >= 0)(lambda d=d: forward(z - d + 1))
            pl.when(z + d - 1 < planes)(lambda d=d: forward(z + d - 1))
    pl.when(z - planes + 1 >= 0)(lambda: forward(z - planes + 1))
    pl.when(z + planes - 1 < planes)(lambda: forward(z + planes - 1))
    group.finish()
    keep.wait()
    load_grads.wait()
    for k in range(1, chips):
        sends[k - 1].wait_send()
        other = lax.rem(c + chips - k, chips)
        remote(down_ref, downs.at[other], chip_sems, k, here).wait_recv()
    out_downs = pltpu.make_async_copy(downs, downs_ref, local.at[4])
    out_downs.start()

    def backward(t, carry):
        block = grads[t].reshape(2 * tokens, width)
        size = units // chips
        for chip in range(chips):
            columns = pl.ds(chip * size, size)
            back[t, :, columns] = rows_product(block, downs[chip])

        def some(i, inner):
            at = pl.ds(pl.multiple_of(i * step, step), step)
            value = back[t, at]
            cross = jnp.sum(value * act[t, at], axis=1, keepdims=True)
            total = jnp.sum(value, axis=1, keepdims=True)
            stat[t, at] = jnp.where(lane == 2, cross, jnp.where(lane == 3, total, stat[t, at]))
            return inner

        lax.fori_loop(0, 2 * tokens // step, some, 0)
        for half in range(2):
            turned = stat[t, pl.ds(half * tokens, tokens)].T
            stat_out[2 * t + half] = turned[:8]
        return carry

    lax.fori_loop(0, planes, backward, 0)
    copies = [
        remote(stat_out, stat_in.at[k], stat_sems, k, device)
        for k, device in enumerate(group_peers, 1)
    ]
    for copy in copies:
        copy.start()
    for copy in copies:
        copy.wait_send()
        copy.wait_recv()

    def finish(t, carry):
        for half in range(2):
            total = stat_out[2 * t + half]
            for k in range(1, count):
                total = total + stat_in[k, 2 * t + half]
            mean, square, cross, first = (total[i : i + 1] / width_ff for i in range(4))
            scaler = lax.rsqrt(square - mean * mean + NORM_EPS)
            second = scaler * (cross - mean * first)
            figures = [scaler, -mean * scaler, scaler * first, scaler * second]
            padded = jnp.concatenate([*figures, jnp.zeros((128 - 4, tokens), F32)], axis=0)
            stat[t, pl.ds(half * tokens, tokens)] = padded.T

        def some(i, inner):
            at = pl.ds(pl.multiple_of(i * step, step), step)
            figures = stat[t, at]
            scaler, shift, first, second = (figures[:, j : j + 1] for j in range(4))
            unit = act[t, at] * scaler + shift
            normed[t, at] = unit.astype(LOW)
            d_act = back[t, at] * scaler - first - unit * second
            d_up[t, at] = (d_act * slope[t, at]).astype(LOW)
            return inner

        lax.fori_loop(0, 2 * tokens // step, some, 0)
        return carry

    lax.fori_loop(0, planes, finish, 0)
    out_normed = pltpu.make_async_copy(normed, normed_ref, local.at[5])
    out_normed.start()
    work = PairScatter(
        planes, here, Halves(d_up, tokens), ups, True, (near_out, own, sums), pair, rise, fall
    )
    work.start()

    flat_normed, flat_d_up = (
        whole[...].reshape(planes * 2 * tokens, units) for whole in (normed, d_up)
    )
    size = units // chips
    swap = ChipSwap(chips, here, lambda index: gdown.at[index], slots_ref, swap_sems)
    turns_left = list(range(1, work.line.steps))

    def turn():
        if turns_left:
            work.line.step(turns_left.pop(0))

    together = max(1, 256 // size)
    for chip in range(0, chips, together):
        left = flat_normed[:, chip * size : (chip + together) * size]
        for at in range(0, width, COLUMNS):
            columns = pl.ds(at, COLUMNS)
            right = grads[:, :, :, columns].reshape(planes * 2 * tokens, COLUMNS)
            term = token_product(left, right).astype(LOW)
            for i in range(together):
                gdown[chip + i, :, columns] = term[i * size : (i + 1) * size]
        if chip // together % 2:
            turn()
    swap.start(local.at[6])
    chunk = gup.shape[1]
    out_gups = [
        pltpu.make_async_copy(
            gup.at[i % 2], gup_ref.at[pl.ds(i * chunk, chunk)], local.at[7 + i % 2]
        )
        for i in range(width // chunk)
    ]
    for i in range(width // chunk):
        if i % 2 == 0:
            turn()
        left = rows[:, :, :, pl.ds(i * chunk, chunk)].reshape(planes * 2 * tokens, chunk)
        term = token_product(left, flat_d_up).astype(LOW)
        if i > 1:
            out_gups[i - 2].wait()
        gup[i % 2] = term
        out_gups[i].start()
    while turns_left:
        turn()
    work.finish(out_ref)
    swap.finish()
    out_downs.wait()
    out_normed.wait()
    for copy in out_gups[-2:]:
        copy.wait()


class Halves:
    def __init__(self, whole, tokens):
        self.whole, self.tokens = whole, tokens

    def __getitem__(self, at):
        t, core = at
        rows = pl.ds(pl.multiple_of(core * self.tokens, self.tokens), self.tokens)
        return self.whole[t, rows]


def feed_forward(planes, chips, width_ff, x_block, up_mine, grads, down_block):
    tokens, width = x_block.shape
    units = up_mine.shape[1]
    size = down_block.shape[0]
    wide = (planes, 2 * tokens, units)
    return call(
        functools.partial(feed_forward_kernel, planes, chips, width_ff),
        "feed_forward",
        [
            shape((tokens, width), F32),
            shape(wide, LOW),
            shape((chips, size, width), LOW),
            shape((width, units), LOW),
            shape((chips, size, width), LOW),
        ],
        (x_block, up_mine, grads, down_block),
        [HBM] * 4,
        [VMEM, HBM, HBM, HBM, HBM],
        [
            pltpu.VMEM((planes, 2, tokens, width), LOW),
            pltpu.VMEM((width, units), LOW),
            pltpu.VMEM((planes, 2, tokens, width), LOW),
            pltpu.VMEM((chips, size, width), LOW),
            *[pltpu.VMEM(wide, F32)] * 3,
            pltpu.VMEM((planes, 2 * tokens, 128), F32),
            pltpu.VMEM((2 * planes, 8, 128), F32),
            pltpu.VMEM((2 * planes, 2 * planes, 8, 128), F32),
            *[pltpu.VMEM(wide, LOW)] * 2,
            *PairScatter.scratch(planes, tokens, width),
            pltpu.VMEM((2, 256, units), LOW),
            pltpu.VMEM((chips, size, width), LOW),
            *GroupGather.sems(planes),
            *pairs_of(chips, 2 * planes),
            *PairScatter.sems(planes, width),
            *pairs_of(chips),
            pltpu.SemaphoreType.DMA((9,)),
        ],
        7,
    )


def swap_lanes(values):
    lane = lax.broadcasted_iota(jnp.int32, values.shape, 1)
    return jnp.where(
        lax.rem(lane, 2) == 0,
        pltpu.roll(values, values.shape[1] - 1, 1),
        pltpu.roll(values, 1, 1),
    )


def twice(table):
    return jnp.concatenate([table, table], axis=1)


def turns(meta_ref, rows):
    cosine, sine, shrink = [twice(meta_ref[rows, pl.ds(i * HD, HD)]) for i in range(3)]
    return (cosine, sine, cosine * shrink, sine * shrink)


def allowed_block(meta_ref, rows, size, columns):
    query = rows + lax.broadcasted_iota(jnp.int32, (size, columns), 0)
    key = lax.broadcasted_iota(jnp.int32, (size, columns), 1)
    offset = meta_ref[pl.ds(rows, size), pl.ds(3 * HD, 1)].astype(jnp.int32)
    return (key <= query) & (key >= query - offset)


BLOCK = 256


def attention_forward_kernel(
    planes, chips, heads, strided,
    x_ref, meta_ref, qkv_ref, out_ref, gain_ref, up_ref, grad_ref,
    q_ref, k_ref, v_ref, att_ref, log_ref, sum_ref,
    rows_ref, metas_ref, qkvs_ref, outs_ref, gains_ref, ups_ref, grads_ref, tiles_ref,
    rows, metas, qkvs, outs, raw, wide, tile, near_out, near_in, far_out, far_in,
    *sems,
):
    here = place()
    z, c, core = here
    seqs = 2 * chips
    count = planes * seqs
    me = 2 * c + core
    flat = z * seqs + me
    groups = [sems[2 * i : 2 * i + 2] for i in range(17)]
    swap_sems, x_far, x_near, meta_far, meta_near, up, down, up_two, down_two = groups[:9]
    gain_sems, up_sems, near, far, tile_sems, grad_up, grad_down, pair = groups[9:]
    local = sems[34]
    tokens, width = x_ref.shape
    part, three = qkv_ref.shape[1:]
    length = seqs * tokens
    span = heads * HD
    barrier = pltpu.get_barrier_semaphore()

    def device_of(k):
        other = lax.rem(flat + k, count)
        return (other // seqs, lax.rem(other, seqs) // 2, lax.rem(other, 2))

    def signal(k, carry):
        greet(barrier, [device_of(k)])
        return carry

    lax.fori_loop(1, count, signal, 0)
    pl.semaphore_wait(barrier, count - 1)

    mine = pltpu.make_async_copy(qkv_ref.at[me], qkvs.at[z, me], local.at[0])
    own_out = pltpu.make_async_copy(out_ref, outs.at[z] if strided else outs, local.at[1])
    units = up_ref.shape[1]
    keeps = [
        pltpu.make_async_copy(x_ref, rows.at[me], local.at[2]),
        pltpu.make_async_copy(meta_ref, metas.at[me], local.at[3]),
        pltpu.make_async_copy(gain_ref, gains_ref.at[flat], local.at[4]),
        pltpu.make_async_copy(up_ref, column_block(ups_ref, units, c), local.at[5]),
    ]
    peers = plane_peers(chips, here)
    swaps = [
        remote(qkv_ref.at[2 * device[1] + device[2]], qkvs.at[z, me], swap_sems, k, device)
        for k, device in enumerate(peers, 1)
    ]
    mine.start()
    own_out.start()
    for copy in swaps:
        copy.start()
    gather = PlaneGather(chips, here, x_ref, rows, x_far, x_near)
    meta_gather = PlaneGather(chips, here, meta_ref, metas, meta_far, meta_near)
    for copy in keeps:
        copy.start()

    def gain_copy(k):
        return remote(gain_ref, gains_ref.at[flat], gain_sems, k, device_of(k))

    def gain_start(k, carry):
        gain_copy(k).start()
        return carry

    mine.wait()
    own_out.wait()
    for k in range(1, seqs):
        index = lax.rem(me + seqs - k, seqs)
        remote(qkv_ref.at[0], qkvs.at[z, index], swap_sems, k, here).wait_recv()
    half = seqs // 2
    line = LineGather(
        planes, here, lambda t: [qkvs.at[t, pl.ds(i * half, half)] for i in range(2)], up, down
    )
    line_two = LineGather(planes, here, lambda t: [outs.at[t]], up_two, down_two)
    line.start()
    gather.start()
    meta_gather.start()
    lax.fori_loop(1, count, gain_start, 0)
    gather.forward()
    meta_gather.forward()
    ups = [
        remote(up_ref, column_block(ups_ref, units, c), up_sems, k, device)
        for k, device in enumerate(chip_peers(chips, here), 1)
    ]
    for copy in ups:
        copy.start()
    gather.finish()
    meta_gather.finish()
    for copy in keeps:
        copy.wait()

    block = seqs * part

    def add(t, fresh=False):
        columns = pl.ds(pl.multiple_of(t * block, 128), block)
        left = rows[:, :, columns].reshape(length, block)
        for i in range(3):
            at = pl.ds(i * span, span)
            term = jnp.dot(left, qkvs[t, :, :, at].reshape(block, span), preferred_element_type=F32)
            raw[:, at] = term if fresh else raw[:, at] + term

    add(z, True)
    for d in range(1, planes):
        line.step(d)
        if d == planes - 1:
            if strided:
                line_two.start()
        pl.when(z - d >= 0)(lambda d=d: add(z - d))
        pl.when(z + d < planes)(lambda d=d: add(z + d))
    outputs = [
        pltpu.make_async_copy(rows, rows_ref, local.at[7]),
        pltpu.make_async_copy(metas, metas_ref, local.at[8]),
        pltpu.make_async_copy(qkvs, qkvs_ref, local.at[9]),
    ]
    for copy in outputs:
        copy.start()

    table = RowBlocks(metas)
    for at in range(0, length, BLOCK):
        at = pl.ds(at, BLOCK)
        tables = turns(table, at)
        for two in range(heads // 2):
            query = raw[at, pl.ds(2 * HD * two, 2 * HD)]
            query = (query * tables[0] + swap_lanes(query) * tables[1]).astype(LOW)
            key = raw[at, pl.ds(span + 2 * HD * two, 2 * HD)]
            key = (key * tables[2] + swap_lanes(key) * tables[3]).astype(LOW)
            value = raw[at, pl.ds(2 * span + 2 * HD * two, 2 * HD)].astype(LOW)
            for side in range(2):
                lanes = slice(side * HD, (side + 1) * HD)
                q_ref[2 * two + side, at] = query[:, lanes]
                k_ref[2 * two + side, at] = key[:, lanes]
                v_ref[2 * two + side, at] = value[:, lanes]
    log_ref[...] = jnp.zeros(log_ref.shape, F32)

    def one_head(head, carry):
        for start in range(0, length, BLOCK):
            columns = start + BLOCK
            at = pl.ds(start, BLOCK)
            scores = lax.dot_general(
                q_ref[head, at],
                k_ref[head, pl.ds(0, columns)],
                (((1,), (1,)), ((), ())),
                preferred_element_type=F32,
            )
            allowed = allowed_block(table, start, BLOCK, columns)
            scores = jnp.where(allowed, scores, NEG_FILL)
            top = jnp.max(scores, axis=1, keepdims=True)
            shifted = jnp.exp(scores - top)
            total = jnp.sum(shifted, axis=1, keepdims=True)
            probs = (shifted * (1.0 / total)).astype(LOW)
            wide[head, at] = jnp.dot(
                probs, v_ref[head, pl.ds(0, columns)], preferred_element_type=F32
            )
            lane = lax.broadcasted_iota(jnp.int32, (BLOCK, 128), 1)
            log_ref[at] = jnp.where(lane == head, top + jnp.log(total), log_ref[at])
        return carry

    first = 0
    for d in range(1, planes):
        last = -(-heads * d // planes)
        lax.fori_loop(first, last, one_head, 0)
        first = last
        if strided:
            line_two.step(d)
    group = GroupGather(planes, here, grad_ref, grads_ref, grad_up, grad_down, pair)
    group.start(local.at[6])
    lax.fori_loop(first, heads, one_head, 0)
    lane = lax.broadcasted_iota(jnp.int32, (tokens, 128), 1)
    column = jnp.sum(outs[...].astype(F32).reshape(span, width), axis=0, keepdims=True)
    for s in range(seqs):
        at = pl.ds(s * tokens, tokens)
        low = jnp.concatenate([wide[head, at] for head in range(heads)], axis=1).astype(LOW)
        att_ref[s] = low
        value = low.astype(F32)
        total = jnp.sum(value, axis=1, keepdims=True)
        square = jnp.sum(value * value, axis=1, keepdims=True)
        both = jnp.where(lane == 0, total, jnp.where(lane == 1, square, 0.0))
        tile[s, pl.ds(0, 8)] = both.T[:8]
        for i in range(width // 128):
            tile[s, pl.ds(8 + i, 1)] = column[:, i * 128 : (i + 1) * 128]
    out_tiles = [
        remote(tile.at[2 * device[1] + device[2]], tiles_ref.at[me], tile_sems, k, device)
        for k, device in enumerate(peers, 1)
    ]
    for copy in out_tiles:
        copy.start()
    keep = pltpu.make_async_copy(tile.at[me], tiles_ref.at[me], local.at[10])
    keep.start()
    out_outs = pltpu.make_async_copy(outs, outs_ref, local.at[11])
    out_outs.start()
    work = PlaneScatter(
        chips, here, att_ref, Flat(outs, span), False, (near_out, near_in, far_out, far_in), near, far
    )
    work.start()
    for d in range(1, planes):
        group.step(d)
    work.finish(sum_ref)
    group.finish()
    for t in range(planes):
        group.other(t)
    line.finish()
    if strided:
        line_two.finish()
    for copy in [*swaps, *ups]:
        copy.wait_send()
    for k in range(1, chips):
        other = lax.rem(c + chips - k, chips)
        remote(up_ref, column_block(ups_ref, units, other), up_sems, k, here).wait_recv()
    for copy in [keep, out_outs, *outputs]:
        copy.wait()
    for k in range(1, seqs):
        out_tiles[k - 1].wait_send()
        index = lax.rem(me + seqs - k, seqs)
        remote(tile.at[0], tiles_ref.at[index], tile_sems, k, here).wait_recv()

    def gain_wait(k, carry):
        gain_copy(k).wait_send()
        other = lax.rem(flat + count - k, count)
        remote(gain_ref, gains_ref.at[other], gain_sems, k, here).wait_recv()
        return carry

    lax.fori_loop(1, count, gain_wait, 0)


class Flat:
    def __init__(self, blocks, count):
        self.blocks, self.count = blocks, count

    def __getitem__(self, at):
        if len(self.blocks.shape) == 2:
            return self.blocks[at]
        _, columns = at
        return self.blocks[:, :, columns].reshape(self.count, columns.size)


class RowBlocks:
    def __init__(self, blocks):
        self.blocks = blocks

    def __getitem__(self, at):
        rows, columns = at
        size = self.blocks.shape[1]
        first, count = rows.start // size, rows.size // size
        return self.blocks[pl.ds(first, count), :, columns].reshape(rows.size, columns.size)


def attention_forward(
    planes, chips, heads, strided, x_block, meta, qkv_blocks, out_rows, gain_tile, up_block, grad
):
    seqs = 2 * chips
    tokens, width = x_block.shape
    part, wide = qkv_blocks.shape[1:]
    units = up_block.shape[1]
    length = seqs * tokens
    span = heads * HD
    outs = (planes, *out_rows.shape) if strided else out_rows.shape
    tile = (seqs, 8 + width // 128, 128)
    return call(
        functools.partial(attention_forward_kernel, planes, chips, heads, strided),
        "attention_forward",
        [
            *[shape((heads, length, HD), LOW)] * 3,
            shape((seqs, tokens, span), LOW),
            shape((length, 128), F32),
            shape((tokens, width), F32),
            shape((seqs, tokens, width), LOW),
            shape((seqs, *meta.shape), F32),
            shape((planes, seqs, part, wide), LOW),
            shape(outs, LOW),
            shape((planes * seqs, *gain_tile.shape), F32),
            shape((width, chips * units) if units % 128 == 0 else (chips, width, units), LOW),
            shape((planes, 2, *grad.shape), LOW),
            shape(tile, F32),
        ],
        (x_block, meta, qkv_blocks, out_rows, gain_tile, up_block, grad),
        [HBM] * 7,
        [*[VMEM] * 6, *[HBM] * 8],
        [
            pltpu.VMEM((seqs, tokens, width), LOW),
            pltpu.VMEM((seqs, *meta.shape), F32),
            pltpu.VMEM((planes, seqs, part, wide), LOW),
            pltpu.VMEM(outs, LOW),
            pltpu.VMEM((length, 3 * span), F32),
            pltpu.VMEM((heads, length, HD), F32),
            pltpu.VMEM(tile, F32),
            *PlaneScatter.scratch(chips, tokens, width),
            *pairs_of(
                seqs, *[chips] * 4, *[2 * planes] * 2, *[planes] * 2, planes * seqs, chips
            ),
            *PlaneScatter.sems(chips, width),
            *pairs_of(seqs),
            *GroupGather.sems(planes),
            pltpu.SemaphoreType.DMA((12,)),
        ],
        1,
    )


def attention_backward_kernel(
    planes, chips, heads, strided,
    x_ref, stat_ref, tile_ref, left_ref, right_ref,
    q_in, k_in, v_in, att_in, out_in, log_in, meta_in, up_ref,
    tiles_ref, ffn_ref, out_ref, total_ref, slots_ref,
    rows, stats, left, right, q_ref, k_ref, v_ref, att_ref, outs, log_ref, meta_ref,
    near_out, near_own, near_sums, grad, dq, dk, dv, normed_all, own, sums, *sems,
):
    here = place()
    z, c, core = here
    seqs = 2 * chips
    count = planes * seqs
    me = 2 * c + core
    flat = z * seqs + me
    x_far, x_near, s_far, s_near, tile_sems, near, up, down, up_two, down_two, swap_sems = [
        sems[2 * i : 2 * i + 2] for i in range(11)
    ]
    local = sems[22]
    pairs = [
        (left_ref, left), (right_ref, right), (att_in, att_ref), (out_in, outs), (meta_in, meta_ref),
        (q_in, q_ref), (k_in, k_ref), (v_in, v_ref), (log_in, log_ref),
    ]
    loads = [pltpu.make_async_copy(*pair, local.at[i]) for i, pair in enumerate(pairs)]
    for copy in loads:
        copy.start()
    barrier = pltpu.get_barrier_semaphore()

    def device_of(k):
        other = lax.rem(flat + k, count)
        return (other // seqs, lax.rem(other, seqs) // 2, lax.rem(other, 2))

    def signal(k, carry):
        greet(barrier, [device_of(k)])
        return carry

    lax.fori_loop(1, count, signal, 0)
    pl.semaphore_wait(barrier, count - 1)
    gather = PlaneGather(chips, here, x_ref, rows, x_far, x_near)
    stat_gather = PlaneGather(chips, here, stat_ref, stats, s_far, s_near)
    gather.start()
    stat_gather.start()
    keeps = [
        pltpu.make_async_copy(x_ref, rows.at[me], local.at[9]),
        pltpu.make_async_copy(stat_ref, stats.at[me], local.at[10]),
        pltpu.make_async_copy(tile_ref.at[flat], tiles_ref.at[flat], local.at[11]),
    ]
    for copy in keeps:
        copy.start()

    def tile_copy(k):
        other = lax.rem(flat + k, count)
        return remote(tile_ref.at[other], tiles_ref.at[flat], tile_sems, k, device_of(k))

    def tile_start(k, carry):
        tile_copy(k).start()
        return carry

    lax.fori_loop(1, count, tile_start, 0)
    tokens, width = x_ref.shape
    for copy in loads[:2]:
        copy.wait()
    work = PairScatter(
        planes, here, Halves(left, tokens), right, False, (near_out, near_own, near_sums),
        near, up, down,
    )
    work.start()
    left_turns = list(range(1, work.line.steps))

    def turn(until=None):
        step = left_turns[0] + 1 if until is None and left_turns else until
        while left_turns and left_turns[0] < step:
            work.line.step(left_turns.pop(0))

    turn()
    turn()
    gather.forward()
    stat_gather.forward()
    gather.finish()
    stat_gather.finish()
    swap = ChipSwap(
        chips, here, lambda index: half_block(up_ref, slots_ref, index, 0), slots_ref, swap_sems
    )
    swap.start(local.at[12])
    for copy in [*loads[2:], *keeps]:
        copy.wait()
    turn()
    length, span = att_ref.shape
    part = own.shape[1]
    per = BLOCK // tokens
    for first in range(0, seqs, per):
        at = pl.ds(first * tokens, BLOCK)
        figures = stats[pl.ds(first, per)].reshape(BLOCK, 128)
        mean, scaler, one, two = (figures[:, i : i + 1] for i in range(4))
        block = rows[pl.ds(first, per)].reshape(BLOCK, width)
        d_sub = product(block, outs, slice(None), True)
        normed = (att_ref[at].astype(F32) - mean) * scaler
        normed_all[at] = normed.astype(LOW)
        d_att = (scaler * (d_sub - one - normed * two)).astype(LOW)
        for head in range(heads):
            grad[head, at] = d_att[:, head * HD : (head + 1) * HD]
    for at in range(0, width, COLUMNS):
        columns = pl.ds(at, COLUMNS)
        term = token_product(normed_all[...], rows[:, :, columns].reshape(length, COLUMNS)).astype(LOW)
        for t in range(planes):
            own[t, :, columns] = term[t * part : (t + 1) * part]
    line = LineScatter(
        planes,
        here,
        1,
        lambda p: (slice(None),),
        lambda p: [(row,) for row in row_tiles(part, 16)],
        lambda t, tile: own[(t, *tile)].astype(F32),
        sums,
        up_two,
        down_two,
    )
    if strided:
        line.step(0)
    dk[...] = jnp.zeros(dk.shape, F32)
    dv[...] = jnp.zeros(dv.shape, F32)

    def one_head(head, carry):
        for start in range(0, length, BLOCK):
            columns = start + BLOCK
            at = pl.ds(start, BLOCK)
            keys = pl.ds(0, columns)
            query, key = q_ref[head, at], k_ref[head, keys]
            out_grad = grad[head, at]
            scores = lax.dot_general(
                query, key, (((1,), (1,)), ((), ())), preferred_element_type=F32
            )
            allowed = allowed_block(meta_ref, start, BLOCK, columns)
            lane = lax.broadcasted_iota(jnp.int32, (BLOCK, 128), 1)
            log_total = jnp.sum(jnp.where(lane == head, log_ref[at], 0.0), axis=1, keepdims=True)
            probs = jnp.where(allowed, jnp.exp(scores - log_total), 0.0)
            d_probs = lax.dot_general(
                out_grad, v_ref[head, keys], (((1,), (1,)), ((), ())), preferred_element_type=F32
            )
            delta = jnp.sum(probs * d_probs, axis=1, keepdims=True)
            d_scores = (probs * (d_probs - delta)).astype(LOW)
            dq[head, at] = jnp.dot(d_scores, key, preferred_element_type=F32)
            dk[head, keys] += token_product(d_scores, query)
            dv[head, keys] += token_product(probs.astype(LOW), out_grad)
        return carry

    first = 0
    for i in range(1, planes - 1):
        last = -(-heads * i // (planes - 1))
        lax.fori_loop(first, last, one_head, 0)
        first = last
        turn()
        if strided:
            line.step(i)
    lax.fori_loop(first, heads, one_head, 0)
    turn(work.line.steps)
    for start in range(0, length, BLOCK):
        at = pl.ds(start, BLOCK)
        tables = turns(meta_ref, at)
        for two in range(heads // 2):
            both = [
                jnp.concatenate([whole[2 * two, at], whole[2 * two + 1, at]], axis=1).astype(LOW)
                for whole in (dq, dk, dv)
            ]
            query, key = both[0].astype(F32), both[1].astype(F32)
            query = query * tables[0] + swap_lanes(query * tables[1])
            key = key * tables[2] + swap_lanes(key * tables[3])
            out_ref[at, pl.ds(2 * HD * two, 2 * HD)] = query.astype(LOW)
            out_ref[at, pl.ds(span + 2 * HD * two, 2 * HD)] = key.astype(LOW)
            out_ref[at, pl.ds(2 * span + 2 * HD * two, 2 * HD)] = both[2]
    work.finish(ffn_ref)
    if strided:

        def store(tile, total):
            total_ref[tile] = total

        line.finish(store)
    else:
        for t in range(planes):
            total_ref[pl.ds(t * part, part)] = own[t].astype(F32)
    swap.finish()

    def tile_wait(k, carry):
        tile_copy(k).wait_send()
        other = lax.rem(flat + count - k, count)
        remote(tile_ref.at[0], tiles_ref.at[other], tile_sems, k, here).wait_recv()
        return carry

    lax.fori_loop(1, count, tile_wait, 0)


def attention_backward(planes, chips, heads, strided, part, units, args):
    tokens, width = args[0].shape
    seqs = 2 * chips
    length, span = args[8].shape
    kept = [pltpu.VMEM(args[i].shape, args[i].dtype) for i in (3, 4, 5, 6, 7, 8, 9, 10, 11)]
    return call(
        functools.partial(attention_backward_kernel, planes, chips, heads, strided),
        "attention_backward",
        [
            shape(args[2].shape, F32),
            shape((tokens, width), F32),
            shape((length, 3 * span), LOW),
            shape((part if strided else span, width), F32),
            shape((chips, width // 2, units), LOW),
        ],
        args,
        [HBM] * 13,
        [HBM, VMEM, VMEM, VMEM, HBM],
        [
            pltpu.VMEM((seqs, tokens, width), LOW),
            pltpu.VMEM((seqs, tokens, 128), F32),
            *kept,
            *PairScatter.scratch(planes, tokens, width),
            pltpu.VMEM((heads, length, HD), LOW),
            *[pltpu.VMEM((heads, length, HD), F32)] * 3,
            pltpu.VMEM((length, span), LOW),
            pltpu.VMEM((planes, part, width), LOW),
            pltpu.VMEM((planes + 1, part, width), LOW),
            *pairs_of(chips, chips, chips, chips, planes * seqs),
            *PairScatter.sems(planes, width),
            *pairs_of(planes, planes, chips),
            pltpu.SemaphoreType.DMA((13,)),
        ],
        2,
    )


def body(
    hidden_in,
    segment_ids,
    position_ids,
    w_qkv,
    w_out,
    w_up,
    w_down,
    gain_attn,
    gain_attn_sub,
    gain_ffn,
    gain_ffn_sub,
    ema_qkv,
    ema_out,
    ema_up,
    ema_down,
    ema_gain_attn,
    ema_gain_attn_sub,
    ema_gain_ffn,
    ema_gain_ffn_sub,
    out_grad,
):
    _, tokens, width = hidden_in.shape
    planes, chips = lax.axis_size("dp"), lax.axis_size("chip")
    seqs = 2 * chips
    length = tokens * seqs
    heads = HEADS // seqs
    span = heads * HD
    part = w_qkv.shape[0]
    strided = part % HD == 0
    width_ff = w_down.shape[0] * planes * seqs
    seq_index = lax.axis_index(SEQ)

    def gain_rows(weight, gain):
        return (weight.astype(F32) * gain.astype(F32)[:, None]).astype(LOW)

    qkv_scaled = gain_rows(w_qkv, gain_attn)
    out_scaled = gain_rows(w_out, gain_attn_sub)
    down_scaled = gain_rows(w_down, gain_ffn_sub)
    if strided:
        qkv_send = qkv_scaled.reshape(part, 3, planes, seqs, HD).transpose(3, 0, 1, 2, 4)
    else:
        qkv_send = qkv_scaled.reshape(part, 3, seqs, span).transpose(2, 0, 1, 3)
    qkv_send = qkv_send.reshape(seqs, part, 3 * span)
    x_in = hidden_in[0].astype(F32)
    normed_one, scaler_one = moments(x_in)
    normed_low = normed_one.astype(LOW)
    gain_tile = jnp.zeros((8, 128), F32).at[0, :part].set(gain_ffn.astype(F32))

    if not strided:
        out_all = lax.all_gather(out_scaled, ALL, axis=0, tiled=True)
        out_scaled = lax.dynamic_slice_in_dim(out_all, seq_index * span, span, axis=0)

    grad_low = out_grad[0]
    (
        queries, keys, values, attended, log_total, out_sum,
        row_in, meta, qkv_mine, out_mine, gain_tiles, up_mine, grad_flat, tiles,
    ) = attention_forward(
        planes,
        chips,
        heads,
        strided,
        normed_low,
        token_tables(position_ids[0]),
        qkv_send,
        out_scaled,
        gain_tile,
        w_up,
        grad_low,
    )
    if up_mine.ndim == 3:
        up_mine = up_mine.transpose(1, 0, 2).reshape(width, -1)
    row_in = row_in.reshape(length, width)
    meta = meta.reshape(length, -1)
    qkv_mine = qkv_mine.reshape(width, 3 * span)
    out_mine = out_mine.reshape(span, width)
    attended = attended.reshape(length, span)
    tiles = jnp.sum(tiles, axis=0)
    column_sum = tiles[8:].reshape(width)
    sums = tiles[:2].T
    gain_three = gain_tiles[:, 0, :part].reshape(width)
    mean_two = sums[:, :1] / width
    scaler_two = lax.rsqrt(sums[:, 1:] / width - mean_two * mean_two + NORM_EPS)
    projected = scaler_two * (out_sum - mean_two * column_sum[None, :])
    hmid = x_in + projected
    normed_three, scaler_three = moments(hmid)
    ffn_in = (normed_three * gain_three).astype(LOW)

    grad_top = grad_low.astype(F32)
    units = w_up.shape[1]
    d_ffn_in, normed_four, down_mine, grad_up, down_slots = feed_forward(
        planes, chips, width_ff, ffn_in, up_mine, grad_flat, down_scaled
    )
    down_mine = down_mine.reshape(-1, width)
    if units % 128:
        grad_up = grad_up.reshape(width, chips, units).transpose(1, 0, 2)

    gain_part = jnp.sum(d_ffn_in * normed_three, axis=0).reshape(planes * seqs, 1, part)
    gain_part = jnp.pad(gain_part, ((0, 0), (0, 7), (0, 128 - part)))
    d_hmid = grad_top + norm_back(d_ffn_in * gain_three, normed_three, scaler_three)
    d_hmid_low = d_hmid.astype(LOW)
    d_hmid_wide = d_hmid_low.astype(F32)
    first_two = jnp.sum(d_hmid_wide * column_sum[None, :], axis=1, keepdims=True) / width
    second_two = jnp.sum(d_hmid_wide * projected, axis=1, keepdims=True) / width
    token_stats = jnp.concatenate([mean_two, scaler_two, first_two, second_two], axis=1)
    gain_part, ffn_out, d_qkv, sum_out, upper_slots = attention_backward(
        planes,
        chips,
        heads,
        strided,
        part,
        units,
        (
            d_hmid_low,
            jnp.pad(token_stats, ((0, 0), (0, 124))),
            gain_part,
            normed_four,
            down_mine,
            queries,
            keys,
            values,
            attended,
            out_mine,
            log_total,
            meta,
            grad_up,
        ),
    )
    output = (hmid + ffn_out).astype(LOW)[None]
    grad_gain_three = jnp.sum(gain_part, axis=0)[0, :part]
    grad_qkv = token_product(row_in, d_qkv).astype(LOW)
    d_in, sum_qkv, grad_gain_one, lower_slots = in_scatter(
        planes,
        chips,
        heads,
        strided,
        d_qkv.reshape(seqs, tokens, 3 * span),
        qkv_mine,
        grad_qkv.reshape(planes, seqs, part, 3 * span),
        grad_up,
        w_qkv,
        jnp.broadcast_to(gain_attn.astype(F32)[:, None], (part, 128)),
        units,
    )
    grad_gain_one = grad_gain_one[:, 0]
    sum_up = jnp.concatenate(
        [jnp.sum(slots.astype(F32), axis=0) for slots in (upper_slots, lower_slots)], axis=0
    )
    sum_down = jnp.sum(down_slots.astype(F32), axis=0)
    input_grad = (d_hmid + norm_back(d_in, normed_one, scaler_one)).astype(LOW)[None]

    if not strided:
        spread = lax.dynamic_update_slice_in_dim(
            jnp.zeros((width, width), LOW), sum_out.astype(LOW), seq_index * span, axis=0
        )
        sum_out = lax.psum_scatter(spread, ALL, scatter_dimension=0, tiled=True).astype(F32)

    def finish(total, weight, gain):
        wide = weight.astype(F32)
        return (total * gain.astype(F32)[:, None], jnp.sum(total * wide, axis=1))

    sum_out, grad_gain_two = finish(sum_out, w_out, gain_attn_sub)
    sum_down, grad_gain_four = finish(sum_down, w_down, gain_ffn_sub)

    def averaged(average, weight):
        return EMA_DECAY * average + (1.0 - EMA_DECAY) * weight.astype(F32)

    return (
        output,
        input_grad,
        sum_qkv,
        sum_out,
        sum_up,
        sum_down,
        grad_gain_one,
        grad_gain_two,
        grad_gain_three,
        grad_gain_four,
        averaged(ema_qkv, w_qkv),
        averaged(ema_out, w_out),
        averaged(ema_up, w_up),
        averaged(ema_down, w_down),
        averaged(ema_gain_attn, gain_attn),
        averaged(ema_gain_attn_sub, gain_attn_sub),
        averaged(ema_gain_ffn, gain_ffn),
        averaged(ema_gain_ffn_sub, gain_ffn_sub),
    )


def solution(mesh):
    split = Mesh(
        mesh.devices.reshape(mesh.shape["dp"], mesh.shape["seq"] // 2, 2), ("dp", "chip", "core")
    )
    tokens = P("dp", SEQ, None)
    ids = P("dp", SEQ)
    rows = P(ALL, None)
    columns = P(None, ALL)
    vector = P(ALL)
    weights = (rows, rows, columns, rows)
    gains = (vector,) * 4
    return jax.shard_map(
        body,
        mesh=split,
        in_specs=(tokens, ids, ids, *weights, *gains, *weights, *gains, tokens),
        out_specs=(tokens, tokens, *weights, *gains, *weights, *gains),
        check_vma=False,
    )
```

```python
import functools
import math

import jax
import jax.numpy as jnp
from jax import lax
from jax.experimental import pallas as pl
from jax.experimental.pallas import tpu as pltpu
from jax.sharding import Mesh
from jax.sharding import PartitionSpec as P

HEADS = 32
HD = 64

NEG_FILL = -1000000000.0
NORM_EPS = 1e-05
EMA_DECAY = 0.7
LOW = jnp.bfloat16
F32 = jnp.float32
SEQ = ("chip", "core")
TP = ("dp", "core")
ALL = ("dp", "chip", "core")


def moments(values):
    mean = jnp.mean(values, axis=-1, keepdims=True)
    centered = values - mean
    scaler = lax.rsqrt(jnp.mean(centered * centered, axis=-1, keepdims=True) + NORM_EPS)
    return (centered * scaler, scaler)


def norm_back(scaled_grad, normed, scaler):
    first_mean = jnp.mean(scaled_grad, axis=-1, keepdims=True)
    second_mean = jnp.mean(scaled_grad * normed, axis=-1, keepdims=True)
    return scaler * (scaled_grad - first_mean - normed * second_mean)


def token_tables(positions):
    half_count = HD // 2
    index_half = jnp.arange(half_count).astype(F32)
    inverse = jnp.exp(-(2.0 * index_half / HD) * math.log(10000.0))
    decay_base = (2.0 * index_half + 0.4 * HD) / (1.4 * HD)
    where_at = positions.astype(F32)[:, None]
    angles = where_at * inverse[None, :]
    factor = jnp.exp(where_at / 512.0 * jnp.log(decay_base)[None, :])
    sign_row = jnp.where(jnp.arange(HD) % 2 == 0, -1.0, 1.0).astype(F32)
    cosine = jnp.repeat(jnp.cos(angles), 2, axis=1)
    sine = jnp.repeat(jnp.sin(angles), 2, axis=1) * sign_row[None, :]
    factor = jnp.repeat(factor, 2, axis=1)
    grow = factor * HD ** (-0.5)
    where_block = jnp.broadcast_to(where_at, (positions.shape[0], HD))
    return jnp.concatenate(
        [cosine * grow, sine * grow, HD**0.5 / (factor * factor), where_block], axis=1
    )


def dot(left_op, right_op):
    return jnp.dot(left_op, right_op, preferred_element_type=F32)


def rows_product(operand, weight_rows):
    return lax.dot_general(
        operand, weight_rows, (((1,), (1,)), ((), ())), preferred_element_type=F32
    )


def token_product(left_op, right_op):
    return lax.dot_general(left_op, right_op, (((0,), (0,)), ((), ())), preferred_element_type=F32)


MESH = pl.DeviceIdType.MESH
HBM = pl.BlockSpec(memory_space=pl.ANY)
VMEM = pl.BlockSpec(memory_space=pltpu.VMEM)
VMEM_BYTES = 60 * 1024 * 1024


def shape(dims, kind):
    return jax.ShapeDtypeStruct(dims, kind)


def pairs_of(*counts):
    return [pltpu.SemaphoreType.DMA((count,)) for count in counts for _ in range(2)]


def call(kernel, name, outs, args, in_specs, out_specs, scratch, collective=None):
    return pl.pallas_call(
        kernel,
        name=name,
        out_shape=outs,
        in_specs=in_specs,
        out_specs=out_specs,
        scratch_shapes=scratch,
        compiler_params=pltpu.CompilerParams(
            collective_id=collective,
            has_side_effects=collective is not None,
            vmem_limit_bytes=VMEM_BYTES,
        ),
    )(*args)


def place():
    return (lax.axis_index("dp"), lax.axis_index("chip"), lax.axis_index("core"))


def remote(source, target, sems, index, device):
    return pltpu.make_async_remote_copy(
        src_ref=source,
        dst_ref=target,
        send_sem=sems[0].at[index],
        recv_sem=sems[1].at[index],
        device_id=device,
        device_id_type=MESH,
    )


def greet(barrier, devices):
    for device in devices:
        pl.semaphore_signal(barrier, inc=1, device_id=device, device_id_type=MESH)


def greet_line(barrier, planes, here):
    z, c, core = here

    @pl.when(z < planes - 1)
    def _():
        greet(barrier, [(z + 1, c, core)])

    @pl.when(z > 0)
    def _():
        greet(barrier, [(z - 1, c, core)])


def line_peers(planes, here):
    z = here[0]
    return (2 * planes - 2 - z) // planes + (z + planes - 1) // planes


def chip_peers(chips, here):
    z, c, core = here
    return [(z, lax.rem(c + k, chips), core) for k in range(1, chips)]


def plane_peers(chips, here):
    z, c, core = here
    seqs = 2 * chips
    me = 2 * c + core
    ids = [lax.rem(me + k, seqs) for k in range(1, seqs)]
    return [(z, index // 2, lax.rem(index, 2)) for index in ids]


def column_block(whole, units, index):
    if len(whole.shape) == 3:
        return whole.at[index]
    return whole.at[:, pl.ds(pl.multiple_of(index * units, 128), units)]


def half_block(whole, slots, index, half):
    rows, units = slots.shape[1:]
    at = pl.ds(half * rows, rows)
    if len(whole.shape) == 3:
        return whole.at[index, at]
    return whole.at[at, pl.ds(pl.multiple_of(index * units, 128), units)]


class ChipSwap:
    def __init__(self, chips, here, source, slots, sems):
        z, c, core = here
        self.sends = [
            remote(source(device[1]), slots.at[c], sems, k, device)
            for k, device in enumerate(chip_peers(chips, here), 1)
        ]
        self.waits = [
            remote(source(c), slots.at[lax.rem(c + chips - k, chips)], sems, k, here)
            for k in range(1, chips)
        ]
        self.keep = (source(c), slots.at[c])

    def start(self, local):
        for copy in self.sends:
            copy.start()
        self.held = pltpu.make_async_copy(*self.keep, local)
        self.held.start()

    def finish(self):
        self.held.wait()
        for send, wait in zip(self.sends, self.waits):
            send.wait_send()
            wait.wait_recv()


class ChipGather:
    def __init__(self, chips, here, source, target, sems):
        z, c, core = here
        self.here, self.sems, self.relayed = here, sems, chips == 4
        if not self.relayed:
            self.sends = [
                remote(source(None), target(c, None), sems, k, device)
                for k, device in enumerate(chip_peers(chips, here), 1)
            ]
            self.arrivals = [
                (lax.rem(c + chips - k, chips), None, k) for k in range(1, chips)
            ]
        else:
            beside = c + 1 - 2 * lax.rem(c, 2)
            above = c + 2 - 4 * (c // 2)
            to_beside, to_above = (z, beside, core), (z, above, core)
            self.sends = [
                remote(source(0), target(c, 0), sems, 0, to_beside),
                remote(source(1), target(c, 1), sems, 3, to_above),
                remote(source(1), target(c, 1), sems, 1, to_beside),
                remote(source(0), target(c, 0), sems, 2, to_above),
            ]
            self.relays = [
                remote(target(beside, 0), target(beside, 0), sems, 4, to_above),
                remote(target(above, 1), target(above, 1), sems, 5, to_beside),
            ]
            self.arrivals = [
                (beside, 0, 0), (above, 1, 3), (beside, 1, 1), (above, 0, 2),
                (3 - c, 0, 4), (3 - c, 1, 5),
            ]
        self.target = target

    def start(self):
        for copy in self.sends:
            copy.start()

    def arrive(self, i):
        chip, half, index = self.arrivals[i]
        block = self.target(chip, half)
        remote(block, block, self.sems, index, self.here).wait_recv()
        if self.relayed and i < 2:
            self.relays[i].start()

    def relay(self):
        for i in range(2 if self.relayed else 0):
            self.arrive(i)

    def rest(self):
        return range(2 if self.relayed else 0, len(self.arrivals))

    def finish(self):
        for i in self.rest():
            self.arrive(i)
        self.sent()

    def sent(self):
        for copy in [*self.sends, *(self.relays if self.relayed else [])]:
            copy.wait_send()

    @staticmethod
    def count(chips):
        return max(chips, 6)


class PlaneGather:
    def __init__(self, chips, here, block, out, far, near):
        z, c, core = here
        self.here, self.block, self.out, self.near = here, block, out, near
        self.me = 2 * c + core
        self.partner = (z, c, 1 - core)
        self.size = block.shape[0] // 2
        self.chips = ChipGather(
            chips,
            here,
            self.piece,
            lambda chip, half: self.place(2 * chip + core, half),
            far,
        )
        self.own = remote(block, out.at[self.me], near, len(self.chips.arrivals), self.partner)

    def rows(self, half):
        return pl.ds(half * self.size, self.size)

    def piece(self, half):
        return self.block if half is None else self.block.at[self.rows(half)]

    def place(self, index, half):
        return self.out.at[index] if half is None else self.out.at[index, self.rows(half)]

    def start(self):
        self.chips.start()
        self.own.start()

    def passed(self, i, other=0):
        chip, half, _ = self.chips.arrivals[i]
        core = self.here[2]
        block = self.place(2 * chip + (1 - core if other else core), half)
        return remote(block, block, self.near, i, self.partner)

    def relay(self):
        for i in range(2 if self.chips.relayed else 0):
            self.chips.arrive(i)
            self.passed(i).start()

    def forward(self):
        for i in self.chips.rest():
            self.chips.arrive(i)
            self.passed(i).start()

    def finish(self):
        self.chips.sent()
        self.own.wait_send()
        mine = self.out.at[2 * self.here[1] + 1 - self.here[2]]
        remote(mine, mine, self.near, len(self.chips.arrivals), self.partner).wait_recv()
        for i in range(len(self.chips.arrivals)):
            self.passed(i).wait_send()
            self.passed(i, 1).wait_recv()

    @staticmethod
    def sems(chips):
        return pairs_of(ChipGather.count(chips), ChipGather.count(chips) + 1)


def row_half(ref, half):
    if half is None:
        return ref
    size = ref.shape[0] // 2
    return ref.at[pl.ds(half * size, size)]


class LineGather:
    def __init__(self, planes, here, parts, up, down):
        self.planes, self.here, self.parts = planes, here, parts
        self.up, self.down = up, down
        self.count = len(parts(here[0]))

    def upward(self, d, p):
        z, c, core = self.here
        block = self.parts(z - d)[p]
        return remote(block, block, self.up, d * self.count + p, (z + 1, c, core))

    def downward(self, d, p):
        z, c, core = self.here
        block = self.parts(z + d)[p]
        return remote(block, block, self.down, d * self.count + p, (z - 1, c, core))

    def each(self, d, p, act):
        z, planes = self.here[0], self.planes
        pl.when((z < planes - 1) & (z - d >= 0))(lambda: act(self.upward(d, p)))
        pl.when((z > 0) & (z + d < planes))(lambda: act(self.downward(d, p)))

    def start(self):
        for p in range(self.count):
            self.each(0, p, lambda copy: copy.start())

    def step(self, d, arrived=None):
        z, planes = self.here[0], self.planes

        def below(p):
            block = self.parts(z - d)[p]
            remote(block, block, self.up, (d - 1) * self.count + p, self.here).wait_recv()
            if d < planes - 1:
                pl.when(z < planes - 1)(lambda: self.upward(d, p).start())
            if arrived is not None:
                arrived(z - d, p)

        def above(p):
            block = self.parts(z + d)[p]
            remote(block, block, self.down, (d - 1) * self.count + p, self.here).wait_recv()
            if d < planes - 1:
                pl.when(z > 0)(lambda: self.downward(d, p).start())
            if arrived is not None:
                arrived(z + d, p)

        for p in range(self.count):
            pl.when(z - d >= 0)(lambda p=p: below(p))
            pl.when(z + d < planes)(lambda p=p: above(p))

    def finish(self):
        for d in range(self.planes - 1):
            for p in range(self.count):
                self.each(d, p, lambda copy: copy.wait_send())


class GroupGather:
    PARTS = 2

    def __init__(self, planes, here, block, out, up, down, near):
        self.planes, self.here, self.block, self.out, self.near = planes, here, block, out, near
        self.partner = (here[0], here[1], 1 - here[2])
        size = block.shape[0] // self.PARTS
        self.slices = [pl.ds(p * size, size) for p in range(self.PARTS)]
        core = here[2]
        self.line = LineGather(planes, here, lambda t: self.parts(t, core), up, down)

    def parts(self, t, core):
        return [self.out.at[t, core, rows] for rows in self.slices]

    def passed(self, t, p):
        block = self.parts(t, self.here[2])[p]
        return remote(block, block, self.near, t * self.PARTS + p, self.partner)

    def start(self, local):
        z, _, core = self.here
        keep = pltpu.make_async_copy(self.block, self.out.at[z, core], local)
        keep.start()
        keep.wait()
        self.line.start()
        for p in range(self.PARTS):
            self.passed(z, p).start()

    def step(self, d):
        self.line.step(d, lambda t, p: self.passed(t, p).start())

    def other(self, t):
        for p in range(self.PARTS):
            block = self.parts(t, 1 - self.here[2])[p]
            remote(block, block, self.near, t * self.PARTS + p, self.partner).wait_recv()

    def finish(self):
        self.line.finish()
        for t in range(self.planes):
            for p in range(self.PARTS):
                self.passed(t, p).wait_send()

    @classmethod
    def sems(cls, planes):
        return pairs_of(*[planes * cls.PARTS] * 3)


COLUMNS = 512


def product(left, right, columns, turned):
    if turned:
        return lax.dot_general(
            left, right[columns, :], (((1,), (1,)), ((), ())), preferred_element_type=F32
        )
    return jnp.dot(left, right[:, columns], preferred_element_type=F32)


class PlaneScatter:
    def __init__(self, chips, here, left, right, turned, buffers, near, far):
        self.chips, self.here = chips, here
        self.left, self.right, self.turned = left, right, turned
        self.near_out, self.near_in, self.far_out, self.far_in = buffers
        self.near, self.far = near, far
        self.tokens, width = self.near_out.shape[1:]
        self.tiles = [pl.ds(at, COLUMNS) for at in range(0, width, COLUMNS)]
        self.order = [*range(1, chips), 0]

    def target(self, k):
        return lax.rem(self.here[1] + k, self.chips)

    def near_copy(self, i):
        z, c, core = self.here
        at = (slice(None), slice(None), self.tiles[i])
        return remote(self.near_out.at[at], self.near_in.at[at], self.near, i, (z, c, 1 - core))

    def far_copy(self, k, i):
        z, _, core = self.here
        at = (k, slice(None), self.tiles[i])
        index = k * len(self.tiles) + i
        return remote(
            self.far_out.at[at], self.far_in.at[at], self.far, index, (z, self.target(k), core)
        )

    def rows(self, position):
        return slice(position * self.tokens, (position + 1) * self.tokens)

    def start(self):
        core = self.here[2]
        blocks = [self.left[2 * self.target(k) + 1 - core] for k in self.order]
        left = jnp.concatenate(blocks, axis=0)
        for i, columns in enumerate(self.tiles):
            part = product(left, self.right, columns, self.turned).astype(LOW)
            for position, k in enumerate(self.order):
                self.near_out[k, :, columns] = part[self.rows(position)]
            self.near_copy(i).start()
        blocks = [self.left[2 * self.target(k) + core] for k in self.order]
        left = jnp.concatenate(blocks, axis=0)
        for i, columns in enumerate(self.tiles):
            part = product(left, self.right, columns, self.turned)
            self.near_copy(i).wait_recv()
            for position, k in enumerate(self.order):
                self.far_out[k, :, columns] = (
                    part[self.rows(position)] + self.near_in[k, :, columns].astype(F32)
                ).astype(LOW)
                if k:
                    self.far_copy(k, i).start()

    def finish(self, out_ref):
        for i, columns in enumerate(self.tiles):
            total = self.far_out[0, :, columns].astype(F32)
            for k in range(1, self.chips):
                self.far_copy(k, i).wait_recv()
                total = total + self.far_in[k, :, columns].astype(F32)
            out_ref[:, columns] = total
        for i in range(len(self.tiles)):
            self.near_copy(i).wait_send()
            for k in range(1, self.chips):
                self.far_copy(k, i).wait_send()

    @staticmethod
    def scratch(chips, tokens, width):
        return [pltpu.VMEM((chips, tokens, width), LOW)] * 4

    @staticmethod
    def sems(chips, width):
        return pairs_of(width // COLUMNS, chips * (width // COLUMNS))


class LineScatter:
    def __init__(self, planes, here, count, part, tiles, own, slots, up, down):
        self.planes, self.here, self.count = planes, here, count
        self.part, self.tiles, self.own, self.slots = part, tiles, own, slots
        self.up, self.down = up, down
        self.steps = (planes - 1) * count

    def upward(self, t, p):
        z, c, core = self.here
        block = self.slots.at[(t, *self.part(p))]
        return remote(block, block, self.up, t * self.count + p, (z + 1, c, core))

    def downward(self, t, p, last):
        z, c, core = self.here
        block = self.slots.at[(t, *self.part(p))]
        target = self.slots.at[(self.planes, *self.part(p))] if last else block
        return remote(block, target, self.down, t * self.count + p, (z - 1, c, core))

    def add(self, t, p, fresh):
        for tile in self.tiles(p):
            total = self.own(t, tile)
            if not fresh:
                total = total + self.slots[(t, *tile)].astype(F32)
            self.slots[(t, *tile)] = total.astype(LOW)

    def step(self, i):
        z, planes, count = self.here[0], self.planes, self.count
        rise, fall = i - z, i - (planes - 1 - z)

        @pl.when((rise >= 0) & (rise < (planes - 1 - z) * count))
        def _():
            t, p = planes - 1 - rise // count, lax.rem(rise, count)

            @pl.when(z > 0)
            def _():
                self.upward(t, p).wait_recv()
                self.add(t, p, False)

            @pl.when(z == 0)
            def _():
                self.add(t, p, True)

            self.upward(t, p).start()

        @pl.when((fall >= 0) & (fall < z * count))
        def _():
            t, p = fall // count, lax.rem(fall, count)

            @pl.when(z < planes - 1)
            def _():
                self.downward(t, p, False).wait_recv()
                self.add(t, p, False)

            @pl.when(z == planes - 1)
            def _():
                self.add(t, p, True)

            pl.when(t == z - 1)(lambda: self.downward(t, p, True).start())
            pl.when(t < z - 1)(lambda: self.downward(t, p, False).start())

    def finish(self, store):
        z, planes = self.here[0], self.planes

        def total(tile, *slots):
            value = self.own(z, tile)
            for slot in slots:
                value = value + self.slots[(slot, *tile)].astype(F32)
            store(tile, value)

        for p in range(self.count):
            tiles = self.tiles(p)

            @pl.when(z > 0)
            def _(p=p):
                self.upward(z, p).wait_recv()

            @pl.when(z < planes - 1)
            def _(p=p):
                self.downward(z, p, True).wait_recv()

            @pl.when((z > 0) & (z < planes - 1))
            def _(tiles=tiles):
                for tile in tiles:
                    total(tile, z, planes)

            @pl.when(z == 0)
            def _(tiles=tiles):
                for tile in tiles:
                    total(tile, planes)

            @pl.when(z == planes - 1)
            def _(tiles=tiles):
                for tile in tiles:
                    total(tile, z)

        for t in range(planes):
            for p in range(self.count):
                pl.when(z < t)(lambda t=t, p=p: self.upward(t, p).wait_send())
                pl.when(z > t)(lambda t=t, p=p: self.downward(t, p, False).wait_send())


def row_tiles(count, size):
    return [pl.ds(at, size) for at in range(0, count, size)]


def in_scatter_kernel(
    planes, chips, heads, strided, left_ref, right_ref, grad_ref, up_ref, weight_ref, gain_ref,
    out_ref, total_ref, gains_ref, slots_ref,
    near_out, near_in, far_out, far_in, sums, mine, parts, *sems,
):
    here = place()
    z, c, core = here
    seqs = 2 * chips
    me = 2 * c + core
    near, far, up, down, swap_sems, chip_sems = [sems[2 * i : 2 * i + 2] for i in range(6)]
    barrier = pltpu.get_barrier_semaphore()
    peers = plane_peers(chips, here)
    greet(barrier, peers)
    greet_line(barrier, planes, here)
    pl.semaphore_wait(barrier, len(peers) + line_peers(planes, here))
    half = seqs // 2
    line = LineScatter(
        planes,
        here,
        2,
        lambda p: (pl.ds(p * half, half),),
        lambda p: [(pl.ds(p * half + i, 1),) for i in range(half)],
        lambda t, tile: grad_ref[(t, *tile)].astype(F32),
        sums,
        up,
        down,
    )
    line.step(0)
    work = PlaneScatter(
        chips, here, left_ref, right_ref, True, (near_out, near_in, far_out, far_in), near, far
    )
    work.start()
    ups = ChipSwap(
        chips, here, lambda index: half_block(up_ref, slots_ref, index, 1), slots_ref, chip_sems
    )
    ups.start(sems[12].at[0])
    for i in range(1, line.steps):
        line.step(i)

    def store(tile, total):
        mine[tile] = total.astype(LOW)

    line.finish(store)
    swaps = [
        remote(mine.at[2 * device[1] + device[2]], parts.at[me], swap_sems, k, device)
        for k, device in enumerate(peers, 1)
    ]
    for copy in swaps:
        copy.start()
    parts[me] = mine[me]
    work.finish(out_ref)
    for k in range(1, seqs):
        swaps[k - 1].wait_send()
        index = lax.rem(me + seqs - k, seqs)
        remote(mine.at[0], parts.at[index], swap_sems, k, here).wait_recv()
    span = heads * HD
    width = seqs * span
    gain = gain_ref[:, pl.ds(0, 1)]
    summed = jnp.zeros(gain.shape, F32)
    for i in range(3):
        step, pieces = (seqs * HD, planes) if strided else (width, 1)
        size = step // seqs
        for piece in range(pieces):
            at = i * span + piece * size
            columns = pl.ds(i * width + piece * step, step)
            total = jnp.concatenate(
                [parts[s, :, pl.ds(at, size)].astype(F32) for s in range(seqs)], axis=1
            )
            weight = weight_ref[:, columns].astype(F32)
            summed = summed + jnp.sum(total * weight, axis=1, keepdims=True)
            total_ref[:, columns] = total * gain
    gains_ref[...] = jnp.broadcast_to(summed, gains_ref.shape)
    ups.finish()


def in_scatter(planes, chips, heads, strided, left, right, grads, up_grads, weight, gain, units):
    _, tokens, _ = left.shape
    width = right.shape[0]
    seqs = 2 * chips
    part, wide = grads.shape[2:]
    return call(
        functools.partial(in_scatter_kernel, planes, chips, heads, strided),
        "in_scatter",
        [
            shape((tokens, width), F32),
            shape(weight.shape, F32),
            shape((part, 128), F32),
            shape((chips, width // 2, units), LOW),
        ],
        (left, right, grads, up_grads, weight, gain),
        [VMEM, VMEM, VMEM, HBM, VMEM, VMEM],
        [VMEM, VMEM, VMEM, HBM],
        [
            *PlaneScatter.scratch(chips, tokens, width),
            pltpu.VMEM((planes + 1, seqs, part, wide), LOW),
            *[pltpu.VMEM((seqs, part, wide), LOW)] * 2,
            *PlaneScatter.sems(chips, width),
            *pairs_of(2 * planes, 2 * planes, seqs, chips),
            pltpu.SemaphoreType.DMA((1,)),
        ],
        4,
    )


class PairScatter:
    PARTS = 2

    def __init__(self, planes, here, left, right, turned, buffers, near, up, down):
        self.planes, self.here = planes, here
        self.left, self.right, self.turned = left, right, turned
        self.near_out, self.own, slots = buffers
        self.near = near
        self.tokens, width = self.near_out.shape[1:]
        self.tiles = [pl.ds(at, COLUMNS) for at in range(0, width, COLUMNS)]
        size = width // self.PARTS

        def part(p):
            at = p * size if isinstance(p, int) else pl.multiple_of(p * size, 128)
            return (slice(None), pl.ds(at, size))

        self.line = LineScatter(
            planes,
            here,
            self.PARTS,
            part,
            lambda p: [(rows, part(p)[1]) for rows in row_tiles(self.tokens, 32)],
            lambda t, tile: self.own[(t, *tile)].astype(F32),
            slots,
            up,
            down,
        )

    def near_copy(self, i):
        z, c, core = self.here
        at = (slice(None), slice(None), self.tiles[i])
        return remote(self.near_out.at[at], self.own.at[at], self.near, i, (z, c, 1 - core))

    def start(self):
        core, tokens = self.here[2], self.tokens
        left = jnp.concatenate([self.left[t, 1 - core] for t in range(self.planes)], axis=0)
        for i, columns in enumerate(self.tiles):
            part = product(left, self.right, columns, self.turned).astype(LOW)
            for t in range(self.planes):
                self.near_out[t, :, columns] = part[t * tokens : (t + 1) * tokens]
            self.near_copy(i).start()
        left = jnp.concatenate([self.left[t, core] for t in range(self.planes)], axis=0)
        for i, columns in enumerate(self.tiles):
            part = product(left, self.right, columns, self.turned)
            self.near_copy(i).wait_recv()
            for t in range(self.planes):
                self.own[t, :, columns] = (
                    part[t * tokens : (t + 1) * tokens] + self.own[t, :, columns].astype(F32)
                ).astype(LOW)
        self.line.step(0)

    def finish(self, out_ref):
        def store(tile, total):
            out_ref[tile] = total

        self.line.finish(store)
        for i in range(len(self.tiles)):
            self.near_copy(i).wait_send()

    @staticmethod
    def scratch(planes, tokens, width):
        return [
            *[pltpu.VMEM((planes, tokens, width), LOW)] * 2,
            pltpu.VMEM((planes + 1, tokens, width), LOW),
        ]

    @classmethod
    def sems(cls, planes, width):
        return pairs_of(width // COLUMNS, cls.PARTS * planes, cls.PARTS * planes)


def feed_forward_kernel(
    planes, chips, width_ff, x_ref, up_ref, grads_ref, down_ref,
    out_ref, normed_ref, downs_ref, gup_ref, slots_ref,
    rows, ups, grads, downs, back, act, slope, stat, stat_out, stat_in,
    normed, d_up, near_out, own, sums, gup, gdown, *sems,
):
    here = place()
    z, c, core = here
    count = 2 * planes
    me = 2 * z + core
    up, down, near, chip_sems, stat_sems, pair, rise, fall, swap_sems = [
        sems[2 * i : 2 * i + 2] for i in range(9)
    ]
    local = sems[18]
    tokens, width = x_ref.shape
    units = ups.shape[1]
    load_up = pltpu.make_async_copy(up_ref, ups, local.at[0])
    load_grads = pltpu.make_async_copy(grads_ref, grads, local.at[1])
    load_up.start()
    load_grads.start()
    barrier = pltpu.get_barrier_semaphore()
    ids = [lax.rem(me + k, count) for k in range(1, count)]
    group_peers = [(index // 2, c, lax.rem(index, 2)) for index in ids]
    peers = [*group_peers, *chip_peers(chips, here)]
    greet(barrier, peers)
    pl.semaphore_wait(barrier, len(peers))

    group = GroupGather(planes, here, x_ref, rows, up, down, near)
    group.start(local.at[2])
    keep = pltpu.make_async_copy(down_ref, downs.at[c], local.at[3])
    keep.start()
    weights = ChipGather(
        chips,
        here,
        lambda half: row_half(down_ref, half),
        lambda chip, half: row_half(downs.at[chip], half),
        chip_sems,
    )
    weights.start()
    load_up.wait()

    step = tokens
    lane = lax.broadcasted_iota(jnp.int32, (step, 128), 1)

    def forward(t):
        group.other(t)
        block = rows[t].reshape(2 * tokens, width)
        for at in range(0, units, COLUMNS):
            columns = pl.ds(at, COLUMNS)
            act[t, :, columns] = jnp.dot(block, ups[:, columns], preferred_element_type=F32)

        def some(i, carry):
            at = pl.ds(pl.multiple_of(i * step, step), step)
            value = act[t, at]
            phi = 0.5 * (1.0 + lax.erf(value * math.sqrt(0.5)))
            result = value * phi
            act[t, at] = result
            slope[t, at] = phi + value * (
                jnp.exp(value * value * -0.5) * (1.0 / math.sqrt(2.0 * math.pi))
            )
            total = jnp.sum(result, axis=1, keepdims=True)
            square = jnp.sum(result * result, axis=1, keepdims=True)
            stat[t, at] = jnp.where(lane == 0, total, jnp.where(lane == 1, square, 0.0))
            return carry

        lax.fori_loop(0, 2 * tokens // step, some, 0)

    forward(z)
    for d in range(1, planes):
        group.step(d)
        if d == 2:
            weights.relay()
        if d > 1:
            pl.when(z - d + 1 >= 0)(lambda d=d: forward(z - d + 1))
            pl.when(z + d - 1 < planes)(lambda d=d: forward(z + d - 1))
    pl.when(z - planes + 1 >= 0)(lambda: forward(z - planes + 1))
    pl.when(z + planes - 1 < planes)(lambda: forward(z + planes - 1))
    group.finish()
    keep.wait()
    load_grads.wait()
    weights.finish()
    out_downs = pltpu.make_async_copy(downs, downs_ref, local.at[4])
    out_downs.start()

    def backward(t, carry):
        block = grads[t].reshape(2 * tokens, width)
        size = units // chips
        for chip in range(chips):
            columns = pl.ds(chip * size, size)
            back[t, :, columns] = rows_product(block, downs[chip])

        def some(i, inner):
            at = pl.ds(pl.multiple_of(i * step, step), step)
            value = back[t, at]
            cross = jnp.sum(value * act[t, at], axis=1, keepdims=True)
            total = jnp.sum(value, axis=1, keepdims=True)
            stat[t, at] = jnp.where(lane == 2, cross, jnp.where(lane == 3, total, stat[t, at]))
            return inner

        lax.fori_loop(0, 2 * tokens // step, some, 0)
        for half in range(2):
            turned = stat[t, pl.ds(half * tokens, tokens)].T
            stat_out[2 * t + half] = turned[:8]
        return carry

    lax.fori_loop(0, planes, backward, 0)
    copies = [
        remote(stat_out, stat_in.at[k], stat_sems, k, device)
        for k, device in enumerate(group_peers, 1)
    ]
    for copy in copies:
        copy.start()
    for copy in copies:
        copy.wait_send()
        copy.wait_recv()

    def finish(t, carry):
        for half in range(2):
            total = stat_out[2 * t + half]
            for k in range(1, count):
                total = total + stat_in[k, 2 * t + half]
            mean, square, cross, first = (total[i : i + 1] / width_ff for i in range(4))
            scaler = lax.rsqrt(square - mean * mean + NORM_EPS)
            second = scaler * (cross - mean * first)
            figures = [scaler, -mean * scaler, scaler * first, scaler * second]
            padded = jnp.concatenate([*figures, jnp.zeros((128 - 4, tokens), F32)], axis=0)
            stat[t, pl.ds(half * tokens, tokens)] = padded.T

        def some(i, inner):
            at = pl.ds(pl.multiple_of(i * step, step), step)
            figures = stat[t, at]
            scaler, shift, first, second = (figures[:, j : j + 1] for j in range(4))
            unit = act[t, at] * scaler + shift
            normed[t, at] = unit.astype(LOW)
            d_act = back[t, at] * scaler - first - unit * second
            d_up[t, at] = (d_act * slope[t, at]).astype(LOW)
            return inner

        lax.fori_loop(0, 2 * tokens // step, some, 0)
        return carry

    lax.fori_loop(0, planes, finish, 0)
    out_normed = pltpu.make_async_copy(normed, normed_ref, local.at[5])
    out_normed.start()
    work = PairScatter(
        planes, here, Halves(d_up, tokens), ups, True, (near_out, own, sums), pair, rise, fall
    )
    work.start()

    flat_normed, flat_d_up = (
        whole[...].reshape(planes * 2 * tokens, units) for whole in (normed, d_up)
    )
    size = units // chips
    swap = ChipSwap(chips, here, lambda index: gdown.at[index], slots_ref, swap_sems)
    turns_left = list(range(1, work.line.steps))

    def turn():
        if turns_left:
            work.line.step(turns_left.pop(0))

    together = max(1, 256 // size)
    for chip in range(0, chips, together):
        left = flat_normed[:, chip * size : (chip + together) * size]
        for at in range(0, width, COLUMNS):
            columns = pl.ds(at, COLUMNS)
            right = grads[:, :, :, columns].reshape(planes * 2 * tokens, COLUMNS)
            term = token_product(left, right).astype(LOW)
            for i in range(together):
                gdown[chip + i, :, columns] = term[i * size : (i + 1) * size]
        if chip // together % 2:
            turn()
    swap.start(local.at[6])
    chunk = gup.shape[1]
    out_gups = [
        pltpu.make_async_copy(
            gup.at[i % 2], gup_ref.at[pl.ds(i * chunk, chunk)], local.at[7 + i % 2]
        )
        for i in range(width // chunk)
    ]
    for i in range(width // chunk):
        if i % 2 == 0:
            turn()
        left = rows[:, :, :, pl.ds(i * chunk, chunk)].reshape(planes * 2 * tokens, chunk)
        term = token_product(left, flat_d_up).astype(LOW)
        if i > 1:
            out_gups[i - 2].wait()
        gup[i % 2] = term
        out_gups[i].start()
    while turns_left:
        turn()
    work.finish(out_ref)
    swap.finish()
    out_downs.wait()
    out_normed.wait()
    for copy in out_gups[-2:]:
        copy.wait()


class Halves:
    def __init__(self, whole, tokens):
        self.whole, self.tokens = whole, tokens

    def __getitem__(self, at):
        t, core = at
        rows = pl.ds(pl.multiple_of(core * self.tokens, self.tokens), self.tokens)
        return self.whole[t, rows]


def feed_forward(planes, chips, width_ff, x_block, up_mine, grads, down_block):
    tokens, width = x_block.shape
    units = up_mine.shape[1]
    size = down_block.shape[0]
    wide = (planes, 2 * tokens, units)
    return call(
        functools.partial(feed_forward_kernel, planes, chips, width_ff),
        "feed_forward",
        [
            shape((tokens, width), F32),
            shape(wide, LOW),
            shape((chips, size, width), LOW),
            shape((width, units), LOW),
            shape((chips, size, width), LOW),
        ],
        (x_block, up_mine, grads, down_block),
        [HBM] * 4,
        [VMEM, HBM, HBM, HBM, HBM],
        [
            pltpu.VMEM((planes, 2, tokens, width), LOW),
            pltpu.VMEM((width, units), LOW),
            pltpu.VMEM((planes, 2, tokens, width), LOW),
            pltpu.VMEM((chips, size, width), LOW),
            *[pltpu.VMEM(wide, F32)] * 3,
            pltpu.VMEM((planes, 2 * tokens, 128), F32),
            pltpu.VMEM((2 * planes, 8, 128), F32),
            pltpu.VMEM((2 * planes, 2 * planes, 8, 128), F32),
            *[pltpu.VMEM(wide, LOW)] * 2,
            *PairScatter.scratch(planes, tokens, width),
            pltpu.VMEM((2, 256, units), LOW),
            pltpu.VMEM((chips, size, width), LOW),
            *GroupGather.sems(planes),
            *pairs_of(ChipGather.count(chips), 2 * planes),
            *PairScatter.sems(planes, width),
            *pairs_of(chips),
            pltpu.SemaphoreType.DMA((9,)),
        ],
        7,
    )


def swap_lanes(values):
    lane = lax.broadcasted_iota(jnp.int32, values.shape, 1)
    return jnp.where(
        lax.rem(lane, 2) == 0,
        pltpu.roll(values, values.shape[1] - 1, 1),
        pltpu.roll(values, 1, 1),
    )


def twice(table):
    return jnp.concatenate([table, table], axis=1)


def turns(meta_ref, rows):
    cosine, sine, shrink = [twice(meta_ref[rows, pl.ds(i * HD, HD)]) for i in range(3)]
    return (cosine, sine, cosine * shrink, sine * shrink)


def allowed_block(meta_ref, rows, size, columns):
    query = rows + lax.broadcasted_iota(jnp.int32, (size, columns), 0)
    key = lax.broadcasted_iota(jnp.int32, (size, columns), 1)
    offset = meta_ref[pl.ds(rows, size), pl.ds(3 * HD, 1)].astype(jnp.int32)
    return (key <= query) & (key >= query - offset)


BLOCK = 256


def attention_forward_kernel(
    planes, chips, heads, strided,
    x_ref, meta_ref, qkv_ref, out_ref, gain_ref, up_ref, grad_ref,
    q_ref, k_ref, v_ref, att_ref, log_ref, sum_ref,
    rows_ref, metas_ref, qkvs_ref, outs_ref, gains_ref, ups_ref, grads_ref, tiles_ref,
    rows, metas, qkvs, outs, raw, wide, tile, near_out, near_in, far_out, far_in,
    *sems,
):
    here = place()
    z, c, core = here
    seqs = 2 * chips
    count = planes * seqs
    me = 2 * c + core
    flat = z * seqs + me
    groups = [sems[2 * i : 2 * i + 2] for i in range(17)]
    swap_sems, x_far, x_near, meta_far, meta_near, up, down, up_two, down_two = groups[:9]
    gain_sems, up_sems, near, far, tile_sems, grad_up, grad_down, pair = groups[9:]
    local = sems[34]
    tokens, width = x_ref.shape
    part, three = qkv_ref.shape[1:]
    length = seqs * tokens
    span = heads * HD
    barrier = pltpu.get_barrier_semaphore()

    def device_of(k):
        other = lax.rem(flat + k, count)
        return (other // seqs, lax.rem(other, seqs) // 2, lax.rem(other, 2))

    def signal(k, carry):
        greet(barrier, [device_of(k)])
        return carry

    lax.fori_loop(1, count, signal, 0)
    pl.semaphore_wait(barrier, count - 1)

    mine = pltpu.make_async_copy(qkv_ref.at[me], qkvs.at[z, me], local.at[0])
    own_out = pltpu.make_async_copy(out_ref, outs.at[z] if strided else outs, local.at[1])
    units = up_ref.shape[1]
    keeps = [
        pltpu.make_async_copy(x_ref, rows.at[me], local.at[2]),
        pltpu.make_async_copy(meta_ref, metas.at[me], local.at[3]),
        pltpu.make_async_copy(gain_ref, gains_ref.at[flat], local.at[4]),
        pltpu.make_async_copy(up_ref, column_block(ups_ref, units, c), local.at[5]),
    ]
    peers = plane_peers(chips, here)
    swaps = [
        remote(qkv_ref.at[2 * device[1] + device[2]], qkvs.at[z, me], swap_sems, k, device)
        for k, device in enumerate(peers, 1)
    ]
    mine.start()
    own_out.start()
    for copy in swaps:
        copy.start()
    gather = PlaneGather(chips, here, x_ref, rows, x_far, x_near)
    meta_gather = PlaneGather(chips, here, meta_ref, metas, meta_far, meta_near)
    for copy in keeps:
        copy.start()

    def gain_copy(k):
        return remote(gain_ref, gains_ref.at[flat], gain_sems, k, device_of(k))

    def gain_start(k, carry):
        gain_copy(k).start()
        return carry

    mine.wait()
    own_out.wait()
    for k in range(1, seqs):
        index = lax.rem(me + seqs - k, seqs)
        remote(qkv_ref.at[0], qkvs.at[z, index], swap_sems, k, here).wait_recv()
    half = seqs // 2
    line = LineGather(
        planes, here, lambda t: [qkvs.at[t, pl.ds(i * half, half)] for i in range(2)], up, down
    )
    line_two = LineGather(planes, here, lambda t: [outs.at[t]], up_two, down_two)
    line.start()
    gather.start()
    meta_gather.start()
    lax.fori_loop(1, count, gain_start, 0)
    gather.relay()
    meta_gather.relay()
    line.step(1)
    gather.forward()
    meta_gather.forward()
    ups = ChipGather(
        chips,
        here,
        lambda part: row_half(up_ref, part),
        lambda chip, part: row_half(column_block(ups_ref, units, chip), part),
        up_sems,
    )
    ups.start()
    line.step(2)
    gather.finish()
    meta_gather.finish()
    for copy in keeps:
        copy.wait()

    block = seqs * part

    def add(t, fresh=False):
        columns = pl.ds(pl.multiple_of(t * block, 128), block)
        left = rows[:, :, columns].reshape(length, block)
        for i in range(3):
            at = pl.ds(i * span, span)
            term = jnp.dot(left, qkvs[t, :, :, at].reshape(block, span), preferred_element_type=F32)
            raw[:, at] = term if fresh else raw[:, at] + term

    add(z, True)
    for d in range(1, planes):
        if d == 3:
            ups.relay()
        if d > 2:
            line.step(d)
        if d == planes - 1:
            if strided:
                line_two.start()
            group = GroupGather(planes, here, grad_ref, grads_ref, grad_up, grad_down, pair)
            group.start(local.at[6])
        pl.when(z - d >= 0)(lambda d=d: add(z - d))
        pl.when(z + d < planes)(lambda d=d: add(z + d))
    outputs = [
        pltpu.make_async_copy(rows, rows_ref, local.at[7]),
        pltpu.make_async_copy(metas, metas_ref, local.at[8]),
        pltpu.make_async_copy(qkvs, qkvs_ref, local.at[9]),
    ]
    for copy in outputs:
        copy.start()

    table = RowBlocks(metas)
    for at in range(0, length, BLOCK):
        at = pl.ds(at, BLOCK)
        tables = turns(table, at)
        for two in range(heads // 2):
            query = raw[at, pl.ds(2 * HD * two, 2 * HD)]
            query = (query * tables[0] + swap_lanes(query) * tables[1]).astype(LOW)
            key = raw[at, pl.ds(span + 2 * HD * two, 2 * HD)]
            key = (key * tables[2] + swap_lanes(key) * tables[3]).astype(LOW)
            value = raw[at, pl.ds(2 * span + 2 * HD * two, 2 * HD)].astype(LOW)
            for side in range(2):
                lanes = slice(side * HD, (side + 1) * HD)
                q_ref[2 * two + side, at] = query[:, lanes]
                k_ref[2 * two + side, at] = key[:, lanes]
                v_ref[2 * two + side, at] = value[:, lanes]
    log_ref[...] = jnp.zeros(log_ref.shape, F32)

    def one_head(head, carry):
        for start in range(0, length, BLOCK):
            columns = start + BLOCK
            at = pl.ds(start, BLOCK)
            scores = lax.dot_general(
                q_ref[head, at],
                k_ref[head, pl.ds(0, columns)],
                (((1,), (1,)), ((), ())),
                preferred_element_type=F32,
            )
            allowed = allowed_block(table, start, BLOCK, columns)
            scores = jnp.where(allowed, scores, NEG_FILL)
            top = jnp.max(scores, axis=1, keepdims=True)
            shifted = jnp.exp(scores - top)
            total = jnp.sum(shifted, axis=1, keepdims=True)
            probs = (shifted * (1.0 / total)).astype(LOW)
            wide[head, at] = jnp.dot(
                probs, v_ref[head, pl.ds(0, columns)], preferred_element_type=F32
            )
            lane = lax.broadcasted_iota(jnp.int32, (BLOCK, 128), 1)
            log_ref[at] = jnp.where(lane == head, top + jnp.log(total), log_ref[at])
        return carry

    first = 0
    for d in range(1, planes):
        last = -(-heads * d // planes)
        lax.fori_loop(first, last, one_head, 0)
        first = last
        if strided:
            line_two.step(d)
        if d == 2:
            group.step(1)
    lax.fori_loop(first, heads, one_head, 0)
    lane = lax.broadcasted_iota(jnp.int32, (tokens, 128), 1)
    column = jnp.sum(outs[...].astype(F32).reshape(span, width), axis=0, keepdims=True)
    for s in range(seqs):
        at = pl.ds(s * tokens, tokens)
        low = jnp.concatenate([wide[head, at] for head in range(heads)], axis=1).astype(LOW)
        att_ref[s] = low
        value = low.astype(F32)
        total = jnp.sum(value, axis=1, keepdims=True)
        square = jnp.sum(value * value, axis=1, keepdims=True)
        both = jnp.where(lane == 0, total, jnp.where(lane == 1, square, 0.0))
        tile[s, pl.ds(0, 8)] = both.T[:8]
        for i in range(width // 128):
            tile[s, pl.ds(8 + i, 1)] = column[:, i * 128 : (i + 1) * 128]
    out_tiles = [
        remote(tile.at[2 * device[1] + device[2]], tiles_ref.at[me], tile_sems, k, device)
        for k, device in enumerate(peers, 1)
    ]
    for copy in out_tiles:
        copy.start()
    keep = pltpu.make_async_copy(tile.at[me], tiles_ref.at[me], local.at[10])
    keep.start()
    out_outs = pltpu.make_async_copy(outs, outs_ref, local.at[11])
    out_outs.start()
    work = PlaneScatter(
        chips, here, att_ref, Flat(outs, span), False, (near_out, near_in, far_out, far_in), near, far
    )
    work.start()
    for d in range(2, planes):
        group.step(d)
    work.finish(sum_ref)
    group.finish()
    for t in range(planes):
        group.other(t)
    line.finish()
    if strided:
        line_two.finish()
    for copy in swaps:
        copy.wait_send()
    ups.finish()
    for copy in [keep, out_outs, *outputs]:
        copy.wait()
    for k in range(1, seqs):
        out_tiles[k - 1].wait_send()
        index = lax.rem(me + seqs - k, seqs)
        remote(tile.at[0], tiles_ref.at[index], tile_sems, k, here).wait_recv()

    def gain_wait(k, carry):
        gain_copy(k).wait_send()
        other = lax.rem(flat + count - k, count)
        remote(gain_ref, gains_ref.at[other], gain_sems, k, here).wait_recv()
        return carry

    lax.fori_loop(1, count, gain_wait, 0)


class Flat:
    def __init__(self, blocks, count):
        self.blocks, self.count = blocks, count

    def __getitem__(self, at):
        if len(self.blocks.shape) == 2:
            return self.blocks[at]
        _, columns = at
        return self.blocks[:, :, columns].reshape(self.count, columns.size)


class RowBlocks:
    def __init__(self, blocks):
        self.blocks = blocks

    def __getitem__(self, at):
        rows, columns = at
        size = self.blocks.shape[1]
        first, count = rows.start // size, rows.size // size
        return self.blocks[pl.ds(first, count), :, columns].reshape(rows.size, columns.size)


def attention_forward(
    planes, chips, heads, strided, x_block, meta, qkv_blocks, out_rows, gain_tile, up_block, grad
):
    seqs = 2 * chips
    tokens, width = x_block.shape
    part, wide = qkv_blocks.shape[1:]
    units = up_block.shape[1]
    length = seqs * tokens
    span = heads * HD
    outs = (planes, *out_rows.shape) if strided else out_rows.shape
    tile = (seqs, 8 + width // 128, 128)
    return call(
        functools.partial(attention_forward_kernel, planes, chips, heads, strided),
        "attention_forward",
        [
            *[shape((heads, length, HD), LOW)] * 3,
            shape((seqs, tokens, span), LOW),
            shape((length, 128), F32),
            shape((tokens, width), F32),
            shape((seqs, tokens, width), LOW),
            shape((seqs, *meta.shape), F32),
            shape((planes, seqs, part, wide), LOW),
            shape(outs, LOW),
            shape((planes * seqs, *gain_tile.shape), F32),
            shape((width, chips * units) if units % 128 == 0 else (chips, width, units), LOW),
            shape((planes, 2, *grad.shape), LOW),
            shape(tile, F32),
        ],
        (x_block, meta, qkv_blocks, out_rows, gain_tile, up_block, grad),
        [HBM] * 7,
        [*[VMEM] * 6, *[HBM] * 8],
        [
            pltpu.VMEM((seqs, tokens, width), LOW),
            pltpu.VMEM((seqs, *meta.shape), F32),
            pltpu.VMEM((planes, seqs, part, wide), LOW),
            pltpu.VMEM(outs, LOW),
            pltpu.VMEM((length, 3 * span), F32),
            pltpu.VMEM((heads, length, HD), F32),
            pltpu.VMEM(tile, F32),
            *PlaneScatter.scratch(chips, tokens, width),
            *pairs_of(seqs),
            *PlaneGather.sems(chips),
            *PlaneGather.sems(chips),
            *pairs_of(*[2 * planes] * 2, *[planes] * 2, planes * seqs, ChipGather.count(chips)),
            *PlaneScatter.sems(chips, width),
            *pairs_of(seqs),
            *GroupGather.sems(planes),
            pltpu.SemaphoreType.DMA((12,)),
        ],
        1,
    )


def attention_backward_kernel(
    planes, chips, heads, strided,
    x_ref, stat_ref, tile_ref, left_ref, right_ref,
    q_in, k_in, v_in, att_in, out_in, log_in, meta_in, up_ref,
    tiles_ref, ffn_ref, out_ref, total_ref, slots_ref,
    rows, stats, left, right, q_ref, k_ref, v_ref, att_ref, outs, log_ref, meta_ref,
    near_out, near_own, near_sums, grad, dq, dk, dv, normed_all, own, sums, *sems,
):
    here = place()
    z, c, core = here
    seqs = 2 * chips
    count = planes * seqs
    me = 2 * c + core
    flat = z * seqs + me
    x_far, x_near, s_far, s_near, tile_sems, near, up, down, up_two, down_two, swap_sems = [
        sems[2 * i : 2 * i + 2] for i in range(11)
    ]
    local = sems[22]
    pairs = [
        (left_ref, left), (right_ref, right), (att_in, att_ref), (out_in, outs), (meta_in, meta_ref),
        (q_in, q_ref), (k_in, k_ref), (v_in, v_ref), (log_in, log_ref),
    ]
    loads = [pltpu.make_async_copy(*pair, local.at[i]) for i, pair in enumerate(pairs)]
    for copy in loads:
        copy.start()
    barrier = pltpu.get_barrier_semaphore()

    def device_of(k):
        other = lax.rem(flat + k, count)
        return (other // seqs, lax.rem(other, seqs) // 2, lax.rem(other, 2))

    def signal(k, carry):
        greet(barrier, [device_of(k)])
        return carry

    lax.fori_loop(1, count, signal, 0)
    pl.semaphore_wait(barrier, count - 1)
    gather = PlaneGather(chips, here, x_ref, rows, x_far, x_near)
    stat_gather = PlaneGather(chips, here, stat_ref, stats, s_far, s_near)
    gather.start()
    stat_gather.start()
    keeps = [
        pltpu.make_async_copy(x_ref, rows.at[me], local.at[9]),
        pltpu.make_async_copy(stat_ref, stats.at[me], local.at[10]),
        pltpu.make_async_copy(tile_ref.at[flat], tiles_ref.at[flat], local.at[11]),
    ]
    for copy in keeps:
        copy.start()

    def tile_copy(k):
        other = lax.rem(flat + k, count)
        return remote(tile_ref.at[other], tiles_ref.at[flat], tile_sems, k, device_of(k))

    def tile_start(k, carry):
        tile_copy(k).start()
        return carry

    lax.fori_loop(1, count, tile_start, 0)
    tokens, width = x_ref.shape
    for copy in loads[:2]:
        copy.wait()
    work = PairScatter(
        planes, here, Halves(left, tokens), right, False, (near_out, near_own, near_sums),
        near, up, down,
    )
    work.start()
    left_turns = list(range(1, work.line.steps))

    def turn(until=None):
        step = left_turns[0] + 1 if until is None and left_turns else until
        while left_turns and left_turns[0] < step:
            work.line.step(left_turns.pop(0))

    turn()
    gather.relay()
    stat_gather.relay()
    turn()
    gather.forward()
    stat_gather.forward()
    gather.finish()
    stat_gather.finish()
    swap = ChipSwap(
        chips, here, lambda index: half_block(up_ref, slots_ref, index, 0), slots_ref, swap_sems
    )
    swap.start(local.at[12])
    for copy in [*loads[2:], *keeps]:
        copy.wait()
    turn()
    length, span = att_ref.shape
    part = own.shape[1]
    per = BLOCK // tokens
    for first in range(0, seqs, per):
        at = pl.ds(first * tokens, BLOCK)
        figures = stats[pl.ds(first, per)].reshape(BLOCK, 128)
        mean, scaler, one, two = (figures[:, i : i + 1] for i in range(4))
        block = rows[pl.ds(first, per)].reshape(BLOCK, width)
        d_sub = product(block, outs, slice(None), True)
        normed = (att_ref[at].astype(F32) - mean) * scaler
        normed_all[at] = normed.astype(LOW)
        d_att = (scaler * (d_sub - one - normed * two)).astype(LOW)
        for head in range(heads):
            grad[head, at] = d_att[:, head * HD : (head + 1) * HD]
    for at in range(0, width, COLUMNS):
        columns = pl.ds(at, COLUMNS)
        term = token_product(normed_all[...], rows[:, :, columns].reshape(length, COLUMNS)).astype(LOW)
        for t in range(planes):
            own[t, :, columns] = term[t * part : (t + 1) * part]
    line = LineScatter(
        planes,
        here,
        1,
        lambda p: (slice(None),),
        lambda p: [(row,) for row in row_tiles(part, 16)],
        lambda t, tile: own[(t, *tile)].astype(F32),
        sums,
        up_two,
        down_two,
    )
    if strided:
        line.step(0)
    dk[...] = jnp.zeros(dk.shape, F32)
    dv[...] = jnp.zeros(dv.shape, F32)

    def one_head(head, carry):
        for start in range(0, length, BLOCK):
            columns = start + BLOCK
            at = pl.ds(start, BLOCK)
            keys = pl.ds(0, columns)
            query, key = q_ref[head, at], k_ref[head, keys]
            out_grad = grad[head, at]
            scores = lax.dot_general(
                query, key, (((1,), (1,)), ((), ())), preferred_element_type=F32
            )
            allowed = allowed_block(meta_ref, start, BLOCK, columns)
            lane = lax.broadcasted_iota(jnp.int32, (BLOCK, 128), 1)
            log_total = jnp.sum(jnp.where(lane == head, log_ref[at], 0.0), axis=1, keepdims=True)
            probs = jnp.where(allowed, jnp.exp(scores - log_total), 0.0)
            d_probs = lax.dot_general(
                out_grad, v_ref[head, keys], (((1,), (1,)), ((), ())), preferred_element_type=F32
            )
            delta = jnp.sum(probs * d_probs, axis=1, keepdims=True)
            d_scores = (probs * (d_probs - delta)).astype(LOW)
            dq[head, at] = jnp.dot(d_scores, key, preferred_element_type=F32)
            dk[head, keys] += token_product(d_scores, query)
            dv[head, keys] += token_product(probs.astype(LOW), out_grad)
        return carry

    first = 0
    for i in range(1, planes - 1):
        last = -(-heads * i // (planes - 1))
        lax.fori_loop(first, last, one_head, 0)
        first = last
        turn()
        if strided:
            line.step(i)
    lax.fori_loop(first, heads, one_head, 0)
    turn(work.line.steps)
    for start in range(0, length, BLOCK):
        at = pl.ds(start, BLOCK)
        tables = turns(meta_ref, at)
        for two in range(heads // 2):
            both = [
                jnp.concatenate([whole[2 * two, at], whole[2 * two + 1, at]], axis=1).astype(LOW)
                for whole in (dq, dk, dv)
            ]
            query, key = both[0].astype(F32), both[1].astype(F32)
            query = query * tables[0] + swap_lanes(query * tables[1])
            key = key * tables[2] + swap_lanes(key * tables[3])
            out_ref[at, pl.ds(2 * HD * two, 2 * HD)] = query.astype(LOW)
            out_ref[at, pl.ds(span + 2 * HD * two, 2 * HD)] = key.astype(LOW)
            out_ref[at, pl.ds(2 * span + 2 * HD * two, 2 * HD)] = both[2]
    work.finish(ffn_ref)
    if strided:

        def store(tile, total):
            total_ref[tile] = total

        line.finish(store)
    else:
        for t in range(planes):
            total_ref[pl.ds(t * part, part)] = own[t].astype(F32)
    swap.finish()

    def tile_wait(k, carry):
        tile_copy(k).wait_send()
        other = lax.rem(flat + count - k, count)
        remote(tile_ref.at[0], tiles_ref.at[other], tile_sems, k, here).wait_recv()
        return carry

    lax.fori_loop(1, count, tile_wait, 0)


def attention_backward(planes, chips, heads, strided, part, units, args):
    tokens, width = args[0].shape
    seqs = 2 * chips
    length, span = args[8].shape
    kept = [pltpu.VMEM(args[i].shape, args[i].dtype) for i in (3, 4, 5, 6, 7, 8, 9, 10, 11)]
    return call(
        functools.partial(attention_backward_kernel, planes, chips, heads, strided),
        "attention_backward",
        [
            shape(args[2].shape, F32),
            shape((tokens, width), F32),
            shape((length, 3 * span), LOW),
            shape((part if strided else span, width), F32),
            shape((chips, width // 2, units), LOW),
        ],
        args,
        [HBM] * 13,
        [HBM, VMEM, VMEM, VMEM, HBM],
        [
            pltpu.VMEM((seqs, tokens, width), LOW),
            pltpu.VMEM((seqs, tokens, 128), F32),
            *kept,
            *PairScatter.scratch(planes, tokens, width),
            pltpu.VMEM((heads, length, HD), LOW),
            *[pltpu.VMEM((heads, length, HD), F32)] * 3,
            pltpu.VMEM((length, span), LOW),
            pltpu.VMEM((planes, part, width), LOW),
            pltpu.VMEM((planes + 1, part, width), LOW),
            *PlaneGather.sems(chips),
            *PlaneGather.sems(chips),
            *pairs_of(planes * seqs),
            *PairScatter.sems(planes, width),
            *pairs_of(planes, planes, chips),
            pltpu.SemaphoreType.DMA((13,)),
        ],
        2,
    )


def body(
    hidden_in,
    segment_ids,
    position_ids,
    w_qkv,
    w_out,
    w_up,
    w_down,
    gain_attn,
    gain_attn_sub,
    gain_ffn,
    gain_ffn_sub,
    ema_qkv,
    ema_out,
    ema_up,
    ema_down,
    ema_gain_attn,
    ema_gain_attn_sub,
    ema_gain_ffn,
    ema_gain_ffn_sub,
    out_grad,
):
    _, tokens, width = hidden_in.shape
    planes, chips = lax.axis_size("dp"), lax.axis_size("chip")
    seqs = 2 * chips
    length = tokens * seqs
    heads = HEADS // seqs
    span = heads * HD
    part = w_qkv.shape[0]
    strided = part % HD == 0
    width_ff = w_down.shape[0] * planes * seqs
    seq_index = lax.axis_index(SEQ)

    def gain_rows(weight, gain):
        return (weight.astype(F32) * gain.astype(F32)[:, None]).astype(LOW)

    qkv_scaled = gain_rows(w_qkv, gain_attn)
    out_scaled = gain_rows(w_out, gain_attn_sub)
    down_scaled = gain_rows(w_down, gain_ffn_sub)
    if strided:
        qkv_send = qkv_scaled.reshape(part, 3, planes, seqs, HD).transpose(3, 0, 1, 2, 4)
    else:
        qkv_send = qkv_scaled.reshape(part, 3, seqs, span).transpose(2, 0, 1, 3)
    qkv_send = qkv_send.reshape(seqs, part, 3 * span)
    x_in = hidden_in[0].astype(F32)
    normed_one, scaler_one = moments(x_in)
    normed_low = normed_one.astype(LOW)
    gain_tile = jnp.zeros((8, 128), F32).at[0, :part].set(gain_ffn.astype(F32))

    if not strided:
        out_all = lax.all_gather(out_scaled, ALL, axis=0, tiled=True)
        out_scaled = lax.dynamic_slice_in_dim(out_all, seq_index * span, span, axis=0)

    grad_low = out_grad[0]
    (
        queries, keys, values, attended, log_total, out_sum,
        row_in, meta, qkv_mine, out_mine, gain_tiles, up_mine, grad_flat, tiles,
    ) = attention_forward(
        planes,
        chips,
        heads,
        strided,
        normed_low,
        token_tables(position_ids[0]),
        qkv_send,
        out_scaled,
        gain_tile,
        w_up,
        grad_low,
    )
    if up_mine.ndim == 3:
        up_mine = up_mine.transpose(1, 0, 2).reshape(width, -1)
    row_in = row_in.reshape(length, width)
    meta = meta.reshape(length, -1)
    qkv_mine = qkv_mine.reshape(width, 3 * span)
    out_mine = out_mine.reshape(span, width)
    attended = attended.reshape(length, span)
    tiles = jnp.sum(tiles, axis=0)
    column_sum = tiles[8:].reshape(width)
    sums = tiles[:2].T
    gain_three = gain_tiles[:, 0, :part].reshape(width)
    mean_two = sums[:, :1] / width
    scaler_two = lax.rsqrt(sums[:, 1:] / width - mean_two * mean_two + NORM_EPS)
    projected = scaler_two * (out_sum - mean_two * column_sum[None, :])
    hmid = x_in + projected
    normed_three, scaler_three = moments(hmid)
    ffn_in = (normed_three * gain_three).astype(LOW)

    grad_top = grad_low.astype(F32)
    units = w_up.shape[1]
    d_ffn_in, normed_four, down_mine, grad_up, down_slots = feed_forward(
        planes, chips, width_ff, ffn_in, up_mine, grad_flat, down_scaled
    )
    down_mine = down_mine.reshape(-1, width)
    if units % 128:
        grad_up = grad_up.reshape(width, chips, units).transpose(1, 0, 2)

    gain_part = jnp.sum(d_ffn_in * normed_three, axis=0).reshape(planes * seqs, 1, part)
    gain_part = jnp.pad(gain_part, ((0, 0), (0, 7), (0, 128 - part)))
    d_hmid = grad_top + norm_back(d_ffn_in * gain_three, normed_three, scaler_three)
    d_hmid_low = d_hmid.astype(LOW)
    d_hmid_wide = d_hmid_low.astype(F32)
    first_two = jnp.sum(d_hmid_wide * column_sum[None, :], axis=1, keepdims=True) / width
    second_two = jnp.sum(d_hmid_wide * projected, axis=1, keepdims=True) / width
    token_stats = jnp.concatenate([mean_two, scaler_two, first_two, second_two], axis=1)
    gain_part, ffn_out, d_qkv, sum_out, upper_slots = attention_backward(
        planes,
        chips,
        heads,
        strided,
        part,
        units,
        (
            d_hmid_low,
            jnp.pad(token_stats, ((0, 0), (0, 124))),
            gain_part,
            normed_four,
            down_mine,
            queries,
            keys,
            values,
            attended,
            out_mine,
            log_total,
            meta,
            grad_up,
        ),
    )
    output = (hmid + ffn_out).astype(LOW)[None]
    grad_gain_three = jnp.sum(gain_part, axis=0)[0, :part]
    grad_qkv = token_product(row_in, d_qkv).astype(LOW)
    d_in, sum_qkv, grad_gain_one, lower_slots = in_scatter(
        planes,
        chips,
        heads,
        strided,
        d_qkv.reshape(seqs, tokens, 3 * span),
        qkv_mine,
        grad_qkv.reshape(planes, seqs, part, 3 * span),
        grad_up,
        w_qkv,
        jnp.broadcast_to(gain_attn.astype(F32)[:, None], (part, 128)),
        units,
    )
    grad_gain_one = grad_gain_one[:, 0]
    sum_up = jnp.concatenate(
        [jnp.sum(slots.astype(F32), axis=0) for slots in (upper_slots, lower_slots)], axis=0
    )
    sum_down = jnp.sum(down_slots.astype(F32), axis=0)
    input_grad = (d_hmid + norm_back(d_in, normed_one, scaler_one)).astype(LOW)[None]

    if not strided:
        spread = lax.dynamic_update_slice_in_dim(
            jnp.zeros((width, width), LOW), sum_out.astype(LOW), seq_index * span, axis=0
        )
        sum_out = lax.psum_scatter(spread, ALL, scatter_dimension=0, tiled=True).astype(F32)

    def finish(total, weight, gain):
        wide = weight.astype(F32)
        return (total * gain.astype(F32)[:, None], jnp.sum(total * wide, axis=1))

    sum_out, grad_gain_two = finish(sum_out, w_out, gain_attn_sub)
    sum_down, grad_gain_four = finish(sum_down, w_down, gain_ffn_sub)

    def averaged(average, weight):
        return EMA_DECAY * average + (1.0 - EMA_DECAY) * weight.astype(F32)

    return (
        output,
        input_grad,
        sum_qkv,
        sum_out,
        sum_up,
        sum_down,
        grad_gain_one,
        grad_gain_two,
        grad_gain_three,
        grad_gain_four,
        averaged(ema_qkv, w_qkv),
        averaged(ema_out, w_out),
        averaged(ema_up, w_up),
        averaged(ema_down, w_down),
        averaged(ema_gain_attn, gain_attn),
        averaged(ema_gain_attn_sub, gain_attn_sub),
        averaged(ema_gain_ffn, gain_ffn),
        averaged(ema_gain_ffn_sub, gain_ffn_sub),
    )


def solution(mesh):
    split = Mesh(
        mesh.devices.reshape(mesh.shape["dp"], mesh.shape["seq"] // 2, 2), ("dp", "chip", "core")
    )
    tokens = P("dp", SEQ, None)
    ids = P("dp", SEQ)
    rows = P(ALL, None)
    columns = P(None, ALL)
    vector = P(ALL)
    weights = (rows, rows, columns, rows)
    gains = (vector,) * 4
    return jax.shard_map(
        body,
        mesh=split,
        in_specs=(tokens, ids, ids, *weights, *gains, *weights, *gains, tokens),
        out_specs=(tokens, tokens, *weights, *gains, *weights, *gains),
        check_vma=False,
    )
```

```python
import functools
import math

import jax
import jax.numpy as jnp
from jax import lax
from jax.experimental import pallas as pl
from jax.experimental.pallas import tpu as pltpu
from jax.sharding import Mesh
from jax.sharding import PartitionSpec as P

HEADS = 32
HD = 64

NEG_FILL = -1000000000.0
NORM_EPS = 1e-05
EMA_DECAY = 0.7
LOW = jnp.bfloat16
F32 = jnp.float32
SEQ = ("chip", "core")
TP = ("dp", "core")
ALL = ("dp", "chip", "core")


def moments(values):
    mean = jnp.mean(values, axis=-1, keepdims=True)
    centered = values - mean
    scaler = lax.rsqrt(jnp.mean(centered * centered, axis=-1, keepdims=True) + NORM_EPS)
    return (centered * scaler, scaler)


def norm_back(scaled_grad, normed, scaler):
    first_mean = jnp.mean(scaled_grad, axis=-1, keepdims=True)
    second_mean = jnp.mean(scaled_grad * normed, axis=-1, keepdims=True)
    return scaler * (scaled_grad - first_mean - normed * second_mean)


def token_tables(positions):
    half_count = HD // 2
    index_half = jnp.arange(half_count).astype(F32)
    inverse = jnp.exp(-(2.0 * index_half / HD) * math.log(10000.0))
    decay_base = (2.0 * index_half + 0.4 * HD) / (1.4 * HD)
    where_at = positions.astype(F32)[:, None]
    angles = where_at * inverse[None, :]
    factor = jnp.exp(where_at / 512.0 * jnp.log(decay_base)[None, :])
    sign_row = jnp.where(jnp.arange(HD) % 2 == 0, -1.0, 1.0).astype(F32)
    cosine = jnp.repeat(jnp.cos(angles), 2, axis=1)
    sine = jnp.repeat(jnp.sin(angles), 2, axis=1) * sign_row[None, :]
    factor = jnp.repeat(factor, 2, axis=1)
    grow = factor * HD ** (-0.5)
    where_block = jnp.broadcast_to(where_at, (positions.shape[0], HD))
    return jnp.concatenate(
        [cosine * grow, sine * grow, HD**0.5 / (factor * factor), where_block], axis=1
    )


def dot(left_op, right_op):
    return jnp.dot(left_op, right_op, preferred_element_type=F32)


def rows_product(operand, weight_rows):
    return lax.dot_general(
        operand, weight_rows, (((1,), (1,)), ((), ())), preferred_element_type=F32
    )


def token_product(left_op, right_op):
    return lax.dot_general(left_op, right_op, (((0,), (0,)), ((), ())), preferred_element_type=F32)


MESH = pl.DeviceIdType.MESH
HBM = pl.BlockSpec(memory_space=pl.ANY)
VMEM = pl.BlockSpec(memory_space=pltpu.VMEM)
VMEM_BYTES = 60 * 1024 * 1024


def shape(dims, kind):
    return jax.ShapeDtypeStruct(dims, kind)


def pairs_of(*counts):
    return [pltpu.SemaphoreType.DMA((count,)) for count in counts for _ in range(2)]


def call(kernel, name, outs, args, in_specs, out_specs, scratch, collective=None, aliases=None):
    return pl.pallas_call(
        kernel,
        input_output_aliases=aliases or {},
        name=name,
        out_shape=outs,
        in_specs=in_specs,
        out_specs=out_specs,
        scratch_shapes=scratch,
        compiler_params=pltpu.CompilerParams(
            collective_id=collective,
            has_side_effects=collective is not None,
            vmem_limit_bytes=VMEM_BYTES,
        ),
    )(*args)


def place():
    return (lax.axis_index("dp"), lax.axis_index("chip"), lax.axis_index("core"))


def remote(source, target, sems, index, device):
    return pltpu.make_async_remote_copy(
        src_ref=source,
        dst_ref=target,
        send_sem=sems[0].at[index],
        recv_sem=sems[1].at[index],
        device_id=device,
        device_id_type=MESH,
    )


def greet(barrier, devices):
    for device in devices:
        pl.semaphore_signal(barrier, inc=1, device_id=device, device_id_type=MESH)


def greet_line(barrier, planes, here):
    z, c, core = here

    @pl.when(z < planes - 1)
    def _():
        greet(barrier, [(z + 1, c, core)])

    @pl.when(z > 0)
    def _():
        greet(barrier, [(z - 1, c, core)])


def line_peers(planes, here):
    z = here[0]
    return (2 * planes - 2 - z) // planes + (z + planes - 1) // planes


def chip_peers(chips, here):
    z, c, core = here
    return [(z, lax.rem(c + k, chips), core) for k in range(1, chips)]


def plane_peers(chips, here):
    z, c, core = here
    seqs = 2 * chips
    me = 2 * c + core
    ids = [lax.rem(me + k, seqs) for k in range(1, seqs)]
    return [(z, index // 2, lax.rem(index, 2)) for index in ids]


def column_block(whole, units, index):
    if len(whole.shape) == 3:
        return whole.at[index]
    return whole.at[:, pl.ds(pl.multiple_of(index * units, 128), units)]


def half_rows(rows, half):
    size = rows // 2
    return pl.ds(half * size, size)


def half_block(whole, units, index, half):
    at = half_rows(whole.shape[-2], half)
    if len(whole.shape) == 3:
        return whole.at[index, at]
    return whole.at[at, pl.ds(pl.multiple_of(index * units, 128), units)]


class ChipSwap:
    def __init__(self, chips, here, source, slot, sems):
        z, c, core = here
        self.sends = [
            remote(source(device[1]), slot(c), sems, k, device)
            for k, device in enumerate(chip_peers(chips, here), 1)
        ]
        self.waits = [
            remote(source(c), slot(lax.rem(c + chips - k, chips)), sems, k, here)
            for k in range(1, chips)
        ]
        self.keep = (source(c), slot(c))

    def start(self, local):
        for copy in self.sends:
            copy.start()
        self.held = pltpu.make_async_copy(*self.keep, local)
        self.held.start()

    def finish(self):
        self.held.wait()
        for send, wait in zip(self.sends, self.waits):
            send.wait_send()
            wait.wait_recv()


class ChipGather:
    def __init__(self, chips, here, source, target, sems):
        z, c, core = here
        self.here, self.sems, self.relayed = here, sems, chips == 4
        if not self.relayed:
            self.sends = [
                remote(source(None), target(c, None), sems, k, device)
                for k, device in enumerate(chip_peers(chips, here), 1)
            ]
            self.arrivals = [
                (lax.rem(c + chips - k, chips), None, k) for k in range(1, chips)
            ]
        else:
            beside = c + 1 - 2 * lax.rem(c, 2)
            above = c + 2 - 4 * (c // 2)
            to_beside, to_above = (z, beside, core), (z, above, core)
            self.sends = [
                remote(source(0), target(c, 0), sems, 0, to_beside),
                remote(source(1), target(c, 1), sems, 3, to_above),
                remote(source(1), target(c, 1), sems, 1, to_beside),
                remote(source(0), target(c, 0), sems, 2, to_above),
            ]
            self.relays = [
                remote(target(beside, 0), target(beside, 0), sems, 4, to_above),
                remote(target(above, 1), target(above, 1), sems, 5, to_beside),
            ]
            self.arrivals = [
                (beside, 0, 0), (above, 1, 3), (beside, 1, 1), (above, 0, 2),
                (3 - c, 0, 4), (3 - c, 1, 5),
            ]
        self.target = target

    def start(self):
        for copy in self.sends:
            copy.start()

    def arrive(self, i):
        chip, half, index = self.arrivals[i]
        block = self.target(chip, half)
        remote(block, block, self.sems, index, self.here).wait_recv()
        if self.relayed and i < 2:
            self.relays[i].start()

    def relay(self):
        for i in range(2 if self.relayed else 0):
            self.arrive(i)

    def rest(self):
        return range(2 if self.relayed else 0, len(self.arrivals))

    def finish(self):
        for i in self.rest():
            self.arrive(i)
        self.sent()

    def sent(self):
        for copy in [*self.sends, *(self.relays if self.relayed else [])]:
            copy.wait_send()

    @staticmethod
    def count(chips):
        return max(chips, 6)


class PlaneGather:
    def __init__(self, chips, here, block, out, far, near):
        z, c, core = here
        self.here, self.block, self.out, self.near = here, block, out, near
        self.me = 2 * c + core
        self.partner = (z, c, 1 - core)
        self.size = block.shape[0] // 2
        self.chips = ChipGather(
            chips,
            here,
            self.piece,
            lambda chip, half: self.place(2 * chip + core, half),
            far,
        )
        self.own = remote(block, out.at[self.me], near, len(self.chips.arrivals), self.partner)

    def rows(self, half):
        return pl.ds(half * self.size, self.size)

    def piece(self, half):
        return self.block if half is None else self.block.at[self.rows(half)]

    def place(self, index, half):
        return self.out.at[index] if half is None else self.out.at[index, self.rows(half)]

    def start(self):
        self.chips.start()
        self.own.start()

    def passed(self, i, other=0):
        chip, half, _ = self.chips.arrivals[i]
        core = self.here[2]
        block = self.place(2 * chip + (1 - core if other else core), half)
        return remote(block, block, self.near, i, self.partner)

    def relay(self):
        for i in range(2 if self.chips.relayed else 0):
            self.chips.arrive(i)
            self.passed(i).start()

    def forward(self):
        for i in self.chips.rest():
            self.chips.arrive(i)
            self.passed(i).start()

    def finish(self):
        self.chips.sent()
        self.own.wait_send()
        mine = self.out.at[2 * self.here[1] + 1 - self.here[2]]
        remote(mine, mine, self.near, len(self.chips.arrivals), self.partner).wait_recv()
        for i in range(len(self.chips.arrivals)):
            self.passed(i).wait_send()
            self.passed(i, 1).wait_recv()

    @staticmethod
    def sems(chips):
        return pairs_of(ChipGather.count(chips), ChipGather.count(chips) + 1)


def row_half(ref, half):
    if half is None:
        return ref
    size = ref.shape[0] // 2
    return ref.at[pl.ds(half * size, size)]


class LineGather:
    def __init__(self, planes, here, parts, up, down):
        self.planes, self.here, self.parts = planes, here, parts
        self.up, self.down = up, down
        self.count = len(parts(here[0]))

    def upward(self, d, p):
        z, c, core = self.here
        block = self.parts(z - d)[p]
        return remote(block, block, self.up, d * self.count + p, (z + 1, c, core))

    def downward(self, d, p):
        z, c, core = self.here
        block = self.parts(z + d)[p]
        return remote(block, block, self.down, d * self.count + p, (z - 1, c, core))

    def each(self, d, p, act):
        z, planes = self.here[0], self.planes
        pl.when((z < planes - 1) & (z - d >= 0))(lambda: act(self.upward(d, p)))
        pl.when((z > 0) & (z + d < planes))(lambda: act(self.downward(d, p)))

    def start(self):
        for p in range(self.count):
            self.each(0, p, lambda copy: copy.start())

    def step(self, d, arrived=None):
        z, planes = self.here[0], self.planes

        def below(p):
            block = self.parts(z - d)[p]
            remote(block, block, self.up, (d - 1) * self.count + p, self.here).wait_recv()
            if d < planes - 1:
                pl.when(z < planes - 1)(lambda: self.upward(d, p).start())
            if arrived is not None:
                arrived(z - d, p)

        def above(p):
            block = self.parts(z + d)[p]
            remote(block, block, self.down, (d - 1) * self.count + p, self.here).wait_recv()
            if d < planes - 1:
                pl.when(z > 0)(lambda: self.downward(d, p).start())
            if arrived is not None:
                arrived(z + d, p)

        for p in range(self.count):
            pl.when(z - d >= 0)(lambda p=p: below(p))
            pl.when(z + d < planes)(lambda p=p: above(p))

    def finish(self):
        for d in range(self.planes - 1):
            for p in range(self.count):
                self.each(d, p, lambda copy: copy.wait_send())


class GroupGather:
    PARTS = 2

    def __init__(self, planes, here, block, out, up, down, near):
        self.planes, self.here, self.block, self.out, self.near = planes, here, block, out, near
        self.partner = (here[0], here[1], 1 - here[2])
        size = block.shape[0] // self.PARTS
        self.slices = [pl.ds(p * size, size) for p in range(self.PARTS)]
        core = here[2]
        self.line = LineGather(planes, here, lambda t: self.parts(t, core), up, down)

    def parts(self, t, core):
        return [self.out.at[t, core, rows] for rows in self.slices]

    def passed(self, t, p):
        block = self.parts(t, self.here[2])[p]
        return remote(block, block, self.near, t * self.PARTS + p, self.partner)

    def start(self, local):
        z, _, core = self.here
        keep = pltpu.make_async_copy(self.block, self.out.at[z, core], local)
        keep.start()
        keep.wait()
        self.line.start()
        for p in range(self.PARTS):
            self.passed(z, p).start()

    def step(self, d):
        self.line.step(d, lambda t, p: self.passed(t, p).start())

    def other(self, t):
        for p in range(self.PARTS):
            block = self.parts(t, 1 - self.here[2])[p]
            remote(block, block, self.near, t * self.PARTS + p, self.partner).wait_recv()

    def finish(self):
        self.line.finish()
        for t in range(self.planes):
            for p in range(self.PARTS):
                self.passed(t, p).wait_send()

    @classmethod
    def sems(cls, planes):
        return pairs_of(*[planes * cls.PARTS] * 3)


COLUMNS = 512


def product(left, right, columns, turned):
    if turned:
        return lax.dot_general(
            left, right[columns, :], (((1,), (1,)), ((), ())), preferred_element_type=F32
        )
    return jnp.dot(left, right[:, columns], preferred_element_type=F32)


class PlaneScatter:
    def __init__(self, chips, here, left, right, turned, buffers, near, far):
        self.chips, self.here = chips, here
        self.left, self.right, self.turned = left, right, turned
        self.near_out, self.near_in, self.far_out, self.far_in = buffers
        self.near, self.far = near, far
        self.tokens, width = self.near_out.shape[1:]
        self.tiles = [pl.ds(at, COLUMNS) for at in range(0, width, COLUMNS)]
        self.order = [*range(1, chips), 0]

    def target(self, k):
        return lax.rem(self.here[1] + k, self.chips)

    def near_copy(self, i):
        z, c, core = self.here
        at = (slice(None), slice(None), self.tiles[i])
        return remote(self.near_out.at[at], self.near_in.at[at], self.near, i, (z, c, 1 - core))

    def far_copy(self, k, i):
        z, _, core = self.here
        at = (k, slice(None), self.tiles[i])
        index = k * len(self.tiles) + i
        return remote(
            self.far_out.at[at], self.far_in.at[at], self.far, index, (z, self.target(k), core)
        )

    def rows(self, position):
        return slice(position * self.tokens, (position + 1) * self.tokens)

    def start(self):
        core = self.here[2]
        blocks = [self.left[2 * self.target(k) + 1 - core] for k in self.order]
        left = jnp.concatenate(blocks, axis=0)
        for i, columns in enumerate(self.tiles):
            part = product(left, self.right, columns, self.turned).astype(LOW)
            for position, k in enumerate(self.order):
                self.near_out[k, :, columns] = part[self.rows(position)]
            self.near_copy(i).start()
        blocks = [self.left[2 * self.target(k) + core] for k in self.order]
        left = jnp.concatenate(blocks, axis=0)
        for i, columns in enumerate(self.tiles):
            part = product(left, self.right, columns, self.turned)
            self.near_copy(i).wait_recv()
            for position, k in enumerate(self.order):
                self.far_out[k, :, columns] = (
                    part[self.rows(position)] + self.near_in[k, :, columns].astype(F32)
                ).astype(LOW)
                if k:
                    self.far_copy(k, i).start()

    def finish(self, out_ref):
        for i, columns in enumerate(self.tiles):
            total = self.far_out[0, :, columns].astype(F32)
            for k in range(1, self.chips):
                self.far_copy(k, i).wait_recv()
                total = total + self.far_in[k, :, columns].astype(F32)
            out_ref[:, columns] = total
        for i in range(len(self.tiles)):
            self.near_copy(i).wait_send()
            for k in range(1, self.chips):
                self.far_copy(k, i).wait_send()

    @staticmethod
    def scratch(chips, tokens, width):
        return [pltpu.VMEM((chips, tokens, width), LOW)] * 4

    @staticmethod
    def sems(chips, width):
        return pairs_of(width // COLUMNS, chips * (width // COLUMNS))


class LineScatter:
    def __init__(self, planes, here, count, part, tiles, own, slots, up, down):
        self.planes, self.here, self.count = planes, here, count
        self.part, self.tiles, self.own, self.slots = part, tiles, own, slots
        self.up, self.down = up, down
        self.steps = (planes - 1) * count

    def upward(self, t, p):
        z, c, core = self.here
        block = self.slots.at[(t, *self.part(p))]
        return remote(block, block, self.up, t * self.count + p, (z + 1, c, core))

    def downward(self, t, p, last):
        z, c, core = self.here
        block = self.slots.at[(t, *self.part(p))]
        target = self.slots.at[(self.planes, *self.part(p))] if last else block
        return remote(block, target, self.down, t * self.count + p, (z - 1, c, core))

    def add(self, t, p, fresh):
        for tile in self.tiles(p):
            total = self.own(t, tile)
            if not fresh:
                total = total + self.slots[(t, *tile)].astype(F32)
            self.slots[(t, *tile)] = total.astype(LOW)

    def step(self, i):
        z, planes, count = self.here[0], self.planes, self.count
        rise, fall = i - z, i - (planes - 1 - z)

        @pl.when((rise >= 0) & (rise < (planes - 1 - z) * count))
        def _():
            t, p = planes - 1 - rise // count, lax.rem(rise, count)

            @pl.when(z > 0)
            def _():
                self.upward(t, p).wait_recv()
                self.add(t, p, False)

            @pl.when(z == 0)
            def _():
                self.add(t, p, True)

            self.upward(t, p).start()

        @pl.when((fall >= 0) & (fall < z * count))
        def _():
            t, p = fall // count, lax.rem(fall, count)

            @pl.when(z < planes - 1)
            def _():
                self.downward(t, p, False).wait_recv()
                self.add(t, p, False)

            @pl.when(z == planes - 1)
            def _():
                self.add(t, p, True)

            pl.when(t == z - 1)(lambda: self.downward(t, p, True).start())
            pl.when(t < z - 1)(lambda: self.downward(t, p, False).start())

    def finish(self, store):
        z, planes = self.here[0], self.planes

        def total(tile, *slots):
            value = self.own(z, tile)
            for slot in slots:
                value = value + self.slots[(slot, *tile)].astype(F32)
            store(tile, value)

        for p in range(self.count):
            tiles = self.tiles(p)

            @pl.when(z > 0)
            def _(p=p):
                self.upward(z, p).wait_recv()

            @pl.when(z < planes - 1)
            def _(p=p):
                self.downward(z, p, True).wait_recv()

            @pl.when((z > 0) & (z < planes - 1))
            def _(tiles=tiles):
                for tile in tiles:
                    total(tile, z, planes)

            @pl.when(z == 0)
            def _(tiles=tiles):
                for tile in tiles:
                    total(tile, planes)

            @pl.when(z == planes - 1)
            def _(tiles=tiles):
                for tile in tiles:
                    total(tile, z)

        for t in range(planes):
            for p in range(self.count):
                pl.when(z < t)(lambda t=t, p=p: self.upward(t, p).wait_send())
                pl.when(z > t)(lambda t=t, p=p: self.downward(t, p, False).wait_send())


def row_tiles(count, size):
    return [pl.ds(at, size) for at in range(0, count, size)]


def in_scatter_kernel(
    planes, chips, heads, strided, left_in, right_in, rows_in, up_ref, weight_ref, gain_ref, _,
    out_ref, total_ref, gains_ref, slots_ref,
    left_ref, right_ref, rows_ref, grad_ref,
    near_out, near_in, far_out, far_in, sums, mine, parts, *sems,
):
    here = place()
    z, c, core = here
    seqs = 2 * chips
    me = 2 * c + core
    near, far, up, down, swap_sems, chip_sems = [sems[2 * i : 2 * i + 2] for i in range(6)]
    local = sems[12]
    loads = [
        pltpu.make_async_copy(rows_in, rows_ref, local.at[1]),
        pltpu.make_async_copy(left_in, left_ref, local.at[2]),
        pltpu.make_async_copy(right_in, right_ref, local.at[3]),
    ]
    for copy in loads:
        copy.start()
    barrier = pltpu.get_barrier_semaphore()
    peers = plane_peers(chips, here)
    greet(barrier, peers)
    greet_line(barrier, planes, here)
    pl.semaphore_wait(barrier, len(peers) + line_peers(planes, here))
    half = seqs // 2
    line = LineScatter(
        planes,
        here,
        2,
        lambda p: (pl.ds(p * half, half),),
        lambda p: [(pl.ds(p * half + i, 1),) for i in range(half)],
        lambda t, tile: grad_ref[(t, *tile)].astype(F32),
        sums,
        up,
        down,
    )
    part = grad_ref.shape[2]
    span = heads * HD
    block = seqs * part
    length = rows_ref.shape[0]
    for copy in loads:
        copy.wait()

    def grads(t):
        left = rows_ref[:, t * block : (t + 1) * block]
        for i in range(3):
            at = pl.ds(i * span, span)
            term = token_product(left, left_ref[:, :, at].reshape(length, span))
            grad_ref[t, :, :, at] = term.astype(LOW).reshape(seqs, part, span)

    order = []
    for i in range((planes + 1) // 2):
        order += [planes - 1 - i, i] if planes - 1 - i != i else [i]
    for t in order[:2]:
        grads(t)
    line.step(0)
    for t in order[2:]:
        grads(t)
    work = PlaneScatter(
        chips, here, left_ref, right_ref, True, (near_out, near_in, far_out, far_in), near, far
    )
    work.start()
    units = slots_ref.shape[2]
    lower = half_rows(slots_ref.shape[1], 1)
    ups = ChipSwap(
        chips,
        here,
        lambda index: half_block(up_ref, units, index, 1),
        lambda index: slots_ref.at[index, lower],
        chip_sems,
    )
    ups.start(local.at[0])
    for i in range(1, line.steps):
        line.step(i)

    def store(tile, total):
        mine[tile] = total.astype(LOW)

    line.finish(store)
    swaps = [
        remote(mine.at[2 * device[1] + device[2]], parts.at[me], swap_sems, k, device)
        for k, device in enumerate(peers, 1)
    ]
    for copy in swaps:
        copy.start()
    parts[me] = mine[me]
    work.finish(out_ref)
    for k in range(1, seqs):
        swaps[k - 1].wait_send()
        index = lax.rem(me + seqs - k, seqs)
        remote(mine.at[0], parts.at[index], swap_sems, k, here).wait_recv()
    width = seqs * span
    gain = gain_ref[:, pl.ds(0, 1)]
    summed = jnp.zeros(gain.shape, F32)
    for i in range(3):
        step, pieces = (seqs * HD, planes) if strided else (width, 1)
        size = step // seqs
        for piece in range(pieces):
            at = i * span + piece * size
            columns = pl.ds(i * width + piece * step, step)
            total = jnp.concatenate(
                [parts[s, :, pl.ds(at, size)].astype(F32) for s in range(seqs)], axis=1
            )
            weight = weight_ref[:, columns].astype(F32)
            summed = summed + jnp.sum(total * weight, axis=1, keepdims=True)
            total_ref[:, columns] = total * gain
    gains_ref[...] = jnp.broadcast_to(summed, gains_ref.shape)
    ups.finish()


def in_scatter(planes, chips, heads, strided, left, right, rows, up_grads, weight, gain, slots):
    _, tokens, _ = left.shape
    width = right.shape[0]
    seqs = 2 * chips
    part, wide = weight.shape[0], left.shape[2]
    return call(
        functools.partial(in_scatter_kernel, planes, chips, heads, strided),
        "in_scatter",
        [
            shape((tokens, width), F32),
            shape(weight.shape, F32),
            shape((part, 128), F32),
            shape(slots.shape, LOW),
        ],
        (left, right, rows, up_grads, weight, gain, slots),
        [HBM, HBM, HBM, HBM, VMEM, VMEM, HBM],
        [VMEM, VMEM, VMEM, HBM],
        [
            *[pltpu.VMEM(whole.shape, LOW) for whole in (left, right, rows)],
            pltpu.VMEM((planes, seqs, part, wide), LOW),
            *PlaneScatter.scratch(chips, tokens, width),
            pltpu.VMEM((planes + 1, seqs, part, wide), LOW),
            *[pltpu.VMEM((seqs, part, wide), LOW)] * 2,
            *PlaneScatter.sems(chips, width),
            *pairs_of(2 * planes, 2 * planes, seqs, chips),
            pltpu.SemaphoreType.DMA((4,)),
        ],
        4,
        {6: 3},
    )


class PairScatter:
    PARTS = 2

    def __init__(self, planes, here, left, right, turned, buffers, near, up, down):
        self.planes, self.here = planes, here
        self.left, self.right, self.turned = left, right, turned
        self.near_out, self.own, slots = buffers
        self.near = near
        self.tokens, width = self.near_out.shape[1:]
        self.tiles = [pl.ds(at, COLUMNS) for at in range(0, width, COLUMNS)]
        size = width // self.PARTS

        def part(p):
            at = p * size if isinstance(p, int) else pl.multiple_of(p * size, 128)
            return (slice(None), pl.ds(at, size))

        self.line = LineScatter(
            planes,
            here,
            self.PARTS,
            part,
            lambda p: [(rows, part(p)[1]) for rows in row_tiles(self.tokens, 32)],
            lambda t, tile: self.own[(t, *tile)].astype(F32),
            slots,
            up,
            down,
        )

    def near_copy(self, i):
        z, c, core = self.here
        at = (slice(None), slice(None), self.tiles[i])
        return remote(self.near_out.at[at], self.own.at[at], self.near, i, (z, c, 1 - core))

    def start(self):
        core, tokens = self.here[2], self.tokens
        left = jnp.concatenate([self.left[t, 1 - core] for t in range(self.planes)], axis=0)
        for i, columns in enumerate(self.tiles):
            part = product(left, self.right, columns, self.turned).astype(LOW)
            for t in range(self.planes):
                self.near_out[t, :, columns] = part[t * tokens : (t + 1) * tokens]
            self.near_copy(i).start()
        left = jnp.concatenate([self.left[t, core] for t in range(self.planes)], axis=0)
        for i, columns in enumerate(self.tiles):
            part = product(left, self.right, columns, self.turned)
            self.near_copy(i).wait_recv()
            for t in range(self.planes):
                self.own[t, :, columns] = (
                    part[t * tokens : (t + 1) * tokens] + self.own[t, :, columns].astype(F32)
                ).astype(LOW)
        self.line.step(0)

    def finish(self, out_ref):
        def store(tile, total):
            out_ref[tile] = total

        self.line.finish(store)
        for i in range(len(self.tiles)):
            self.near_copy(i).wait_send()

    @staticmethod
    def scratch(planes, tokens, width):
        return [
            *[pltpu.VMEM((planes, tokens, width), LOW)] * 2,
            pltpu.VMEM((planes + 1, tokens, width), LOW),
        ]

    @classmethod
    def sems(cls, planes, width):
        return pairs_of(width // COLUMNS, cls.PARTS * planes, cls.PARTS * planes)


def feed_forward_kernel(
    planes, chips, width_ff, x_ref, up_ref, grads_ref, down_ref,
    out_ref, normed_ref, downs_ref, gup_ref, gdown_ref, slots_ref,
    rows, ups, grads, downs, back, act, slope, stat, stat_out, stat_in,
    normed, d_up, near_out, own, sums, gup, gdown, *sems,
):
    here = place()
    z, c, core = here
    count = 2 * planes
    me = 2 * z + core
    up, down, near, chip_sems, stat_sems, pair, rise, fall, swap_sems = [
        sems[2 * i : 2 * i + 2] for i in range(9)
    ]
    local = sems[18]
    tokens, width = x_ref.shape
    units = ups.shape[1]
    load_up = pltpu.make_async_copy(up_ref, ups, local.at[0])
    load_grads = pltpu.make_async_copy(grads_ref, grads, local.at[1])
    load_up.start()
    load_grads.start()
    barrier = pltpu.get_barrier_semaphore()
    ids = [lax.rem(me + k, count) for k in range(1, count)]
    group_peers = [(index // 2, c, lax.rem(index, 2)) for index in ids]
    peers = [*group_peers, *chip_peers(chips, here)]
    greet(barrier, peers)
    pl.semaphore_wait(barrier, len(peers))

    group = GroupGather(planes, here, x_ref, rows, up, down, near)
    group.start(local.at[2])
    keep = pltpu.make_async_copy(down_ref, downs.at[c], local.at[3])
    keep.start()
    weights = ChipGather(
        chips,
        here,
        lambda half: row_half(down_ref, half),
        lambda chip, half: row_half(downs.at[chip], half),
        chip_sems,
    )
    weights.start()
    load_up.wait()

    step = tokens
    lane = lax.broadcasted_iota(jnp.int32, (step, 128), 1)

    def forward(t):
        group.other(t)
        block = rows[t].reshape(2 * tokens, width)
        for at in range(0, units, COLUMNS):
            columns = pl.ds(at, COLUMNS)
            act[t, :, columns] = jnp.dot(block, ups[:, columns], preferred_element_type=F32)

        def some(i, carry):
            at = pl.ds(pl.multiple_of(i * step, step), step)
            value = act[t, at]
            phi = 0.5 * (1.0 + lax.erf(value * math.sqrt(0.5)))
            result = value * phi
            act[t, at] = result
            slope[t, at] = phi + value * (
                jnp.exp(value * value * -0.5) * (1.0 / math.sqrt(2.0 * math.pi))
            )
            total = jnp.sum(result, axis=1, keepdims=True)
            square = jnp.sum(result * result, axis=1, keepdims=True)
            stat[t, at] = jnp.where(lane == 0, total, jnp.where(lane == 1, square, 0.0))
            return carry

        lax.fori_loop(0, 2 * tokens // step, some, 0)

    forward(z)
    for d in range(1, planes):
        group.step(d)
        if d == 2:
            weights.relay()
        if d > 1:
            pl.when(z - d + 1 >= 0)(lambda d=d: forward(z - d + 1))
            pl.when(z + d - 1 < planes)(lambda d=d: forward(z + d - 1))
    pl.when(z - planes + 1 >= 0)(lambda: forward(z - planes + 1))
    pl.when(z + planes - 1 < planes)(lambda: forward(z + planes - 1))
    group.finish()
    keep.wait()
    load_grads.wait()
    weights.finish()
    out_downs = pltpu.make_async_copy(downs, downs_ref, local.at[4])
    out_downs.start()

    def backward(t, carry):
        block = grads[t].reshape(2 * tokens, width)
        size = units // chips
        for chip in range(chips):
            columns = pl.ds(chip * size, size)
            back[t, :, columns] = rows_product(block, downs[chip])

        def some(i, inner):
            at = pl.ds(pl.multiple_of(i * step, step), step)
            value = back[t, at]
            cross = jnp.sum(value * act[t, at], axis=1, keepdims=True)
            total = jnp.sum(value, axis=1, keepdims=True)
            stat[t, at] = jnp.where(lane == 2, cross, jnp.where(lane == 3, total, stat[t, at]))
            return inner

        lax.fori_loop(0, 2 * tokens // step, some, 0)
        for half in range(2):
            turned = stat[t, pl.ds(half * tokens, tokens)].T
            stat_out[2 * t + half] = turned[:8]
        return carry

    lax.fori_loop(0, planes, backward, 0)
    copies = [
        remote(stat_out, stat_in.at[k], stat_sems, k, device)
        for k, device in enumerate(group_peers, 1)
    ]
    for copy in copies:
        copy.start()
    for copy in copies:
        copy.wait_send()
        copy.wait_recv()

    def finish(t, carry):
        for half in range(2):
            total = stat_out[2 * t + half]
            for k in range(1, count):
                total = total + stat_in[k, 2 * t + half]
            mean, square, cross, first = (total[i : i + 1] / width_ff for i in range(4))
            scaler = lax.rsqrt(square - mean * mean + NORM_EPS)
            second = scaler * (cross - mean * first)
            figures = [scaler, -mean * scaler, scaler * first, scaler * second]
            padded = jnp.concatenate([*figures, jnp.zeros((128 - 4, tokens), F32)], axis=0)
            stat[t, pl.ds(half * tokens, tokens)] = padded.T

        def some(i, inner):
            at = pl.ds(pl.multiple_of(i * step, step), step)
            figures = stat[t, at]
            scaler, shift, first, second = (figures[:, j : j + 1] for j in range(4))
            unit = act[t, at] * scaler + shift
            normed[t, at] = unit.astype(LOW)
            d_act = back[t, at] * scaler - first - unit * second
            d_up[t, at] = (d_act * slope[t, at]).astype(LOW)
            return inner

        lax.fori_loop(0, 2 * tokens // step, some, 0)
        return carry

    lax.fori_loop(0, planes, finish, 0)
    out_normed = pltpu.make_async_copy(normed, normed_ref, local.at[5])
    out_normed.start()
    work = PairScatter(
        planes, here, Halves(d_up, tokens), ups, True, (near_out, own, sums), pair, rise, fall
    )
    work.start()

    flat_normed, flat_d_up = (
        whole[...].reshape(planes * 2 * tokens, units) for whole in (normed, d_up)
    )
    size = units // chips
    upper = half_rows(size, 0)
    swap = ChipSwap(
        chips,
        here,
        lambda index: gdown.at[index, upper],
        lambda index: slots_ref.at[index, upper],
        swap_sems,
    )
    turns_left = list(range(1, work.line.steps))

    def turn():
        if turns_left:
            work.line.step(turns_left.pop(0))

    together = max(1, 256 // size)
    for chip in range(0, chips, together):
        left = flat_normed[:, chip * size : (chip + together) * size]
        for at in range(0, width, COLUMNS):
            columns = pl.ds(at, COLUMNS)
            right = grads[:, :, :, columns].reshape(planes * 2 * tokens, COLUMNS)
            term = token_product(left, right).astype(LOW)
            for i in range(together):
                gdown[chip + i, :, columns] = term[i * size : (i + 1) * size]
        if chip // together % 2:
            turn()
    swap.start(local.at[6])
    out_gdown = pltpu.make_async_copy(gdown, gdown_ref, local.at[9])
    out_gdown.start()
    chunk = gup.shape[1]
    out_gups = [
        pltpu.make_async_copy(
            gup.at[i % 2], gup_ref.at[pl.ds(i * chunk, chunk)], local.at[7 + i % 2]
        )
        for i in range(width // chunk)
    ]
    for i in range(width // chunk):
        if i % 2 == 0:
            turn()
        left = rows[:, :, :, pl.ds(i * chunk, chunk)].reshape(planes * 2 * tokens, chunk)
        term = token_product(left, flat_d_up).astype(LOW)
        if i > 1:
            out_gups[i - 2].wait()
        gup[i % 2] = term
        out_gups[i].start()
    while turns_left:
        turn()
    work.finish(out_ref)
    swap.finish()
    out_downs.wait()
    out_normed.wait()
    out_gdown.wait()
    for copy in out_gups[-2:]:
        copy.wait()


class Halves:
    def __init__(self, whole, tokens):
        self.whole, self.tokens = whole, tokens

    def __getitem__(self, at):
        t, core = at
        rows = pl.ds(pl.multiple_of(core * self.tokens, self.tokens), self.tokens)
        return self.whole[t, rows]


def feed_forward(planes, chips, width_ff, x_block, up_mine, grads, down_block):
    tokens, width = x_block.shape
    units = up_mine.shape[1]
    size = down_block.shape[0]
    wide = (planes, 2 * tokens, units)
    return call(
        functools.partial(feed_forward_kernel, planes, chips, width_ff),
        "feed_forward",
        [
            shape((tokens, width), F32),
            shape(wide, LOW),
            shape((chips, size, width), LOW),
            shape((width, units), LOW),
            *[shape((chips, size, width), LOW)] * 2,
        ],
        (x_block, up_mine, grads, down_block),
        [HBM] * 4,
        [VMEM, *[HBM] * 5],
        [
            pltpu.VMEM((planes, 2, tokens, width), LOW),
            pltpu.VMEM((width, units), LOW),
            pltpu.VMEM((planes, 2, tokens, width), LOW),
            pltpu.VMEM((chips, size, width), LOW),
            *[pltpu.VMEM(wide, F32)] * 3,
            pltpu.VMEM((planes, 2 * tokens, 128), F32),
            pltpu.VMEM((2 * planes, 8, 128), F32),
            pltpu.VMEM((2 * planes, 2 * planes, 8, 128), F32),
            *[pltpu.VMEM(wide, LOW)] * 2,
            *PairScatter.scratch(planes, tokens, width),
            pltpu.VMEM((2, 256, units), LOW),
            pltpu.VMEM((chips, size, width), LOW),
            *GroupGather.sems(planes),
            *pairs_of(ChipGather.count(chips), 2 * planes),
            *PairScatter.sems(planes, width),
            *pairs_of(chips),
            pltpu.SemaphoreType.DMA((10,)),
        ],
        7,
    )


def swap_lanes(values):
    lane = lax.broadcasted_iota(jnp.int32, values.shape, 1)
    return jnp.where(
        lax.rem(lane, 2) == 0,
        pltpu.roll(values, values.shape[1] - 1, 1),
        pltpu.roll(values, 1, 1),
    )


def twice(table):
    return jnp.concatenate([table, table], axis=1)


def turns(meta_ref, rows):
    cosine, sine, shrink = [twice(meta_ref[rows, pl.ds(i * HD, HD)]) for i in range(3)]
    return (cosine, sine, cosine * shrink, sine * shrink)


def allowed_block(meta_ref, rows, size, columns):
    query = rows + lax.broadcasted_iota(jnp.int32, (size, columns), 0)
    key = lax.broadcasted_iota(jnp.int32, (size, columns), 1)
    offset = meta_ref[pl.ds(rows, size), pl.ds(3 * HD, 1)].astype(jnp.int32)
    return (key <= query) & (key >= query - offset)


BLOCK = 256


def attention_forward_kernel(
    planes, chips, heads, strided,
    x_ref, meta_ref, weight_ref, scale_ref, out_ref, gain_ref, up_ref, grad_ref,
    q_ref, k_ref, v_ref, att_ref, log_ref, sum_ref,
    rows_ref, metas_ref, qkvs_ref, outs_ref, gains_ref, ups_ref, grads_ref, tiles_ref,
    qkv_ref, rows, metas, qkvs, outs, raw, wide, tile, near_out, near_in, far_out, far_in,
    *sems,
):
    here = place()
    z, c, core = here
    seqs = 2 * chips
    count = planes * seqs
    me = 2 * c + core
    flat = z * seqs + me
    groups = [sems[2 * i : 2 * i + 2] for i in range(17)]
    swap_sems, x_far, x_near, meta_far, meta_near, up, down, up_two, down_two = groups[:9]
    gain_sems, up_sems, near, far, tile_sems, grad_up, grad_down, pair = groups[9:]
    local = sems[34]
    tokens, width = x_ref.shape
    part = qkv_ref.shape[1]
    length = seqs * tokens
    span = heads * HD
    barrier = pltpu.get_barrier_semaphore()

    def device_of(k):
        other = lax.rem(flat + k, count)
        return (other // seqs, lax.rem(other, seqs) // 2, lax.rem(other, 2))

    def signal(k, carry):
        greet(barrier, [device_of(k)])
        return carry

    lax.fori_loop(1, count, signal, 0)
    scale = scale_ref[:, pl.ds(0, 1)]
    for s in range(seqs):
        for i in range(3):
            if strided:
                starts = [i * width + (t * seqs + s) * HD for t in range(planes)]
                size = span // planes
            else:
                starts, size = [i * width + s * span], span
            piece = jnp.concatenate([weight_ref[:, pl.ds(at, size)] for at in starts], axis=1)
            qkv_ref[s, :, pl.ds(i * span, span)] = (piece.astype(F32) * scale).astype(LOW)
    pl.semaphore_wait(barrier, count - 1)

    mine = pltpu.make_async_copy(qkv_ref.at[me], qkvs.at[z, me], local.at[0])
    own_out = pltpu.make_async_copy(out_ref, outs.at[z] if strided else outs, local.at[1])
    units = up_ref.shape[1]
    keeps = [
        pltpu.make_async_copy(x_ref, rows.at[me], local.at[2]),
        pltpu.make_async_copy(meta_ref, metas.at[me], local.at[3]),
        pltpu.make_async_copy(gain_ref, gains_ref.at[flat], local.at[4]),
        pltpu.make_async_copy(up_ref, column_block(ups_ref, units, c), local.at[5]),
    ]
    peers = plane_peers(chips, here)
    swaps = [
        remote(qkv_ref.at[2 * device[1] + device[2]], qkvs.at[z, me], swap_sems, k, device)
        for k, device in enumerate(peers, 1)
    ]
    mine.start()
    own_out.start()
    for copy in swaps:
        copy.start()
    gather = PlaneGather(chips, here, x_ref, rows, x_far, x_near)
    meta_gather = PlaneGather(chips, here, meta_ref, metas, meta_far, meta_near)
    for copy in keeps:
        copy.start()

    def gain_copy(k):
        return remote(gain_ref, gains_ref.at[flat], gain_sems, k, device_of(k))

    def gain_start(k, carry):
        gain_copy(k).start()
        return carry

    mine.wait()
    own_out.wait()
    for k in range(1, seqs):
        index = lax.rem(me + seqs - k, seqs)
        remote(qkv_ref.at[0], qkvs.at[z, index], swap_sems, k, here).wait_recv()
    half = seqs // 2
    line = LineGather(
        planes, here, lambda t: [qkvs.at[t, pl.ds(i * half, half)] for i in range(2)], up, down
    )
    line_two = LineGather(planes, here, lambda t: [outs.at[t]], up_two, down_two)
    line.start()
    gather.start()
    meta_gather.start()
    lax.fori_loop(1, count, gain_start, 0)
    gather.relay()
    meta_gather.relay()
    line.step(1)
    gather.forward()
    meta_gather.forward()
    ups = ChipGather(
        chips,
        here,
        lambda part: row_half(up_ref, part),
        lambda chip, part: row_half(column_block(ups_ref, units, chip), part),
        up_sems,
    )
    ups.start()
    line.step(2)
    gather.finish()
    meta_gather.finish()
    for copy in keeps:
        copy.wait()

    block = seqs * part

    def add(t, fresh=False):
        columns = pl.ds(pl.multiple_of(t * block, 128), block)
        left = rows[:, :, columns].reshape(length, block)
        for i in range(3):
            at = pl.ds(i * span, span)
            term = jnp.dot(left, qkvs[t, :, :, at].reshape(block, span), preferred_element_type=F32)
            raw[:, at] = term if fresh else raw[:, at] + term

    add(z, True)
    for d in range(1, planes):
        if d == 3:
            ups.relay()
        if d > 2:
            line.step(d)
        if d == planes - 1:
            if strided:
                line_two.start()
            group = GroupGather(planes, here, grad_ref, grads_ref, grad_up, grad_down, pair)
            group.start(local.at[6])
        pl.when(z - d >= 0)(lambda d=d: add(z - d))
        pl.when(z + d < planes)(lambda d=d: add(z + d))
    outputs = [
        pltpu.make_async_copy(rows, rows_ref, local.at[7]),
        pltpu.make_async_copy(metas, metas_ref, local.at[8]),
        pltpu.make_async_copy(qkvs, qkvs_ref, local.at[9]),
    ]
    for copy in outputs:
        copy.start()

    table = RowBlocks(metas)
    for at in range(0, length, BLOCK):
        at = pl.ds(at, BLOCK)
        tables = turns(table, at)
        for two in range(heads // 2):
            query = raw[at, pl.ds(2 * HD * two, 2 * HD)]
            query = (query * tables[0] + swap_lanes(query) * tables[1]).astype(LOW)
            key = raw[at, pl.ds(span + 2 * HD * two, 2 * HD)]
            key = (key * tables[2] + swap_lanes(key) * tables[3]).astype(LOW)
            value = raw[at, pl.ds(2 * span + 2 * HD * two, 2 * HD)].astype(LOW)
            for side in range(2):
                lanes = slice(side * HD, (side + 1) * HD)
                q_ref[2 * two + side, at] = query[:, lanes]
                k_ref[2 * two + side, at] = key[:, lanes]
                v_ref[2 * two + side, at] = value[:, lanes]
    log_ref[...] = jnp.zeros(log_ref.shape, F32)

    def one_head(head, carry):
        for start in range(0, length, BLOCK):
            columns = start + BLOCK
            at = pl.ds(start, BLOCK)
            scores = lax.dot_general(
                q_ref[head, at],
                k_ref[head, pl.ds(0, columns)],
                (((1,), (1,)), ((), ())),
                preferred_element_type=F32,
            )
            allowed = allowed_block(table, start, BLOCK, columns)
            scores = jnp.where(allowed, scores, NEG_FILL)
            top = jnp.max(scores, axis=1, keepdims=True)
            shifted = jnp.exp(scores - top)
            total = jnp.sum(shifted, axis=1, keepdims=True)
            probs = (shifted * (1.0 / total)).astype(LOW)
            wide[head, at] = jnp.dot(
                probs, v_ref[head, pl.ds(0, columns)], preferred_element_type=F32
            )
            lane = lax.broadcasted_iota(jnp.int32, (BLOCK, 128), 1)
            log_ref[at] = jnp.where(lane == head, top + jnp.log(total), log_ref[at])
        return carry

    first = 0
    for d in range(1, planes):
        last = -(-heads * d // planes)
        lax.fori_loop(first, last, one_head, 0)
        first = last
        if strided:
            line_two.step(d)
        if d == 2:
            group.step(1)
    lax.fori_loop(first, heads, one_head, 0)
    lane = lax.broadcasted_iota(jnp.int32, (tokens, 128), 1)
    column = jnp.sum(outs[...].astype(F32).reshape(span, width), axis=0, keepdims=True)
    for s in range(seqs):
        at = pl.ds(s * tokens, tokens)
        low = jnp.concatenate([wide[head, at] for head in range(heads)], axis=1).astype(LOW)
        att_ref[s] = low
        value = low.astype(F32)
        total = jnp.sum(value, axis=1, keepdims=True)
        square = jnp.sum(value * value, axis=1, keepdims=True)
        both = jnp.where(lane == 0, total, jnp.where(lane == 1, square, 0.0))
        tile[s, pl.ds(0, 8)] = both.T[:8]
        for i in range(width // 128):
            tile[s, pl.ds(8 + i, 1)] = column[:, i * 128 : (i + 1) * 128]
    out_tiles = [
        remote(tile.at[2 * device[1] + device[2]], tiles_ref.at[me], tile_sems, k, device)
        for k, device in enumerate(peers, 1)
    ]
    for copy in out_tiles:
        copy.start()
    keep = pltpu.make_async_copy(tile.at[me], tiles_ref.at[me], local.at[10])
    keep.start()
    out_outs = pltpu.make_async_copy(outs, outs_ref, local.at[11])
    out_outs.start()
    work = PlaneScatter(
        chips, here, att_ref, Flat(outs, span), False, (near_out, near_in, far_out, far_in), near, far
    )
    work.start()
    for d in range(2, planes):
        group.step(d)
    work.finish(sum_ref)
    group.finish()
    for t in range(planes):
        group.other(t)
    line.finish()
    if strided:
        line_two.finish()
    for copy in swaps:
        copy.wait_send()
    ups.finish()
    for copy in [keep, out_outs, *outputs]:
        copy.wait()
    for k in range(1, seqs):
        out_tiles[k - 1].wait_send()
        index = lax.rem(me + seqs - k, seqs)
        remote(tile.at[0], tiles_ref.at[index], tile_sems, k, here).wait_recv()

    def gain_wait(k, carry):
        gain_copy(k).wait_send()
        other = lax.rem(flat + count - k, count)
        remote(gain_ref, gains_ref.at[other], gain_sems, k, here).wait_recv()
        return carry

    lax.fori_loop(1, count, gain_wait, 0)


class Flat:
    def __init__(self, blocks, count):
        self.blocks, self.count = blocks, count

    def __getitem__(self, at):
        if len(self.blocks.shape) == 2:
            return self.blocks[at]
        _, columns = at
        return self.blocks[:, :, columns].reshape(self.count, columns.size)


class RowBlocks:
    def __init__(self, blocks):
        self.blocks = blocks

    def __getitem__(self, at):
        rows, columns = at
        size = self.blocks.shape[1]
        first, count = rows.start // size, rows.size // size
        return self.blocks[pl.ds(first, count), :, columns].reshape(rows.size, columns.size)


def attention_forward(
    planes, chips, heads, strided, x_block, meta, weight, scale, out_rows, gain_tile, up_block, grad
):
    seqs = 2 * chips
    tokens, width = x_block.shape
    part, wide = weight.shape[0], 3 * heads * HD
    units = up_block.shape[1]
    length = seqs * tokens
    span = heads * HD
    outs = (planes, *out_rows.shape) if strided else out_rows.shape
    tile = (seqs, 8 + width // 128, 128)
    return call(
        functools.partial(attention_forward_kernel, planes, chips, heads, strided),
        "attention_forward",
        [
            *[shape((heads, length, HD), LOW)] * 3,
            shape((seqs, tokens, span), LOW),
            shape((length, 128), F32),
            shape((tokens, width), F32),
            shape((seqs, tokens, width), LOW),
            shape((seqs, *meta.shape), F32),
            shape((planes, seqs, part, wide), LOW),
            shape(outs, LOW),
            shape((planes * seqs, *gain_tile.shape), F32),
            shape((width, chips * units) if units % 128 == 0 else (chips, width, units), LOW),
            shape((planes, 2, *grad.shape), LOW),
            shape(tile, F32),
        ],
        (x_block, meta, weight, scale, out_rows, gain_tile, up_block, grad),
        [HBM, HBM, VMEM, VMEM, HBM, HBM, HBM, HBM],
        [*[VMEM] * 6, *[HBM] * 8],
        [
            pltpu.VMEM((seqs, part, wide), LOW),
            pltpu.VMEM((seqs, tokens, width), LOW),
            pltpu.VMEM((seqs, *meta.shape), F32),
            pltpu.VMEM((planes, seqs, part, wide), LOW),
            pltpu.VMEM(outs, LOW),
            pltpu.VMEM((length, 3 * span), F32),
            pltpu.VMEM((heads, length, HD), F32),
            pltpu.VMEM(tile, F32),
            *PlaneScatter.scratch(chips, tokens, width),
            *pairs_of(seqs),
            *PlaneGather.sems(chips),
            *PlaneGather.sems(chips),
            *pairs_of(*[2 * planes] * 2, *[planes] * 2, planes * seqs, ChipGather.count(chips)),
            *PlaneScatter.sems(chips, width),
            *pairs_of(seqs),
            *GroupGather.sems(planes),
            pltpu.SemaphoreType.DMA((12,)),
        ],
        1,
    )


def attention_backward_kernel(
    planes, chips, heads, strided,
    x_ref, stat_ref, tile_ref, left_ref, right_ref,
    q_in, k_in, v_in, att_in, out_in, log_in, meta_in, up_ref, down_ref, _,
    tiles_ref, ffn_ref, out_ref, total_ref, slots_ref, down_slots_ref,
    rows, stats, left, right, q_ref, k_ref, v_ref, att_ref, outs, log_ref, meta_ref,
    near_out, near_own, near_sums, grad, dq, dk, dv, normed_all, own, sums, *sems,
):
    here = place()
    z, c, core = here
    seqs = 2 * chips
    count = planes * seqs
    me = 2 * c + core
    flat = z * seqs + me
    x_far, x_near, s_far, s_near, tile_sems, near, up, down, up_two, down_two, swap_sems = [
        sems[2 * i : 2 * i + 2] for i in range(11)
    ]
    down_sems = sems[22:24]
    local = sems[24]
    pairs = [
        (left_ref, left), (right_ref, right), (att_in, att_ref), (out_in, outs), (meta_in, meta_ref),
        (q_in, q_ref), (k_in, k_ref), (v_in, v_ref), (log_in, log_ref),
    ]
    loads = [pltpu.make_async_copy(*pair, local.at[i]) for i, pair in enumerate(pairs)]
    for copy in loads:
        copy.start()
    barrier = pltpu.get_barrier_semaphore()

    def device_of(k):
        other = lax.rem(flat + k, count)
        return (other // seqs, lax.rem(other, seqs) // 2, lax.rem(other, 2))

    def signal(k, carry):
        greet(barrier, [device_of(k)])
        return carry

    lax.fori_loop(1, count, signal, 0)
    pl.semaphore_wait(barrier, count - 1)
    gather = PlaneGather(chips, here, x_ref, rows, x_far, x_near)
    stat_gather = PlaneGather(chips, here, stat_ref, stats, s_far, s_near)
    gather.start()
    stat_gather.start()
    keeps = [
        pltpu.make_async_copy(x_ref, rows.at[me], local.at[9]),
        pltpu.make_async_copy(stat_ref, stats.at[me], local.at[10]),
        pltpu.make_async_copy(tile_ref.at[flat], tiles_ref.at[flat], local.at[11]),
    ]
    for copy in keeps:
        copy.start()

    def tile_copy(k):
        other = lax.rem(flat + k, count)
        return remote(tile_ref.at[other], tiles_ref.at[flat], tile_sems, k, device_of(k))

    def tile_start(k, carry):
        tile_copy(k).start()
        return carry

    lax.fori_loop(1, count, tile_start, 0)
    tokens, width = x_ref.shape
    for copy in loads[:2]:
        copy.wait()
    work = PairScatter(
        planes, here, Halves(left, tokens), right, False, (near_out, near_own, near_sums),
        near, up, down,
    )
    work.start()
    left_turns = list(range(1, work.line.steps))

    def turn(until=None):
        step = left_turns[0] + 1 if until is None and left_turns else until
        while left_turns and left_turns[0] < step:
            work.line.step(left_turns.pop(0))

    turn()
    gather.relay()
    stat_gather.relay()
    turn()
    gather.forward()
    stat_gather.forward()
    gather.finish()
    stat_gather.finish()
    units = slots_ref.shape[2]
    upper, lower = half_rows(width, 0), half_rows(down_ref.shape[1], 1)
    swaps = [
        ChipSwap(
            chips,
            here,
            lambda index: half_block(up_ref, units, index, 0),
            lambda index: slots_ref.at[index, upper],
            swap_sems,
        ),
        ChipSwap(
            chips,
            here,
            lambda index: down_ref.at[index, lower],
            lambda index: down_slots_ref.at[index, lower],
            down_sems,
        ),
    ]
    for i, swap in enumerate(swaps):
        swap.start(local.at[12 + i])
    for copy in [*loads[2:], *keeps]:
        copy.wait()
    turn()
    length, span = att_ref.shape
    part = own.shape[1]
    per = BLOCK // tokens
    for first in range(0, seqs, per):
        at = pl.ds(first * tokens, BLOCK)
        figures = stats[pl.ds(first, per)].reshape(BLOCK, 128)
        mean, scaler, one, two = (figures[:, i : i + 1] for i in range(4))
        block = rows[pl.ds(first, per)].reshape(BLOCK, width)
        d_sub = product(block, outs, slice(None), True)
        normed = (att_ref[at].astype(F32) - mean) * scaler
        normed_all[at] = normed.astype(LOW)
        d_att = (scaler * (d_sub - one - normed * two)).astype(LOW)
        for head in range(heads):
            grad[head, at] = d_att[:, head * HD : (head + 1) * HD]
    for at in range(0, width, COLUMNS):
        columns = pl.ds(at, COLUMNS)
        term = token_product(normed_all[...], rows[:, :, columns].reshape(length, COLUMNS)).astype(LOW)
        for t in range(planes):
            own[t, :, columns] = term[t * part : (t + 1) * part]
    line = LineScatter(
        planes,
        here,
        1,
        lambda p: (slice(None),),
        lambda p: [(row,) for row in row_tiles(part, 16)],
        lambda t, tile: own[(t, *tile)].astype(F32),
        sums,
        up_two,
        down_two,
    )
    if strided:
        line.step(0)
    dk[...] = jnp.zeros(dk.shape, F32)
    dv[...] = jnp.zeros(dv.shape, F32)

    def one_head(head, carry):
        for start in range(0, length, BLOCK):
            columns = start + BLOCK
            at = pl.ds(start, BLOCK)
            keys = pl.ds(0, columns)
            query, key = q_ref[head, at], k_ref[head, keys]
            out_grad = grad[head, at]
            scores = lax.dot_general(
                query, key, (((1,), (1,)), ((), ())), preferred_element_type=F32
            )
            allowed = allowed_block(meta_ref, start, BLOCK, columns)
            lane = lax.broadcasted_iota(jnp.int32, (BLOCK, 128), 1)
            log_total = jnp.sum(jnp.where(lane == head, log_ref[at], 0.0), axis=1, keepdims=True)
            probs = jnp.where(allowed, jnp.exp(scores - log_total), 0.0)
            d_probs = lax.dot_general(
                out_grad, v_ref[head, keys], (((1,), (1,)), ((), ())), preferred_element_type=F32
            )
            delta = jnp.sum(probs * d_probs, axis=1, keepdims=True)
            d_scores = (probs * (d_probs - delta)).astype(LOW)
            dq[head, at] = jnp.dot(d_scores, key, preferred_element_type=F32)
            dk[head, keys] += token_product(d_scores, query)
            dv[head, keys] += token_product(probs.astype(LOW), out_grad)
        return carry

    first = 0
    for i in range(1, planes - 1):
        last = -(-heads * i // (planes - 1))
        lax.fori_loop(first, last, one_head, 0)
        first = last
        turn()
        if strided:
            line.step(i)
    lax.fori_loop(first, heads, one_head, 0)
    turn(work.line.steps)
    for start in range(0, length, BLOCK):
        at = pl.ds(start, BLOCK)
        tables = turns(meta_ref, at)
        for two in range(heads // 2):
            both = [
                jnp.concatenate([whole[2 * two, at], whole[2 * two + 1, at]], axis=1).astype(LOW)
                for whole in (dq, dk, dv)
            ]
            query, key = both[0].astype(F32), both[1].astype(F32)
            query = query * tables[0] + swap_lanes(query * tables[1])
            key = key * tables[2] + swap_lanes(key * tables[3])
            out_ref[at, pl.ds(2 * HD * two, 2 * HD)] = query.astype(LOW)
            out_ref[at, pl.ds(span + 2 * HD * two, 2 * HD)] = key.astype(LOW)
            out_ref[at, pl.ds(2 * span + 2 * HD * two, 2 * HD)] = both[2]
    work.finish(ffn_ref)
    if strided:

        def store(tile, total):
            total_ref[tile] = total

        line.finish(store)
    else:
        for t in range(planes):
            total_ref[pl.ds(t * part, part)] = own[t].astype(F32)
    for swap in swaps:
        swap.finish()

    def tile_wait(k, carry):
        tile_copy(k).wait_send()
        other = lax.rem(flat + count - k, count)
        remote(tile_ref.at[0], tiles_ref.at[other], tile_sems, k, here).wait_recv()
        return carry

    lax.fori_loop(1, count, tile_wait, 0)


def attention_backward(planes, chips, heads, strided, part, units, args):
    tokens, width = args[0].shape
    seqs = 2 * chips
    length, span = args[8].shape
    kept = [pltpu.VMEM(args[i].shape, args[i].dtype) for i in (3, 4, 5, 6, 7, 8, 9, 10, 11)]
    return call(
        functools.partial(attention_backward_kernel, planes, chips, heads, strided),
        "attention_backward",
        [
            shape(args[2].shape, F32),
            shape((tokens, width), F32),
            shape((length, 3 * span), LOW),
            shape((part if strided else span, width), F32),
            shape((chips, width, units), LOW),
            shape(args[14].shape, LOW),
        ],
        args,
        [HBM] * 15,
        [HBM, VMEM, VMEM, VMEM, HBM, HBM],
        [
            pltpu.VMEM((seqs, tokens, width), LOW),
            pltpu.VMEM((seqs, tokens, 128), F32),
            *kept,
            *PairScatter.scratch(planes, tokens, width),
            pltpu.VMEM((heads, length, HD), LOW),
            *[pltpu.VMEM((heads, length, HD), F32)] * 3,
            pltpu.VMEM((length, span), LOW),
            pltpu.VMEM((planes, part, width), LOW),
            pltpu.VMEM((planes + 1, part, width), LOW),
            *PlaneGather.sems(chips),
            *PlaneGather.sems(chips),
            *pairs_of(planes * seqs),
            *PairScatter.sems(planes, width),
            *pairs_of(planes, planes, chips, chips),
            pltpu.SemaphoreType.DMA((14,)),
        ],
        2,
        {14: 5},
    )


def body(
    hidden_in,
    segment_ids,
    position_ids,
    w_qkv,
    w_out,
    w_up,
    w_down,
    gain_attn,
    gain_attn_sub,
    gain_ffn,
    gain_ffn_sub,
    ema_qkv,
    ema_out,
    ema_up,
    ema_down,
    ema_gain_attn,
    ema_gain_attn_sub,
    ema_gain_ffn,
    ema_gain_ffn_sub,
    out_grad,
):
    _, tokens, width = hidden_in.shape
    planes, chips = lax.axis_size("dp"), lax.axis_size("chip")
    seqs = 2 * chips
    length = tokens * seqs
    heads = HEADS // seqs
    span = heads * HD
    part = w_qkv.shape[0]
    strided = part % HD == 0
    width_ff = w_down.shape[0] * planes * seqs
    seq_index = lax.axis_index(SEQ)

    def gain_rows(weight, gain):
        return (weight.astype(F32) * gain.astype(F32)[:, None]).astype(LOW)

    out_scaled = gain_rows(w_out, gain_attn_sub)
    down_scaled = gain_rows(w_down, gain_ffn_sub)
    x_in = hidden_in[0].astype(F32)
    normed_one, scaler_one = moments(x_in)
    normed_low = normed_one.astype(LOW)
    qkv_gain = jnp.broadcast_to(gain_attn.astype(F32)[:, None], (part, 128))
    gain_tile = jnp.zeros((8, 128), F32).at[0, :part].set(gain_ffn.astype(F32))

    if not strided:
        out_all = lax.all_gather(out_scaled, ALL, axis=0, tiled=True)
        out_scaled = lax.dynamic_slice_in_dim(out_all, seq_index * span, span, axis=0)

    grad_low = out_grad[0]
    (
        queries, keys, values, attended, log_total, out_sum,
        row_in, meta, qkv_mine, out_mine, gain_tiles, up_mine, grad_flat, tiles,
    ) = attention_forward(
        planes,
        chips,
        heads,
        strided,
        normed_low,
        token_tables(position_ids[0]),
        w_qkv,
        qkv_gain,
        out_scaled,
        gain_tile,
        w_up,
        grad_low,
    )
    if up_mine.ndim == 3:
        up_mine = up_mine.transpose(1, 0, 2).reshape(width, -1)
    row_in = row_in.reshape(length, width)
    meta = meta.reshape(length, -1)
    qkv_mine = qkv_mine.reshape(width, 3 * span)
    out_mine = out_mine.reshape(span, width)
    attended = attended.reshape(length, span)
    tiles = jnp.sum(tiles, axis=0)
    column_sum = tiles[8:].reshape(width)
    sums = tiles[:2].T
    gain_three = gain_tiles[:, 0, :part].reshape(width)
    mean_two = sums[:, :1] / width
    scaler_two = lax.rsqrt(sums[:, 1:] / width - mean_two * mean_two + NORM_EPS)
    projected = scaler_two * (out_sum - mean_two * column_sum[None, :])
    hmid = x_in + projected
    normed_three, scaler_three = moments(hmid)
    ffn_in = (normed_three * gain_three).astype(LOW)

    grad_top = grad_low.astype(F32)
    units = w_up.shape[1]
    d_ffn_in, normed_four, down_mine, grad_up, grad_down, down_slots = feed_forward(
        planes, chips, width_ff, ffn_in, up_mine, grad_flat, down_scaled
    )
    down_mine = down_mine.reshape(-1, width)
    if units % 128:
        grad_up = grad_up.reshape(width, chips, units).transpose(1, 0, 2)

    gain_part = jnp.sum(d_ffn_in * normed_three, axis=0).reshape(planes * seqs, 1, part)
    gain_part = jnp.pad(gain_part, ((0, 0), (0, 7), (0, 128 - part)))
    d_hmid = grad_top + norm_back(d_ffn_in * gain_three, normed_three, scaler_three)
    d_hmid_low = d_hmid.astype(LOW)
    d_hmid_wide = d_hmid_low.astype(F32)
    first_two = jnp.sum(d_hmid_wide * column_sum[None, :], axis=1, keepdims=True) / width
    second_two = jnp.sum(d_hmid_wide * projected, axis=1, keepdims=True) / width
    token_stats = jnp.concatenate([mean_two, scaler_two, first_two, second_two], axis=1)
    gain_part, ffn_out, d_qkv, sum_out, up_slots, down_slots = attention_backward(
        planes,
        chips,
        heads,
        strided,
        part,
        units,
        (
            d_hmid_low,
            jnp.pad(token_stats, ((0, 0), (0, 124))),
            gain_part,
            normed_four,
            down_mine,
            queries,
            keys,
            values,
            attended,
            out_mine,
            log_total,
            meta,
            grad_up,
            grad_down,
            down_slots,
        ),
    )
    output = (hmid + ffn_out).astype(LOW)[None]
    grad_gain_three = jnp.sum(gain_part, axis=0)[0, :part]
    d_in, sum_qkv, grad_gain_one, up_slots = in_scatter(
        planes,
        chips,
        heads,
        strided,
        d_qkv.reshape(seqs, tokens, 3 * span),
        qkv_mine,
        row_in,
        grad_up,
        w_qkv,
        qkv_gain,
        up_slots,
    )
    grad_gain_one = grad_gain_one[:, 0]
    sum_up = jnp.sum(up_slots.astype(F32), axis=0)
    sum_down = jnp.sum(down_slots.astype(F32), axis=0)
    input_grad = (d_hmid + norm_back(d_in, normed_one, scaler_one)).astype(LOW)[None]

    if not strided:
        spread = lax.dynamic_update_slice_in_dim(
            jnp.zeros((width, width), LOW), sum_out.astype(LOW), seq_index * span, axis=0
        )
        sum_out = lax.psum_scatter(spread, ALL, scatter_dimension=0, tiled=True).astype(F32)

    def finish(total, weight, gain):
        wide = weight.astype(F32)
        return (total * gain.astype(F32)[:, None], jnp.sum(total * wide, axis=1))

    sum_out, grad_gain_two = finish(sum_out, w_out, gain_attn_sub)
    sum_down, grad_gain_four = finish(sum_down, w_down, gain_ffn_sub)

    def averaged(average, weight):
        return EMA_DECAY * average + (1.0 - EMA_DECAY) * weight.astype(F32)

    return (
        output,
        input_grad,
        sum_qkv,
        sum_out,
        sum_up,
        sum_down,
        grad_gain_one,
        grad_gain_two,
        grad_gain_three,
        grad_gain_four,
        averaged(ema_qkv, w_qkv),
        averaged(ema_out, w_out),
        averaged(ema_up, w_up),
        averaged(ema_down, w_down),
        averaged(ema_gain_attn, gain_attn),
        averaged(ema_gain_attn_sub, gain_attn_sub),
        averaged(ema_gain_ffn, gain_ffn),
        averaged(ema_gain_ffn_sub, gain_ffn_sub),
    )


def solution(mesh):
    split = Mesh(
        mesh.devices.reshape(mesh.shape["dp"], mesh.shape["seq"] // 2, 2), ("dp", "chip", "core")
    )
    tokens = P("dp", SEQ, None)
    ids = P("dp", SEQ)
    rows = P(ALL, None)
    columns = P(None, ALL)
    vector = P(ALL)
    weights = (rows, rows, columns, rows)
    gains = (vector,) * 4
    return jax.shard_map(
        body,
        mesh=split,
        in_specs=(tokens, ids, ids, *weights, *gains, *weights, *gains, tokens),
        out_specs=(tokens, tokens, *weights, *gains, *weights, *gains),
        check_vma=False,
    )
```

```python
import functools
import math

import jax
import jax.numpy as jnp
from jax import lax
from jax.experimental import pallas as pl
from jax.experimental.pallas import tpu as pltpu
from jax.sharding import Mesh
from jax.sharding import PartitionSpec as P

HEADS = 32
HD = 64

NEG_FILL = -1000000000.0
NORM_EPS = 1e-05
EMA_DECAY = 0.7
LOW = jnp.bfloat16
F32 = jnp.float32
SEQ = ("chip", "core")
TP = ("dp", "core")
ALL = ("dp", "chip", "core")


def moments(values):
    mean = jnp.mean(values, axis=-1, keepdims=True)
    centered = values - mean
    scaler = lax.rsqrt(jnp.mean(centered * centered, axis=-1, keepdims=True) + NORM_EPS)
    return (centered * scaler, scaler)


def norm_back(scaled_grad, normed, scaler):
    first_mean = jnp.mean(scaled_grad, axis=-1, keepdims=True)
    second_mean = jnp.mean(scaled_grad * normed, axis=-1, keepdims=True)
    return scaler * (scaled_grad - first_mean - normed * second_mean)


def token_tables(positions):
    half_count = HD // 2
    index_half = jnp.arange(half_count).astype(F32)
    inverse = jnp.exp(-(2.0 * index_half / HD) * math.log(10000.0))
    decay_base = (2.0 * index_half + 0.4 * HD) / (1.4 * HD)
    where_at = positions.astype(F32)[:, None]
    angles = where_at * inverse[None, :]
    factor = jnp.exp(where_at / 512.0 * jnp.log(decay_base)[None, :])
    sign_row = jnp.where(jnp.arange(HD) % 2 == 0, -1.0, 1.0).astype(F32)
    cosine = jnp.repeat(jnp.cos(angles), 2, axis=1)
    sine = jnp.repeat(jnp.sin(angles), 2, axis=1) * sign_row[None, :]
    factor = jnp.repeat(factor, 2, axis=1)
    grow = factor * HD ** (-0.5)
    where_block = jnp.broadcast_to(where_at, (positions.shape[0], HD))
    return jnp.concatenate(
        [cosine * grow, sine * grow, HD**0.5 / (factor * factor), where_block], axis=1
    )


def dot(left_op, right_op):
    return jnp.dot(left_op, right_op, preferred_element_type=F32)


def rows_product(operand, weight_rows):
    return lax.dot_general(
        operand, weight_rows, (((1,), (1,)), ((), ())), preferred_element_type=F32
    )


def token_product(left_op, right_op):
    return lax.dot_general(left_op, right_op, (((0,), (0,)), ((), ())), preferred_element_type=F32)


MESH = pl.DeviceIdType.MESH
HBM = pl.BlockSpec(memory_space=pl.ANY)
VMEM = pl.BlockSpec(memory_space=pltpu.VMEM)
VMEM_BYTES = 60 * 1024 * 1024


def shape(dims, kind):
    return jax.ShapeDtypeStruct(dims, kind)


def pairs_of(*counts):
    return [pltpu.SemaphoreType.DMA((count,)) for count in counts for _ in range(2)]


def call(kernel, name, outs, args, in_specs, out_specs, scratch, collective=None, aliases=None):
    return pl.pallas_call(
        kernel,
        input_output_aliases=aliases or {},
        name=name,
        out_shape=outs,
        in_specs=in_specs,
        out_specs=out_specs,
        scratch_shapes=scratch,
        compiler_params=pltpu.CompilerParams(
            collective_id=collective,
            has_side_effects=collective is not None,
            vmem_limit_bytes=VMEM_BYTES,
        ),
    )(*args)


def place():
    return (lax.axis_index("dp"), lax.axis_index("chip"), lax.axis_index("core"))


def remote(source, target, sems, index, device):
    return pltpu.make_async_remote_copy(
        src_ref=source,
        dst_ref=target,
        send_sem=sems[0].at[index],
        recv_sem=sems[1].at[index],
        device_id=device,
        device_id_type=MESH,
    )


def greet(barrier, devices):
    for device in devices:
        pl.semaphore_signal(barrier, inc=1, device_id=device, device_id_type=MESH)


def greet_line(barrier, planes, here):
    z, c, core = here

    @pl.when(z < planes - 1)
    def _():
        greet(barrier, [(z + 1, c, core)])

    @pl.when(z > 0)
    def _():
        greet(barrier, [(z - 1, c, core)])


def line_peers(planes, here):
    z = here[0]
    return (2 * planes - 2 - z) // planes + (z + planes - 1) // planes


def chip_peers(chips, here):
    z, c, core = here
    return [(z, lax.rem(c + k, chips), core) for k in range(1, chips)]


def plane_peers(chips, here):
    z, c, core = here
    seqs = 2 * chips
    me = 2 * c + core
    ids = [lax.rem(me + k, seqs) for k in range(1, seqs)]
    return [(z, index // 2, lax.rem(index, 2)) for index in ids]


def column_block(whole, units, index):
    if len(whole.shape) == 3:
        return whole.at[index]
    return whole.at[:, pl.ds(pl.multiple_of(index * units, 128), units)]


UP_FIRST = 3
DOWN_FIRST = 5


def share(rows, second, eighths):
    first = rows * eighths // 128 * 16
    return pl.ds(first, rows - first) if second else pl.ds(0, first)


def half_block(whole, units, index, second):
    at = share(whole.shape[-2], second, UP_FIRST)
    if len(whole.shape) == 3:
        return whole.at[index, at]
    return whole.at[at, pl.ds(pl.multiple_of(index * units, 128), units)]


class ChipSwap:
    def __init__(self, chips, here, source, slot, sems):
        z, c, core = here
        self.sends = [
            remote(source(device[1]), slot(c), sems, k, device)
            for k, device in enumerate(chip_peers(chips, here), 1)
        ]
        self.waits = [
            remote(source(c), slot(lax.rem(c + chips - k, chips)), sems, k, here)
            for k in range(1, chips)
        ]
        self.keep = (source(c), slot(c))

    def start(self, local):
        for copy in self.sends:
            copy.start()
        self.held = pltpu.make_async_copy(*self.keep, local)
        self.held.start()

    def finish(self):
        self.held.wait()
        for send, wait in zip(self.sends, self.waits):
            send.wait_send()
            wait.wait_recv()


class ChipGather:
    def __init__(self, chips, here, source, target, sems):
        z, c, core = here
        self.here, self.sems, self.relayed = here, sems, chips == 4
        if not self.relayed:
            self.sends = [
                remote(source(None), target(c, None), sems, k, device)
                for k, device in enumerate(chip_peers(chips, here), 1)
            ]
            self.arrivals = [
                (lax.rem(c + chips - k, chips), None, k) for k in range(1, chips)
            ]
        else:
            beside = c + 1 - 2 * lax.rem(c, 2)
            above = c + 2 - 4 * (c // 2)
            to_beside, to_above = (z, beside, core), (z, above, core)
            self.sends = [
                remote(source(0), target(c, 0), sems, 0, to_beside),
                remote(source(1), target(c, 1), sems, 3, to_above),
                remote(source(1), target(c, 1), sems, 1, to_beside),
                remote(source(0), target(c, 0), sems, 2, to_above),
            ]
            self.relays = [
                remote(target(beside, 0), target(beside, 0), sems, 4, to_above),
                remote(target(above, 1), target(above, 1), sems, 5, to_beside),
            ]
            self.arrivals = [
                (beside, 0, 0), (above, 1, 3), (beside, 1, 1), (above, 0, 2),
                (3 - c, 0, 4), (3 - c, 1, 5),
            ]
        self.target = target

    def start(self):
        for copy in self.sends:
            copy.start()

    def arrive(self, i):
        chip, half, index = self.arrivals[i]
        block = self.target(chip, half)
        remote(block, block, self.sems, index, self.here).wait_recv()
        if self.relayed and i < 2:
            self.relays[i].start()

    def relay(self):
        for i in range(2 if self.relayed else 0):
            self.arrive(i)

    def rest(self):
        return range(2 if self.relayed else 0, len(self.arrivals))

    def finish(self):
        for i in self.rest():
            self.arrive(i)
        self.sent()

    def sent(self):
        for copy in [*self.sends, *(self.relays if self.relayed else [])]:
            copy.wait_send()

    @staticmethod
    def count(chips):
        return max(chips, 6)


class PlaneGather:
    def __init__(self, chips, here, block, out, far, near):
        z, c, core = here
        self.here, self.block, self.out, self.near = here, block, out, near
        self.me = 2 * c + core
        self.partner = (z, c, 1 - core)
        self.size = block.shape[0] // 2
        self.chips = ChipGather(
            chips,
            here,
            self.piece,
            lambda chip, half: self.place(2 * chip + core, half),
            far,
        )
        self.own = remote(block, out.at[self.me], near, len(self.chips.arrivals), self.partner)

    def rows(self, half):
        return pl.ds(half * self.size, self.size)

    def piece(self, half):
        return self.block if half is None else self.block.at[self.rows(half)]

    def place(self, index, half):
        return self.out.at[index] if half is None else self.out.at[index, self.rows(half)]

    def start(self):
        self.chips.start()
        self.own.start()

    def passed(self, i, other=0):
        chip, half, _ = self.chips.arrivals[i]
        core = self.here[2]
        block = self.place(2 * chip + (1 - core if other else core), half)
        return remote(block, block, self.near, i, self.partner)

    def relay(self):
        for i in range(2 if self.chips.relayed else 0):
            self.chips.arrive(i)
            self.passed(i).start()

    def forward(self):
        for i in self.chips.rest():
            self.chips.arrive(i)
            self.passed(i).start()

    def finish(self):
        self.chips.sent()
        self.own.wait_send()
        mine = self.out.at[2 * self.here[1] + 1 - self.here[2]]
        remote(mine, mine, self.near, len(self.chips.arrivals), self.partner).wait_recv()
        for i in range(len(self.chips.arrivals)):
            self.passed(i).wait_send()
            self.passed(i, 1).wait_recv()

    @staticmethod
    def sems(chips):
        return pairs_of(ChipGather.count(chips), ChipGather.count(chips) + 1)


def row_half(ref, half):
    if half is None:
        return ref
    size = ref.shape[0] // 2
    return ref.at[pl.ds(half * size, size)]


class LineGather:
    def __init__(self, planes, here, parts, up, down):
        self.planes, self.here, self.parts = planes, here, parts
        self.up, self.down = up, down
        self.count = len(parts(here[0]))

    def upward(self, d, p):
        z, c, core = self.here
        block = self.parts(z - d)[p]
        return remote(block, block, self.up, d * self.count + p, (z + 1, c, core))

    def downward(self, d, p):
        z, c, core = self.here
        block = self.parts(z + d)[p]
        return remote(block, block, self.down, d * self.count + p, (z - 1, c, core))

    def each(self, d, p, act):
        z, planes = self.here[0], self.planes
        pl.when((z < planes - 1) & (z - d >= 0))(lambda: act(self.upward(d, p)))
        pl.when((z > 0) & (z + d < planes))(lambda: act(self.downward(d, p)))

    def start(self):
        for p in range(self.count):
            self.each(0, p, lambda copy: copy.start())

    def step(self, d, arrived=None):
        z, planes = self.here[0], self.planes

        def below(p):
            block = self.parts(z - d)[p]
            remote(block, block, self.up, (d - 1) * self.count + p, self.here).wait_recv()
            if d < planes - 1:
                pl.when(z < planes - 1)(lambda: self.upward(d, p).start())
            if arrived is not None:
                arrived(z - d, p)

        def above(p):
            block = self.parts(z + d)[p]
            remote(block, block, self.down, (d - 1) * self.count + p, self.here).wait_recv()
            if d < planes - 1:
                pl.when(z > 0)(lambda: self.downward(d, p).start())
            if arrived is not None:
                arrived(z + d, p)

        for p in range(self.count):
            pl.when(z - d >= 0)(lambda p=p: below(p))
            pl.when(z + d < planes)(lambda p=p: above(p))

    def finish(self):
        for d in range(self.planes - 1):
            for p in range(self.count):
                self.each(d, p, lambda copy: copy.wait_send())


class GroupGather:
    PARTS = 2

    def __init__(self, planes, here, block, out, up, down, near):
        self.planes, self.here, self.block, self.out, self.near = planes, here, block, out, near
        self.partner = (here[0], here[1], 1 - here[2])
        size = block.shape[0] // self.PARTS
        self.slices = [pl.ds(p * size, size) for p in range(self.PARTS)]
        core = here[2]
        self.line = LineGather(planes, here, lambda t: self.parts(t, core), up, down)

    def parts(self, t, core):
        return [self.out.at[t, core, rows] for rows in self.slices]

    def passed(self, t, p):
        block = self.parts(t, self.here[2])[p]
        return remote(block, block, self.near, t * self.PARTS + p, self.partner)

    def start(self, local):
        z, _, core = self.here
        keep = pltpu.make_async_copy(self.block, self.out.at[z, core], local)
        keep.start()
        keep.wait()
        self.line.start()
        for p in range(self.PARTS):
            self.passed(z, p).start()

    def step(self, d):
        self.line.step(d, lambda t, p: self.passed(t, p).start())

    def other(self, t):
        for p in range(self.PARTS):
            block = self.parts(t, 1 - self.here[2])[p]
            remote(block, block, self.near, t * self.PARTS + p, self.partner).wait_recv()

    def finish(self):
        self.line.finish()
        for t in range(self.planes):
            for p in range(self.PARTS):
                self.passed(t, p).wait_send()

    @classmethod
    def sems(cls, planes):
        return pairs_of(*[planes * cls.PARTS] * 3)


COLUMNS = 512


def product(left, right, columns, turned):
    if turned:
        return lax.dot_general(
            left, right[columns, :], (((1,), (1,)), ((), ())), preferred_element_type=F32
        )
    return jnp.dot(left, right[:, columns], preferred_element_type=F32)


class PlaneScatter:
    def __init__(self, chips, here, left, right, turned, buffers, near, far):
        self.chips, self.here = chips, here
        self.left, self.right, self.turned = left, right, turned
        self.near_out, self.near_in, self.far_out, self.far_in = buffers
        self.near, self.far = near, far
        self.tokens, width = self.near_out.shape[1:]
        self.tiles = [pl.ds(at, COLUMNS) for at in range(0, width, COLUMNS)]
        self.order = [*range(1, chips), 0]

    def target(self, k):
        return lax.rem(self.here[1] + k, self.chips)

    def near_copy(self, i):
        z, c, core = self.here
        at = (slice(None), slice(None), self.tiles[i])
        return remote(self.near_out.at[at], self.near_in.at[at], self.near, i, (z, c, 1 - core))

    def far_copy(self, k, i):
        z, _, core = self.here
        at = (k, slice(None), self.tiles[i])
        index = k * len(self.tiles) + i
        return remote(
            self.far_out.at[at], self.far_in.at[at], self.far, index, (z, self.target(k), core)
        )

    def rows(self, position):
        return slice(position * self.tokens, (position + 1) * self.tokens)

    def start(self):
        core = self.here[2]
        blocks = [self.left[2 * self.target(k) + 1 - core] for k in self.order]
        left = jnp.concatenate(blocks, axis=0)
        for i, columns in enumerate(self.tiles):
            part = product(left, self.right, columns, self.turned).astype(LOW)
            for position, k in enumerate(self.order):
                self.near_out[k, :, columns] = part[self.rows(position)]
            self.near_copy(i).start()
        blocks = [self.left[2 * self.target(k) + core] for k in self.order]
        left = jnp.concatenate(blocks, axis=0)
        for i, columns in enumerate(self.tiles):
            part = product(left, self.right, columns, self.turned)
            self.near_copy(i).wait_recv()
            for position, k in enumerate(self.order):
                self.far_out[k, :, columns] = (
                    part[self.rows(position)] + self.near_in[k, :, columns].astype(F32)
                ).astype(LOW)
                if k:
                    self.far_copy(k, i).start()

    def finish(self, out_ref):
        for i, columns in enumerate(self.tiles):
            total = self.far_out[0, :, columns].astype(F32)
            for k in range(1, self.chips):
                self.far_copy(k, i).wait_recv()
                total = total + self.far_in[k, :, columns].astype(F32)
            out_ref[:, columns] = total
        for i in range(len(self.tiles)):
            self.near_copy(i).wait_send()
            for k in range(1, self.chips):
                self.far_copy(k, i).wait_send()

    @staticmethod
    def scratch(chips, tokens, width):
        return [pltpu.VMEM((chips, tokens, width), LOW)] * 4

    @staticmethod
    def sems(chips, width):
        return pairs_of(width // COLUMNS, chips * (width // COLUMNS))


class LineScatter:
    def __init__(self, planes, here, count, part, tiles, own, slots, up, down):
        self.planes, self.here, self.count = planes, here, count
        self.part, self.tiles, self.own, self.slots = part, tiles, own, slots
        self.up, self.down = up, down
        self.steps = (planes - 1) * count

    def upward(self, t, p):
        z, c, core = self.here
        block = self.slots.at[(t, *self.part(p))]
        return remote(block, block, self.up, t * self.count + p, (z + 1, c, core))

    def downward(self, t, p, last):
        z, c, core = self.here
        block = self.slots.at[(t, *self.part(p))]
        target = self.slots.at[(self.planes, *self.part(p))] if last else block
        return remote(block, target, self.down, t * self.count + p, (z - 1, c, core))

    def add(self, t, p, fresh):
        for tile in self.tiles(p):
            total = self.own(t, tile)
            if not fresh:
                total = total + self.slots[(t, *tile)].astype(F32)
            self.slots[(t, *tile)] = total.astype(LOW)

    def step(self, i):
        z, planes, count = self.here[0], self.planes, self.count
        rise, fall = i - z, i - (planes - 1 - z)

        @pl.when((rise >= 0) & (rise < (planes - 1 - z) * count))
        def _():
            t, p = planes - 1 - rise // count, lax.rem(rise, count)

            @pl.when(z > 0)
            def _():
                self.upward(t, p).wait_recv()
                self.add(t, p, False)

            @pl.when(z == 0)
            def _():
                self.add(t, p, True)

            self.upward(t, p).start()

        @pl.when((fall >= 0) & (fall < z * count))
        def _():
            t, p = fall // count, lax.rem(fall, count)

            @pl.when(z < planes - 1)
            def _():
                self.downward(t, p, False).wait_recv()
                self.add(t, p, False)

            @pl.when(z == planes - 1)
            def _():
                self.add(t, p, True)

            pl.when(t == z - 1)(lambda: self.downward(t, p, True).start())
            pl.when(t < z - 1)(lambda: self.downward(t, p, False).start())

    def finish(self, store, after=None):
        z, planes = self.here[0], self.planes

        def total(tile, *slots):
            value = self.own(z, tile)
            for slot in slots:
                value = value + self.slots[(slot, *tile)].astype(F32)
            store(tile, value)

        for p in range(self.count):
            tiles = self.tiles(p)

            @pl.when(z > 0)
            def _(p=p):
                self.upward(z, p).wait_recv()

            @pl.when(z < planes - 1)
            def _(p=p):
                self.downward(z, p, True).wait_recv()

            @pl.when((z > 0) & (z < planes - 1))
            def _(tiles=tiles):
                for tile in tiles:
                    total(tile, z, planes)

            @pl.when(z == 0)
            def _(tiles=tiles):
                for tile in tiles:
                    total(tile, planes)

            @pl.when(z == planes - 1)
            def _(tiles=tiles):
                for tile in tiles:
                    total(tile, z)

            if after is not None:
                after(p)

        for t in range(planes):
            for p in range(self.count):
                pl.when(z < t)(lambda t=t, p=p: self.upward(t, p).wait_send())
                pl.when(z > t)(lambda t=t, p=p: self.downward(t, p, False).wait_send())


def row_tiles(count, size):
    return [pl.ds(at, size) for at in range(0, count, size)]


def in_scatter_kernel(
    planes, chips, heads, strided, left_in, right_in, rows_in, up_ref, weight_ref, gain_ref, _,
    out_ref, total_ref, gains_ref, slots_ref,
    left_ref, right_ref, rows_ref, grad_ref,
    near_out, near_in, far_out, far_in, sums, mine, parts, *sems,
):
    here = place()
    z, c, core = here
    seqs = 2 * chips
    me = 2 * c + core
    near, far, up, down, swap_sems, chip_sems = [sems[2 * i : 2 * i + 2] for i in range(6)]
    local = sems[12]
    loads = [
        pltpu.make_async_copy(rows_in, rows_ref, local.at[1]),
        pltpu.make_async_copy(left_in, left_ref, local.at[2]),
        pltpu.make_async_copy(right_in, right_ref, local.at[3]),
    ]
    for copy in loads:
        copy.start()
    barrier = pltpu.get_barrier_semaphore()
    peers = plane_peers(chips, here)
    greet(barrier, peers)
    greet_line(barrier, planes, here)
    pl.semaphore_wait(barrier, len(peers) + line_peers(planes, here))
    units = slots_ref.shape[2]
    lower = share(slots_ref.shape[1], 1, UP_FIRST)
    ups = ChipSwap(
        chips,
        here,
        lambda index: half_block(up_ref, units, index, 1),
        lambda index: slots_ref.at[index, lower],
        chip_sems,
    )
    ups.start(local.at[0])
    half = seqs // 2
    line = LineScatter(
        planes,
        here,
        2,
        lambda p: (pl.ds(p * half, half),),
        lambda p: [(pl.ds(p * half + i, 1),) for i in range(half)],
        lambda t, tile: grad_ref[(t, *tile)].astype(F32),
        sums,
        up,
        down,
    )
    part = grad_ref.shape[2]
    span = heads * HD
    block = seqs * part
    length = rows_ref.shape[0]
    for copy in loads:
        copy.wait()

    def grads(t):
        left = rows_ref[:, t * block : (t + 1) * block]
        for i in range(3):
            at = pl.ds(i * span, span)
            term = token_product(left, left_ref[:, :, at].reshape(length, span))
            grad_ref[t, :, :, at] = term.astype(LOW).reshape(seqs, part, span)

    order = []
    for i in range((planes + 1) // 2):
        order += [planes - 1 - i, i] if planes - 1 - i != i else [i]
    for t in order[:2]:
        grads(t)
    line.step(0)
    for t in order[2:]:
        grads(t)
    work = PlaneScatter(
        chips, here, left_ref, right_ref, True, (near_out, near_in, far_out, far_in), near, far
    )
    work.start()
    for i in range(1, line.steps):
        line.step(i)

    def store(tile, total):
        mine[tile] = total.astype(LOW)

    owners = [2 * device[1] + device[2] for device in peers]
    swaps = [
        remote(mine.at[owner], parts.at[me], swap_sems, k, device)
        for k, (owner, device) in enumerate(zip(owners, peers), 1)
    ]

    def send(p):
        for owner, copy in zip(owners, swaps):
            pl.when(owner // half == p)(copy.start)

    line.finish(store, send)
    parts[me] = mine[me]
    work.finish(out_ref)
    for k in range(1, seqs):
        swaps[k - 1].wait_send()
        index = lax.rem(me + seqs - k, seqs)
        remote(mine.at[0], parts.at[index], swap_sems, k, here).wait_recv()
    width = seqs * span
    gain = gain_ref[:, pl.ds(0, 1)]
    summed = jnp.zeros(gain.shape, F32)
    for i in range(3):
        step, pieces = (seqs * HD, planes) if strided else (width, 1)
        size = step // seqs
        for piece in range(pieces):
            at = i * span + piece * size
            columns = pl.ds(i * width + piece * step, step)
            total = jnp.concatenate(
                [parts[s, :, pl.ds(at, size)].astype(F32) for s in range(seqs)], axis=1
            )
            weight = weight_ref[:, columns].astype(F32)
            summed = summed + jnp.sum(total * weight, axis=1, keepdims=True)
            total_ref[:, columns] = total * gain
    gains_ref[...] = jnp.broadcast_to(summed, gains_ref.shape)
    ups.finish()


def in_scatter(planes, chips, heads, strided, left, right, rows, up_grads, weight, gain, slots):
    _, tokens, _ = left.shape
    width = right.shape[0]
    seqs = 2 * chips
    part, wide = weight.shape[0], left.shape[2]
    return call(
        functools.partial(in_scatter_kernel, planes, chips, heads, strided),
        "in_scatter",
        [
            shape((tokens, width), F32),
            shape(weight.shape, F32),
            shape((part, 128), F32),
            shape(slots.shape, LOW),
        ],
        (left, right, rows, up_grads, weight, gain, slots),
        [HBM, HBM, HBM, HBM, VMEM, VMEM, HBM],
        [VMEM, VMEM, VMEM, HBM],
        [
            *[pltpu.VMEM(whole.shape, LOW) for whole in (left, right, rows)],
            pltpu.VMEM((planes, seqs, part, wide), LOW),
            *PlaneScatter.scratch(chips, tokens, width),
            pltpu.VMEM((planes + 1, seqs, part, wide), LOW),
            *[pltpu.VMEM((seqs, part, wide), LOW)] * 2,
            *PlaneScatter.sems(chips, width),
            *pairs_of(2 * planes, 2 * planes, seqs, chips),
            pltpu.SemaphoreType.DMA((4,)),
        ],
        4,
        {6: 3},
    )


class PairScatter:
    PARTS = 2

    def __init__(self, planes, here, left, right, turned, buffers, near, up, down):
        self.planes, self.here = planes, here
        self.left, self.right, self.turned = left, right, turned
        self.near_out, self.own, slots = buffers
        self.near = near
        self.tokens, width = self.near_out.shape[1:]
        self.tiles = [pl.ds(at, COLUMNS) for at in range(0, width, COLUMNS)]
        size = width // self.PARTS

        def part(p):
            at = p * size if isinstance(p, int) else pl.multiple_of(p * size, 128)
            return (slice(None), pl.ds(at, size))

        self.line = LineScatter(
            planes,
            here,
            self.PARTS,
            part,
            lambda p: [(rows, part(p)[1]) for rows in row_tiles(self.tokens, 32)],
            lambda t, tile: self.own[(t, *tile)].astype(F32),
            slots,
            up,
            down,
        )

    def near_copy(self, i):
        z, c, core = self.here
        at = (slice(None), slice(None), self.tiles[i])
        return remote(self.near_out.at[at], self.own.at[at], self.near, i, (z, c, 1 - core))

    def start(self):
        core, tokens = self.here[2], self.tokens
        left = jnp.concatenate([self.left[t, 1 - core] for t in range(self.planes)], axis=0)
        for i, columns in enumerate(self.tiles):
            part = product(left, self.right, columns, self.turned).astype(LOW)
            for t in range(self.planes):
                self.near_out[t, :, columns] = part[t * tokens : (t + 1) * tokens]
            self.near_copy(i).start()
        left = jnp.concatenate([self.left[t, core] for t in range(self.planes)], axis=0)
        for i, columns in enumerate(self.tiles):
            part = product(left, self.right, columns, self.turned)
            self.near_copy(i).wait_recv()
            for t in range(self.planes):
                self.own[t, :, columns] = (
                    part[t * tokens : (t + 1) * tokens] + self.own[t, :, columns].astype(F32)
                ).astype(LOW)
        self.line.step(0)

    def finish(self, out_ref):
        def store(tile, total):
            out_ref[tile] = total

        self.line.finish(store)
        for i in range(len(self.tiles)):
            self.near_copy(i).wait_send()

    @staticmethod
    def scratch(planes, tokens, width):
        return [
            *[pltpu.VMEM((planes, tokens, width), LOW)] * 2,
            pltpu.VMEM((planes + 1, tokens, width), LOW),
        ]

    @classmethod
    def sems(cls, planes, width):
        return pairs_of(width // COLUMNS, cls.PARTS * planes, cls.PARTS * planes)


def feed_forward_kernel(
    planes, chips, width_ff, x_ref, up_ref, grads_ref, down_ref,
    out_ref, normed_ref, downs_ref, gup_ref, gdown_ref, slots_ref,
    rows, ups, grads, downs, back, act, slope, stat, stat_out, stat_in,
    normed, d_up, near_out, own, sums, gup, gdown, *sems,
):
    here = place()
    z, c, core = here
    count = 2 * planes
    me = 2 * z + core
    up, down, near, chip_sems, stat_sems, pair, rise, fall, swap_sems = [
        sems[2 * i : 2 * i + 2] for i in range(9)
    ]
    local = sems[18]
    tokens, width = x_ref.shape
    units = ups.shape[1]
    load_up = pltpu.make_async_copy(up_ref, ups, local.at[0])
    load_grads = pltpu.make_async_copy(grads_ref, grads, local.at[1])
    load_up.start()
    load_grads.start()
    barrier = pltpu.get_barrier_semaphore()
    ids = [lax.rem(me + k, count) for k in range(1, count)]
    group_peers = [(index // 2, c, lax.rem(index, 2)) for index in ids]
    peers = [*group_peers, *chip_peers(chips, here)]
    greet(barrier, peers)
    pl.semaphore_wait(barrier, len(peers))

    group = GroupGather(planes, here, x_ref, rows, up, down, near)
    group.start(local.at[2])
    keep = pltpu.make_async_copy(down_ref, downs.at[c], local.at[3])
    keep.start()
    weights = ChipGather(
        chips,
        here,
        lambda half: row_half(down_ref, half),
        lambda chip, half: row_half(downs.at[chip], half),
        chip_sems,
    )
    weights.start()
    load_up.wait()

    step = tokens
    lane = lax.broadcasted_iota(jnp.int32, (step, 128), 1)

    def forward(t):
        group.other(t)
        block = rows[t].reshape(2 * tokens, width)
        for at in range(0, units, COLUMNS):
            columns = pl.ds(at, COLUMNS)
            act[t, :, columns] = jnp.dot(block, ups[:, columns], preferred_element_type=F32)

        def some(i, carry):
            at = pl.ds(pl.multiple_of(i * step, step), step)
            value = act[t, at]
            phi = 0.5 * (1.0 + lax.erf(value * math.sqrt(0.5)))
            result = value * phi
            act[t, at] = result
            slope[t, at] = phi + value * (
                jnp.exp(value * value * -0.5) * (1.0 / math.sqrt(2.0 * math.pi))
            )
            total = jnp.sum(result, axis=1, keepdims=True)
            square = jnp.sum(result * result, axis=1, keepdims=True)
            stat[t, at] = jnp.where(lane == 0, total, jnp.where(lane == 1, square, 0.0))
            return carry

        lax.fori_loop(0, 2 * tokens // step, some, 0)

    forward(z)
    for d in range(1, planes):
        group.step(d)
        if d == 2:
            weights.relay()
        if d > 1:
            pl.when(z - d + 1 >= 0)(lambda d=d: forward(z - d + 1))
            pl.when(z + d - 1 < planes)(lambda d=d: forward(z + d - 1))
    pl.when(z - planes + 1 >= 0)(lambda: forward(z - planes + 1))
    pl.when(z + planes - 1 < planes)(lambda: forward(z + planes - 1))
    group.finish()
    keep.wait()
    load_grads.wait()
    weights.finish()
    out_downs = pltpu.make_async_copy(downs, downs_ref, local.at[4])
    out_downs.start()

    def backward(t, carry):
        block = grads[t].reshape(2 * tokens, width)
        size = units // chips
        for chip in range(chips):
            columns = pl.ds(chip * size, size)
            back[t, :, columns] = rows_product(block, downs[chip])

        def some(i, inner):
            at = pl.ds(pl.multiple_of(i * step, step), step)
            value = back[t, at]
            cross = jnp.sum(value * act[t, at], axis=1, keepdims=True)
            total = jnp.sum(value, axis=1, keepdims=True)
            stat[t, at] = jnp.where(lane == 2, cross, jnp.where(lane == 3, total, stat[t, at]))
            return inner

        lax.fori_loop(0, 2 * tokens // step, some, 0)
        for half in range(2):
            turned = stat[t, pl.ds(half * tokens, tokens)].T
            stat_out[2 * t + half] = turned[:8]
        return carry

    lax.fori_loop(0, planes, backward, 0)
    copies = [
        remote(stat_out, stat_in.at[k], stat_sems, k, device)
        for k, device in enumerate(group_peers, 1)
    ]
    for copy in copies:
        copy.start()
    for copy in copies:
        copy.wait_send()
        copy.wait_recv()

    def finish(t, carry):
        for half in range(2):
            total = stat_out[2 * t + half]
            for k in range(1, count):
                total = total + stat_in[k, 2 * t + half]
            mean, square, cross, first = (total[i : i + 1] / width_ff for i in range(4))
            scaler = lax.rsqrt(square - mean * mean + NORM_EPS)
            second = scaler * (cross - mean * first)
            figures = [scaler, -mean * scaler, scaler * first, scaler * second]
            padded = jnp.concatenate([*figures, jnp.zeros((128 - 4, tokens), F32)], axis=0)
            stat[t, pl.ds(half * tokens, tokens)] = padded.T

        def some(i, inner):
            at = pl.ds(pl.multiple_of(i * step, step), step)
            figures = stat[t, at]
            scaler, shift, first, second = (figures[:, j : j + 1] for j in range(4))
            unit = act[t, at] * scaler + shift
            normed[t, at] = unit.astype(LOW)
            d_act = back[t, at] * scaler - first - unit * second
            d_up[t, at] = (d_act * slope[t, at]).astype(LOW)
            return inner

        lax.fori_loop(0, 2 * tokens // step, some, 0)
        return carry

    lax.fori_loop(0, planes, finish, 0)
    out_normed = pltpu.make_async_copy(normed, normed_ref, local.at[5])
    out_normed.start()
    work = PairScatter(
        planes, here, Halves(d_up, tokens), ups, True, (near_out, own, sums), pair, rise, fall
    )
    work.start()

    flat_normed, flat_d_up = (
        whole[...].reshape(planes * 2 * tokens, units) for whole in (normed, d_up)
    )
    size = units // chips
    upper = share(size, 0, DOWN_FIRST)
    swap = ChipSwap(
        chips,
        here,
        lambda index: gdown.at[index, upper],
        lambda index: slots_ref.at[index, upper],
        swap_sems,
    )
    turns_left = list(range(1, work.line.steps))

    def turn():
        if turns_left:
            work.line.step(turns_left.pop(0))

    together = max(1, 256 // size)
    for chip in range(0, chips, together):
        left = flat_normed[:, chip * size : (chip + together) * size]
        for at in range(0, width, COLUMNS):
            columns = pl.ds(at, COLUMNS)
            right = grads[:, :, :, columns].reshape(planes * 2 * tokens, COLUMNS)
            term = token_product(left, right).astype(LOW)
            for i in range(together):
                gdown[chip + i, :, columns] = term[i * size : (i + 1) * size]
    swap.start(local.at[6])
    out_gdown = pltpu.make_async_copy(gdown, gdown_ref, local.at[9])
    out_gdown.start()
    chunk = gup.shape[1]
    out_gups = [
        pltpu.make_async_copy(
            gup.at[i % 2], gup_ref.at[pl.ds(i * chunk, chunk)], local.at[7 + i % 2]
        )
        for i in range(width // chunk)
    ]
    for i in range(width // chunk):
        if i == 0 or i % 2:
            turn()
        left = rows[:, :, :, pl.ds(i * chunk, chunk)].reshape(planes * 2 * tokens, chunk)
        term = token_product(left, flat_d_up).astype(LOW)
        if i > 1:
            out_gups[i - 2].wait()
        gup[i % 2] = term
        out_gups[i].start()
    while turns_left:
        turn()
    work.finish(out_ref)
    swap.finish()
    out_downs.wait()
    out_normed.wait()
    out_gdown.wait()
    for copy in out_gups[-2:]:
        copy.wait()


class Halves:
    def __init__(self, whole, tokens):
        self.whole, self.tokens = whole, tokens

    def __getitem__(self, at):
        t, core = at
        rows = pl.ds(pl.multiple_of(core * self.tokens, self.tokens), self.tokens)
        return self.whole[t, rows]


def feed_forward(planes, chips, width_ff, x_block, up_mine, grads, down_block):
    tokens, width = x_block.shape
    units = up_mine.shape[1]
    size = down_block.shape[0]
    wide = (planes, 2 * tokens, units)
    return call(
        functools.partial(feed_forward_kernel, planes, chips, width_ff),
        "feed_forward",
        [
            shape((tokens, width), F32),
            shape(wide, LOW),
            shape((chips, size, width), LOW),
            shape((width, units), LOW),
            *[shape((chips, size, width), LOW)] * 2,
        ],
        (x_block, up_mine, grads, down_block),
        [HBM] * 4,
        [VMEM, *[HBM] * 5],
        [
            pltpu.VMEM((planes, 2, tokens, width), LOW),
            pltpu.VMEM((width, units), LOW),
            pltpu.VMEM((planes, 2, tokens, width), LOW),
            pltpu.VMEM((chips, size, width), LOW),
            *[pltpu.VMEM(wide, F32)] * 3,
            pltpu.VMEM((planes, 2 * tokens, 128), F32),
            pltpu.VMEM((2 * planes, 8, 128), F32),
            pltpu.VMEM((2 * planes, 2 * planes, 8, 128), F32),
            *[pltpu.VMEM(wide, LOW)] * 2,
            *PairScatter.scratch(planes, tokens, width),
            pltpu.VMEM((2, 256, units), LOW),
            pltpu.VMEM((chips, size, width), LOW),
            *GroupGather.sems(planes),
            *pairs_of(ChipGather.count(chips), 2 * planes),
            *PairScatter.sems(planes, width),
            *pairs_of(chips),
            pltpu.SemaphoreType.DMA((10,)),
        ],
        7,
    )


def swap_lanes(values):
    lane = lax.broadcasted_iota(jnp.int32, values.shape, 1)
    return jnp.where(
        lax.rem(lane, 2) == 0,
        pltpu.roll(values, values.shape[1] - 1, 1),
        pltpu.roll(values, 1, 1),
    )


def twice(table):
    return jnp.concatenate([table, table], axis=1)


def turns(meta_ref, rows):
    cosine, sine, shrink = [twice(meta_ref[rows, pl.ds(i * HD, HD)]) for i in range(3)]
    return (cosine, sine, cosine * shrink, sine * shrink)


def allowed_block(meta_ref, rows, size, columns):
    query = rows + lax.broadcasted_iota(jnp.int32, (size, columns), 0)
    key = lax.broadcasted_iota(jnp.int32, (size, columns), 1)
    offset = meta_ref[pl.ds(rows, size), pl.ds(3 * HD, 1)].astype(jnp.int32)
    return (key <= query) & (key >= query - offset)


BLOCK = 256


def attention_forward_kernel(
    planes, chips, heads, strided,
    x_ref, meta_ref, weight_ref, scale_ref, out_ref, gain_ref, up_ref, grad_ref,
    q_ref, k_ref, v_ref, att_ref, log_ref, sum_ref,
    rows_ref, metas_ref, qkvs_ref, outs_ref, gains_ref, ups_ref, grads_ref, tiles_ref,
    qkv_ref, rows, metas, qkvs, outs, raw, wide, tile, near_out, near_in, far_out, far_in,
    *sems,
):
    here = place()
    z, c, core = here
    seqs = 2 * chips
    count = planes * seqs
    me = 2 * c + core
    flat = z * seqs + me
    groups = [sems[2 * i : 2 * i + 2] for i in range(17)]
    swap_sems, x_far, x_near, meta_far, meta_near, up, down, up_two, down_two = groups[:9]
    gain_sems, up_sems, near, far, tile_sems, grad_up, grad_down, pair = groups[9:]
    local = sems[34]
    tokens, width = x_ref.shape
    part = qkv_ref.shape[1]
    length = seqs * tokens
    span = heads * HD
    barrier = pltpu.get_barrier_semaphore()

    def device_of(k):
        other = lax.rem(flat + k, count)
        return (other // seqs, lax.rem(other, seqs) // 2, lax.rem(other, 2))

    def signal(k, carry):
        greet(barrier, [device_of(k)])
        return carry

    lax.fori_loop(1, count, signal, 0)
    scale = scale_ref[:, pl.ds(0, 1)]
    for s in range(seqs):
        for i in range(3):
            if strided:
                starts = [i * width + (t * seqs + s) * HD for t in range(planes)]
                size = span // planes
            else:
                starts, size = [i * width + s * span], span
            piece = jnp.concatenate([weight_ref[:, pl.ds(at, size)] for at in starts], axis=1)
            qkv_ref[s, :, pl.ds(i * span, span)] = (piece.astype(F32) * scale).astype(LOW)
    pl.semaphore_wait(barrier, count - 1)

    mine = pltpu.make_async_copy(qkv_ref.at[me], qkvs.at[z, me], local.at[0])
    own_out = pltpu.make_async_copy(out_ref, outs.at[z] if strided else outs, local.at[1])
    units = up_ref.shape[1]
    keeps = [
        pltpu.make_async_copy(x_ref, rows.at[me], local.at[2]),
        pltpu.make_async_copy(meta_ref, metas.at[me], local.at[3]),
        pltpu.make_async_copy(gain_ref, gains_ref.at[flat], local.at[4]),
        pltpu.make_async_copy(up_ref, column_block(ups_ref, units, c), local.at[5]),
    ]
    peers = plane_peers(chips, here)
    swaps = [
        remote(qkv_ref.at[2 * device[1] + device[2]], qkvs.at[z, me], swap_sems, k, device)
        for k, device in enumerate(peers, 1)
    ]
    mine.start()
    own_out.start()
    for copy in swaps:
        copy.start()
    gather = PlaneGather(chips, here, x_ref, rows, x_far, x_near)
    meta_gather = PlaneGather(chips, here, meta_ref, metas, meta_far, meta_near)
    for copy in keeps:
        copy.start()

    def gain_copy(k):
        return remote(gain_ref, gains_ref.at[flat], gain_sems, k, device_of(k))

    def gain_start(k, carry):
        gain_copy(k).start()
        return carry

    mine.wait()
    own_out.wait()
    for k in range(1, seqs):
        index = lax.rem(me + seqs - k, seqs)
        remote(qkv_ref.at[0], qkvs.at[z, index], swap_sems, k, here).wait_recv()
    half = seqs // 2
    line = LineGather(
        planes, here, lambda t: [qkvs.at[t, pl.ds(i * half, half)] for i in range(2)], up, down
    )
    line_two = LineGather(planes, here, lambda t: [outs.at[t]], up_two, down_two)
    line.start()
    gather.start()
    meta_gather.start()
    lax.fori_loop(1, count, gain_start, 0)
    gather.relay()
    meta_gather.relay()
    line.step(1)
    gather.forward()
    meta_gather.forward()
    ups = ChipGather(
        chips,
        here,
        lambda part: row_half(up_ref, part),
        lambda chip, part: row_half(column_block(ups_ref, units, chip), part),
        up_sems,
    )
    ups.start()
    line.step(2)
    gather.finish()
    meta_gather.finish()
    for copy in keeps:
        copy.wait()

    block = seqs * part

    def add(t, fresh=False):
        columns = pl.ds(pl.multiple_of(t * block, 128), block)
        left = rows[:, :, columns].reshape(length, block)
        for i in range(3):
            at = pl.ds(i * span, span)
            term = jnp.dot(left, qkvs[t, :, :, at].reshape(block, span), preferred_element_type=F32)
            raw[:, at] = term if fresh else raw[:, at] + term

    add(z, True)
    for d in range(1, planes):
        if d == 3:
            ups.relay()
        if d > 2:
            line.step(d)
        if d == planes - 1:
            if strided:
                line_two.start()
            group = GroupGather(planes, here, grad_ref, grads_ref, grad_up, grad_down, pair)
            group.start(local.at[6])
        pl.when(z - d >= 0)(lambda d=d: add(z - d))
        pl.when(z + d < planes)(lambda d=d: add(z + d))
    outputs = [
        pltpu.make_async_copy(rows, rows_ref, local.at[7]),
        pltpu.make_async_copy(metas, metas_ref, local.at[8]),
        pltpu.make_async_copy(qkvs, qkvs_ref, local.at[9]),
    ]
    for copy in outputs:
        copy.start()

    table = RowBlocks(metas)
    for at in range(0, length, BLOCK):
        at = pl.ds(at, BLOCK)
        tables = turns(table, at)
        for two in range(heads // 2):
            query = raw[at, pl.ds(2 * HD * two, 2 * HD)]
            query = (query * tables[0] + swap_lanes(query) * tables[1]).astype(LOW)
            key = raw[at, pl.ds(span + 2 * HD * two, 2 * HD)]
            key = (key * tables[2] + swap_lanes(key) * tables[3]).astype(LOW)
            value = raw[at, pl.ds(2 * span + 2 * HD * two, 2 * HD)].astype(LOW)
            for side in range(2):
                lanes = slice(side * HD, (side + 1) * HD)
                q_ref[2 * two + side, at] = query[:, lanes]
                k_ref[2 * two + side, at] = key[:, lanes]
                v_ref[2 * two + side, at] = value[:, lanes]
    log_ref[...] = jnp.zeros(log_ref.shape, F32)

    def one_head(head, carry):
        for start in range(0, length, BLOCK):
            columns = start + BLOCK
            at = pl.ds(start, BLOCK)
            scores = lax.dot_general(
                q_ref[head, at],
                k_ref[head, pl.ds(0, columns)],
                (((1,), (1,)), ((), ())),
                preferred_element_type=F32,
            )
            allowed = allowed_block(table, start, BLOCK, columns)
            scores = jnp.where(allowed, scores, NEG_FILL)
            top = jnp.max(scores, axis=1, keepdims=True)
            shifted = jnp.exp(scores - top)
            total = jnp.sum(shifted, axis=1, keepdims=True)
            probs = (shifted * (1.0 / total)).astype(LOW)
            wide[head, at] = jnp.dot(
                probs, v_ref[head, pl.ds(0, columns)], preferred_element_type=F32
            )
            lane = lax.broadcasted_iota(jnp.int32, (BLOCK, 128), 1)
            log_ref[at] = jnp.where(lane == head, top + jnp.log(total), log_ref[at])
        return carry

    first = 0
    for d in range(1, planes):
        last = -(-heads * d // planes)
        lax.fori_loop(first, last, one_head, 0)
        first = last
        if strided:
            line_two.step(d)
        if d == 2:
            group.step(1)
    lax.fori_loop(first, heads, one_head, 0)
    lane = lax.broadcasted_iota(jnp.int32, (tokens, 128), 1)
    column = jnp.sum(outs[...].astype(F32).reshape(span, width), axis=0, keepdims=True)
    for s in range(seqs):
        at = pl.ds(s * tokens, tokens)
        low = jnp.concatenate([wide[head, at] for head in range(heads)], axis=1).astype(LOW)
        att_ref[s] = low
        value = low.astype(F32)
        total = jnp.sum(value, axis=1, keepdims=True)
        square = jnp.sum(value * value, axis=1, keepdims=True)
        both = jnp.where(lane == 0, total, jnp.where(lane == 1, square, 0.0))
        tile[s, pl.ds(0, 8)] = both.T[:8]
        for i in range(width // 128):
            tile[s, pl.ds(8 + i, 1)] = column[:, i * 128 : (i + 1) * 128]
    out_tiles = [
        remote(tile.at[2 * device[1] + device[2]], tiles_ref.at[me], tile_sems, k, device)
        for k, device in enumerate(peers, 1)
    ]
    for copy in out_tiles:
        copy.start()
    keep = pltpu.make_async_copy(tile.at[me], tiles_ref.at[me], local.at[10])
    keep.start()
    out_outs = pltpu.make_async_copy(outs, outs_ref, local.at[11])
    out_outs.start()
    work = PlaneScatter(
        chips, here, att_ref, Flat(outs, span), False, (near_out, near_in, far_out, far_in), near, far
    )
    work.start()
    for d in range(2, planes):
        group.step(d)
    work.finish(sum_ref)
    group.finish()
    for t in range(planes):
        group.other(t)
    line.finish()
    if strided:
        line_two.finish()
    for copy in swaps:
        copy.wait_send()
    ups.finish()
    for copy in [keep, out_outs, *outputs]:
        copy.wait()
    for k in range(1, seqs):
        out_tiles[k - 1].wait_send()
        index = lax.rem(me + seqs - k, seqs)
        remote(tile.at[0], tiles_ref.at[index], tile_sems, k, here).wait_recv()

    def gain_wait(k, carry):
        gain_copy(k).wait_send()
        other = lax.rem(flat + count - k, count)
        remote(gain_ref, gains_ref.at[other], gain_sems, k, here).wait_recv()
        return carry

    lax.fori_loop(1, count, gain_wait, 0)


class Flat:
    def __init__(self, blocks, count):
        self.blocks, self.count = blocks, count

    def __getitem__(self, at):
        if len(self.blocks.shape) == 2:
            return self.blocks[at]
        _, columns = at
        return self.blocks[:, :, columns].reshape(self.count, columns.size)


class RowBlocks:
    def __init__(self, blocks):
        self.blocks = blocks

    def __getitem__(self, at):
        rows, columns = at
        size = self.blocks.shape[1]
        first, count = rows.start // size, rows.size // size
        return self.blocks[pl.ds(first, count), :, columns].reshape(rows.size, columns.size)


def attention_forward(
    planes, chips, heads, strided, x_block, meta, weight, scale, out_rows, gain_tile, up_block, grad
):
    seqs = 2 * chips
    tokens, width = x_block.shape
    part, wide = weight.shape[0], 3 * heads * HD
    units = up_block.shape[1]
    length = seqs * tokens
    span = heads * HD
    outs = (planes, *out_rows.shape) if strided else out_rows.shape
    tile = (seqs, 8 + width // 128, 128)
    return call(
        functools.partial(attention_forward_kernel, planes, chips, heads, strided),
        "attention_forward",
        [
            *[shape((heads, length, HD), LOW)] * 3,
            shape((seqs, tokens, span), LOW),
            shape((length, 128), F32),
            shape((tokens, width), F32),
            shape((seqs, tokens, width), LOW),
            shape((seqs, *meta.shape), F32),
            shape((planes, seqs, part, wide), LOW),
            shape(outs, LOW),
            shape((planes * seqs, *gain_tile.shape), F32),
            shape((width, chips * units) if units % 128 == 0 else (chips, width, units), LOW),
            shape((planes, 2, *grad.shape), LOW),
            shape(tile, F32),
        ],
        (x_block, meta, weight, scale, out_rows, gain_tile, up_block, grad),
        [HBM, HBM, VMEM, VMEM, HBM, HBM, HBM, HBM],
        [*[VMEM] * 6, *[HBM] * 8],
        [
            pltpu.VMEM((seqs, part, wide), LOW),
            pltpu.VMEM((seqs, tokens, width), LOW),
            pltpu.VMEM((seqs, *meta.shape), F32),
            pltpu.VMEM((planes, seqs, part, wide), LOW),
            pltpu.VMEM(outs, LOW),
            pltpu.VMEM((length, 3 * span), F32),
            pltpu.VMEM((heads, length, HD), F32),
            pltpu.VMEM(tile, F32),
            *PlaneScatter.scratch(chips, tokens, width),
            *pairs_of(seqs),
            *PlaneGather.sems(chips),
            *PlaneGather.sems(chips),
            *pairs_of(*[2 * planes] * 2, *[planes] * 2, planes * seqs, ChipGather.count(chips)),
            *PlaneScatter.sems(chips, width),
            *pairs_of(seqs),
            *GroupGather.sems(planes),
            pltpu.SemaphoreType.DMA((12,)),
        ],
        1,
    )


def attention_backward_kernel(
    planes, chips, heads, strided,
    x_ref, stat_ref, tile_ref, left_ref, right_ref,
    q_in, k_in, v_in, att_in, out_in, log_in, meta_in, up_ref, down_ref, _,
    tiles_ref, ffn_ref, out_ref, total_ref, slots_ref, down_slots_ref,
    rows, stats, left, right, q_ref, k_ref, v_ref, att_ref, outs, log_ref, meta_ref,
    near_out, near_own, near_sums, grad, dq, dk, dv, normed_all, own, sums, *sems,
):
    here = place()
    z, c, core = here
    seqs = 2 * chips
    count = planes * seqs
    me = 2 * c + core
    flat = z * seqs + me
    x_far, x_near, s_far, s_near, tile_sems, near, up, down, up_two, down_two, swap_sems = [
        sems[2 * i : 2 * i + 2] for i in range(11)
    ]
    down_sems = sems[22:24]
    local = sems[24]
    pairs = [
        (left_ref, left), (right_ref, right), (att_in, att_ref), (out_in, outs), (meta_in, meta_ref),
        (q_in, q_ref), (k_in, k_ref), (v_in, v_ref), (log_in, log_ref),
    ]
    loads = [pltpu.make_async_copy(*pair, local.at[i]) for i, pair in enumerate(pairs)]
    for copy in loads:
        copy.start()
    barrier = pltpu.get_barrier_semaphore()

    def device_of(k):
        other = lax.rem(flat + k, count)
        return (other // seqs, lax.rem(other, seqs) // 2, lax.rem(other, 2))

    def signal(k, carry):
        greet(barrier, [device_of(k)])
        return carry

    lax.fori_loop(1, count, signal, 0)
    pl.semaphore_wait(barrier, count - 1)
    gather = PlaneGather(chips, here, x_ref, rows, x_far, x_near)
    stat_gather = PlaneGather(chips, here, stat_ref, stats, s_far, s_near)
    gather.start()
    stat_gather.start()
    keeps = [
        pltpu.make_async_copy(x_ref, rows.at[me], local.at[9]),
        pltpu.make_async_copy(stat_ref, stats.at[me], local.at[10]),
        pltpu.make_async_copy(tile_ref.at[flat], tiles_ref.at[flat], local.at[11]),
    ]
    for copy in keeps:
        copy.start()

    def tile_copy(k):
        other = lax.rem(flat + k, count)
        return remote(tile_ref.at[other], tiles_ref.at[flat], tile_sems, k, device_of(k))

    def tile_start(k, carry):
        tile_copy(k).start()
        return carry

    lax.fori_loop(1, count, tile_start, 0)
    tokens, width = x_ref.shape
    for copy in loads[:2]:
        copy.wait()
    work = PairScatter(
        planes, here, Halves(left, tokens), right, False, (near_out, near_own, near_sums),
        near, up, down,
    )
    work.start()
    left_turns = list(range(1, work.line.steps))

    def turn(until=None):
        step = left_turns[0] + 1 if until is None and left_turns else until
        while left_turns and left_turns[0] < step:
            work.line.step(left_turns.pop(0))

    turn()
    gather.relay()
    stat_gather.relay()
    turn()
    gather.forward()
    stat_gather.forward()
    gather.finish()
    stat_gather.finish()
    units = slots_ref.shape[2]
    upper, lower = share(width, 0, UP_FIRST), share(down_ref.shape[1], 1, DOWN_FIRST)
    swaps = [
        ChipSwap(
            chips,
            here,
            lambda index: half_block(up_ref, units, index, 0),
            lambda index: slots_ref.at[index, upper],
            swap_sems,
        ),
        ChipSwap(
            chips,
            here,
            lambda index: down_ref.at[index, lower],
            lambda index: down_slots_ref.at[index, lower],
            down_sems,
        ),
    ]
    for i, swap in enumerate(swaps):
        swap.start(local.at[12 + i])
    for copy in [*loads[2:], *keeps]:
        copy.wait()
    turn()
    length, span = att_ref.shape
    part = own.shape[1]
    per = BLOCK // tokens
    for first in range(0, seqs, per):
        at = pl.ds(first * tokens, BLOCK)
        figures = stats[pl.ds(first, per)].reshape(BLOCK, 128)
        mean, scaler, one, two = (figures[:, i : i + 1] for i in range(4))
        block = rows[pl.ds(first, per)].reshape(BLOCK, width)
        d_sub = product(block, outs, slice(None), True)
        normed = (att_ref[at].astype(F32) - mean) * scaler
        normed_all[at] = normed.astype(LOW)
        d_att = (scaler * (d_sub - one - normed * two)).astype(LOW)
        for head in range(heads):
            grad[head, at] = d_att[:, head * HD : (head + 1) * HD]
    for at in range(0, width, COLUMNS):
        columns = pl.ds(at, COLUMNS)
        term = token_product(normed_all[...], rows[:, :, columns].reshape(length, COLUMNS)).astype(LOW)
        for t in range(planes):
            own[t, :, columns] = term[t * part : (t + 1) * part]
    line = LineScatter(
        planes,
        here,
        1,
        lambda p: (slice(None),),
        lambda p: [(row,) for row in row_tiles(part, 16)],
        lambda t, tile: own[(t, *tile)].astype(F32),
        sums,
        up_two,
        down_two,
    )
    if strided:
        line.step(0)
    dk[...] = jnp.zeros(dk.shape, F32)
    dv[...] = jnp.zeros(dv.shape, F32)

    def one_head(head, carry):
        for start in range(0, length, BLOCK):
            columns = start + BLOCK
            at = pl.ds(start, BLOCK)
            keys = pl.ds(0, columns)
            query, key = q_ref[head, at], k_ref[head, keys]
            out_grad = grad[head, at]
            scores = lax.dot_general(
                query, key, (((1,), (1,)), ((), ())), preferred_element_type=F32
            )
            allowed = allowed_block(meta_ref, start, BLOCK, columns)
            lane = lax.broadcasted_iota(jnp.int32, (BLOCK, 128), 1)
            log_total = jnp.sum(jnp.where(lane == head, log_ref[at], 0.0), axis=1, keepdims=True)
            probs = jnp.where(allowed, jnp.exp(scores - log_total), 0.0)
            d_probs = lax.dot_general(
                out_grad, v_ref[head, keys], (((1,), (1,)), ((), ())), preferred_element_type=F32
            )
            delta = jnp.sum(probs * d_probs, axis=1, keepdims=True)
            d_scores = (probs * (d_probs - delta)).astype(LOW)
            dq[head, at] = jnp.dot(d_scores, key, preferred_element_type=F32)
            dk[head, keys] += token_product(d_scores, query)
            dv[head, keys] += token_product(probs.astype(LOW), out_grad)
        return carry

    first = 0
    for i in range(1, planes - 1):
        last = -(-heads * i // (planes - 1))
        lax.fori_loop(first, last, one_head, 0)
        first = last
        turn()
        if strided:
            line.step(i)
    lax.fori_loop(first, heads, one_head, 0)
    turn(work.line.steps)
    for start in range(0, length, BLOCK):
        at = pl.ds(start, BLOCK)
        tables = turns(meta_ref, at)
        for two in range(heads // 2):
            both = [
                jnp.concatenate([whole[2 * two, at], whole[2 * two + 1, at]], axis=1).astype(LOW)
                for whole in (dq, dk, dv)
            ]
            query, key = both[0].astype(F32), both[1].astype(F32)
            query = query * tables[0] + swap_lanes(query * tables[1])
            key = key * tables[2] + swap_lanes(key * tables[3])
            out_ref[at, pl.ds(2 * HD * two, 2 * HD)] = query.astype(LOW)
            out_ref[at, pl.ds(span + 2 * HD * two, 2 * HD)] = key.astype(LOW)
            out_ref[at, pl.ds(2 * span + 2 * HD * two, 2 * HD)] = both[2]
    work.finish(ffn_ref)
    if strided:

        def store(tile, total):
            total_ref[tile] = total

        line.finish(store)
    else:
        for t in range(planes):
            total_ref[pl.ds(t * part, part)] = own[t].astype(F32)
    for swap in swaps:
        swap.finish()

    def tile_wait(k, carry):
        tile_copy(k).wait_send()
        other = lax.rem(flat + count - k, count)
        remote(tile_ref.at[0], tiles_ref.at[other], tile_sems, k, here).wait_recv()
        return carry

    lax.fori_loop(1, count, tile_wait, 0)


def attention_backward(planes, chips, heads, strided, part, units, args):
    tokens, width = args[0].shape
    seqs = 2 * chips
    length, span = args[8].shape
    kept = [pltpu.VMEM(args[i].shape, args[i].dtype) for i in (3, 4, 5, 6, 7, 8, 9, 10, 11)]
    return call(
        functools.partial(attention_backward_kernel, planes, chips, heads, strided),
        "attention_backward",
        [
            shape(args[2].shape, F32),
            shape((tokens, width), F32),
            shape((length, 3 * span), LOW),
            shape((part if strided else span, width), F32),
            shape((chips, width, units), LOW),
            shape(args[14].shape, LOW),
        ],
        args,
        [HBM] * 15,
        [HBM, VMEM, VMEM, VMEM, HBM, HBM],
        [
            pltpu.VMEM((seqs, tokens, width), LOW),
            pltpu.VMEM((seqs, tokens, 128), F32),
            *kept,
            *PairScatter.scratch(planes, tokens, width),
            pltpu.VMEM((heads, length, HD), LOW),
            *[pltpu.VMEM((heads, length, HD), F32)] * 3,
            pltpu.VMEM((length, span), LOW),
            pltpu.VMEM((planes, part, width), LOW),
            pltpu.VMEM((planes + 1, part, width), LOW),
            *PlaneGather.sems(chips),
            *PlaneGather.sems(chips),
            *pairs_of(planes * seqs),
            *PairScatter.sems(planes, width),
            *pairs_of(planes, planes, chips, chips),
            pltpu.SemaphoreType.DMA((14,)),
        ],
        2,
        {14: 5},
    )


def body(
    hidden_in,
    segment_ids,
    position_ids,
    w_qkv,
    w_out,
    w_up,
    w_down,
    gain_attn,
    gain_attn_sub,
    gain_ffn,
    gain_ffn_sub,
    ema_qkv,
    ema_out,
    ema_up,
    ema_down,
    ema_gain_attn,
    ema_gain_attn_sub,
    ema_gain_ffn,
    ema_gain_ffn_sub,
    out_grad,
):
    _, tokens, width = hidden_in.shape
    planes, chips = lax.axis_size("dp"), lax.axis_size("chip")
    seqs = 2 * chips
    length = tokens * seqs
    heads = HEADS // seqs
    span = heads * HD
    part = w_qkv.shape[0]
    strided = part % HD == 0
    width_ff = w_down.shape[0] * planes * seqs
    seq_index = lax.axis_index(SEQ)

    def gain_rows(weight, gain):
        return (weight.astype(F32) * gain.astype(F32)[:, None]).astype(LOW)

    out_scaled = gain_rows(w_out, gain_attn_sub)
    down_scaled = gain_rows(w_down, gain_ffn_sub)
    x_in = hidden_in[0].astype(F32)
    normed_one, scaler_one = moments(x_in)
    normed_low = normed_one.astype(LOW)
    qkv_gain = jnp.broadcast_to(gain_attn.astype(F32)[:, None], (part, 128))
    gain_tile = jnp.zeros((8, 128), F32).at[0, :part].set(gain_ffn.astype(F32))

    if not strided:
        out_all = lax.all_gather(out_scaled, ALL, axis=0, tiled=True)
        out_scaled = lax.dynamic_slice_in_dim(out_all, seq_index * span, span, axis=0)

    grad_low = out_grad[0]
    (
        queries, keys, values, attended, log_total, out_sum,
        row_in, meta, qkv_mine, out_mine, gain_tiles, up_mine, grad_flat, tiles,
    ) = attention_forward(
        planes,
        chips,
        heads,
        strided,
        normed_low,
        token_tables(position_ids[0]),
        w_qkv,
        qkv_gain,
        out_scaled,
        gain_tile,
        w_up,
        grad_low,
    )
    if up_mine.ndim == 3:
        up_mine = up_mine.transpose(1, 0, 2).reshape(width, -1)
    row_in = row_in.reshape(length, width)
    meta = meta.reshape(length, -1)
    qkv_mine = qkv_mine.reshape(width, 3 * span)
    out_mine = out_mine.reshape(span, width)
    attended = attended.reshape(length, span)
    tiles = jnp.sum(tiles, axis=0)
    column_sum = tiles[8:].reshape(width)
    sums = tiles[:2].T
    gain_three = gain_tiles[:, 0, :part].reshape(width)
    mean_two = sums[:, :1] / width
    scaler_two = lax.rsqrt(sums[:, 1:] / width - mean_two * mean_two + NORM_EPS)
    projected = scaler_two * (out_sum - mean_two * column_sum[None, :])
    hmid = x_in + projected
    normed_three, scaler_three = moments(hmid)
    ffn_in = (normed_three * gain_three).astype(LOW)

    grad_top = grad_low.astype(F32)
    units = w_up.shape[1]
    d_ffn_in, normed_four, down_mine, grad_up, grad_down, down_slots = feed_forward(
        planes, chips, width_ff, ffn_in, up_mine, grad_flat, down_scaled
    )
    down_mine = down_mine.reshape(-1, width)
    if units % 128:
        grad_up = grad_up.reshape(width, chips, units).transpose(1, 0, 2)

    gain_part = jnp.sum(d_ffn_in * normed_three, axis=0).reshape(planes * seqs, 1, part)
    gain_part = jnp.pad(gain_part, ((0, 0), (0, 7), (0, 128 - part)))
    d_hmid = grad_top + norm_back(d_ffn_in * gain_three, normed_three, scaler_three)
    d_hmid_low = d_hmid.astype(LOW)
    d_hmid_wide = d_hmid_low.astype(F32)
    first_two = jnp.sum(d_hmid_wide * column_sum[None, :], axis=1, keepdims=True) / width
    second_two = jnp.sum(d_hmid_wide * projected, axis=1, keepdims=True) / width
    token_stats = jnp.concatenate([mean_two, scaler_two, first_two, second_two], axis=1)
    gain_part, ffn_out, d_qkv, sum_out, up_slots, down_slots = attention_backward(
        planes,
        chips,
        heads,
        strided,
        part,
        units,
        (
            d_hmid_low,
            jnp.pad(token_stats, ((0, 0), (0, 124))),
            gain_part,
            normed_four,
            down_mine,
            queries,
            keys,
            values,
            attended,
            out_mine,
            log_total,
            meta,
            grad_up,
            grad_down,
            down_slots,
        ),
    )
    output = (hmid + ffn_out).astype(LOW)[None]
    grad_gain_three = jnp.sum(gain_part, axis=0)[0, :part]
    d_in, sum_qkv, grad_gain_one, up_slots = in_scatter(
        planes,
        chips,
        heads,
        strided,
        d_qkv.reshape(seqs, tokens, 3 * span),
        qkv_mine,
        row_in,
        grad_up,
        w_qkv,
        qkv_gain,
        up_slots,
    )
    grad_gain_one = grad_gain_one[:, 0]
    sum_up = jnp.sum(up_slots.astype(F32), axis=0)
    sum_down = jnp.sum(down_slots.astype(F32), axis=0)
    input_grad = (d_hmid + norm_back(d_in, normed_one, scaler_one)).astype(LOW)[None]

    if not strided:
        spread = lax.dynamic_update_slice_in_dim(
            jnp.zeros((width, width), LOW), sum_out.astype(LOW), seq_index * span, axis=0
        )
        sum_out = lax.psum_scatter(spread, ALL, scatter_dimension=0, tiled=True).astype(F32)

    def finish(total, weight, gain):
        wide = weight.astype(F32)
        return (total * gain.astype(F32)[:, None], jnp.sum(total * wide, axis=1))

    sum_out, grad_gain_two = finish(sum_out, w_out, gain_attn_sub)
    sum_down, grad_gain_four = finish(sum_down, w_down, gain_ffn_sub)

    def averaged(average, weight):
        return EMA_DECAY * average + (1.0 - EMA_DECAY) * weight.astype(F32)

    return (
        output,
        input_grad,
        sum_qkv,
        sum_out,
        sum_up,
        sum_down,
        grad_gain_one,
        grad_gain_two,
        grad_gain_three,
        grad_gain_four,
        averaged(ema_qkv, w_qkv),
        averaged(ema_out, w_out),
        averaged(ema_up, w_up),
        averaged(ema_down, w_down),
        averaged(ema_gain_attn, gain_attn),
        averaged(ema_gain_attn_sub, gain_attn_sub),
        averaged(ema_gain_ffn, gain_ffn),
        averaged(ema_gain_ffn_sub, gain_ffn_sub),
    )


def solution(mesh):
    split = Mesh(
        mesh.devices.reshape(mesh.shape["dp"], mesh.shape["seq"] // 2, 2), ("dp", "chip", "core")
    )
    tokens = P("dp", SEQ, None)
    ids = P("dp", SEQ)
    rows = P(ALL, None)
    columns = P(None, ALL)
    vector = P(ALL)
    weights = (rows, rows, columns, rows)
    gains = (vector,) * 4
    return jax.shard_map(
        body,
        mesh=split,
        in_specs=(tokens, ids, ids, *weights, *gains, *weights, *gains, tokens),
        out_specs=(tokens, tokens, *weights, *gains, *weights, *gains),
        check_vma=False,
    )
```

```python
import functools
import math

import jax
import jax.numpy as jnp
from jax import lax
from jax.experimental import pallas as pl
from jax.experimental.pallas import tpu as pltpu
from jax.sharding import Mesh
from jax.sharding import PartitionSpec as P

HEADS = 32
HD = 64

NEG_FILL = -1000000000.0
NORM_EPS = 1e-05
EMA_DECAY = 0.7
LOW = jnp.bfloat16
F32 = jnp.float32
SEQ = ("chip", "core")
TP = ("dp", "core")
ALL = ("dp", "chip", "core")


def moments(values):
    mean = jnp.mean(values, axis=-1, keepdims=True)
    centered = values - mean
    scaler = lax.rsqrt(jnp.mean(centered * centered, axis=-1, keepdims=True) + NORM_EPS)
    return (centered * scaler, scaler)


def norm_back(scaled_grad, normed, scaler):
    first_mean = jnp.mean(scaled_grad, axis=-1, keepdims=True)
    second_mean = jnp.mean(scaled_grad * normed, axis=-1, keepdims=True)
    return scaler * (scaled_grad - first_mean - normed * second_mean)


def token_tables(positions):
    half_count = HD // 2
    index_half = jnp.arange(half_count).astype(F32)
    inverse = jnp.exp(-(2.0 * index_half / HD) * math.log(10000.0))
    decay_base = (2.0 * index_half + 0.4 * HD) / (1.4 * HD)
    where_at = positions.astype(F32)[:, None]
    angles = where_at * inverse[None, :]
    factor = jnp.exp(where_at / 512.0 * jnp.log(decay_base)[None, :])
    sign_row = jnp.where(jnp.arange(HD) % 2 == 0, -1.0, 1.0).astype(F32)
    cosine = jnp.repeat(jnp.cos(angles), 2, axis=1)
    sine = jnp.repeat(jnp.sin(angles), 2, axis=1) * sign_row[None, :]
    factor = jnp.repeat(factor, 2, axis=1)
    grow = factor * HD ** (-0.5)
    where_block = jnp.broadcast_to(where_at, (positions.shape[0], HD))
    return jnp.concatenate(
        [cosine * grow, sine * grow, HD**0.5 / (factor * factor), where_block], axis=1
    )


def dot(left_op, right_op):
    return jnp.dot(left_op, right_op, preferred_element_type=F32)


def rows_product(operand, weight_rows):
    return lax.dot_general(
        operand, weight_rows, (((1,), (1,)), ((), ())), preferred_element_type=F32
    )


def token_product(left_op, right_op):
    return lax.dot_general(left_op, right_op, (((0,), (0,)), ((), ())), preferred_element_type=F32)


MESH = pl.DeviceIdType.MESH
HBM = pl.BlockSpec(memory_space=pl.ANY)
VMEM = pl.BlockSpec(memory_space=pltpu.VMEM)
VMEM_BYTES = 60 * 1024 * 1024


def shape(dims, kind):
    return jax.ShapeDtypeStruct(dims, kind)


def pairs_of(*counts):
    return [pltpu.SemaphoreType.DMA((count,)) for count in counts for _ in range(2)]


def call(kernel, name, outs, args, in_specs, out_specs, scratch, collective=None, aliases=None):
    return pl.pallas_call(
        kernel,
        input_output_aliases=aliases or {},
        name=name,
        out_shape=outs,
        in_specs=in_specs,
        out_specs=out_specs,
        scratch_shapes=scratch,
        compiler_params=pltpu.CompilerParams(
            collective_id=collective,
            has_side_effects=collective is not None,
            vmem_limit_bytes=VMEM_BYTES,
        ),
    )(*args)


def place():
    return (lax.axis_index("dp"), lax.axis_index("chip"), lax.axis_index("core"))


def remote(source, target, sems, index, device):
    return pltpu.make_async_remote_copy(
        src_ref=source,
        dst_ref=target,
        send_sem=sems[0].at[index],
        recv_sem=sems[1].at[index],
        device_id=device,
        device_id_type=MESH,
    )


def greet(barrier, devices):
    for device in devices:
        pl.semaphore_signal(barrier, inc=1, device_id=device, device_id_type=MESH)


def greet_line(barrier, planes, here):
    z, c, core = here

    @pl.when(z < planes - 1)
    def _():
        greet(barrier, [(z + 1, c, core)])

    @pl.when(z > 0)
    def _():
        greet(barrier, [(z - 1, c, core)])


def line_peers(planes, here):
    z = here[0]
    return (2 * planes - 2 - z) // planes + (z + planes - 1) // planes


def chip_peers(chips, here):
    z, c, core = here
    return [(z, lax.rem(c + k, chips), core) for k in range(1, chips)]


def plane_peers(chips, here):
    z, c, core = here
    seqs = 2 * chips
    me = 2 * c + core
    ids = [lax.rem(me + k, seqs) for k in range(1, seqs)]
    return [(z, index // 2, lax.rem(index, 2)) for index in ids]


def column_block(whole, units, index):
    if len(whole.shape) == 3:
        return whole.at[index]
    return whole.at[:, pl.ds(pl.multiple_of(index * units, 128), units)]


UP_FIRST = 3
DOWN_FIRST = 5


def share(rows, second, eighths):
    first = rows * eighths // 128 * 16
    return pl.ds(first, rows - first) if second else pl.ds(0, first)


def half_block(whole, units, index, second):
    at = share(whole.shape[-2], second, UP_FIRST)
    if len(whole.shape) == 3:
        return whole.at[index, at]
    return whole.at[at, pl.ds(pl.multiple_of(index * units, 128), units)]


class ChipSwap:
    def __init__(self, chips, here, source, slot, sems):
        z, c, core = here
        self.sends = [
            remote(source(device[1]), slot(c), sems, k, device)
            for k, device in enumerate(chip_peers(chips, here), 1)
        ]
        self.waits = [
            remote(source(c), slot(lax.rem(c + chips - k, chips)), sems, k, here)
            for k in range(1, chips)
        ]
        self.keep = (source(c), slot(c))

    def start(self, local):
        for copy in self.sends:
            copy.start()
        self.held = pltpu.make_async_copy(*self.keep, local)
        self.held.start()

    def finish(self):
        self.held.wait()
        for send, wait in zip(self.sends, self.waits):
            send.wait_send()
            wait.wait_recv()


class ChipGather:
    def __init__(self, chips, here, source, target, sems):
        z, c, core = here
        self.here, self.sems, self.relayed = here, sems, chips == 4
        if not self.relayed:
            self.sends = [
                remote(source(None), target(c, None), sems, k, device)
                for k, device in enumerate(chip_peers(chips, here), 1)
            ]
            self.arrivals = [
                (lax.rem(c + chips - k, chips), None, k) for k in range(1, chips)
            ]
        else:
            beside = c + 1 - 2 * lax.rem(c, 2)
            above = c + 2 - 4 * (c // 2)
            to_beside, to_above = (z, beside, core), (z, above, core)
            self.sends = [
                remote(source(0), target(c, 0), sems, 0, to_beside),
                remote(source(1), target(c, 1), sems, 3, to_above),
                remote(source(1), target(c, 1), sems, 1, to_beside),
                remote(source(0), target(c, 0), sems, 2, to_above),
            ]
            self.relays = [
                remote(target(beside, 0), target(beside, 0), sems, 4, to_above),
                remote(target(above, 1), target(above, 1), sems, 5, to_beside),
            ]
            self.arrivals = [
                (beside, 0, 0), (above, 1, 3), (beside, 1, 1), (above, 0, 2),
                (3 - c, 0, 4), (3 - c, 1, 5),
            ]
        self.target = target

    def start(self):
        for copy in self.sends:
            copy.start()

    def arrive(self, i):
        chip, half, index = self.arrivals[i]
        block = self.target(chip, half)
        remote(block, block, self.sems, index, self.here).wait_recv()
        if self.relayed and i < 2:
            self.relays[i].start()

    def relay(self):
        for i in range(2 if self.relayed else 0):
            self.arrive(i)

    def rest(self):
        return range(2 if self.relayed else 0, len(self.arrivals))

    def finish(self):
        for i in self.rest():
            self.arrive(i)
        self.sent()

    def sent(self):
        for copy in [*self.sends, *(self.relays if self.relayed else [])]:
            copy.wait_send()

    @staticmethod
    def count(chips):
        return max(chips, 6)


class PlaneGather:
    def __init__(self, chips, here, block, out, far, near):
        z, c, core = here
        self.here, self.block, self.out, self.near = here, block, out, near
        self.me = 2 * c + core
        self.partner = (z, c, 1 - core)
        self.size = block.shape[0] // 2
        self.chips = ChipGather(
            chips,
            here,
            self.piece,
            lambda chip, half: self.place(2 * chip + core, half),
            far,
        )
        self.own = remote(block, out.at[self.me], near, len(self.chips.arrivals), self.partner)

    def rows(self, half):
        return pl.ds(half * self.size, self.size)

    def piece(self, half):
        return self.block if half is None else self.block.at[self.rows(half)]

    def place(self, index, half):
        return self.out.at[index] if half is None else self.out.at[index, self.rows(half)]

    def start(self):
        self.chips.start()
        self.own.start()

    def passed(self, i, other=0):
        chip, half, _ = self.chips.arrivals[i]
        core = self.here[2]
        block = self.place(2 * chip + (1 - core if other else core), half)
        return remote(block, block, self.near, i, self.partner)

    def relay(self):
        for i in range(2 if self.chips.relayed else 0):
            self.chips.arrive(i)
            self.passed(i).start()

    def forward(self):
        for i in self.chips.rest():
            self.chips.arrive(i)
            self.passed(i).start()

    def finish(self):
        self.chips.sent()
        self.own.wait_send()
        mine = self.out.at[2 * self.here[1] + 1 - self.here[2]]
        remote(mine, mine, self.near, len(self.chips.arrivals), self.partner).wait_recv()
        for i in range(len(self.chips.arrivals)):
            self.passed(i).wait_send()
            self.passed(i, 1).wait_recv()

    @staticmethod
    def sems(chips):
        return pairs_of(ChipGather.count(chips), ChipGather.count(chips) + 1)


def row_half(ref, half):
    if half is None:
        return ref
    size = ref.shape[0] // 2
    return ref.at[pl.ds(half * size, size)]


class LineGather:
    def __init__(self, planes, here, parts, up, down):
        self.planes, self.here, self.parts = planes, here, parts
        self.up, self.down = up, down
        self.count = len(parts(here[0]))

    def upward(self, d, p):
        z, c, core = self.here
        block = self.parts(z - d)[p]
        return remote(block, block, self.up, d * self.count + p, (z + 1, c, core))

    def downward(self, d, p):
        z, c, core = self.here
        block = self.parts(z + d)[p]
        return remote(block, block, self.down, d * self.count + p, (z - 1, c, core))

    def each(self, d, p, act):
        z, planes = self.here[0], self.planes
        pl.when((z < planes - 1) & (z - d >= 0))(lambda: act(self.upward(d, p)))
        pl.when((z > 0) & (z + d < planes))(lambda: act(self.downward(d, p)))

    def start(self):
        for p in range(self.count):
            self.each(0, p, lambda copy: copy.start())

    def step(self, d, arrived=None):
        z, planes = self.here[0], self.planes

        def below(p):
            block = self.parts(z - d)[p]
            remote(block, block, self.up, (d - 1) * self.count + p, self.here).wait_recv()
            if d < planes - 1:
                pl.when(z < planes - 1)(lambda: self.upward(d, p).start())
            if arrived is not None:
                arrived(z - d, p)

        def above(p):
            block = self.parts(z + d)[p]
            remote(block, block, self.down, (d - 1) * self.count + p, self.here).wait_recv()
            if d < planes - 1:
                pl.when(z > 0)(lambda: self.downward(d, p).start())
            if arrived is not None:
                arrived(z + d, p)

        for p in range(self.count):
            pl.when(z - d >= 0)(lambda p=p: below(p))
            pl.when(z + d < planes)(lambda p=p: above(p))

    def finish(self):
        for d in range(self.planes - 1):
            for p in range(self.count):
                self.each(d, p, lambda copy: copy.wait_send())


class GroupGather:
    PARTS = 2

    def __init__(self, planes, here, block, out, up, down, near):
        self.planes, self.here, self.block, self.out, self.near = planes, here, block, out, near
        self.partner = (here[0], here[1], 1 - here[2])
        size = block.shape[0] // self.PARTS
        self.slices = [pl.ds(p * size, size) for p in range(self.PARTS)]
        core = here[2]
        self.line = LineGather(planes, here, lambda t: self.parts(t, core), up, down)

    def parts(self, t, core):
        return [self.out.at[t, core, rows] for rows in self.slices]

    def passed(self, t, p):
        block = self.parts(t, self.here[2])[p]
        return remote(block, block, self.near, t * self.PARTS + p, self.partner)

    def start(self, local):
        z, _, core = self.here
        keep = pltpu.make_async_copy(self.block, self.out.at[z, core], local)
        keep.start()
        keep.wait()
        self.line.start()
        for p in range(self.PARTS):
            self.passed(z, p).start()

    def step(self, d):
        self.line.step(d, lambda t, p: self.passed(t, p).start())

    def other(self, t):
        for p in range(self.PARTS):
            block = self.parts(t, 1 - self.here[2])[p]
            remote(block, block, self.near, t * self.PARTS + p, self.partner).wait_recv()

    def finish(self):
        self.line.finish()
        for t in range(self.planes):
            for p in range(self.PARTS):
                self.passed(t, p).wait_send()

    @classmethod
    def sems(cls, planes):
        return pairs_of(*[planes * cls.PARTS] * 3)


COLUMNS = 512


def product(left, right, columns, turned):
    if turned:
        return lax.dot_general(
            left, right[columns, :], (((1,), (1,)), ((), ())), preferred_element_type=F32
        )
    return jnp.dot(left, right[:, columns], preferred_element_type=F32)


class PlaneScatter:
    def __init__(self, chips, here, left, right, turned, buffers, near, far):
        self.chips, self.here = chips, here
        self.left, self.right, self.turned = left, right, turned
        self.near_out, self.near_in, self.far_out, self.far_in = buffers
        self.near, self.far = near, far
        self.tokens, width = self.near_out.shape[1:]
        self.tiles = [pl.ds(at, COLUMNS) for at in range(0, width, COLUMNS)]
        self.order = [*range(1, chips), 0]

    def target(self, k):
        return lax.rem(self.here[1] + k, self.chips)

    def near_copy(self, i):
        z, c, core = self.here
        at = (slice(None), slice(None), self.tiles[i])
        return remote(self.near_out.at[at], self.near_in.at[at], self.near, i, (z, c, 1 - core))

    def far_copy(self, k, i):
        z, _, core = self.here
        at = (k, slice(None), self.tiles[i])
        index = k * len(self.tiles) + i
        return remote(
            self.far_out.at[at], self.far_in.at[at], self.far, index, (z, self.target(k), core)
        )

    def rows(self, position):
        return slice(position * self.tokens, (position + 1) * self.tokens)

    def start(self):
        core = self.here[2]
        blocks = [self.left[2 * self.target(k) + 1 - core] for k in self.order]
        left = jnp.concatenate(blocks, axis=0)
        for i, columns in enumerate(self.tiles):
            part = product(left, self.right, columns, self.turned).astype(LOW)
            for position, k in enumerate(self.order):
                self.near_out[k, :, columns] = part[self.rows(position)]
            self.near_copy(i).start()
        blocks = [self.left[2 * self.target(k) + core] for k in self.order]
        left = jnp.concatenate(blocks, axis=0)
        for i, columns in enumerate(self.tiles):
            part = product(left, self.right, columns, self.turned)
            self.near_copy(i).wait_recv()
            for position, k in enumerate(self.order):
                self.far_out[k, :, columns] = (
                    part[self.rows(position)] + self.near_in[k, :, columns].astype(F32)
                ).astype(LOW)
                if k:
                    self.far_copy(k, i).start()

    def finish(self, out_ref):
        for i, columns in enumerate(self.tiles):
            total = self.far_out[0, :, columns].astype(F32)
            for k in range(1, self.chips):
                self.far_copy(k, i).wait_recv()
                total = total + self.far_in[k, :, columns].astype(F32)
            out_ref[:, columns] = total
        for i in range(len(self.tiles)):
            self.near_copy(i).wait_send()
            for k in range(1, self.chips):
                self.far_copy(k, i).wait_send()

    @staticmethod
    def scratch(chips, tokens, width):
        return [pltpu.VMEM((chips, tokens, width), LOW)] * 4

    @staticmethod
    def sems(chips, width):
        return pairs_of(width // COLUMNS, chips * (width // COLUMNS))


class LineScatter:
    def __init__(self, planes, here, count, part, tiles, own, slots, up, down):
        self.planes, self.here, self.count = planes, here, count
        self.part, self.tiles, self.own, self.slots = part, tiles, own, slots
        self.up, self.down = up, down
        self.steps = (planes - 1) * count

    def upward(self, t, p):
        z, c, core = self.here
        block = self.slots.at[(t, *self.part(p))]
        return remote(block, block, self.up, t * self.count + p, (z + 1, c, core))

    def downward(self, t, p, last):
        z, c, core = self.here
        block = self.slots.at[(t, *self.part(p))]
        target = self.slots.at[(self.planes, *self.part(p))] if last else block
        return remote(block, target, self.down, t * self.count + p, (z - 1, c, core))

    def add(self, t, p, fresh):
        for tile in self.tiles(p):
            total = self.own(t, tile)
            if not fresh:
                total = total + self.slots[(t, *tile)].astype(F32)
            self.slots[(t, *tile)] = total.astype(LOW)

    def step(self, i):
        z, planes, count = self.here[0], self.planes, self.count
        rise, fall = i - z, i - (planes - 1 - z)

        @pl.when((rise >= 0) & (rise < (planes - 1 - z) * count))
        def _():
            t, p = planes - 1 - rise // count, lax.rem(rise, count)

            @pl.when(z > 0)
            def _():
                self.upward(t, p).wait_recv()
                self.add(t, p, False)

            @pl.when(z == 0)
            def _():
                self.add(t, p, True)

            self.upward(t, p).start()

        @pl.when((fall >= 0) & (fall < z * count))
        def _():
            t, p = fall // count, lax.rem(fall, count)

            @pl.when(z < planes - 1)
            def _():
                self.downward(t, p, False).wait_recv()
                self.add(t, p, False)

            @pl.when(z == planes - 1)
            def _():
                self.add(t, p, True)

            pl.when(t == z - 1)(lambda: self.downward(t, p, True).start())
            pl.when(t < z - 1)(lambda: self.downward(t, p, False).start())

    def finish(self, store, after=None):
        z, planes = self.here[0], self.planes

        def total(tile, *slots):
            value = self.own(z, tile)
            for slot in slots:
                value = value + self.slots[(slot, *tile)].astype(F32)
            store(tile, value)

        for p in range(self.count):
            tiles = self.tiles(p)

            @pl.when(z > 0)
            def _(p=p):
                self.upward(z, p).wait_recv()

            @pl.when(z < planes - 1)
            def _(p=p):
                self.downward(z, p, True).wait_recv()

            @pl.when((z > 0) & (z < planes - 1))
            def _(tiles=tiles):
                for tile in tiles:
                    total(tile, z, planes)

            @pl.when(z == 0)
            def _(tiles=tiles):
                for tile in tiles:
                    total(tile, planes)

            @pl.when(z == planes - 1)
            def _(tiles=tiles):
                for tile in tiles:
                    total(tile, z)

            if after is not None:
                after(p)

        for t in range(planes):
            for p in range(self.count):
                pl.when(z < t)(lambda t=t, p=p: self.upward(t, p).wait_send())
                pl.when(z > t)(lambda t=t, p=p: self.downward(t, p, False).wait_send())


def row_tiles(count, size):
    return [pl.ds(at, size) for at in range(0, count, size)]


def in_scatter_kernel(
    planes, chips, heads, strided, left_in, right_in, rows_in, up_ref, weight_ref, gain_ref, _,
    out_ref, total_ref, gains_ref, slots_ref,
    left_ref, right_ref, rows_ref, grad_ref,
    near_out, near_in, far_out, far_in, sums, mine, parts, *sems,
):
    here = place()
    z, c, core = here
    seqs = 2 * chips
    me = 2 * c + core
    near, far, up, down, swap_sems, chip_sems = [sems[2 * i : 2 * i + 2] for i in range(6)]
    local = sems[12]
    loads = [
        pltpu.make_async_copy(rows_in, rows_ref, local.at[1]),
        pltpu.make_async_copy(left_in, left_ref, local.at[2]),
        pltpu.make_async_copy(right_in, right_ref, local.at[3]),
    ]
    for copy in loads:
        copy.start()
    barrier = pltpu.get_barrier_semaphore()
    peers = plane_peers(chips, here)
    greet(barrier, peers)
    greet_line(barrier, planes, here)
    pl.semaphore_wait(barrier, len(peers) + line_peers(planes, here))
    units = slots_ref.shape[2]
    lower = share(slots_ref.shape[1], 1, UP_FIRST)
    ups = ChipSwap(
        chips,
        here,
        lambda index: half_block(up_ref, units, index, 1),
        lambda index: slots_ref.at[index, lower],
        chip_sems,
    )
    ups.start(local.at[0])
    half = seqs // 2
    line = LineScatter(
        planes,
        here,
        2,
        lambda p: (pl.ds(p * half, half),),
        lambda p: [(pl.ds(p * half + i, 1),) for i in range(half)],
        lambda t, tile: grad_ref[(t, *tile)].astype(F32),
        sums,
        up,
        down,
    )
    part = grad_ref.shape[2]
    span = heads * HD
    block = seqs * part
    length = rows_ref.shape[0]
    for copy in loads:
        copy.wait()

    def grads(t):
        left = rows_ref[:, t * block : (t + 1) * block]
        for i in range(3):
            at = pl.ds(i * span, span)
            term = token_product(left, left_ref[:, :, at].reshape(length, span))
            grad_ref[t, :, :, at] = term.astype(LOW).reshape(seqs, part, span)

    order = []
    for i in range((planes + 1) // 2):
        order += [planes - 1 - i, i] if planes - 1 - i != i else [i]
    for t in order[:2]:
        grads(t)
    line.step(0)
    for t in order[2:]:
        grads(t)
    work = PlaneScatter(
        chips, here, left_ref, right_ref, True, (near_out, near_in, far_out, far_in), near, far
    )
    work.start()
    for i in range(1, line.steps):
        line.step(i)

    def store(tile, total):
        mine[tile] = total.astype(LOW)

    owners = [2 * device[1] + device[2] for device in peers]
    swaps = [
        remote(mine.at[owner], parts.at[me], swap_sems, k, device)
        for k, (owner, device) in enumerate(zip(owners, peers), 1)
    ]

    def send(p):
        for owner, copy in zip(owners, swaps):
            pl.when(owner // half == p)(copy.start)

    line.finish(store, send)
    parts[me] = mine[me]
    work.finish(out_ref)
    for k in range(1, seqs):
        swaps[k - 1].wait_send()
        index = lax.rem(me + seqs - k, seqs)
        remote(mine.at[0], parts.at[index], swap_sems, k, here).wait_recv()
    width = seqs * span
    gain = gain_ref[:, pl.ds(0, 1)]
    summed = jnp.zeros(gain.shape, F32)
    for i in range(3):
        step, pieces = (seqs * HD, planes) if strided else (width, 1)
        size = step // seqs
        for piece in range(pieces):
            at = i * span + piece * size
            columns = pl.ds(i * width + piece * step, step)
            total = jnp.concatenate(
                [parts[s, :, pl.ds(at, size)].astype(F32) for s in range(seqs)], axis=1
            )
            weight = weight_ref[:, columns].astype(F32)
            summed = summed + jnp.sum(total * weight, axis=1, keepdims=True)
            total_ref[:, columns] = total * gain
    gains_ref[...] = jnp.broadcast_to(summed, gains_ref.shape)
    ups.finish()


def in_scatter(planes, chips, heads, strided, left, right, rows, up_grads, weight, gain, slots):
    _, tokens, _ = left.shape
    width = right.shape[0]
    seqs = 2 * chips
    part, wide = weight.shape[0], left.shape[2]
    return call(
        functools.partial(in_scatter_kernel, planes, chips, heads, strided),
        "in_scatter",
        [
            shape((tokens, width), F32),
            shape(weight.shape, F32),
            shape((part, 128), F32),
            shape(slots.shape, LOW),
        ],
        (left, right, rows, up_grads, weight, gain, slots),
        [HBM, HBM, HBM, HBM, VMEM, VMEM, HBM],
        [VMEM, VMEM, VMEM, HBM],
        [
            *[pltpu.VMEM(whole.shape, LOW) for whole in (left, right, rows)],
            pltpu.VMEM((planes, seqs, part, wide), LOW),
            *PlaneScatter.scratch(chips, tokens, width),
            pltpu.VMEM((planes + 1, seqs, part, wide), LOW),
            *[pltpu.VMEM((seqs, part, wide), LOW)] * 2,
            *PlaneScatter.sems(chips, width),
            *pairs_of(2 * planes, 2 * planes, seqs, chips),
            pltpu.SemaphoreType.DMA((4,)),
        ],
        4,
        {6: 3},
    )


class PairScatter:
    PARTS = 2

    def __init__(self, planes, here, left, right, turned, buffers, near, up, down):
        self.planes, self.here = planes, here
        self.left, self.right, self.turned = left, right, turned
        self.near_out, self.own, slots = buffers
        self.near = near
        self.tokens, width = self.near_out.shape[1:]
        self.tiles = [pl.ds(at, COLUMNS) for at in range(0, width, COLUMNS)]
        size = width // self.PARTS

        def part(p):
            at = p * size if isinstance(p, int) else pl.multiple_of(p * size, 128)
            return (slice(None), pl.ds(at, size))

        self.line = LineScatter(
            planes,
            here,
            self.PARTS,
            part,
            lambda p: [(rows, part(p)[1]) for rows in row_tiles(self.tokens, 32)],
            lambda t, tile: self.own[(t, *tile)].astype(F32),
            slots,
            up,
            down,
        )

    def near_copy(self, i):
        z, c, core = self.here
        at = (slice(None), slice(None), self.tiles[i])
        return remote(self.near_out.at[at], self.own.at[at], self.near, i, (z, c, 1 - core))

    def start(self):
        core, tokens = self.here[2], self.tokens
        left = jnp.concatenate([self.left[t, 1 - core] for t in range(self.planes)], axis=0)
        for i, columns in enumerate(self.tiles):
            part = product(left, self.right, columns, self.turned).astype(LOW)
            for t in range(self.planes):
                self.near_out[t, :, columns] = part[t * tokens : (t + 1) * tokens]
            self.near_copy(i).start()
        left = jnp.concatenate([self.left[t, core] for t in range(self.planes)], axis=0)
        for i, columns in enumerate(self.tiles):
            part = product(left, self.right, columns, self.turned)
            self.near_copy(i).wait_recv()
            for t in range(self.planes):
                self.own[t, :, columns] = (
                    part[t * tokens : (t + 1) * tokens] + self.own[t, :, columns].astype(F32)
                ).astype(LOW)
        self.line.step(0)

    def finish(self, out_ref):
        def store(tile, total):
            out_ref[tile] = total

        self.line.finish(store)
        for i in range(len(self.tiles)):
            self.near_copy(i).wait_send()

    @staticmethod
    def scratch(planes, tokens, width):
        return [
            *[pltpu.VMEM((planes, tokens, width), LOW)] * 2,
            pltpu.VMEM((planes + 1, tokens, width), LOW),
        ]

    @classmethod
    def sems(cls, planes, width):
        return pairs_of(width // COLUMNS, cls.PARTS * planes, cls.PARTS * planes)


def feed_forward_kernel(
    planes, chips, width_ff, x_ref, up_ref, grads_ref, downs_ref,
    out_ref, normed_ref, gup_ref, gdown_ref, slots_ref,
    rows, ups, grads, downs, back, act, slope, stat, stat_out, stat_in,
    normed, d_up, near_out, own, sums, gup, gdown, *sems,
):
    here = place()
    z, c, core = here
    count = 2 * planes
    me = 2 * z + core
    up, down, near, stat_sems, pair, rise, fall, swap_sems = [
        sems[2 * i : 2 * i + 2] for i in range(8)
    ]
    local = sems[16]
    tokens, width = x_ref.shape
    units = ups.shape[1]
    load_up = pltpu.make_async_copy(up_ref, ups, local.at[0])
    load_grads = pltpu.make_async_copy(grads_ref, grads, local.at[1])
    load_up.start()
    load_grads.start()
    load_downs = pltpu.make_async_copy(downs_ref, downs, local.at[3])
    load_downs.start()
    barrier = pltpu.get_barrier_semaphore()
    ids = [lax.rem(me + k, count) for k in range(1, count)]
    group_peers = [(index // 2, c, lax.rem(index, 2)) for index in ids]
    peers = [*group_peers, *chip_peers(chips, here)]
    greet(barrier, peers)
    pl.semaphore_wait(barrier, len(peers))

    group = GroupGather(planes, here, x_ref, rows, up, down, near)
    group.start(local.at[2])
    load_up.wait()

    step = tokens
    lane = lax.broadcasted_iota(jnp.int32, (step, 128), 1)

    def forward(t):
        group.other(t)
        block = rows[t].reshape(2 * tokens, width)
        for at in range(0, units, COLUMNS):
            columns = pl.ds(at, COLUMNS)
            act[t, :, columns] = jnp.dot(block, ups[:, columns], preferred_element_type=F32)

        def some(i, carry):
            at = pl.ds(pl.multiple_of(i * step, step), step)
            value = act[t, at]
            phi = 0.5 * (1.0 + lax.erf(value * math.sqrt(0.5)))
            result = value * phi
            act[t, at] = result
            slope[t, at] = phi + value * (
                jnp.exp(value * value * -0.5) * (1.0 / math.sqrt(2.0 * math.pi))
            )
            total = jnp.sum(result, axis=1, keepdims=True)
            square = jnp.sum(result * result, axis=1, keepdims=True)
            stat[t, at] = jnp.where(lane == 0, total, jnp.where(lane == 1, square, 0.0))
            return carry

        lax.fori_loop(0, 2 * tokens // step, some, 0)

    def project(t):
        block = grads[t].reshape(2 * tokens, width)
        size = units // chips
        for chip in range(chips):
            back[t, :, pl.ds(chip * size, size)] = rows_product(block, downs[chip])

    forward(z)
    load_grads.wait()
    load_downs.wait()
    project(0)
    for d in range(1, planes):
        group.step(d)
        project(d)
        if d > 1:
            pl.when(z - d + 1 >= 0)(lambda d=d: forward(z - d + 1))
            pl.when(z + d - 1 < planes)(lambda d=d: forward(z + d - 1))
    pl.when(z - planes + 1 >= 0)(lambda: forward(z - planes + 1))
    pl.when(z + planes - 1 < planes)(lambda: forward(z + planes - 1))
    group.finish()

    def backward(t, carry):
        def some(i, inner):
            at = pl.ds(pl.multiple_of(i * step, step), step)
            value = back[t, at]
            cross = jnp.sum(value * act[t, at], axis=1, keepdims=True)
            total = jnp.sum(value, axis=1, keepdims=True)
            stat[t, at] = jnp.where(lane == 2, cross, jnp.where(lane == 3, total, stat[t, at]))
            return inner

        lax.fori_loop(0, 2 * tokens // step, some, 0)
        for half in range(2):
            turned = stat[t, pl.ds(half * tokens, tokens)].T
            stat_out[2 * t + half] = turned[:8]
        return carry

    lax.fori_loop(0, planes, backward, 0)
    copies = [
        remote(stat_out, stat_in.at[k], stat_sems, k, device)
        for k, device in enumerate(group_peers, 1)
    ]
    for copy in copies:
        copy.start()
    for copy in copies:
        copy.wait_send()
        copy.wait_recv()

    def finish(t, carry):
        for half in range(2):
            total = stat_out[2 * t + half]
            for k in range(1, count):
                total = total + stat_in[k, 2 * t + half]
            mean, square, cross, first = (total[i : i + 1] / width_ff for i in range(4))
            scaler = lax.rsqrt(square - mean * mean + NORM_EPS)
            second = scaler * (cross - mean * first)
            figures = [scaler, -mean * scaler, scaler * first, scaler * second]
            padded = jnp.concatenate([*figures, jnp.zeros((128 - 4, tokens), F32)], axis=0)
            stat[t, pl.ds(half * tokens, tokens)] = padded.T

        def some(i, inner):
            at = pl.ds(pl.multiple_of(i * step, step), step)
            figures = stat[t, at]
            scaler, shift, first, second = (figures[:, j : j + 1] for j in range(4))
            unit = act[t, at] * scaler + shift
            normed[t, at] = unit.astype(LOW)
            d_act = back[t, at] * scaler - first - unit * second
            d_up[t, at] = (d_act * slope[t, at]).astype(LOW)
            return inner

        lax.fori_loop(0, 2 * tokens // step, some, 0)
        return carry

    lax.fori_loop(0, planes, finish, 0)
    out_normed = pltpu.make_async_copy(normed, normed_ref, local.at[5])
    out_normed.start()
    work = PairScatter(
        planes, here, Halves(d_up, tokens), ups, True, (near_out, own, sums), pair, rise, fall
    )
    work.start()

    flat_normed, flat_d_up = (
        whole[...].reshape(planes * 2 * tokens, units) for whole in (normed, d_up)
    )
    size = units // chips
    upper = share(size, 0, DOWN_FIRST)
    swap = ChipSwap(
        chips,
        here,
        lambda index: gdown.at[index, upper],
        lambda index: slots_ref.at[index, upper],
        swap_sems,
    )
    turns_left = list(range(1, work.line.steps))

    def turn():
        if turns_left:
            work.line.step(turns_left.pop(0))

    together = max(1, 256 // size)
    for chip in range(0, chips, together):
        left = flat_normed[:, chip * size : (chip + together) * size]
        for at in range(0, width, COLUMNS):
            columns = pl.ds(at, COLUMNS)
            right = grads[:, :, :, columns].reshape(planes * 2 * tokens, COLUMNS)
            term = token_product(left, right).astype(LOW)
            for i in range(together):
                gdown[chip + i, :, columns] = term[i * size : (i + 1) * size]
    swap.start(local.at[6])
    out_gdown = pltpu.make_async_copy(gdown, gdown_ref, local.at[9])
    out_gdown.start()
    chunk = gup.shape[1]
    out_gups = [
        pltpu.make_async_copy(
            gup.at[i % 2], gup_ref.at[pl.ds(i * chunk, chunk)], local.at[7 + i % 2]
        )
        for i in range(width // chunk)
    ]
    for i in range(width // chunk):
        if i == 0 or i % 2:
            turn()
        left = rows[:, :, :, pl.ds(i * chunk, chunk)].reshape(planes * 2 * tokens, chunk)
        term = token_product(left, flat_d_up).astype(LOW)
        if i > 1:
            out_gups[i - 2].wait()
        gup[i % 2] = term
        out_gups[i].start()
    while turns_left:
        turn()
    work.finish(out_ref)
    swap.finish()
    out_normed.wait()
    out_gdown.wait()
    for copy in out_gups[-2:]:
        copy.wait()


class Halves:
    def __init__(self, whole, tokens):
        self.whole, self.tokens = whole, tokens

    def __getitem__(self, at):
        t, core = at
        rows = pl.ds(pl.multiple_of(core * self.tokens, self.tokens), self.tokens)
        return self.whole[t, rows]


def feed_forward(planes, chips, width_ff, x_block, up_mine, grads, downs):
    tokens, width = x_block.shape
    units = up_mine.shape[1]
    size = downs.shape[1]
    wide = (planes, 2 * tokens, units)
    return call(
        functools.partial(feed_forward_kernel, planes, chips, width_ff),
        "feed_forward",
        [
            shape((tokens, width), F32),
            shape(wide, LOW),
            shape((width, units), LOW),
            *[shape((chips, size, width), LOW)] * 2,
        ],
        (x_block, up_mine, grads, downs),
        [HBM] * 4,
        [VMEM, *[HBM] * 4],
        [
            pltpu.VMEM((planes, 2, tokens, width), LOW),
            pltpu.VMEM((width, units), LOW),
            pltpu.VMEM((planes, 2, tokens, width), LOW),
            pltpu.VMEM((chips, size, width), LOW),
            *[pltpu.VMEM(wide, F32)] * 3,
            pltpu.VMEM((planes, 2 * tokens, 128), F32),
            pltpu.VMEM((2 * planes, 8, 128), F32),
            pltpu.VMEM((2 * planes, 2 * planes, 8, 128), F32),
            *[pltpu.VMEM(wide, LOW)] * 2,
            *PairScatter.scratch(planes, tokens, width),
            pltpu.VMEM((2, 256, units), LOW),
            pltpu.VMEM((chips, size, width), LOW),
            *GroupGather.sems(planes),
            *pairs_of(2 * planes),
            *PairScatter.sems(planes, width),
            *pairs_of(chips),
            pltpu.SemaphoreType.DMA((10,)),
        ],
        7,
    )


def swap_lanes(values):
    lane = lax.broadcasted_iota(jnp.int32, values.shape, 1)
    return jnp.where(
        lax.rem(lane, 2) == 0,
        pltpu.roll(values, values.shape[1] - 1, 1),
        pltpu.roll(values, 1, 1),
    )


def twice(table):
    return jnp.concatenate([table, table], axis=1)


def turns(meta_ref, rows):
    cosine, sine, shrink = [twice(meta_ref[rows, pl.ds(i * HD, HD)]) for i in range(3)]
    return (cosine, sine, cosine * shrink, sine * shrink)


def allowed_block(meta_ref, rows, size, columns):
    query = rows + lax.broadcasted_iota(jnp.int32, (size, columns), 0)
    key = lax.broadcasted_iota(jnp.int32, (size, columns), 1)
    offset = meta_ref[pl.ds(rows, size), pl.ds(3 * HD, 1)].astype(jnp.int32)
    return (key <= query) & (key >= query - offset)


BLOCK = 256


def attention_forward_kernel(
    planes, chips, heads, strided,
    x_ref, meta_ref, weight_ref, scale_ref, out_ref, gain_ref, up_ref, down_ref, grad_ref,
    q_ref, k_ref, v_ref, att_ref, log_ref, sum_ref,
    rows_ref, metas_ref, qkvs_ref, outs_ref, gains_ref, ups_ref, downs_ref, grads_ref, tiles_ref,
    qkv_ref, rows, metas, qkvs, outs, raw, wide, tile, near_out, near_in, far_out, far_in,
    *sems,
):
    here = place()
    z, c, core = here
    seqs = 2 * chips
    count = planes * seqs
    me = 2 * c + core
    flat = z * seqs + me
    groups = [sems[2 * i : 2 * i + 2] for i in range(18)]
    swap_sems, x_far, x_near, meta_far, meta_near, up, down, up_two, down_two = groups[:9]
    gain_sems, up_sems, near, far, tile_sems, grad_up, grad_down, pair, weight_sems = groups[9:]
    local = sems[36]
    tokens, width = x_ref.shape
    part = qkv_ref.shape[1]
    length = seqs * tokens
    span = heads * HD
    barrier = pltpu.get_barrier_semaphore()

    def device_of(k):
        other = lax.rem(flat + k, count)
        return (other // seqs, lax.rem(other, seqs) // 2, lax.rem(other, 2))

    def signal(k, carry):
        greet(barrier, [device_of(k)])
        return carry

    lax.fori_loop(1, count, signal, 0)
    scale = scale_ref[:, pl.ds(0, 1)]
    for s in range(seqs):
        for i in range(3):
            if strided:
                starts = [i * width + (t * seqs + s) * HD for t in range(planes)]
                size = span // planes
            else:
                starts, size = [i * width + s * span], span
            piece = jnp.concatenate([weight_ref[:, pl.ds(at, size)] for at in starts], axis=1)
            qkv_ref[s, :, pl.ds(i * span, span)] = (piece.astype(F32) * scale).astype(LOW)
    pl.semaphore_wait(barrier, count - 1)

    mine = pltpu.make_async_copy(qkv_ref.at[me], qkvs.at[z, me], local.at[0])
    own_out = pltpu.make_async_copy(out_ref, outs.at[z] if strided else outs, local.at[1])
    units = up_ref.shape[1]
    keeps = [
        pltpu.make_async_copy(x_ref, rows.at[me], local.at[2]),
        pltpu.make_async_copy(meta_ref, metas.at[me], local.at[3]),
        pltpu.make_async_copy(gain_ref, gains_ref.at[flat], local.at[4]),
        pltpu.make_async_copy(up_ref, column_block(ups_ref, units, c), local.at[5]),
        pltpu.make_async_copy(down_ref, downs_ref.at[c], local.at[12]),
    ]
    peers = plane_peers(chips, here)
    swaps = [
        remote(qkv_ref.at[2 * device[1] + device[2]], qkvs.at[z, me], swap_sems, k, device)
        for k, device in enumerate(peers, 1)
    ]
    mine.start()
    own_out.start()
    for copy in swaps:
        copy.start()
    gather = PlaneGather(chips, here, x_ref, rows, x_far, x_near)
    meta_gather = PlaneGather(chips, here, meta_ref, metas, meta_far, meta_near)
    for copy in keeps:
        copy.start()

    def gain_copy(k):
        return remote(gain_ref, gains_ref.at[flat], gain_sems, k, device_of(k))

    def gain_start(k, carry):
        gain_copy(k).start()
        return carry

    mine.wait()
    own_out.wait()
    for k in range(1, seqs):
        index = lax.rem(me + seqs - k, seqs)
        remote(qkv_ref.at[0], qkvs.at[z, index], swap_sems, k, here).wait_recv()
    half = seqs // 2
    line = LineGather(
        planes, here, lambda t: [qkvs.at[t, pl.ds(i * half, half)] for i in range(2)], up, down
    )
    line_two = LineGather(planes, here, lambda t: [outs.at[t]], up_two, down_two)
    line.start()
    gather.start()
    meta_gather.start()
    lax.fori_loop(1, count, gain_start, 0)
    gather.relay()
    meta_gather.relay()
    line.step(1)
    gather.forward()
    meta_gather.forward()
    ups = ChipGather(
        chips,
        here,
        lambda part: row_half(up_ref, part),
        lambda chip, part: row_half(column_block(ups_ref, units, chip), part),
        up_sems,
    )
    ups.start()
    weights = ChipGather(
        chips,
        here,
        lambda half: row_half(down_ref, half),
        lambda chip, half: row_half(downs_ref.at[chip], half),
        weight_sems,
    )
    line.step(2)
    gather.finish()
    meta_gather.finish()
    for copy in keeps:
        copy.wait()

    block = seqs * part

    def add(t, fresh=False):
        columns = pl.ds(pl.multiple_of(t * block, 128), block)
        left = rows[:, :, columns].reshape(length, block)
        for i in range(3):
            at = pl.ds(i * span, span)
            term = jnp.dot(left, qkvs[t, :, :, at].reshape(block, span), preferred_element_type=F32)
            raw[:, at] = term if fresh else raw[:, at] + term

    add(z, True)
    for d in range(1, planes):
        if d == planes - 1:
            ups.relay()
            weights.start()
        if d > 2:
            line.step(d)
        if d == planes - 1:
            if strided:
                line_two.start()
            group = GroupGather(planes, here, grad_ref, grads_ref, grad_up, grad_down, pair)
            group.start(local.at[6])
        pl.when(z - d >= 0)(lambda d=d: add(z - d))
        pl.when(z + d < planes)(lambda d=d: add(z + d))
    outputs = [
        pltpu.make_async_copy(rows, rows_ref, local.at[7]),
        pltpu.make_async_copy(metas, metas_ref, local.at[8]),
        pltpu.make_async_copy(qkvs, qkvs_ref, local.at[9]),
    ]
    for copy in outputs:
        copy.start()

    table = RowBlocks(metas)
    for at in range(0, length, BLOCK):
        at = pl.ds(at, BLOCK)
        tables = turns(table, at)
        for two in range(heads // 2):
            query = raw[at, pl.ds(2 * HD * two, 2 * HD)]
            query = (query * tables[0] + swap_lanes(query) * tables[1]).astype(LOW)
            key = raw[at, pl.ds(span + 2 * HD * two, 2 * HD)]
            key = (key * tables[2] + swap_lanes(key) * tables[3]).astype(LOW)
            value = raw[at, pl.ds(2 * span + 2 * HD * two, 2 * HD)].astype(LOW)
            for side in range(2):
                lanes = slice(side * HD, (side + 1) * HD)
                q_ref[2 * two + side, at] = query[:, lanes]
                k_ref[2 * two + side, at] = key[:, lanes]
                v_ref[2 * two + side, at] = value[:, lanes]
    log_ref[...] = jnp.zeros(log_ref.shape, F32)

    def one_head(head, carry):
        for start in range(0, length, BLOCK):
            columns = start + BLOCK
            at = pl.ds(start, BLOCK)
            scores = lax.dot_general(
                q_ref[head, at],
                k_ref[head, pl.ds(0, columns)],
                (((1,), (1,)), ((), ())),
                preferred_element_type=F32,
            )
            allowed = allowed_block(table, start, BLOCK, columns)
            scores = jnp.where(allowed, scores, NEG_FILL)
            top = jnp.max(scores, axis=1, keepdims=True)
            shifted = jnp.exp(scores - top)
            total = jnp.sum(shifted, axis=1, keepdims=True)
            probs = (shifted * (1.0 / total)).astype(LOW)
            wide[head, at] = jnp.dot(
                probs, v_ref[head, pl.ds(0, columns)], preferred_element_type=F32
            )
            lane = lax.broadcasted_iota(jnp.int32, (BLOCK, 128), 1)
            log_ref[at] = jnp.where(lane == head, top + jnp.log(total), log_ref[at])
        return carry

    first = 0
    for d in range(1, planes):
        last = -(-heads * d // planes)
        lax.fori_loop(first, last, one_head, 0)
        first = last
        if strided:
            line_two.step(d)
        if d == 2:
            group.step(1)
    lax.fori_loop(first, heads, one_head, 0)
    lane = lax.broadcasted_iota(jnp.int32, (tokens, 128), 1)
    column = jnp.sum(outs[...].astype(F32).reshape(span, width), axis=0, keepdims=True)
    for s in range(seqs):
        at = pl.ds(s * tokens, tokens)
        low = jnp.concatenate([wide[head, at] for head in range(heads)], axis=1).astype(LOW)
        att_ref[s] = low
        value = low.astype(F32)
        total = jnp.sum(value, axis=1, keepdims=True)
        square = jnp.sum(value * value, axis=1, keepdims=True)
        both = jnp.where(lane == 0, total, jnp.where(lane == 1, square, 0.0))
        tile[s, pl.ds(0, 8)] = both.T[:8]
        for i in range(width // 128):
            tile[s, pl.ds(8 + i, 1)] = column[:, i * 128 : (i + 1) * 128]
    out_tiles = [
        remote(tile.at[2 * device[1] + device[2]], tiles_ref.at[me], tile_sems, k, device)
        for k, device in enumerate(peers, 1)
    ]
    for copy in out_tiles:
        copy.start()
    keep = pltpu.make_async_copy(tile.at[me], tiles_ref.at[me], local.at[10])
    keep.start()
    out_outs = pltpu.make_async_copy(outs, outs_ref, local.at[11])
    out_outs.start()
    weights.relay()
    work = PlaneScatter(
        chips, here, att_ref, Flat(outs, span), False, (near_out, near_in, far_out, far_in), near, far
    )
    work.start()
    for d in range(2, planes):
        group.step(d)
    work.finish(sum_ref)
    group.finish()
    for t in range(planes):
        group.other(t)
    line.finish()
    if strided:
        line_two.finish()
    for copy in swaps:
        copy.wait_send()
    ups.finish()
    weights.finish()
    for copy in [keep, out_outs, *outputs]:
        copy.wait()
    for k in range(1, seqs):
        out_tiles[k - 1].wait_send()
        index = lax.rem(me + seqs - k, seqs)
        remote(tile.at[0], tiles_ref.at[index], tile_sems, k, here).wait_recv()

    def gain_wait(k, carry):
        gain_copy(k).wait_send()
        other = lax.rem(flat + count - k, count)
        remote(gain_ref, gains_ref.at[other], gain_sems, k, here).wait_recv()
        return carry

    lax.fori_loop(1, count, gain_wait, 0)


class Flat:
    def __init__(self, blocks, count):
        self.blocks, self.count = blocks, count

    def __getitem__(self, at):
        if len(self.blocks.shape) == 2:
            return self.blocks[at]
        _, columns = at
        return self.blocks[:, :, columns].reshape(self.count, columns.size)


class RowBlocks:
    def __init__(self, blocks):
        self.blocks = blocks

    def __getitem__(self, at):
        rows, columns = at
        size = self.blocks.shape[1]
        first, count = rows.start // size, rows.size // size
        return self.blocks[pl.ds(first, count), :, columns].reshape(rows.size, columns.size)


def attention_forward(
    planes, chips, heads, strided,
    x_block, meta, weight, scale, out_rows, gain_tile, up_block, down_block, grad,
):
    seqs = 2 * chips
    tokens, width = x_block.shape
    part, wide = weight.shape[0], 3 * heads * HD
    units = up_block.shape[1]
    length = seqs * tokens
    span = heads * HD
    outs = (planes, *out_rows.shape) if strided else out_rows.shape
    tile = (seqs, 8 + width // 128, 128)
    return call(
        functools.partial(attention_forward_kernel, planes, chips, heads, strided),
        "attention_forward",
        [
            *[shape((heads, length, HD), LOW)] * 3,
            shape((seqs, tokens, span), LOW),
            shape((length, 128), F32),
            shape((tokens, width), F32),
            shape((seqs, tokens, width), LOW),
            shape((seqs, *meta.shape), F32),
            shape((planes, seqs, part, wide), LOW),
            shape(outs, LOW),
            shape((planes * seqs, *gain_tile.shape), F32),
            shape((width, chips * units) if units % 128 == 0 else (chips, width, units), LOW),
            shape((chips, *down_block.shape), LOW),
            shape((planes, 2, *grad.shape), LOW),
            shape(tile, F32),
        ],
        (x_block, meta, weight, scale, out_rows, gain_tile, up_block, down_block, grad),
        [HBM, HBM, VMEM, VMEM, HBM, HBM, HBM, HBM, HBM],
        [*[VMEM] * 6, *[HBM] * 9],
        [
            pltpu.VMEM((seqs, part, wide), LOW),
            pltpu.VMEM((seqs, tokens, width), LOW),
            pltpu.VMEM((seqs, *meta.shape), F32),
            pltpu.VMEM((planes, seqs, part, wide), LOW),
            pltpu.VMEM(outs, LOW),
            pltpu.VMEM((length, 3 * span), F32),
            pltpu.VMEM((heads, length, HD), F32),
            pltpu.VMEM(tile, F32),
            *PlaneScatter.scratch(chips, tokens, width),
            *pairs_of(seqs),
            *PlaneGather.sems(chips),
            *PlaneGather.sems(chips),
            *pairs_of(*[2 * planes] * 2, *[planes] * 2, planes * seqs, ChipGather.count(chips)),
            *PlaneScatter.sems(chips, width),
            *pairs_of(seqs),
            *GroupGather.sems(planes),
            *pairs_of(ChipGather.count(chips)),
            pltpu.SemaphoreType.DMA((13,)),
        ],
        1,
    )


def attention_backward_kernel(
    planes, chips, heads, strided,
    x_ref, stat_ref, tile_ref, left_ref, right_ref,
    q_in, k_in, v_in, att_in, out_in, log_in, meta_in, up_ref, down_ref, _,
    tiles_ref, ffn_ref, out_ref, total_ref, slots_ref, down_slots_ref,
    rows, stats, left, right, q_ref, k_ref, v_ref, att_ref, outs, log_ref, meta_ref,
    near_out, near_own, near_sums, grad, dq, dk, dv, normed_all, own, sums, *sems,
):
    here = place()
    z, c, core = here
    seqs = 2 * chips
    count = planes * seqs
    me = 2 * c + core
    flat = z * seqs + me
    x_far, x_near, s_far, s_near, tile_sems, near, up, down, up_two, down_two, swap_sems = [
        sems[2 * i : 2 * i + 2] for i in range(11)
    ]
    down_sems = sems[22:24]
    local = sems[24]
    pairs = [
        (left_ref, left), (right_ref, right), (att_in, att_ref), (out_in, outs), (meta_in, meta_ref),
        (q_in, q_ref), (k_in, k_ref), (v_in, v_ref), (log_in, log_ref),
    ]
    loads = [pltpu.make_async_copy(*pair, local.at[i]) for i, pair in enumerate(pairs)]
    for copy in loads:
        copy.start()
    barrier = pltpu.get_barrier_semaphore()

    def device_of(k):
        other = lax.rem(flat + k, count)
        return (other // seqs, lax.rem(other, seqs) // 2, lax.rem(other, 2))

    def signal(k, carry):
        greet(barrier, [device_of(k)])
        return carry

    lax.fori_loop(1, count, signal, 0)
    pl.semaphore_wait(barrier, count - 1)
    gather = PlaneGather(chips, here, x_ref, rows, x_far, x_near)
    stat_gather = PlaneGather(chips, here, stat_ref, stats, s_far, s_near)
    gather.start()
    stat_gather.start()
    keeps = [
        pltpu.make_async_copy(x_ref, rows.at[me], local.at[9]),
        pltpu.make_async_copy(stat_ref, stats.at[me], local.at[10]),
        pltpu.make_async_copy(tile_ref.at[flat], tiles_ref.at[flat], local.at[11]),
    ]
    for copy in keeps:
        copy.start()

    def tile_copy(k):
        other = lax.rem(flat + k, count)
        return remote(tile_ref.at[other], tiles_ref.at[flat], tile_sems, k, device_of(k))

    def tile_start(k, carry):
        tile_copy(k).start()
        return carry

    lax.fori_loop(1, count, tile_start, 0)
    tokens, width = x_ref.shape
    for copy in loads[:2]:
        copy.wait()
    work = PairScatter(
        planes, here, Halves(left, tokens), right, False, (near_out, near_own, near_sums),
        near, up, down,
    )
    work.start()
    left_turns = list(range(1, work.line.steps))

    def turn(until=None):
        step = left_turns[0] + 1 if until is None and left_turns else until
        while left_turns and left_turns[0] < step:
            work.line.step(left_turns.pop(0))

    turn()
    gather.relay()
    stat_gather.relay()
    turn()
    gather.forward()
    stat_gather.forward()
    gather.finish()
    stat_gather.finish()
    units = slots_ref.shape[2]
    upper, lower = share(width, 0, UP_FIRST), share(down_ref.shape[1], 1, DOWN_FIRST)
    swaps = [
        ChipSwap(
            chips,
            here,
            lambda index: half_block(up_ref, units, index, 0),
            lambda index: slots_ref.at[index, upper],
            swap_sems,
        ),
        ChipSwap(
            chips,
            here,
            lambda index: down_ref.at[index, lower],
            lambda index: down_slots_ref.at[index, lower],
            down_sems,
        ),
    ]
    for i, swap in enumerate(swaps):
        swap.start(local.at[12 + i])
    for copy in [*loads[2:], *keeps]:
        copy.wait()
    turn()
    length, span = att_ref.shape
    part = own.shape[1]
    per = BLOCK // tokens
    for first in range(0, seqs, per):
        at = pl.ds(first * tokens, BLOCK)
        figures = stats[pl.ds(first, per)].reshape(BLOCK, 128)
        mean, scaler, one, two = (figures[:, i : i + 1] for i in range(4))
        block = rows[pl.ds(first, per)].reshape(BLOCK, width)
        d_sub = product(block, outs, slice(None), True)
        normed = (att_ref[at].astype(F32) - mean) * scaler
        normed_all[at] = normed.astype(LOW)
        d_att = (scaler * (d_sub - one - normed * two)).astype(LOW)
        for head in range(heads):
            grad[head, at] = d_att[:, head * HD : (head + 1) * HD]
    for at in range(0, width, COLUMNS):
        columns = pl.ds(at, COLUMNS)
        term = token_product(normed_all[...], rows[:, :, columns].reshape(length, COLUMNS)).astype(LOW)
        for t in range(planes):
            own[t, :, columns] = term[t * part : (t + 1) * part]
    line = LineScatter(
        planes,
        here,
        1,
        lambda p: (slice(None),),
        lambda p: [(row,) for row in row_tiles(part, 16)],
        lambda t, tile: own[(t, *tile)].astype(F32),
        sums,
        up_two,
        down_two,
    )
    if strided:
        line.step(0)
    dk[...] = jnp.zeros(dk.shape, F32)
    dv[...] = jnp.zeros(dv.shape, F32)

    def one_head(head, carry):
        for start in range(0, length, BLOCK):
            columns = start + BLOCK
            at = pl.ds(start, BLOCK)
            keys = pl.ds(0, columns)
            query, key = q_ref[head, at], k_ref[head, keys]
            out_grad = grad[head, at]
            scores = lax.dot_general(
                query, key, (((1,), (1,)), ((), ())), preferred_element_type=F32
            )
            allowed = allowed_block(meta_ref, start, BLOCK, columns)
            lane = lax.broadcasted_iota(jnp.int32, (BLOCK, 128), 1)
            log_total = jnp.sum(jnp.where(lane == head, log_ref[at], 0.0), axis=1, keepdims=True)
            probs = jnp.where(allowed, jnp.exp(scores - log_total), 0.0)
            d_probs = lax.dot_general(
                out_grad, v_ref[head, keys], (((1,), (1,)), ((), ())), preferred_element_type=F32
            )
            delta = jnp.sum(probs * d_probs, axis=1, keepdims=True)
            d_scores = (probs * (d_probs - delta)).astype(LOW)
            dq[head, at] = jnp.dot(d_scores, key, preferred_element_type=F32)
            dk[head, keys] += token_product(d_scores, query)
            dv[head, keys] += token_product(probs.astype(LOW), out_grad)
        return carry

    first = 0
    for i in range(1, planes - 1):
        last = -(-heads * i // (planes - 1))
        lax.fori_loop(first, last, one_head, 0)
        first = last
        turn()
        if strided:
            line.step(i)
    lax.fori_loop(first, heads, one_head, 0)
    turn(work.line.steps)
    for start in range(0, length, BLOCK):
        at = pl.ds(start, BLOCK)
        tables = turns(meta_ref, at)
        for two in range(heads // 2):
            both = [
                jnp.concatenate([whole[2 * two, at], whole[2 * two + 1, at]], axis=1).astype(LOW)
                for whole in (dq, dk, dv)
            ]
            query, key = both[0].astype(F32), both[1].astype(F32)
            query = query * tables[0] + swap_lanes(query * tables[1])
            key = key * tables[2] + swap_lanes(key * tables[3])
            out_ref[at, pl.ds(2 * HD * two, 2 * HD)] = query.astype(LOW)
            out_ref[at, pl.ds(span + 2 * HD * two, 2 * HD)] = key.astype(LOW)
            out_ref[at, pl.ds(2 * span + 2 * HD * two, 2 * HD)] = both[2]
    work.finish(ffn_ref)
    if strided:

        def store(tile, total):
            total_ref[tile] = total

        line.finish(store)
    else:
        for t in range(planes):
            total_ref[pl.ds(t * part, part)] = own[t].astype(F32)
    for swap in swaps:
        swap.finish()

    def tile_wait(k, carry):
        tile_copy(k).wait_send()
        other = lax.rem(flat + count - k, count)
        remote(tile_ref.at[0], tiles_ref.at[other], tile_sems, k, here).wait_recv()
        return carry

    lax.fori_loop(1, count, tile_wait, 0)


def attention_backward(planes, chips, heads, strided, part, units, args):
    tokens, width = args[0].shape
    seqs = 2 * chips
    length, span = args[8].shape
    kept = [pltpu.VMEM(args[i].shape, args[i].dtype) for i in (3, 4, 5, 6, 7, 8, 9, 10, 11)]
    return call(
        functools.partial(attention_backward_kernel, planes, chips, heads, strided),
        "attention_backward",
        [
            shape(args[2].shape, F32),
            shape((tokens, width), F32),
            shape((length, 3 * span), LOW),
            shape((part if strided else span, width), F32),
            shape((chips, width, units), LOW),
            shape(args[14].shape, LOW),
        ],
        args,
        [HBM] * 15,
        [HBM, VMEM, VMEM, VMEM, HBM, HBM],
        [
            pltpu.VMEM((seqs, tokens, width), LOW),
            pltpu.VMEM((seqs, tokens, 128), F32),
            *kept,
            *PairScatter.scratch(planes, tokens, width),
            pltpu.VMEM((heads, length, HD), LOW),
            *[pltpu.VMEM((heads, length, HD), F32)] * 3,
            pltpu.VMEM((length, span), LOW),
            pltpu.VMEM((planes, part, width), LOW),
            pltpu.VMEM((planes + 1, part, width), LOW),
            *PlaneGather.sems(chips),
            *PlaneGather.sems(chips),
            *pairs_of(planes * seqs),
            *PairScatter.sems(planes, width),
            *pairs_of(planes, planes, chips, chips),
            pltpu.SemaphoreType.DMA((14,)),
        ],
        2,
        {14: 5},
    )


def body(
    hidden_in,
    segment_ids,
    position_ids,
    w_qkv,
    w_out,
    w_up,
    w_down,
    gain_attn,
    gain_attn_sub,
    gain_ffn,
    gain_ffn_sub,
    ema_qkv,
    ema_out,
    ema_up,
    ema_down,
    ema_gain_attn,
    ema_gain_attn_sub,
    ema_gain_ffn,
    ema_gain_ffn_sub,
    out_grad,
):
    _, tokens, width = hidden_in.shape
    planes, chips = lax.axis_size("dp"), lax.axis_size("chip")
    seqs = 2 * chips
    length = tokens * seqs
    heads = HEADS // seqs
    span = heads * HD
    part = w_qkv.shape[0]
    strided = part % HD == 0
    width_ff = w_down.shape[0] * planes * seqs
    seq_index = lax.axis_index(SEQ)

    def gain_rows(weight, gain):
        return (weight.astype(F32) * gain.astype(F32)[:, None]).astype(LOW)

    out_scaled = gain_rows(w_out, gain_attn_sub)
    down_scaled = gain_rows(w_down, gain_ffn_sub)
    x_in = hidden_in[0].astype(F32)
    normed_one, scaler_one = moments(x_in)
    normed_low = normed_one.astype(LOW)
    qkv_gain = jnp.broadcast_to(gain_attn.astype(F32)[:, None], (part, 128))
    gain_tile = jnp.zeros((8, 128), F32).at[0, :part].set(gain_ffn.astype(F32))

    if not strided:
        out_all = lax.all_gather(out_scaled, ALL, axis=0, tiled=True)
        out_scaled = lax.dynamic_slice_in_dim(out_all, seq_index * span, span, axis=0)

    grad_low = out_grad[0]
    (
        queries, keys, values, attended, log_total, out_sum,
        row_in, meta, qkv_mine, out_mine, gain_tiles, up_mine, down_mine, grad_flat, tiles,
    ) = attention_forward(
        planes,
        chips,
        heads,
        strided,
        normed_low,
        token_tables(position_ids[0]),
        w_qkv,
        qkv_gain,
        out_scaled,
        gain_tile,
        w_up,
        down_scaled,
        grad_low,
    )
    if up_mine.ndim == 3:
        up_mine = up_mine.transpose(1, 0, 2).reshape(width, -1)
    row_in = row_in.reshape(length, width)
    meta = meta.reshape(length, -1)
    qkv_mine = qkv_mine.reshape(width, 3 * span)
    out_mine = out_mine.reshape(span, width)
    attended = attended.reshape(length, span)
    tiles = jnp.sum(tiles, axis=0)
    column_sum = tiles[8:].reshape(width)
    sums = tiles[:2].T
    gain_three = gain_tiles[:, 0, :part].reshape(width)
    mean_two = sums[:, :1] / width
    scaler_two = lax.rsqrt(sums[:, 1:] / width - mean_two * mean_two + NORM_EPS)
    projected = scaler_two * (out_sum - mean_two * column_sum[None, :])
    hmid = x_in + projected
    normed_three, scaler_three = moments(hmid)
    ffn_in = (normed_three * gain_three).astype(LOW)

    grad_top = grad_low.astype(F32)
    units = w_up.shape[1]
    d_ffn_in, normed_four, grad_up, grad_down, down_slots = feed_forward(
        planes, chips, width_ff, ffn_in, up_mine, grad_flat, down_mine
    )
    down_mine = down_mine.reshape(-1, width)
    if units % 128:
        grad_up = grad_up.reshape(width, chips, units).transpose(1, 0, 2)

    gain_part = jnp.sum(d_ffn_in * normed_three, axis=0).reshape(planes * seqs, 1, part)
    gain_part = jnp.pad(gain_part, ((0, 0), (0, 7), (0, 128 - part)))
    d_hmid = grad_top + norm_back(d_ffn_in * gain_three, normed_three, scaler_three)
    d_hmid_low = d_hmid.astype(LOW)
    d_hmid_wide = d_hmid_low.astype(F32)
    first_two = jnp.sum(d_hmid_wide * column_sum[None, :], axis=1, keepdims=True) / width
    second_two = jnp.sum(d_hmid_wide * projected, axis=1, keepdims=True) / width
    token_stats = jnp.concatenate([mean_two, scaler_two, first_two, second_two], axis=1)
    gain_part, ffn_out, d_qkv, sum_out, up_slots, down_slots = attention_backward(
        planes,
        chips,
        heads,
        strided,
        part,
        units,
        (
            d_hmid_low,
            jnp.pad(token_stats, ((0, 0), (0, 124))),
            gain_part,
            normed_four,
            down_mine,
            queries,
            keys,
            values,
            attended,
            out_mine,
            log_total,
            meta,
            grad_up,
            grad_down,
            down_slots,
        ),
    )
    output = (hmid + ffn_out).astype(LOW)[None]
    grad_gain_three = jnp.sum(gain_part, axis=0)[0, :part]
    d_in, sum_qkv, grad_gain_one, up_slots = in_scatter(
        planes,
        chips,
        heads,
        strided,
        d_qkv.reshape(seqs, tokens, 3 * span),
        qkv_mine,
        row_in,
        grad_up,
        w_qkv,
        qkv_gain,
        up_slots,
    )
    grad_gain_one = grad_gain_one[:, 0]
    sum_up = jnp.sum(up_slots.astype(F32), axis=0)
    sum_down = jnp.sum(down_slots.astype(F32), axis=0)
    input_grad = (d_hmid + norm_back(d_in, normed_one, scaler_one)).astype(LOW)[None]

    if not strided:
        spread = lax.dynamic_update_slice_in_dim(
            jnp.zeros((width, width), LOW), sum_out.astype(LOW), seq_index * span, axis=0
        )
        sum_out = lax.psum_scatter(spread, ALL, scatter_dimension=0, tiled=True).astype(F32)

    def finish(total, weight, gain):
        wide = weight.astype(F32)
        return (total * gain.astype(F32)[:, None], jnp.sum(total * wide, axis=1))

    sum_out, grad_gain_two = finish(sum_out, w_out, gain_attn_sub)
    sum_down, grad_gain_four = finish(sum_down, w_down, gain_ffn_sub)

    def averaged(average, weight):
        return EMA_DECAY * average + (1.0 - EMA_DECAY) * weight.astype(F32)

    return (
        output,
        input_grad,
        sum_qkv,
        sum_out,
        sum_up,
        sum_down,
        grad_gain_one,
        grad_gain_two,
        grad_gain_three,
        grad_gain_four,
        averaged(ema_qkv, w_qkv),
        averaged(ema_out, w_out),
        averaged(ema_up, w_up),
        averaged(ema_down, w_down),
        averaged(ema_gain_attn, gain_attn),
        averaged(ema_gain_attn_sub, gain_attn_sub),
        averaged(ema_gain_ffn, gain_ffn),
        averaged(ema_gain_ffn_sub, gain_ffn_sub),
    )


def solution(mesh):
    split = Mesh(
        mesh.devices.reshape(mesh.shape["dp"], mesh.shape["seq"] // 2, 2), ("dp", "chip", "core")
    )
    tokens = P("dp", SEQ, None)
    ids = P("dp", SEQ)
    rows = P(ALL, None)
    columns = P(None, ALL)
    vector = P(ALL)
    weights = (rows, rows, columns, rows)
    gains = (vector,) * 4
    return jax.shard_map(
        body,
        mesh=split,
        in_specs=(tokens, ids, ids, *weights, *gains, *weights, *gains, tokens),
        out_specs=(tokens, tokens, *weights, *gains, *weights, *gains),
        check_vma=False,
    )
```

```python
import functools
import math

import jax
import jax.numpy as jnp
from jax import lax
from jax.experimental import pallas as pl
from jax.experimental.pallas import tpu as pltpu
from jax.sharding import Mesh
from jax.sharding import PartitionSpec as P

HEADS = 32
HD = 64

NEG_FILL = -1000000000.0
NORM_EPS = 1e-05
EMA_DECAY = 0.7
LOW = jnp.bfloat16
F32 = jnp.float32
SEQ = ("chip", "core")
TP = ("dp", "core")
ALL = ("dp", "chip", "core")


def moments(values):
    mean = jnp.mean(values, axis=-1, keepdims=True)
    centered = values - mean
    scaler = lax.rsqrt(jnp.mean(centered * centered, axis=-1, keepdims=True) + NORM_EPS)
    return (centered * scaler, scaler)


def norm_back(scaled_grad, normed, scaler):
    first_mean = jnp.mean(scaled_grad, axis=-1, keepdims=True)
    second_mean = jnp.mean(scaled_grad * normed, axis=-1, keepdims=True)
    return scaler * (scaled_grad - first_mean - normed * second_mean)


def token_tables(positions):
    half_count = HD // 2
    index_half = jnp.arange(half_count).astype(F32)
    inverse = jnp.exp(-(2.0 * index_half / HD) * math.log(10000.0))
    decay_base = (2.0 * index_half + 0.4 * HD) / (1.4 * HD)
    where_at = positions.astype(F32)[:, None]
    angles = where_at * inverse[None, :]
    factor = jnp.exp(where_at / 512.0 * jnp.log(decay_base)[None, :])
    sign_row = jnp.where(jnp.arange(HD) % 2 == 0, -1.0, 1.0).astype(F32)
    cosine = jnp.repeat(jnp.cos(angles), 2, axis=1)
    sine = jnp.repeat(jnp.sin(angles), 2, axis=1) * sign_row[None, :]
    factor = jnp.repeat(factor, 2, axis=1)
    grow = factor * HD ** (-0.5)
    where_block = jnp.broadcast_to(where_at, (positions.shape[0], HD))
    return jnp.concatenate(
        [cosine * grow, sine * grow, HD**0.5 / (factor * factor), where_block], axis=1
    )


def dot(left_op, right_op):
    return jnp.dot(left_op, right_op, preferred_element_type=F32)


def rows_product(operand, weight_rows):
    return lax.dot_general(
        operand, weight_rows, (((1,), (1,)), ((), ())), preferred_element_type=F32
    )


def token_product(left_op, right_op):
    return lax.dot_general(left_op, right_op, (((0,), (0,)), ((), ())), preferred_element_type=F32)


MESH = pl.DeviceIdType.MESH
HBM = pl.BlockSpec(memory_space=pl.ANY)
VMEM = pl.BlockSpec(memory_space=pltpu.VMEM)
VMEM_BYTES = 60 * 1024 * 1024


def shape(dims, kind):
    return jax.ShapeDtypeStruct(dims, kind)


def pairs_of(*counts):
    return [pltpu.SemaphoreType.DMA((count,)) for count in counts for _ in range(2)]


def call(kernel, name, outs, args, in_specs, out_specs, scratch, collective=None, aliases=None):
    return pl.pallas_call(
        kernel,
        input_output_aliases=aliases or {},
        name=name,
        out_shape=outs,
        in_specs=in_specs,
        out_specs=out_specs,
        scratch_shapes=scratch,
        compiler_params=pltpu.CompilerParams(
            collective_id=collective,
            has_side_effects=collective is not None,
            vmem_limit_bytes=VMEM_BYTES,
        ),
    )(*args)


def place():
    return (lax.axis_index("dp"), lax.axis_index("chip"), lax.axis_index("core"))


def remote(source, target, sems, index, device):
    return pltpu.make_async_remote_copy(
        src_ref=source,
        dst_ref=target,
        send_sem=sems[0].at[index],
        recv_sem=sems[1].at[index],
        device_id=device,
        device_id_type=MESH,
    )


def greet(barrier, devices):
    for device in devices:
        pl.semaphore_signal(barrier, inc=1, device_id=device, device_id_type=MESH)


def greet_line(barrier, planes, here):
    z, c, core = here

    @pl.when(z < planes - 1)
    def _():
        greet(barrier, [(z + 1, c, core)])

    @pl.when(z > 0)
    def _():
        greet(barrier, [(z - 1, c, core)])


def line_peers(planes, here):
    z = here[0]
    return (2 * planes - 2 - z) // planes + (z + planes - 1) // planes


def chip_peers(chips, here):
    z, c, core = here
    return [(z, lax.rem(c + k, chips), core) for k in range(1, chips)]


def plane_peers(chips, here):
    z, c, core = here
    seqs = 2 * chips
    me = 2 * c + core
    ids = [lax.rem(me + k, seqs) for k in range(1, seqs)]
    return [(z, index // 2, lax.rem(index, 2)) for index in ids]


def column_block(whole, units, index):
    if len(whole.shape) == 3:
        return whole.at[index]
    return whole.at[:, pl.ds(pl.multiple_of(index * units, 128), units)]


UP_FIRST = 3
DOWN_FIRST = 5


def share(rows, second, eighths):
    first = rows * eighths // 128 * 16
    return pl.ds(first, rows - first) if second else pl.ds(0, first)


def half_block(whole, units, index, second):
    at = share(whole.shape[-2], second, UP_FIRST)
    if len(whole.shape) == 3:
        return whole.at[index, at]
    return whole.at[at, pl.ds(pl.multiple_of(index * units, 128), units)]


class ChipSwap:
    def __init__(self, chips, here, source, slot, sems):
        z, c, core = here
        self.sends = [
            remote(source(device[1]), slot(c), sems, k, device)
            for k, device in enumerate(chip_peers(chips, here), 1)
        ]
        self.waits = [
            remote(source(c), slot(lax.rem(c + chips - k, chips)), sems, k, here)
            for k in range(1, chips)
        ]
        self.keep = (source(c), slot(c))

    def start(self, local):
        for copy in self.sends:
            copy.start()
        self.held = pltpu.make_async_copy(*self.keep, local)
        self.held.start()

    def finish(self):
        self.held.wait()
        for send, wait in zip(self.sends, self.waits):
            send.wait_send()
            wait.wait_recv()


class ChipGather:
    def __init__(self, chips, here, source, target, sems):
        z, c, core = here
        self.here, self.sems, self.relayed = here, sems, chips == 4
        if not self.relayed:
            self.sends = [
                remote(source(None), target(c, None), sems, k, device)
                for k, device in enumerate(chip_peers(chips, here), 1)
            ]
            self.arrivals = [
                (lax.rem(c + chips - k, chips), None, k) for k in range(1, chips)
            ]
        else:
            beside = c + 1 - 2 * lax.rem(c, 2)
            above = c + 2 - 4 * (c // 2)
            to_beside, to_above = (z, beside, core), (z, above, core)
            self.sends = [
                remote(source(0), target(c, 0), sems, 0, to_beside),
                remote(source(1), target(c, 1), sems, 3, to_above),
                remote(source(1), target(c, 1), sems, 1, to_beside),
                remote(source(0), target(c, 0), sems, 2, to_above),
            ]
            self.relays = [
                remote(target(beside, 0), target(beside, 0), sems, 4, to_above),
                remote(target(above, 1), target(above, 1), sems, 5, to_beside),
            ]
            self.arrivals = [
                (beside, 0, 0), (above, 1, 3), (beside, 1, 1), (above, 0, 2),
                (3 - c, 0, 4), (3 - c, 1, 5),
            ]
        self.target = target

    def start(self):
        for copy in self.sends:
            copy.start()

    def arrive(self, i):
        chip, half, index = self.arrivals[i]
        block = self.target(chip, half)
        remote(block, block, self.sems, index, self.here).wait_recv()
        if self.relayed and i < 2:
            self.relays[i].start()

    def relay(self):
        for i in range(2 if self.relayed else 0):
            self.arrive(i)

    def rest(self):
        return range(2 if self.relayed else 0, len(self.arrivals))

    def finish(self):
        for i in self.rest():
            self.arrive(i)
        self.sent()

    def sent(self):
        for copy in [*self.sends, *(self.relays if self.relayed else [])]:
            copy.wait_send()

    @staticmethod
    def count(chips):
        return max(chips, 6)


class PlaneGather:
    def __init__(self, chips, here, block, out, far, near):
        z, c, core = here
        self.here, self.block, self.out, self.near = here, block, out, near
        self.me = 2 * c + core
        self.partner = (z, c, 1 - core)
        self.size = block.shape[0] // 2
        self.chips = ChipGather(
            chips,
            here,
            self.piece,
            lambda chip, half: self.place(2 * chip + core, half),
            far,
        )
        self.own = remote(block, out.at[self.me], near, len(self.chips.arrivals), self.partner)

    def rows(self, half):
        return pl.ds(half * self.size, self.size)

    def piece(self, half):
        return self.block if half is None else self.block.at[self.rows(half)]

    def place(self, index, half):
        return self.out.at[index] if half is None else self.out.at[index, self.rows(half)]

    def start(self):
        self.chips.start()
        self.own.start()

    def passed(self, i, other=0):
        chip, half, _ = self.chips.arrivals[i]
        core = self.here[2]
        block = self.place(2 * chip + (1 - core if other else core), half)
        return remote(block, block, self.near, i, self.partner)

    def relay(self):
        for i in range(2 if self.chips.relayed else 0):
            self.chips.arrive(i)
            self.passed(i).start()

    def forward(self):
        for i in self.chips.rest():
            self.chips.arrive(i)
            self.passed(i).start()

    def finish(self):
        self.chips.sent()
        self.own.wait_send()
        mine = self.out.at[2 * self.here[1] + 1 - self.here[2]]
        remote(mine, mine, self.near, len(self.chips.arrivals), self.partner).wait_recv()
        for i in range(len(self.chips.arrivals)):
            self.passed(i).wait_send()
            self.passed(i, 1).wait_recv()

    @staticmethod
    def sems(chips):
        return pairs_of(ChipGather.count(chips), ChipGather.count(chips) + 1)


def row_half(ref, half):
    if half is None:
        return ref
    size = ref.shape[0] // 2
    return ref.at[pl.ds(half * size, size)]


class LineGather:
    def __init__(self, planes, here, parts, up, down):
        self.planes, self.here, self.parts = planes, here, parts
        self.up, self.down = up, down
        self.count = len(parts(here[0]))

    def upward(self, d, p):
        z, c, core = self.here
        block = self.parts(z - d)[p]
        return remote(block, block, self.up, d * self.count + p, (z + 1, c, core))

    def downward(self, d, p):
        z, c, core = self.here
        block = self.parts(z + d)[p]
        return remote(block, block, self.down, d * self.count + p, (z - 1, c, core))

    def each(self, d, p, act):
        z, planes = self.here[0], self.planes
        pl.when((z < planes - 1) & (z - d >= 0))(lambda: act(self.upward(d, p)))
        pl.when((z > 0) & (z + d < planes))(lambda: act(self.downward(d, p)))

    def start(self):
        for p in range(self.count):
            self.each(0, p, lambda copy: copy.start())

    def step(self, d, arrived=None):
        z, planes = self.here[0], self.planes

        def below(p):
            block = self.parts(z - d)[p]
            remote(block, block, self.up, (d - 1) * self.count + p, self.here).wait_recv()
            if d < planes - 1:
                pl.when(z < planes - 1)(lambda: self.upward(d, p).start())
            if arrived is not None:
                arrived(z - d, p)

        def above(p):
            block = self.parts(z + d)[p]
            remote(block, block, self.down, (d - 1) * self.count + p, self.here).wait_recv()
            if d < planes - 1:
                pl.when(z > 0)(lambda: self.downward(d, p).start())
            if arrived is not None:
                arrived(z + d, p)

        for p in range(self.count):
            pl.when(z - d >= 0)(lambda p=p: below(p))
            pl.when(z + d < planes)(lambda p=p: above(p))

    def finish(self):
        for d in range(self.planes - 1):
            for p in range(self.count):
                self.each(d, p, lambda copy: copy.wait_send())


class GroupGather:
    PARTS = 2

    def __init__(self, planes, here, block, out, up, down, near):
        self.planes, self.here, self.block, self.out, self.near = planes, here, block, out, near
        self.partner = (here[0], here[1], 1 - here[2])
        size = block.shape[0] // self.PARTS
        self.slices = [pl.ds(p * size, size) for p in range(self.PARTS)]
        core = here[2]
        self.line = LineGather(planes, here, lambda t: self.parts(t, core), up, down)

    def parts(self, t, core):
        return [self.out.at[t, core, rows] for rows in self.slices]

    def passed(self, t, p):
        block = self.parts(t, self.here[2])[p]
        return remote(block, block, self.near, t * self.PARTS + p, self.partner)

    def start(self, local):
        z, _, core = self.here
        keep = pltpu.make_async_copy(self.block, self.out.at[z, core], local)
        keep.start()
        keep.wait()
        self.line.start()
        for p in range(self.PARTS):
            self.passed(z, p).start()

    def step(self, d):
        self.line.step(d, lambda t, p: self.passed(t, p).start())

    def other(self, t):
        for p in range(self.PARTS):
            block = self.parts(t, 1 - self.here[2])[p]
            remote(block, block, self.near, t * self.PARTS + p, self.partner).wait_recv()

    def finish(self):
        self.line.finish()
        for t in range(self.planes):
            for p in range(self.PARTS):
                self.passed(t, p).wait_send()

    @classmethod
    def sems(cls, planes):
        return pairs_of(*[planes * cls.PARTS] * 3)


COLUMNS = 512


def product(left, right, columns, turned):
    if turned:
        return lax.dot_general(
            left, right[columns, :], (((1,), (1,)), ((), ())), preferred_element_type=F32
        )
    return jnp.dot(left, right[:, columns], preferred_element_type=F32)


class PlaneScatter:
    def __init__(self, chips, here, left, right, turned, buffers, near, far):
        self.chips, self.here = chips, here
        self.left, self.right, self.turned = left, right, turned
        self.near_out, self.near_in, self.far_out, self.far_in = buffers
        self.near, self.far = near, far
        self.tokens, width = self.near_out.shape[1:]
        self.tiles = [pl.ds(at, COLUMNS) for at in range(0, width, COLUMNS)]
        self.order = [*range(1, chips), 0]

    def target(self, k):
        return lax.rem(self.here[1] + k, self.chips)

    def near_copy(self, i):
        z, c, core = self.here
        at = (slice(None), slice(None), self.tiles[i])
        return remote(self.near_out.at[at], self.near_in.at[at], self.near, i, (z, c, 1 - core))

    def far_copy(self, k, i):
        z, _, core = self.here
        at = (k, slice(None), self.tiles[i])
        index = k * len(self.tiles) + i
        return remote(
            self.far_out.at[at], self.far_in.at[at], self.far, index, (z, self.target(k), core)
        )

    def rows(self, position):
        return slice(position * self.tokens, (position + 1) * self.tokens)

    def start(self):
        core = self.here[2]
        blocks = [self.left[2 * self.target(k) + 1 - core] for k in self.order]
        left = jnp.concatenate(blocks, axis=0)
        for i, columns in enumerate(self.tiles):
            part = product(left, self.right, columns, self.turned).astype(LOW)
            for position, k in enumerate(self.order):
                self.near_out[k, :, columns] = part[self.rows(position)]
            self.near_copy(i).start()
        blocks = [self.left[2 * self.target(k) + core] for k in self.order]
        left = jnp.concatenate(blocks, axis=0)
        for i, columns in enumerate(self.tiles):
            part = product(left, self.right, columns, self.turned)
            self.near_copy(i).wait_recv()
            for position, k in enumerate(self.order):
                self.far_out[k, :, columns] = (
                    part[self.rows(position)] + self.near_in[k, :, columns].astype(F32)
                ).astype(LOW)
                if k:
                    self.far_copy(k, i).start()

    def finish(self, out_ref):
        for i, columns in enumerate(self.tiles):
            total = self.far_out[0, :, columns].astype(F32)
            for k in range(1, self.chips):
                self.far_copy(k, i).wait_recv()
                total = total + self.far_in[k, :, columns].astype(F32)
            out_ref[:, columns] = total
        for i in range(len(self.tiles)):
            self.near_copy(i).wait_send()
            for k in range(1, self.chips):
                self.far_copy(k, i).wait_send()

    @staticmethod
    def scratch(chips, tokens, width):
        return [pltpu.VMEM((chips, tokens, width), LOW)] * 4

    @staticmethod
    def sems(chips, width):
        return pairs_of(width // COLUMNS, chips * (width // COLUMNS))


class LineScatter:
    def __init__(self, planes, here, count, part, tiles, own, slots, up, down):
        self.planes, self.here, self.count = planes, here, count
        self.part, self.tiles, self.own, self.slots = part, tiles, own, slots
        self.up, self.down = up, down
        self.steps = (planes - 1) * count

    def upward(self, t, p):
        z, c, core = self.here
        block = self.slots.at[(t, *self.part(p))]
        return remote(block, block, self.up, t * self.count + p, (z + 1, c, core))

    def downward(self, t, p, last):
        z, c, core = self.here
        block = self.slots.at[(t, *self.part(p))]
        target = self.slots.at[(self.planes, *self.part(p))] if last else block
        return remote(block, target, self.down, t * self.count + p, (z - 1, c, core))

    def add(self, t, p, fresh):
        for tile in self.tiles(p):
            total = self.own(t, tile)
            if not fresh:
                total = total + self.slots[(t, *tile)].astype(F32)
            self.slots[(t, *tile)] = total.astype(LOW)

    def step(self, i):
        z, planes, count = self.here[0], self.planes, self.count
        rise, fall = i - z, i - (planes - 1 - z)

        @pl.when((rise >= 0) & (rise < (planes - 1 - z) * count))
        def _():
            t, p = planes - 1 - rise // count, lax.rem(rise, count)

            @pl.when(z > 0)
            def _():
                self.upward(t, p).wait_recv()
                self.add(t, p, False)

            @pl.when(z == 0)
            def _():
                self.add(t, p, True)

            self.upward(t, p).start()

        @pl.when((fall >= 0) & (fall < z * count))
        def _():
            t, p = fall // count, lax.rem(fall, count)

            @pl.when(z < planes - 1)
            def _():
                self.downward(t, p, False).wait_recv()
                self.add(t, p, False)

            @pl.when(z == planes - 1)
            def _():
                self.add(t, p, True)

            pl.when(t == z - 1)(lambda: self.downward(t, p, True).start())
            pl.when(t < z - 1)(lambda: self.downward(t, p, False).start())

    def finish(self, store, after=None):
        z, planes = self.here[0], self.planes

        def total(tile, *slots):
            value = self.own(z, tile)
            for slot in slots:
                value = value + self.slots[(slot, *tile)].astype(F32)
            store(tile, value)

        for p in range(self.count):
            tiles = self.tiles(p)

            @pl.when(z > 0)
            def _(p=p):
                self.upward(z, p).wait_recv()

            @pl.when(z < planes - 1)
            def _(p=p):
                self.downward(z, p, True).wait_recv()

            @pl.when((z > 0) & (z < planes - 1))
            def _(tiles=tiles):
                for tile in tiles:
                    total(tile, z, planes)

            @pl.when(z == 0)
            def _(tiles=tiles):
                for tile in tiles:
                    total(tile, planes)

            @pl.when(z == planes - 1)
            def _(tiles=tiles):
                for tile in tiles:
                    total(tile, z)

            if after is not None:
                after(p)

        for t in range(planes):
            for p in range(self.count):
                pl.when(z < t)(lambda t=t, p=p: self.upward(t, p).wait_send())
                pl.when(z > t)(lambda t=t, p=p: self.downward(t, p, False).wait_send())


def row_tiles(count, size):
    return [pl.ds(at, size) for at in range(0, count, size)]


def in_scatter_kernel(
    planes, chips, heads, strided, left_in, right_in, rows_in, up_ref, weight_ref, gain_ref, _,
    out_ref, total_ref, gains_ref, slots_ref,
    left_ref, right_ref, rows_ref, grad_ref,
    near_out, near_in, far_out, far_in, sums, mine, parts, *sems,
):
    here = place()
    z, c, core = here
    seqs = 2 * chips
    me = 2 * c + core
    near, far, up, down, swap_sems, chip_sems = [sems[2 * i : 2 * i + 2] for i in range(6)]
    local = sems[12]
    loads = [
        pltpu.make_async_copy(rows_in, rows_ref, local.at[1]),
        pltpu.make_async_copy(left_in, left_ref, local.at[2]),
        pltpu.make_async_copy(right_in, right_ref, local.at[3]),
    ]
    for copy in loads:
        copy.start()
    barrier = pltpu.get_barrier_semaphore()
    peers = plane_peers(chips, here)
    greet(barrier, peers)
    greet_line(barrier, planes, here)
    pl.semaphore_wait(barrier, len(peers) + line_peers(planes, here))
    units = slots_ref.shape[2]
    lower = share(slots_ref.shape[1], 1, UP_FIRST)
    ups = ChipSwap(
        chips,
        here,
        lambda index: half_block(up_ref, units, index, 1),
        lambda index: slots_ref.at[index, lower],
        chip_sems,
    )
    ups.start(local.at[0])
    half = seqs // 2
    line = LineScatter(
        planes,
        here,
        2,
        lambda p: (pl.ds(p * half, half),),
        lambda p: [(pl.ds(p * half + i, 1),) for i in range(half)],
        lambda t, tile: grad_ref[(t, *tile)].astype(F32),
        sums,
        up,
        down,
    )
    part = grad_ref.shape[2]
    span = heads * HD
    block = seqs * part
    length = rows_ref.shape[0]
    for copy in loads:
        copy.wait()

    def grads(t):
        left = rows_ref[:, t * block : (t + 1) * block]
        for i in range(3):
            at = pl.ds(i * span, span)
            term = token_product(left, left_ref[:, :, at].reshape(length, span))
            grad_ref[t, :, :, at] = term.astype(LOW).reshape(seqs, part, span)

    order = []
    for i in range((planes + 1) // 2):
        order += [planes - 1 - i, i] if planes - 1 - i != i else [i]
    for t in order[:2]:
        grads(t)
    line.step(0)
    for t in order[2:]:
        grads(t)
    work = PlaneScatter(
        chips, here, left_ref, right_ref, True, (near_out, near_in, far_out, far_in), near, far
    )
    work.start()
    for i in range(1, line.steps):
        line.step(i)

    def store(tile, total):
        mine[tile] = total.astype(LOW)

    owners = [2 * device[1] + device[2] for device in peers]
    swaps = [
        remote(mine.at[owner], parts.at[me], swap_sems, k, device)
        for k, (owner, device) in enumerate(zip(owners, peers), 1)
    ]

    def send(p):
        for owner, copy in zip(owners, swaps):
            pl.when(owner // half == p)(copy.start)

    line.finish(store, send)
    parts[me] = mine[me]
    work.finish(out_ref)
    for k in range(1, seqs):
        swaps[k - 1].wait_send()
        index = lax.rem(me + seqs - k, seqs)
        remote(mine.at[0], parts.at[index], swap_sems, k, here).wait_recv()
    width = seqs * span
    gain = gain_ref[:, pl.ds(0, 1)]
    summed = jnp.zeros(gain.shape, F32)
    for i in range(3):
        step, pieces = (seqs * HD, planes) if strided else (width, 1)
        size = step // seqs
        for piece in range(pieces):
            at = i * span + piece * size
            columns = pl.ds(i * width + piece * step, step)
            total = jnp.concatenate(
                [parts[s, :, pl.ds(at, size)].astype(F32) for s in range(seqs)], axis=1
            )
            weight = weight_ref[:, columns].astype(F32)
            summed = summed + jnp.sum(total * weight, axis=1, keepdims=True)
            total_ref[:, columns] = total * gain
    gains_ref[...] = jnp.broadcast_to(summed, gains_ref.shape)
    ups.finish()


def in_scatter(planes, chips, heads, strided, left, right, rows, up_grads, weight, gain, slots):
    _, tokens, _ = left.shape
    width = right.shape[0]
    seqs = 2 * chips
    part, wide = weight.shape[0], left.shape[2]
    return call(
        functools.partial(in_scatter_kernel, planes, chips, heads, strided),
        "in_scatter",
        [
            shape((tokens, width), F32),
            shape(weight.shape, F32),
            shape((part, 128), F32),
            shape(slots.shape, LOW),
        ],
        (left, right, rows, up_grads, weight, gain, slots),
        [HBM, HBM, HBM, HBM, VMEM, VMEM, HBM],
        [VMEM, VMEM, VMEM, HBM],
        [
            *[pltpu.VMEM(whole.shape, LOW) for whole in (left, right, rows)],
            pltpu.VMEM((planes, seqs, part, wide), LOW),
            *PlaneScatter.scratch(chips, tokens, width),
            pltpu.VMEM((planes + 1, seqs, part, wide), LOW),
            *[pltpu.VMEM((seqs, part, wide), LOW)] * 2,
            *PlaneScatter.sems(chips, width),
            *pairs_of(2 * planes, 2 * planes, seqs, chips),
            pltpu.SemaphoreType.DMA((4,)),
        ],
        4,
        {6: 3},
    )


class PairScatter:
    PARTS = 2

    def __init__(self, planes, here, left, right, turned, buffers, near, up, down):
        self.planes, self.here = planes, here
        self.left, self.right, self.turned = left, right, turned
        self.near_out, self.own, slots = buffers
        self.near = near
        self.tokens, width = self.near_out.shape[1:]
        self.tiles = [pl.ds(at, COLUMNS) for at in range(0, width, COLUMNS)]
        size = width // self.PARTS

        def part(p):
            at = p * size if isinstance(p, int) else pl.multiple_of(p * size, 128)
            return (slice(None), pl.ds(at, size))

        self.line = LineScatter(
            planes,
            here,
            self.PARTS,
            part,
            lambda p: [(rows, part(p)[1]) for rows in row_tiles(self.tokens, 32)],
            lambda t, tile: self.own[(t, *tile)].astype(F32),
            slots,
            up,
            down,
        )

    def near_copy(self, i):
        z, c, core = self.here
        at = (slice(None), slice(None), self.tiles[i])
        return remote(self.near_out.at[at], self.own.at[at], self.near, i, (z, c, 1 - core))

    def start(self):
        core, tokens = self.here[2], self.tokens
        left = jnp.concatenate([self.left[t, 1 - core] for t in range(self.planes)], axis=0)
        for i, columns in enumerate(self.tiles):
            part = product(left, self.right, columns, self.turned).astype(LOW)
            for t in range(self.planes):
                self.near_out[t, :, columns] = part[t * tokens : (t + 1) * tokens]
            self.near_copy(i).start()
        left = jnp.concatenate([self.left[t, core] for t in range(self.planes)], axis=0)
        for i, columns in enumerate(self.tiles):
            part = product(left, self.right, columns, self.turned)
            self.near_copy(i).wait_recv()
            for t in range(self.planes):
                self.own[t, :, columns] = (
                    part[t * tokens : (t + 1) * tokens] + self.own[t, :, columns].astype(F32)
                ).astype(LOW)
        self.line.step(0)

    def finish(self, out_ref):
        def store(tile, total):
            out_ref[tile] = total

        self.line.finish(store)
        for i in range(len(self.tiles)):
            self.near_copy(i).wait_send()

    @staticmethod
    def scratch(planes, tokens, width):
        return [
            *[pltpu.VMEM((planes, tokens, width), LOW)] * 2,
            pltpu.VMEM((planes + 1, tokens, width), LOW),
        ]

    @classmethod
    def sems(cls, planes, width):
        return pairs_of(width // COLUMNS, cls.PARTS * planes, cls.PARTS * planes)


def feed_forward_kernel(
    planes, chips, width_ff, x_ref, up_ref, grads_ref, down_ref,
    out_ref, normed_ref, downs_ref, gup_ref, gdown_ref, slots_ref,
    rows, ups, grads, downs, back, act, slope, stat, stat_out, stat_in,
    normed, d_up, near_out, own, sums, gup, gdown, *sems,
):
    here = place()
    z, c, core = here
    count = 2 * planes
    me = 2 * z + core
    up, down, near, chip_sems, stat_sems, pair, rise, fall, swap_sems = [
        sems[2 * i : 2 * i + 2] for i in range(9)
    ]
    local = sems[18]
    tokens, width = x_ref.shape
    units = ups.shape[1]
    load_up = pltpu.make_async_copy(up_ref, ups, local.at[0])
    load_grads = pltpu.make_async_copy(grads_ref, grads, local.at[1])
    load_up.start()
    load_grads.start()
    barrier = pltpu.get_barrier_semaphore()
    ids = [lax.rem(me + k, count) for k in range(1, count)]
    group_peers = [(index // 2, c, lax.rem(index, 2)) for index in ids]
    peers = [*group_peers, *chip_peers(chips, here)]
    greet(barrier, peers)
    pl.semaphore_wait(barrier, len(peers))

    group = GroupGather(planes, here, x_ref, rows, up, down, near)
    group.start(local.at[2])
    keep = pltpu.make_async_copy(down_ref, downs.at[c], local.at[3])
    keep.start()
    weights = ChipGather(
        chips,
        here,
        lambda half: row_half(down_ref, half),
        lambda chip, half: row_half(downs.at[chip], half),
        chip_sems,
    )
    weights.start()
    load_up.wait()

    step = tokens
    lane = lax.broadcasted_iota(jnp.int32, (step, 128), 1)

    def forward(t):
        group.other(t)
        block = rows[t].reshape(2 * tokens, width)
        for at in range(0, units, COLUMNS):
            columns = pl.ds(at, COLUMNS)
            act[t, :, columns] = jnp.dot(block, ups[:, columns], preferred_element_type=F32)

        def some(i, carry):
            at = pl.ds(pl.multiple_of(i * step, step), step)
            value = act[t, at]
            phi = 0.5 * (1.0 + lax.erf(value * math.sqrt(0.5)))
            result = value * phi
            act[t, at] = result
            slope[t, at] = phi + value * (
                jnp.exp(value * value * -0.5) * (1.0 / math.sqrt(2.0 * math.pi))
            )
            total = jnp.sum(result, axis=1, keepdims=True)
            square = jnp.sum(result * result, axis=1, keepdims=True)
            stat[t, at] = jnp.where(lane == 0, total, jnp.where(lane == 1, square, 0.0))
            return carry

        lax.fori_loop(0, 2 * tokens // step, some, 0)

    forward(z)
    for d in range(1, planes):
        group.step(d)
        if d == 2:
            weights.relay()
        if d > 1:
            pl.when(z - d + 1 >= 0)(lambda d=d: forward(z - d + 1))
            pl.when(z + d - 1 < planes)(lambda d=d: forward(z + d - 1))
    pl.when(z - planes + 1 >= 0)(lambda: forward(z - planes + 1))
    pl.when(z + planes - 1 < planes)(lambda: forward(z + planes - 1))
    group.finish()
    keep.wait()
    load_grads.wait()
    weights.finish()
    out_downs = pltpu.make_async_copy(downs, downs_ref, local.at[4])
    out_downs.start()

    def backward(t, carry):
        block = grads[t].reshape(2 * tokens, width)
        size = units // chips
        for chip in range(chips):
            columns = pl.ds(chip * size, size)
            back[t, :, columns] = rows_product(block, downs[chip])

        def some(i, inner):
            at = pl.ds(pl.multiple_of(i * step, step), step)
            value = back[t, at]
            cross = jnp.sum(value * act[t, at], axis=1, keepdims=True)
            total = jnp.sum(value, axis=1, keepdims=True)
            stat[t, at] = jnp.where(lane == 2, cross, jnp.where(lane == 3, total, stat[t, at]))
            return inner

        lax.fori_loop(0, 2 * tokens // step, some, 0)
        for half in range(2):
            turned = stat[t, pl.ds(half * tokens, tokens)].T
            stat_out[2 * t + half] = turned[:8]
        return carry

    lax.fori_loop(0, planes, backward, 0)
    copies = [
        remote(stat_out, stat_in.at[k], stat_sems, k, device)
        for k, device in enumerate(group_peers, 1)
    ]
    for copy in copies:
        copy.start()
    for copy in copies:
        copy.wait_send()
        copy.wait_recv()

    def finish(t, carry):
        for half in range(2):
            total = stat_out[2 * t + half]
            for k in range(1, count):
                total = total + stat_in[k, 2 * t + half]
            mean, square, cross, first = (total[i : i + 1] / width_ff for i in range(4))
            scaler = lax.rsqrt(square - mean * mean + NORM_EPS)
            second = scaler * (cross - mean * first)
            figures = [scaler, -mean * scaler, scaler * first, scaler * second]
            padded = jnp.concatenate([*figures, jnp.zeros((128 - 4, tokens), F32)], axis=0)
            stat[t, pl.ds(half * tokens, tokens)] = padded.T

        def some(i, inner):
            at = pl.ds(pl.multiple_of(i * step, step), step)
            figures = stat[t, at]
            scaler, shift, first, second = (figures[:, j : j + 1] for j in range(4))
            unit = act[t, at] * scaler + shift
            normed[t, at] = unit.astype(LOW)
            d_act = back[t, at] * scaler - first - unit * second
            d_up[t, at] = (d_act * slope[t, at]).astype(LOW)
            return inner

        lax.fori_loop(0, 2 * tokens // step, some, 0)
        return carry

    lax.fori_loop(0, planes, finish, 0)
    out_normed = pltpu.make_async_copy(normed, normed_ref, local.at[5])
    out_normed.start()
    work = PairScatter(
        planes, here, Halves(d_up, tokens), ups, True, (near_out, own, sums), pair, rise, fall
    )
    work.start()

    flat_normed, flat_d_up = (
        whole[...].reshape(planes * 2 * tokens, units) for whole in (normed, d_up)
    )
    size = units // chips
    upper = share(size, 0, DOWN_FIRST)
    swap = ChipSwap(
        chips,
        here,
        lambda index: gdown.at[index, upper],
        lambda index: slots_ref.at[index, upper],
        swap_sems,
    )
    turns_left = list(range(1, work.line.steps))

    def turn():
        if turns_left:
            work.line.step(turns_left.pop(0))

    together = max(1, 256 // size)
    for chip in range(0, chips, together):
        left = flat_normed[:, chip * size : (chip + together) * size]
        for at in range(0, width, COLUMNS):
            columns = pl.ds(at, COLUMNS)
            right = grads[:, :, :, columns].reshape(planes * 2 * tokens, COLUMNS)
            term = token_product(left, right).astype(LOW)
            for i in range(together):
                gdown[chip + i, :, columns] = term[i * size : (i + 1) * size]
    swap.start(local.at[6])
    out_gdown = pltpu.make_async_copy(gdown, gdown_ref, local.at[9])
    out_gdown.start()
    chunk = gup.shape[1]
    out_gups = [
        pltpu.make_async_copy(
            gup.at[i % 2], gup_ref.at[pl.ds(i * chunk, chunk)], local.at[7 + i % 2]
        )
        for i in range(width // chunk)
    ]
    for i in range(width // chunk):
        if i == 0 or i % 2:
            turn()
        left = rows[:, :, :, pl.ds(i * chunk, chunk)].reshape(planes * 2 * tokens, chunk)
        term = token_product(left, flat_d_up).astype(LOW)
        if i > 1:
            out_gups[i - 2].wait()
        gup[i % 2] = term
        out_gups[i].start()
    while turns_left:
        turn()
    work.finish(out_ref)
    swap.finish()
    out_downs.wait()
    out_normed.wait()
    out_gdown.wait()
    for copy in out_gups[-2:]:
        copy.wait()


class Halves:
    def __init__(self, whole, tokens):
        self.whole, self.tokens = whole, tokens

    def __getitem__(self, at):
        t, core = at
        rows = pl.ds(pl.multiple_of(core * self.tokens, self.tokens), self.tokens)
        return self.whole[t, rows]


def feed_forward(planes, chips, width_ff, x_block, up_mine, grads, down_block):
    tokens, width = x_block.shape
    units = up_mine.shape[1]
    size = down_block.shape[0]
    wide = (planes, 2 * tokens, units)
    return call(
        functools.partial(feed_forward_kernel, planes, chips, width_ff),
        "feed_forward",
        [
            shape((tokens, width), F32),
            shape(wide, LOW),
            shape((chips, size, width), LOW),
            shape((width, units), LOW),
            *[shape((chips, size, width), LOW)] * 2,
        ],
        (x_block, up_mine, grads, down_block),
        [HBM] * 4,
        [VMEM, *[HBM] * 5],
        [
            pltpu.VMEM((planes, 2, tokens, width), LOW),
            pltpu.VMEM((width, units), LOW),
            pltpu.VMEM((planes, 2, tokens, width), LOW),
            pltpu.VMEM((chips, size, width), LOW),
            *[pltpu.VMEM(wide, F32)] * 3,
            pltpu.VMEM((planes, 2 * tokens, 128), F32),
            pltpu.VMEM((2 * planes, 8, 128), F32),
            pltpu.VMEM((2 * planes, 2 * planes, 8, 128), F32),
            *[pltpu.VMEM(wide, LOW)] * 2,
            *PairScatter.scratch(planes, tokens, width),
            pltpu.VMEM((2, 256, units), LOW),
            pltpu.VMEM((chips, size, width), LOW),
            *GroupGather.sems(planes),
            *pairs_of(ChipGather.count(chips), 2 * planes),
            *PairScatter.sems(planes, width),
            *pairs_of(chips),
            pltpu.SemaphoreType.DMA((10,)),
        ],
        7,
    )


def swap_lanes(values):
    lane = lax.broadcasted_iota(jnp.int32, values.shape, 1)
    return jnp.where(
        lax.rem(lane, 2) == 0,
        pltpu.roll(values, values.shape[1] - 1, 1),
        pltpu.roll(values, 1, 1),
    )


def twice(table):
    return jnp.concatenate([table, table], axis=1)


def turns(meta_ref, rows):
    cosine, sine, shrink = [twice(meta_ref[rows, pl.ds(i * HD, HD)]) for i in range(3)]
    return (cosine, sine, cosine * shrink, sine * shrink)


def allowed_block(meta_ref, rows, size, columns):
    query = rows + lax.broadcasted_iota(jnp.int32, (size, columns), 0)
    key = lax.broadcasted_iota(jnp.int32, (size, columns), 1)
    offset = meta_ref[pl.ds(rows, size), pl.ds(3 * HD, 1)].astype(jnp.int32)
    return (key <= query) & (key >= query - offset)


BLOCK = 256


def attention_forward_kernel(
    planes, chips, heads, strided,
    x_ref, meta_ref, weight_ref, scale_ref, out_ref, gain_ref, up_ref, grad_ref,
    q_ref, k_ref, v_ref, att_ref, log_ref, sum_ref,
    rows_ref, metas_ref, qkvs_ref, outs_ref, gains_ref, ups_ref, grads_ref, tiles_ref,
    qkv_ref, rows, metas, qkvs, outs, raw, wide, tile, near_out, near_in, far_out, far_in,
    *sems,
):
    here = place()
    z, c, core = here
    seqs = 2 * chips
    count = planes * seqs
    me = 2 * c + core
    flat = z * seqs + me
    groups = [sems[2 * i : 2 * i + 2] for i in range(17)]
    swap_sems, x_far, x_near, meta_far, meta_near, up, down, up_two, down_two = groups[:9]
    gain_sems, up_sems, near, far, tile_sems, grad_up, grad_down, pair = groups[9:]
    local = sems[34]
    tokens, width = x_ref.shape
    part = qkv_ref.shape[1]
    length = seqs * tokens
    span = heads * HD
    barrier = pltpu.get_barrier_semaphore()

    def device_of(k):
        other = lax.rem(flat + k, count)
        return (other // seqs, lax.rem(other, seqs) // 2, lax.rem(other, 2))

    def signal(k, carry):
        greet(barrier, [device_of(k)])
        return carry

    lax.fori_loop(1, count, signal, 0)
    scale = scale_ref[:, pl.ds(0, 1)]
    for s in range(seqs):
        for i in range(3):
            if strided:
                starts = [i * width + (t * seqs + s) * HD for t in range(planes)]
                size = span // planes
            else:
                starts, size = [i * width + s * span], span
            piece = jnp.concatenate([weight_ref[:, pl.ds(at, size)] for at in starts], axis=1)
            qkv_ref[s, :, pl.ds(i * span, span)] = (piece.astype(F32) * scale).astype(LOW)
    pl.semaphore_wait(barrier, count - 1)

    mine = pltpu.make_async_copy(qkv_ref.at[me], qkvs.at[z, me], local.at[0])
    own_out = pltpu.make_async_copy(out_ref, outs.at[z] if strided else outs, local.at[1])
    units = up_ref.shape[1]
    keeps = [
        pltpu.make_async_copy(x_ref, rows.at[me], local.at[2]),
        pltpu.make_async_copy(meta_ref, metas.at[me], local.at[3]),
        pltpu.make_async_copy(gain_ref, gains_ref.at[flat], local.at[4]),
        pltpu.make_async_copy(up_ref, column_block(ups_ref, units, c), local.at[5]),
    ]
    peers = plane_peers(chips, here)
    swaps = [
        remote(qkv_ref.at[2 * device[1] + device[2]], qkvs.at[z, me], swap_sems, k, device)
        for k, device in enumerate(peers, 1)
    ]
    mine.start()
    own_out.start()
    for copy in swaps:
        copy.start()
    gather = PlaneGather(chips, here, x_ref, rows, x_far, x_near)
    meta_gather = PlaneGather(chips, here, meta_ref, metas, meta_far, meta_near)
    for copy in keeps:
        copy.start()

    def gain_copy(k):
        return remote(gain_ref, gains_ref.at[flat], gain_sems, k, device_of(k))

    def gain_start(k, carry):
        gain_copy(k).start()
        return carry

    mine.wait()
    own_out.wait()
    for k in range(1, seqs):
        index = lax.rem(me + seqs - k, seqs)
        remote(qkv_ref.at[0], qkvs.at[z, index], swap_sems, k, here).wait_recv()
    half = seqs // 2
    line = LineGather(
        planes, here, lambda t: [qkvs.at[t, pl.ds(i * half, half)] for i in range(2)], up, down
    )
    line_two = LineGather(planes, here, lambda t: [outs.at[t]], up_two, down_two)
    line.start()
    gather.start()
    meta_gather.start()
    lax.fori_loop(1, count, gain_start, 0)
    gather.relay()
    meta_gather.relay()
    line.step(1)
    gather.forward()
    meta_gather.forward()
    ups = ChipGather(
        chips,
        here,
        lambda part: row_half(up_ref, part),
        lambda chip, part: row_half(column_block(ups_ref, units, chip), part),
        up_sems,
    )
    ups.start()
    line.step(2)
    gather.finish()
    meta_gather.finish()
    for copy in keeps:
        copy.wait()

    block = seqs * part

    def add(t, fresh=False):
        columns = pl.ds(pl.multiple_of(t * block, 128), block)
        left = rows[:, :, columns].reshape(length, block)
        for i in range(3):
            at = pl.ds(i * span, span)
            term = jnp.dot(left, qkvs[t, :, :, at].reshape(block, span), preferred_element_type=F32)
            raw[:, at] = term if fresh else raw[:, at] + term

    add(z, True)
    for d in range(1, planes):
        if d == 3:
            ups.relay()
        if d > 2:
            line.step(d)
        if d == planes - 1:
            if strided:
                line_two.start()
            group = GroupGather(planes, here, grad_ref, grads_ref, grad_up, grad_down, pair)
            group.start(local.at[6])
        pl.when(z - d >= 0)(lambda d=d: add(z - d))
        pl.when(z + d < planes)(lambda d=d: add(z + d))
    outputs = [
        pltpu.make_async_copy(rows, rows_ref, local.at[7]),
        pltpu.make_async_copy(metas, metas_ref, local.at[8]),
        pltpu.make_async_copy(qkvs, qkvs_ref, local.at[9]),
    ]
    for copy in outputs:
        copy.start()

    table = RowBlocks(metas)
    for at in range(0, length, BLOCK):
        at = pl.ds(at, BLOCK)
        tables = turns(table, at)
        for two in range(heads // 2):
            query = raw[at, pl.ds(2 * HD * two, 2 * HD)]
            query = (query * tables[0] + swap_lanes(query) * tables[1]).astype(LOW)
            key = raw[at, pl.ds(span + 2 * HD * two, 2 * HD)]
            key = (key * tables[2] + swap_lanes(key) * tables[3]).astype(LOW)
            value = raw[at, pl.ds(2 * span + 2 * HD * two, 2 * HD)].astype(LOW)
            for side in range(2):
                lanes = slice(side * HD, (side + 1) * HD)
                q_ref[2 * two + side, at] = query[:, lanes]
                k_ref[2 * two + side, at] = key[:, lanes]
                v_ref[2 * two + side, at] = value[:, lanes]
    log_ref[...] = jnp.zeros(log_ref.shape, F32)

    def one_head(head, carry):
        for start in range(0, length, BLOCK):
            columns = start + BLOCK
            at = pl.ds(start, BLOCK)
            scores = lax.dot_general(
                q_ref[head, at],
                k_ref[head, pl.ds(0, columns)],
                (((1,), (1,)), ((), ())),
                preferred_element_type=F32,
            )
            allowed = allowed_block(table, start, BLOCK, columns)
            scores = jnp.where(allowed, scores, NEG_FILL)
            top = jnp.max(scores, axis=1, keepdims=True)
            shifted = jnp.exp(scores - top)
            total = jnp.sum(shifted, axis=1, keepdims=True)
            probs = (shifted * (1.0 / total)).astype(LOW)
            wide[head, at] = jnp.dot(
                probs, v_ref[head, pl.ds(0, columns)], preferred_element_type=F32
            )
            lane = lax.broadcasted_iota(jnp.int32, (BLOCK, 128), 1)
            log_ref[at] = jnp.where(lane == head, top + jnp.log(total), log_ref[at])
        return carry

    first = 0
    for d in range(1, planes):
        last = -(-heads * d // planes)
        lax.fori_loop(first, last, one_head, 0)
        first = last
        if strided:
            line_two.step(d)
        if d == 2:
            group.step(1)
    lax.fori_loop(first, heads, one_head, 0)
    lane = lax.broadcasted_iota(jnp.int32, (tokens, 128), 1)
    column = jnp.sum(outs[...].astype(F32).reshape(span, width), axis=0, keepdims=True)
    for s in range(seqs):
        at = pl.ds(s * tokens, tokens)
        low = jnp.concatenate([wide[head, at] for head in range(heads)], axis=1).astype(LOW)
        att_ref[s] = low
        value = low.astype(F32)
        total = jnp.sum(value, axis=1, keepdims=True)
        square = jnp.sum(value * value, axis=1, keepdims=True)
        both = jnp.where(lane == 0, total, jnp.where(lane == 1, square, 0.0))
        tile[s, pl.ds(0, 8)] = both.T[:8]
        for i in range(width // 128):
            tile[s, pl.ds(8 + i, 1)] = column[:, i * 128 : (i + 1) * 128]
    out_tiles = [
        remote(tile.at[2 * device[1] + device[2]], tiles_ref.at[me], tile_sems, k, device)
        for k, device in enumerate(peers, 1)
    ]
    for copy in out_tiles:
        copy.start()
    keep = pltpu.make_async_copy(tile.at[me], tiles_ref.at[me], local.at[10])
    keep.start()
    out_outs = pltpu.make_async_copy(outs, outs_ref, local.at[11])
    out_outs.start()
    work = PlaneScatter(
        chips, here, att_ref, Flat(outs, span), False, (near_out, near_in, far_out, far_in), near, far
    )
    work.start()
    for d in range(2, planes):
        group.step(d)
    work.finish(sum_ref)
    group.finish()
    for t in range(planes):
        group.other(t)
    line.finish()
    if strided:
        line_two.finish()
    for copy in swaps:
        copy.wait_send()
    ups.finish()
    for copy in [keep, out_outs, *outputs]:
        copy.wait()
    for k in range(1, seqs):
        out_tiles[k - 1].wait_send()
        index = lax.rem(me + seqs - k, seqs)
        remote(tile.at[0], tiles_ref.at[index], tile_sems, k, here).wait_recv()

    def gain_wait(k, carry):
        gain_copy(k).wait_send()
        other = lax.rem(flat + count - k, count)
        remote(gain_ref, gains_ref.at[other], gain_sems, k, here).wait_recv()
        return carry

    lax.fori_loop(1, count, gain_wait, 0)


class Flat:
    def __init__(self, blocks, count):
        self.blocks, self.count = blocks, count

    def __getitem__(self, at):
        if len(self.blocks.shape) == 2:
            return self.blocks[at]
        _, columns = at
        return self.blocks[:, :, columns].reshape(self.count, columns.size)


class RowBlocks:
    def __init__(self, blocks):
        self.blocks = blocks

    def __getitem__(self, at):
        rows, columns = at
        size = self.blocks.shape[1]
        first, count = rows.start // size, rows.size // size
        return self.blocks[pl.ds(first, count), :, columns].reshape(rows.size, columns.size)


def attention_forward(
    planes, chips, heads, strided, x_block, meta, weight, scale, out_rows, gain_tile, up_block, grad
):
    seqs = 2 * chips
    tokens, width = x_block.shape
    part, wide = weight.shape[0], 3 * heads * HD
    units = up_block.shape[1]
    length = seqs * tokens
    span = heads * HD
    outs = (planes, *out_rows.shape) if strided else out_rows.shape
    tile = (seqs, 8 + width // 128, 128)
    return call(
        functools.partial(attention_forward_kernel, planes, chips, heads, strided),
        "attention_forward",
        [
            *[shape((heads, length, HD), LOW)] * 3,
            shape((seqs, tokens, span), LOW),
            shape((length, 128), F32),
            shape((tokens, width), F32),
            shape((seqs, tokens, width), LOW),
            shape((seqs, *meta.shape), F32),
            shape((planes, seqs, part, wide), LOW),
            shape(outs, LOW),
            shape((planes * seqs, *gain_tile.shape), F32),
            shape((width, chips * units) if units % 128 == 0 else (chips, width, units), LOW),
            shape((planes, 2, *grad.shape), LOW),
            shape(tile, F32),
        ],
        (x_block, meta, weight, scale, out_rows, gain_tile, up_block, grad),
        [HBM, HBM, VMEM, VMEM, HBM, HBM, HBM, HBM],
        [*[VMEM] * 6, *[HBM] * 8],
        [
            pltpu.VMEM((seqs, part, wide), LOW),
            pltpu.VMEM((seqs, tokens, width), LOW),
            pltpu.VMEM((seqs, *meta.shape), F32),
            pltpu.VMEM((planes, seqs, part, wide), LOW),
            pltpu.VMEM(outs, LOW),
            pltpu.VMEM((length, 3 * span), F32),
            pltpu.VMEM((heads, length, HD), F32),
            pltpu.VMEM(tile, F32),
            *PlaneScatter.scratch(chips, tokens, width),
            *pairs_of(seqs),
            *PlaneGather.sems(chips),
            *PlaneGather.sems(chips),
            *pairs_of(*[2 * planes] * 2, *[planes] * 2, planes * seqs, ChipGather.count(chips)),
            *PlaneScatter.sems(chips, width),
            *pairs_of(seqs),
            *GroupGather.sems(planes),
            pltpu.SemaphoreType.DMA((12,)),
        ],
        1,
    )


def attention_backward_kernel(
    planes, chips, heads, strided,
    x_ref, stat_ref, tile_ref, left_ref, right_ref,
    q_in, k_in, v_in, att_in, out_in, log_in, meta_in, up_ref, down_ref, _,
    tiles_ref, ffn_ref, out_ref, total_ref, slots_ref, down_slots_ref,
    rows, stats, left, right, q_ref, k_ref, v_ref, att_ref, outs, log_ref, meta_ref,
    near_out, near_own, near_sums, grad, dq, dk, dv, normed_all, own, sums, *sems,
):
    here = place()
    z, c, core = here
    seqs = 2 * chips
    count = planes * seqs
    me = 2 * c + core
    flat = z * seqs + me
    x_far, x_near, s_far, s_near, tile_sems, near, up, down, up_two, down_two, swap_sems = [
        sems[2 * i : 2 * i + 2] for i in range(11)
    ]
    down_sems = sems[22:24]
    local = sems[24]
    pairs = [
        (left_ref, left), (right_ref, right), (att_in, att_ref), (out_in, outs), (meta_in, meta_ref),
        (q_in, q_ref), (k_in, k_ref), (v_in, v_ref), (log_in, log_ref),
    ]
    loads = [pltpu.make_async_copy(*pair, local.at[i]) for i, pair in enumerate(pairs)]
    for copy in loads:
        copy.start()
    barrier = pltpu.get_barrier_semaphore()

    def device_of(k):
        other = lax.rem(flat + k, count)
        return (other // seqs, lax.rem(other, seqs) // 2, lax.rem(other, 2))

    def signal(k, carry):
        greet(barrier, [device_of(k)])
        return carry

    lax.fori_loop(1, count, signal, 0)
    pl.semaphore_wait(barrier, count - 1)
    gather = PlaneGather(chips, here, x_ref, rows, x_far, x_near)
    stat_gather = PlaneGather(chips, here, stat_ref, stats, s_far, s_near)
    gather.start()
    stat_gather.start()
    keeps = [
        pltpu.make_async_copy(x_ref, rows.at[me], local.at[9]),
        pltpu.make_async_copy(stat_ref, stats.at[me], local.at[10]),
        pltpu.make_async_copy(tile_ref.at[flat], tiles_ref.at[flat], local.at[11]),
    ]
    for copy in keeps:
        copy.start()

    def tile_copy(k):
        other = lax.rem(flat + k, count)
        return remote(tile_ref.at[other], tiles_ref.at[flat], tile_sems, k, device_of(k))

    def tile_start(k, carry):
        tile_copy(k).start()
        return carry

    lax.fori_loop(1, count, tile_start, 0)
    tokens, width = x_ref.shape
    for copy in loads[:2]:
        copy.wait()
    work = PairScatter(
        planes, here, Halves(left, tokens), right, False, (near_out, near_own, near_sums),
        near, up, down,
    )
    work.start()
    left_turns = list(range(1, work.line.steps))

    def turn(until=None):
        step = left_turns[0] + 1 if until is None and left_turns else until
        while left_turns and left_turns[0] < step:
            work.line.step(left_turns.pop(0))

    turn()
    gather.relay()
    stat_gather.relay()
    turn()
    gather.forward()
    stat_gather.forward()
    units = slots_ref.shape[2]
    upper, lower = share(width, 0, UP_FIRST), share(down_ref.shape[1], 1, DOWN_FIRST)
    swaps = [
        ChipSwap(
            chips,
            here,
            lambda index: half_block(up_ref, units, index, 0),
            lambda index: slots_ref.at[index, upper],
            swap_sems,
        ),
        ChipSwap(
            chips,
            here,
            lambda index: down_ref.at[index, lower],
            lambda index: down_slots_ref.at[index, lower],
            down_sems,
        ),
    ]
    for i, swap in enumerate(swaps):
        swap.start(local.at[12 + i])
    gather.finish()
    stat_gather.finish()
    for copy in [*loads[2:], *keeps]:
        copy.wait()
    turn()
    length, span = att_ref.shape
    part = own.shape[1]
    per = BLOCK // tokens
    for first in range(0, seqs, per):
        at = pl.ds(first * tokens, BLOCK)
        figures = stats[pl.ds(first, per)].reshape(BLOCK, 128)
        mean, scaler, one, two = (figures[:, i : i + 1] for i in range(4))
        block = rows[pl.ds(first, per)].reshape(BLOCK, width)
        d_sub = product(block, outs, slice(None), True)
        normed = (att_ref[at].astype(F32) - mean) * scaler
        normed_all[at] = normed.astype(LOW)
        d_att = (scaler * (d_sub - one - normed * two)).astype(LOW)
        for head in range(heads):
            grad[head, at] = d_att[:, head * HD : (head + 1) * HD]
    for at in range(0, width, COLUMNS):
        columns = pl.ds(at, COLUMNS)
        term = token_product(normed_all[...], rows[:, :, columns].reshape(length, COLUMNS)).astype(LOW)
        for t in range(planes):
            own[t, :, columns] = term[t * part : (t + 1) * part]
    line = LineScatter(
        planes,
        here,
        1,
        lambda p: (slice(None),),
        lambda p: [(row,) for row in row_tiles(part, 16)],
        lambda t, tile: own[(t, *tile)].astype(F32),
        sums,
        up_two,
        down_two,
    )
    if strided:
        line.step(0)
    dk[...] = jnp.zeros(dk.shape, F32)
    dv[...] = jnp.zeros(dv.shape, F32)

    def one_head(head, carry):
        for start in range(0, length, BLOCK):
            columns = start + BLOCK
            at = pl.ds(start, BLOCK)
            keys = pl.ds(0, columns)
            query, key = q_ref[head, at], k_ref[head, keys]
            out_grad = grad[head, at]
            scores = lax.dot_general(
                query, key, (((1,), (1,)), ((), ())), preferred_element_type=F32
            )
            allowed = allowed_block(meta_ref, start, BLOCK, columns)
            lane = lax.broadcasted_iota(jnp.int32, (BLOCK, 128), 1)
            log_total = jnp.sum(jnp.where(lane == head, log_ref[at], 0.0), axis=1, keepdims=True)
            probs = jnp.where(allowed, jnp.exp(scores - log_total), 0.0)
            d_probs = lax.dot_general(
                out_grad, v_ref[head, keys], (((1,), (1,)), ((), ())), preferred_element_type=F32
            )
            delta = jnp.sum(probs * d_probs, axis=1, keepdims=True)
            d_scores = (probs * (d_probs - delta)).astype(LOW)
            dq[head, at] = jnp.dot(d_scores, key, preferred_element_type=F32)
            dk[head, keys] += token_product(d_scores, query)
            dv[head, keys] += token_product(probs.astype(LOW), out_grad)
        return carry

    first = 0
    for i in range(1, planes - 1):
        last = -(-heads * i // (planes - 1))
        lax.fori_loop(first, last, one_head, 0)
        first = last
        turn()
        if strided:
            line.step(i)
    lax.fori_loop(first, heads, one_head, 0)
    turn(work.line.steps)
    for start in range(0, length, BLOCK):
        at = pl.ds(start, BLOCK)
        tables = turns(meta_ref, at)
        for two in range(heads // 2):
            both = [
                jnp.concatenate([whole[2 * two, at], whole[2 * two + 1, at]], axis=1).astype(LOW)
                for whole in (dq, dk, dv)
            ]
            query, key = both[0].astype(F32), both[1].astype(F32)
            query = query * tables[0] + swap_lanes(query * tables[1])
            key = key * tables[2] + swap_lanes(key * tables[3])
            out_ref[at, pl.ds(2 * HD * two, 2 * HD)] = query.astype(LOW)
            out_ref[at, pl.ds(span + 2 * HD * two, 2 * HD)] = key.astype(LOW)
            out_ref[at, pl.ds(2 * span + 2 * HD * two, 2 * HD)] = both[2]
    work.finish(ffn_ref)
    if strided:

        def store(tile, total):
            total_ref[tile] = total

        line.finish(store)
    else:
        for t in range(planes):
            total_ref[pl.ds(t * part, part)] = own[t].astype(F32)
    for swap in swaps:
        swap.finish()

    def tile_wait(k, carry):
        tile_copy(k).wait_send()
        other = lax.rem(flat + count - k, count)
        remote(tile_ref.at[0], tiles_ref.at[other], tile_sems, k, here).wait_recv()
        return carry

    lax.fori_loop(1, count, tile_wait, 0)


def attention_backward(planes, chips, heads, strided, part, units, args):
    tokens, width = args[0].shape
    seqs = 2 * chips
    length, span = args[8].shape
    kept = [pltpu.VMEM(args[i].shape, args[i].dtype) for i in (3, 4, 5, 6, 7, 8, 9, 10, 11)]
    return call(
        functools.partial(attention_backward_kernel, planes, chips, heads, strided),
        "attention_backward",
        [
            shape(args[2].shape, F32),
            shape((tokens, width), F32),
            shape((length, 3 * span), LOW),
            shape((part if strided else span, width), F32),
            shape((chips, width, units), LOW),
            shape(args[14].shape, LOW),
        ],
        args,
        [HBM] * 15,
        [HBM, VMEM, VMEM, VMEM, HBM, HBM],
        [
            pltpu.VMEM((seqs, tokens, width), LOW),
            pltpu.VMEM((seqs, tokens, 128), F32),
            *kept,
            *PairScatter.scratch(planes, tokens, width),
            pltpu.VMEM((heads, length, HD), LOW),
            *[pltpu.VMEM((heads, length, HD), F32)] * 3,
            pltpu.VMEM((length, span), LOW),
            pltpu.VMEM((planes, part, width), LOW),
            pltpu.VMEM((planes + 1, part, width), LOW),
            *PlaneGather.sems(chips),
            *PlaneGather.sems(chips),
            *pairs_of(planes * seqs),
            *PairScatter.sems(planes, width),
            *pairs_of(planes, planes, chips, chips),
            pltpu.SemaphoreType.DMA((14,)),
        ],
        2,
        {14: 5},
    )


def body(
    hidden_in,
    segment_ids,
    position_ids,
    w_qkv,
    w_out,
    w_up,
    w_down,
    gain_attn,
    gain_attn_sub,
    gain_ffn,
    gain_ffn_sub,
    ema_qkv,
    ema_out,
    ema_up,
    ema_down,
    ema_gain_attn,
    ema_gain_attn_sub,
    ema_gain_ffn,
    ema_gain_ffn_sub,
    out_grad,
):
    _, tokens, width = hidden_in.shape
    planes, chips = lax.axis_size("dp"), lax.axis_size("chip")
    seqs = 2 * chips
    length = tokens * seqs
    heads = HEADS // seqs
    span = heads * HD
    part = w_qkv.shape[0]
    strided = part % HD == 0
    width_ff = w_down.shape[0] * planes * seqs
    seq_index = lax.axis_index(SEQ)

    def gain_rows(weight, gain):
        return (weight.astype(F32) * gain.astype(F32)[:, None]).astype(LOW)

    out_scaled = gain_rows(w_out, gain_attn_sub)
    down_scaled = gain_rows(w_down, gain_ffn_sub)
    x_in = hidden_in[0].astype(F32)
    normed_one, scaler_one = moments(x_in)
    normed_low = normed_one.astype(LOW)
    qkv_gain = jnp.broadcast_to(gain_attn.astype(F32)[:, None], (part, 128))
    gain_tile = jnp.zeros((8, 128), F32).at[0, :part].set(gain_ffn.astype(F32))

    if not strided:
        out_all = lax.all_gather(out_scaled, ALL, axis=0, tiled=True)
        out_scaled = lax.dynamic_slice_in_dim(out_all, seq_index * span, span, axis=0)

    grad_low = out_grad[0]
    (
        queries, keys, values, attended, log_total, out_sum,
        row_in, meta, qkv_mine, out_mine, gain_tiles, up_mine, grad_flat, tiles,
    ) = attention_forward(
        planes,
        chips,
        heads,
        strided,
        normed_low,
        token_tables(position_ids[0]),
        w_qkv,
        qkv_gain,
        out_scaled,
        gain_tile,
        w_up,
        grad_low,
    )
    if up_mine.ndim == 3:
        up_mine = up_mine.transpose(1, 0, 2).reshape(width, -1)
    row_in = row_in.reshape(length, width)
    meta = meta.reshape(length, -1)
    qkv_mine = qkv_mine.reshape(width, 3 * span)
    out_mine = out_mine.reshape(span, width)
    attended = attended.reshape(length, span)
    tiles = jnp.sum(tiles, axis=0)
    column_sum = tiles[8:].reshape(width)
    sums = tiles[:2].T
    gain_three = gain_tiles[:, 0, :part].reshape(width)
    mean_two = sums[:, :1] / width
    scaler_two = lax.rsqrt(sums[:, 1:] / width - mean_two * mean_two + NORM_EPS)
    projected = scaler_two * (out_sum - mean_two * column_sum[None, :])
    hmid = x_in + projected
    normed_three, scaler_three = moments(hmid)
    ffn_in = (normed_three * gain_three).astype(LOW)

    grad_top = grad_low.astype(F32)
    units = w_up.shape[1]
    d_ffn_in, normed_four, down_mine, grad_up, grad_down, down_slots = feed_forward(
        planes, chips, width_ff, ffn_in, up_mine, grad_flat, down_scaled
    )
    down_mine = down_mine.reshape(-1, width)
    if units % 128:
        grad_up = grad_up.reshape(width, chips, units).transpose(1, 0, 2)

    gain_part = jnp.sum(d_ffn_in * normed_three, axis=0).reshape(planes * seqs, 1, part)
    gain_part = jnp.pad(gain_part, ((0, 0), (0, 7), (0, 128 - part)))
    d_hmid = grad_top + norm_back(d_ffn_in * gain_three, normed_three, scaler_three)
    d_hmid_low = d_hmid.astype(LOW)
    d_hmid_wide = d_hmid_low.astype(F32)
    first_two = jnp.sum(d_hmid_wide * column_sum[None, :], axis=1, keepdims=True) / width
    second_two = jnp.sum(d_hmid_wide * projected, axis=1, keepdims=True) / width
    token_stats = jnp.concatenate([mean_two, scaler_two, first_two, second_two], axis=1)
    gain_part, ffn_out, d_qkv, sum_out, up_slots, down_slots = attention_backward(
        planes,
        chips,
        heads,
        strided,
        part,
        units,
        (
            d_hmid_low,
            jnp.pad(token_stats, ((0, 0), (0, 124))),
            gain_part,
            normed_four,
            down_mine,
            queries,
            keys,
            values,
            attended,
            out_mine,
            log_total,
            meta,
            grad_up,
            grad_down,
            down_slots,
        ),
    )
    output = (hmid + ffn_out).astype(LOW)[None]
    grad_gain_three = jnp.sum(gain_part, axis=0)[0, :part]
    d_in, sum_qkv, grad_gain_one, up_slots = in_scatter(
        planes,
        chips,
        heads,
        strided,
        d_qkv.reshape(seqs, tokens, 3 * span),
        qkv_mine,
        row_in,
        grad_up,
        w_qkv,
        qkv_gain,
        up_slots,
    )
    grad_gain_one = grad_gain_one[:, 0]
    sum_up = jnp.sum(up_slots.astype(F32), axis=0)
    sum_down = jnp.sum(down_slots.astype(F32), axis=0)
    input_grad = (d_hmid + norm_back(d_in, normed_one, scaler_one)).astype(LOW)[None]

    if not strided:
        spread = lax.dynamic_update_slice_in_dim(
            jnp.zeros((width, width), LOW), sum_out.astype(LOW), seq_index * span, axis=0
        )
        sum_out = lax.psum_scatter(spread, ALL, scatter_dimension=0, tiled=True).astype(F32)

    def finish(total, weight, gain):
        wide = weight.astype(F32)
        return (total * gain.astype(F32)[:, None], jnp.sum(total * wide, axis=1))

    sum_out, grad_gain_two = finish(sum_out, w_out, gain_attn_sub)
    sum_down, grad_gain_four = finish(sum_down, w_down, gain_ffn_sub)

    def averaged(average, weight):
        return EMA_DECAY * average + (1.0 - EMA_DECAY) * weight.astype(F32)

    return (
        output,
        input_grad,
        sum_qkv,
        sum_out,
        sum_up,
        sum_down,
        grad_gain_one,
        grad_gain_two,
        grad_gain_three,
        grad_gain_four,
        averaged(ema_qkv, w_qkv),
        averaged(ema_out, w_out),
        averaged(ema_up, w_up),
        averaged(ema_down, w_down),
        averaged(ema_gain_attn, gain_attn),
        averaged(ema_gain_attn_sub, gain_attn_sub),
        averaged(ema_gain_ffn, gain_ffn),
        averaged(ema_gain_ffn_sub, gain_ffn_sub),
    )


def solution(mesh):
    split = Mesh(
        mesh.devices.reshape(mesh.shape["dp"], mesh.shape["seq"] // 2, 2), ("dp", "chip", "core")
    )
    tokens = P("dp", SEQ, None)
    ids = P("dp", SEQ)
    rows = P(ALL, None)
    columns = P(None, ALL)
    vector = P(ALL)
    weights = (rows, rows, columns, rows)
    gains = (vector,) * 4
    return jax.shard_map(
        body,
        mesh=split,
        in_specs=(tokens, ids, ids, *weights, *gains, *weights, *gains, tokens),
        out_specs=(tokens, tokens, *weights, *gains, *weights, *gains),
        check_vma=False,
    )
```
